32 devices in a mesh: batch: 4 (over y, x), seq: 8 (over z, core).
Axes of the slice: x: 2, y: 2, z: 4, core: 2. Of those that a mesh axis runs over, the one named last changes fastest.
Arguments:
- tokens: bfloat16 [2, 4, 1536, 512], P(None, 'batch', 'seq'), may hold values from -6 to 6
- lengths: int32 [2, 4, 2], P(None, 'batch'), may hold values from 499 to 1032, as said below
- ln1_gain: bfloat16 [512], P(('batch', 'seq')), may hold values from 0.5 to 1.5
- ln1_bias: bfloat16 [512], P(('batch', 'seq')), may hold values from -4 to 4
- w_query: bfloat16 [512, 512], P(('batch', 'seq')), may hold values from -0.25 to 0.25
- w_key: bfloat16 [512, 512], P(('batch', 'seq')), may hold values from -0.25 to 0.25
- w_value: bfloat16 [512, 512], P(('batch', 'seq')), may hold values from -0.25 to 0.25
- conv_key: bfloat16 [3, 512, 512], P(None, ('batch', 'seq')), may hold values from -0.15625 to 0.15625
- conv_value: bfloat16 [3, 512, 512], P(None, ('batch', 'seq')), may hold values from -0.15625 to 0.15625
- w_out: bfloat16 [512, 512], P(('batch', 'seq')), may hold values from -0.75 to 0.75
- ln2_gain: bfloat16 [512], P(('batch', 'seq')), may hold values from 0.5 to 1.5
- ln2_bias: bfloat16 [512], P(('batch', 'seq')), may hold values from -4 to 4
- w_up: bfloat16 [512, 2048], P(('batch', 'seq')), may hold values from -0.25 to 0.25
- b_up: bfloat16 [2048], P(('batch', 'seq')), may hold values from -6 to 6
- w_down: bfloat16 [2048, 512], P(('batch', 'seq')), may hold values from -0.125 to 0.125
- b_down: bfloat16 [512], P(('batch', 'seq')), may hold values from -4 to 4
- cotangent: bfloat16 [2, 4, 1536, 512], P(None, 'batch', 'seq'), may hold values from -6 to 6
Outputs:
- layer_out: bfloat16 [2, 4, 1536, 512], P(None, 'batch', 'seq')
- input_grad: bfloat16 [2, 4, 1536, 512], P(None, 'batch', 'seq')
- grad_ln1_gain: float32 [512], P(('batch', 'seq'))
- grad_ln1_bias: float32 [512], P(('batch', 'seq'))
- grad_w_query: float32 [512, 512], P(('batch', 'seq'))
- grad_w_key: float32 [512, 512], P(('batch', 'seq'))
- grad_w_value: float32 [512, 512], P(('batch', 'seq'))
- grad_conv_key: float32 [3, 512, 512], P(None, ('batch', 'seq'))
- grad_conv_value: float32 [3, 512, 512], P(None, ('batch', 'seq'))
- grad_w_out: float32 [512, 512], P(('batch', 'seq'))
- grad_ln2_gain: float32 [512], P(('batch', 'seq'))
- grad_ln2_bias: float32 [512], P(('batch', 'seq'))
- grad_w_up: float32 [512, 2048], P(('batch', 'seq'))
- grad_b_up: float32 [2048], P(('batch', 'seq'))
- grad_w_down: float32 [2048, 512], P(('batch', 'seq'))
- grad_b_down: float32 [512], P(('batch', 'seq'))
The draws below stay inside these ranges and needn't reach their ends.
Inputs may be any that keep to these rules, and one draw needn't show every extreme that they name: Each row holds two items; their lengths padded up to multiples of 3 sum to 1533. The shorter one, first or second, has a padded length of 3 * min(167, 170) or more and at most half of 1533.
All inputs are finite; a program needn't handle non-finite values.
Results may differ from the reference program's by a relative error of at most 0.019.
Values may be sent and summed in bfloat16 or wider, within the bound.
No kernel may reach another device: no remote copies, remote signals or barrier semaphores. Data moves between devices by JAX's collectives and lax.ppermute only.
A program may use at most 128 MiB of HBM per device.

```python
import math
import jax
import jax.numpy as jnp
from jax import lax

D = 512
HEADS = 8
HEAD_DIM = 64
FF = 2048
MICRO = 2
ITEMS = 2
ROWS = 4
ROW_LEN = 1536
MEMORY = 512


def draw_lengths(key, part):
    key = jax.random.fold_in(key, 7)
    key_pad, key_trim, key_order = jax.random.split(key, 3)
    least_third = min(167, ROW_LEN // 9)
    most_third = (ROW_LEN - 3) // 6
    small_pad = 3 * jax.random.randint(key_pad, (MICRO, ROWS), least_third, most_third + 1)
    small_pad = small_pad.at[0, 0].set(3 * least_third)
    large_pad = ROW_LEN - 3 - small_pad
    trims = jax.random.randint(key_trim, (MICRO, ROWS, 2), 0, 3)
    trims = trims.at[0, 0, 0].set(2)
    trims = trims.at[0, 0, 1].set(0)
    small_len = small_pad - trims[..., 0]
    large_len = large_pad - trims[..., 1]
    large_first = jax.random.randint(key_order, (MICRO, ROWS), 0, 2)
    first_len = jnp.where(large_first == 1, large_len, small_len)
    second_len = jnp.where(large_first == 1, small_len, large_len)
    return jnp.stack([first_len, second_len], axis=-1).astype(jnp.int32)


def block_levels(own_key, extent, shards, low, largest):
    def one(axis_at, blocks):
        draws = jax.random.uniform(jax.random.fold_in(jax.random.fold_in(own_key, 6), axis_at), (blocks,), jnp.float32, low / len(shards), largest / len(shards))
        return jnp.repeat(jnp.exp(draws), extent[axis_at] // blocks).reshape((-1,) + (1,) * (len(extent) - axis_at - 1))

    loudness = one(*shards[0])
    for cut in shards[1:]:
        loudness = loudness * one(*cut)
    return loudness


def bell_draw(key, shape, width, most, shards=(), kind=jnp.bfloat16):
    array = width * jax.random.normal(key, shape, jnp.float32)
    if shards:
        array = array * block_levels(key, shape, shards, -0.22, 0.18)
    return jnp.clip(array, -most, most).astype(kind)


def setup_inputs(seed: int = 0) -> dict:
    key_of = jax.random.split(jax.random.key(seed), 18)
    return {
        "tokens": bell_draw(key_of[0], (MICRO, ROWS, ROW_LEN, D), 1.0, 6.0, ((1, 4), (2, 8))),
        "lengths": draw_lengths(jax.random.fold_in(key_of[17], 71), 0),
        "ln1_gain": jnp.clip(1.0 + 0.1 * jax.random.normal(key_of[2], (D,), jnp.float32), 0.5, 1.5).astype(jnp.bfloat16),
        "ln1_bias": bell_draw(key_of[3], (D,), 0.3, 4.0, ((0, 32),)),
        "w_query": bell_draw(key_of[4], (D, D), D ** -0.5, 0.25, ((0, 32),)),
        "w_key": bell_draw(key_of[5], (D, D), D ** -0.5, 0.25, ((0, 32),)),
        "w_value": bell_draw(key_of[6], (D, D), D ** -0.5, 0.25, ((0, 32),)),
        "conv_key": bell_draw(key_of[7], (3, D, D), (3 * D) ** -0.5, 0.15625, ((1, 32),)),
        "conv_value": bell_draw(key_of[8], (3, D, D), (3 * D) ** -0.5, 0.15625, ((1, 32),)),
        "w_out": bell_draw(key_of[9], (D, D), (D // 8) ** -0.5, 0.75, ((0, 32),)),
        "ln2_gain": jnp.clip(1.0 + 0.1 * jax.random.normal(key_of[10], (D,), jnp.float32), 0.5, 1.5).astype(jnp.bfloat16),
        "ln2_bias": bell_draw(key_of[11], (D,), 0.3, 4.0, ((0, 32),)),
        "w_up": bell_draw(key_of[12], (D, FF), D ** -0.5, 0.25, ((0, 32),)),
        "b_up": bell_draw(key_of[13], (FF,), 0.5, 6.0, ((0, 32),)),
        "w_down": bell_draw(key_of[14], (FF, D), FF ** -0.5, 0.125, ((0, 32),)),
        "b_down": bell_draw(key_of[15], (D,), 0.3, 4.0, ((0, 32),)),
        "cotangent": bell_draw(key_of[16], (MICRO, ROWS, ROW_LEN, D), 1.0, 6.0, ((1, 4), (2, 8))),
    }


@jax.custom_vjp
def low(v):
    return lax.optimization_barrier(v.astype(jnp.bfloat16)).astype(jnp.float32)

@jax.custom_vjp
def low_back(v):
    return v

def low_keep(v):
    return (low(v), None)

def low_pass(kept, grad):
    return (grad,)

def back_keep(v):
    return (v, None)

def back_low(kept, grad):
    return (low(grad),)
low.defvjp(low_keep, low_pass)
low_back.defvjp(back_keep, back_low)
EPSILON = 1e-06
PRECISE = lax.Precision.HIGHEST

def layer_norm(field_in, norm_gain, norm_bias):
    center = field_in - lax.optimization_barrier(jnp.mean(field_in, axis=-1, keepdims=True))
    spread = lax.optimization_barrier(jnp.mean(center * center, axis=-1, keepdims=True))
    return center * lax.rsqrt(spread + EPSILON) * norm_gain + norm_bias

def gelu_exact(field_in):
    return jax.nn.gelu(field_in, approximate=False)

def item_layout(row_lengths, positions):
    first_len = row_lengths[0]
    second_len = row_lengths[1]
    first_pad = 3 * ((first_len + 2) // 3)
    second_start = 1 + first_pad
    second_pad = 3 * ((second_len + 2) // 3)
    tail_start = second_start + second_pad
    segment = (positions >= 1).astype(jnp.int32) + (positions >= second_start).astype(jnp.int32) + (positions >= tail_start).astype(jnp.int32)
    valid_mask = (positions >= 1) & (positions < 1 + first_len) | (positions >= second_start) & (positions < second_start + second_len)
    return (segment, valid_mask)

def compress(kept_rows, kernel):
    windows = jnp.concatenate([jnp.zeros((2, D), jnp.float32), kept_rows[:ROW_LEN - 2]], axis=0).reshape(ROW_LEN // 3, 3 * D)
    return low(low_back(jnp.dot(windows, kernel.reshape(3 * D, D), precision=PRECISE)))

def row_forward(params, row_input, row_lengths):
    ln1_gain, ln1_bias, w_query, w_key, w_value, conv_key, conv_value, w_out, ln2_gain, ln2_bias, w_up, b_up, w_down, b_down = params
    positions = jnp.arange(ROW_LEN, dtype=jnp.int32)
    segment, valid_mask = item_layout(row_lengths, positions)
    valid_f = valid_mask.astype(jnp.float32)[:, None]
    normed = low(layer_norm(row_input, ln1_gain, ln1_bias))
    queries = low(low_back(jnp.dot(normed, w_query, precision=PRECISE)))
    keys_raw = low_back(jnp.dot(normed, w_key, precision=PRECISE))
    values_raw = low_back(jnp.dot(normed, w_value, precision=PRECISE))
    key_kept = low(keys_raw * valid_f)
    value_kept = low(values_raw * valid_f)
    memory_key = compress(key_kept, conv_key).reshape(MEMORY, HEADS, HEAD_DIM)
    memory_value = compress(value_kept, conv_value).reshape(MEMORY, HEADS, HEAD_DIM)
    block_ends = 3 * jnp.arange(MEMORY, dtype=jnp.int32)
    memory_segment, ignored_mask = item_layout(row_lengths, block_ends)
    query_block = math.gcd(ROW_LEN, 512)
    score_scale = HEAD_DIM ** (-0.5)

    def attend_block(block_index):
        block_start = (block_index * query_block).astype(jnp.int32)
        query_rows = lax.dynamic_slice_in_dim(queries, block_start, query_block, 0).reshape(query_block, HEADS, HEAD_DIM)
        key_rows = lax.dynamic_slice_in_dim(key_kept, block_start, query_block, 0).reshape(query_block, HEADS, HEAD_DIM)
        value_rows = lax.dynamic_slice_in_dim(value_kept, block_start, query_block, 0).reshape(query_block, HEADS, HEAD_DIM)
        place_rows = lax.dynamic_slice_in_dim(positions, block_start, query_block, 0)
        segment_rows = lax.dynamic_slice_in_dim(segment, block_start, query_block, 0)
        mem_scores = jnp.einsum('thd,jhd->thj', query_rows, memory_key, precision=PRECISE) * score_scale
        allowed = (block_ends[None, :] <= place_rows[:, None]) & (memory_segment[None, :] == segment_rows[:, None])
        mem_scores = jnp.where(allowed[:, None, :], mem_scores, -1000000000.0)
        self_scores = lax.optimization_barrier(jnp.sum(query_rows * key_rows, axis=-1)) * score_scale
        all_scores = low_back(jnp.concatenate([mem_scores, self_scores[..., None]], axis=-1))
        row_top = lax.optimization_barrier(jnp.max(all_scores, axis=-1, keepdims=True))
        expos = jnp.exp(all_scores - row_top)
        probs_f = expos / lax.optimization_barrier(jnp.sum(expos, axis=-1, keepdims=True))
        mixed = jnp.einsum('thj,jhd->thd', low(probs_f[..., :MEMORY]), memory_value, precision=PRECISE)
        mixed = mixed + probs_f[..., MEMORY:] * value_rows
        return mixed.reshape(query_block, D)
    attended = lax.map(jax.checkpoint(attend_block), jnp.arange(ROW_LEN // query_block, dtype=jnp.int32))
    attended = low_back(attended.reshape(ROW_LEN, D))
    branch = low_back(jnp.dot(low(attended), w_out, precision=PRECISE))
    middle = row_input + branch
    normed2 = low(layer_norm(middle, ln2_gain, ln2_bias))
    hidden = low_back(jnp.dot(normed2, w_up, precision=PRECISE) + b_up)
    active = low(gelu_exact(hidden))
    ff_out = low_back(jnp.dot(active, w_down, precision=PRECISE) + b_down)
    return middle + ff_out

def reference(tokens, lengths, ln1_gain, ln1_bias, w_query, w_key, w_value, conv_key, conv_value, w_out, ln2_gain, ln2_bias, w_up, b_up, w_down, b_down, cotangent):
    params = tuple((weight_arg.astype(jnp.float32) for weight_arg in (ln1_gain, ln1_bias, w_query, w_key, w_value, conv_key, conv_value, w_out, ln2_gain, ln2_bias, w_up, b_up, w_down, b_down)))
    rows_in = tokens.astype(jnp.float32).reshape(MICRO * ROWS, ROW_LEN, D)
    row_lengths = lengths.reshape(MICRO * ROWS, ITEMS)

    def whole(params_in, inputs_in):

        def one_row(row_pair):
            return row_forward(params_in, row_pair[0], row_pair[1])
        return lax.map(jax.checkpoint(one_row), (inputs_in, row_lengths))
    outputs, pullback = jax.vjp(whole, params, rows_in)
    weight_grads, input_grads = pullback(cotangent.astype(jnp.float32).reshape(MICRO * ROWS, ROW_LEN, D))
    shape_out = (MICRO, ROWS, ROW_LEN, D)
    return (outputs.reshape(shape_out).astype(jnp.bfloat16), input_grads.reshape(shape_out).astype(jnp.bfloat16), weight_grads[0], weight_grads[1], weight_grads[2], weight_grads[3], weight_grads[4], weight_grads[5], weight_grads[6], weight_grads[7], weight_grads[8], weight_grads[9], weight_grads[10], weight_grads[11], weight_grads[12], weight_grads[13])
```

```python
import jax
import jax.numpy as jnp
from jax import lax
from jax.sharding import PartitionSpec as P

HEADS = 8
HEAD_DIM = 64
EPSILON = 1e-06
AXES = ("batch", "seq")
F32 = jnp.float32
BF16 = jnp.bfloat16


def device_count():
    return lax.axis_size("batch") * lax.axis_size("seq")


def device_index():
    return lax.axis_index("batch") * lax.axis_size("seq") + lax.axis_index("seq")


def gather_order():
    count, seq = device_count(), lax.axis_size("seq")
    masks = []
    bit = seq // 2
    while bit > 1:
        masks.append(bit)
        bit //= 2
    bit = seq
    while bit < count:
        masks.append(bit)
        bit *= 2
    return masks + [1]


def bit_axis(mask):
    return device_count().bit_length() - 1 - mask.bit_length()


def swap(array, mask):
    count = device_count()
    return lax.ppermute(array, AXES, [(i, i ^ mask) for i in range(count)])


def gather_rows(rows):
    count, me = device_count(), device_index()
    bits = count.bit_length() - 1
    held = rows.reshape((1,) * bits + rows.shape)
    for mask in gather_order():
        axis = bit_axis(mask)
        other = swap(held, mask)
        upper = (me & mask) != 0
        held = jnp.concatenate(
            [jnp.where(upper, other, held), jnp.where(upper, held, other)], axis=axis
        )
    return held.reshape((count,) + rows.shape)


def reduce_rows(blocks):
    count, me = device_count(), device_index()
    bits = count.bit_length() - 1
    held = blocks.reshape((2,) * bits + blocks.shape[1:])
    for mask in reversed(gather_order()):
        axis = bit_axis(mask)
        upper = ((me & mask) != 0).astype(jnp.int32)
        send = lax.dynamic_slice_in_dim(held, 1 - upper, 1, axis)
        keep = lax.dynamic_slice_in_dim(held, upper, 1, axis)
        total = keep.astype(F32) + swap(send, mask).astype(F32)
        held = total.astype(BF16)
    return total.reshape(blocks.shape[1:])


def layer_norm(field_in, norm_gain, norm_bias):
    center = field_in - jnp.mean(field_in, axis=-1, keepdims=True)
    spread = jnp.mean(center * center, axis=-1, keepdims=True)
    return center * lax.rsqrt(spread + EPSILON) * norm_gain + norm_bias


def gelu_exact(field_in):
    return jax.nn.gelu(field_in, approximate=False)


def item_layout(lengths, positions):
    first_len = lengths[:, 0:1]
    second_len = lengths[:, 1:2]
    first_pad = 3 * ((first_len + 2) // 3)
    second_start = 1 + first_pad
    second_pad = 3 * ((second_len + 2) // 3)
    tail_start = second_start + second_pad
    positions = positions[None, :]
    segment = (
        (positions >= 1).astype(jnp.int32)
        + (positions >= second_start).astype(jnp.int32)
        + (positions >= tail_start).astype(jnp.int32)
    )
    valid_mask = (positions >= 1) & (positions < 1 + first_len) | (positions >= second_start) & (
        positions < second_start + second_len
    )
    return (segment, valid_mask)


def dot(a, b, dims=((1,), (0,))):
    return lax.dot_general(a, b, (dims, ((), ())), preferred_element_type=F32)


TN = ((0,), (0,))
NT = ((1,), (1,))


def per_device(
    tokens,
    lengths,
    ln1_gain,
    ln1_bias,
    w_query,
    w_key,
    w_value,
    conv_key,
    conv_value,
    w_out,
    ln2_gain,
    ln2_bias,
    w_up,
    b_up,
    w_down,
    b_down,
    cotangent,
):
    count = device_count()
    micro, _, tok, width = tokens.shape
    ff = w_up.shape[1]
    wide = ff // width
    share = width // count
    seq = lax.axis_size("seq")
    slots = tok // 3
    memory_len = slots * seq
    lengths = lengths[:, 0]

    vectors = jnp.concatenate([ln1_gain, ln1_bias, ln2_gain, ln2_bias, b_down, b_up])
    vector_rows = jnp.zeros((16, width), BF16).at[0, : vectors.shape[0]].set(vectors)
    first = gather_rows(jnp.concatenate([w_query, w_key, w_value, vector_rows], axis=0))
    up_tiles = [w_up[:, width * c : width * (c + 1)] for c in range(wide)]
    rest = jnp.concatenate(
        [conv_key[i] for i in range(3)]
        + [conv_value[i] for i in range(3)]
        + [w_out]
        + up_tiles
        + [w_down],
        axis=0,
    )
    rest = lax.all_gather(rest, AXES, axis=0, tiled=False)

    def tile(buffer, number):
        return buffer[:, share * number : share * (number + 1)].reshape(width, width)

    w_query, w_key, w_value = (tile(first, i) for i in range(3))
    vectors = first[:, 3 * share, :]

    def vector(number, length=share):
        return vectors[:, share * number : share * number + length].reshape(-1).astype(F32)

    ln1_gain, ln1_bias, ln2_gain, ln2_bias, b_down = (vector(i) for i in range(5))
    b_up = vector(5, ff // count)
    conv_key = jnp.concatenate([tile(rest, i) for i in range(3)], axis=0)
    conv_value = jnp.concatenate([tile(rest, i) for i in range(3, 6)], axis=0)
    w_out = tile(rest, 6)
    w_up = jnp.concatenate([tile(rest, 7 + i) for i in range(wide)], axis=1)
    w_down = rest[:, share * (7 + wide) :].reshape(ff, width)

    positions = lax.axis_index("seq") * tok + jnp.arange(tok, dtype=jnp.int32)
    segment, valid_mask = item_layout(lengths, positions)
    block_ends = 3 * jnp.arange(memory_len, dtype=jnp.int32)
    memory_segment, _ = item_layout(lengths, block_ends)
    valid_f = valid_mask.astype(F32).reshape(-1, 1)
    scale = HEAD_DIM ** (-0.5)

    inputs_f = tokens.reshape(micro * tok, width).astype(F32)
    cot = cotangent.reshape(micro * tok, width)
    normed_f, norm1_pull = jax.vjp(layer_norm, inputs_f, ln1_gain, ln1_bias)
    normed = normed_f.astype(BF16)
    queries = dot(normed, w_query).astype(BF16)
    key_kept = (dot(normed, w_key) * valid_f).astype(BF16)
    value_kept = (dot(normed, w_value) * valid_f).astype(BF16)
    kept = jnp.stack([key_kept, value_kept]).reshape(2, micro, tok, width)
    rim = lax.ppermute(kept[:, :, tok - 2 :], "seq", [(i, i + 1) for i in range(seq - 1)])
    windows = jnp.concatenate([rim, kept[:, :, : tok - 2]], axis=2).reshape(
        2, micro * slots, 3 * width
    )
    memory_own = jnp.stack([dot(windows[0], conv_key), dot(windows[1], conv_value)]).astype(BF16)
    memory = lax.all_gather(
        memory_own.reshape(2, micro, slots, width), "seq", axis=0, tiled=False
    )
    memory = memory.transpose(1, 2, 0, 3, 4).reshape(2, micro, memory_len, HEADS, HEAD_DIM)

    def heads(array):
        return array.reshape(micro, tok, HEADS, HEAD_DIM)

    query_heads, key_heads, value_heads = heads(queries), heads(key_kept), heads(value_kept)
    self_scores = jnp.einsum("mthd,mthd->mth", query_heads, key_heads, preferred_element_type=F32)
    self_scores = self_scores * scale
    scores = jnp.einsum("mthd,mjhd->mhtj", query_heads, memory[0], preferred_element_type=F32)
    allowed = (block_ends[None, None, :] <= positions[None, :, None]) & (
        memory_segment[:, None, :] == segment[:, :, None]
    )
    scores = jnp.where(allowed[:, None], scores * scale, -1000000000.0)
    self_t = self_scores.transpose(0, 2, 1)
    top = jnp.maximum(jnp.max(scores, axis=-1), self_t)
    expos = jnp.exp(scores - top[..., None])
    self_expo = jnp.exp(self_t - top)
    total = self_expo + jnp.sum(expos, axis=-1)
    probs = expos / total[..., None]
    probs_low = probs.astype(BF16)
    self_weight = (self_expo / total).transpose(0, 2, 1)
    attended = jnp.einsum("mhtj,mjhd->mthd", probs_low, memory[1], preferred_element_type=F32)
    attended = attended + self_weight[..., None] * value_heads.astype(F32)
    attended_low = attended.reshape(micro * tok, width).astype(BF16)
    middle = inputs_f + dot(attended_low, w_out)
    normed2_f, norm2_pull = jax.vjp(layer_norm, middle, ln2_gain, ln2_bias)
    normed2 = normed2_f.astype(BF16)
    hidden = dot(normed2, w_up) + b_up
    active_f, gelu_pull = jax.vjp(gelu_exact, hidden)
    active = active_f.astype(BF16)
    output = (middle + dot(active, w_down) + b_down).astype(BF16)

    cot_f = cot.astype(F32)
    grad_w_down = dot(active, cot, TN)
    grad_b_down = jnp.sum(cot_f, axis=0)
    grad_active = dot(cot, w_down, NT)
    (grad_hidden_f,) = gelu_pull(grad_active)
    grad_hidden = grad_hidden_f.astype(BF16)
    grad_w_up = dot(normed2, grad_hidden, TN)
    grad_b_up = jnp.sum(grad_hidden.astype(F32), axis=0)
    grad_normed2 = dot(grad_hidden, w_up, NT)
    grad_middle_norm, grad_ln2_gain, grad_ln2_bias = norm2_pull(grad_normed2)

    def tiles_of(array):
        return array.astype(BF16).reshape(count, share, width)

    feed_grads = jnp.concatenate(
        [tiles_of(grad_w_up[:, width * c : width * (c + 1)]) for c in range(wide)]
        + [grad_w_down.astype(BF16).reshape(count, share * wide, width)],
        axis=1,
    )
    batch = lax.axis_size("batch")
    feed_grads = feed_grads.reshape(batch, seq, -1, width).transpose(1, 0, 2, 3)
    feed_grads = lax.psum_scatter(feed_grads, "seq", scatter_dimension=0, tiled=False)
    feed_grads = lax.psum_scatter(feed_grads, "batch", scatter_dimension=0, tiled=False)
    feed_grads = feed_grads.astype(F32)

    grad_middle = cot_f + grad_middle_norm
    grad_branch = grad_middle.astype(BF16)
    grad_w_out = dot(attended_low, grad_branch, TN)
    grad_attended = heads(dot(grad_branch, w_out, NT).astype(BF16))
    grad_attended_f = grad_attended.astype(F32)
    self_grad = jnp.sum(grad_attended_f * value_heads.astype(F32), axis=-1)
    row_delta = jnp.sum(grad_attended_f * attended, axis=-1)
    grad_self_score = (self_weight * (self_grad - row_delta)).astype(BF16).astype(F32)[..., None]
    grad_probs = jnp.einsum(
        "mthd,mjhd->mhtj", grad_attended, memory[1], preferred_element_type=F32
    )
    grad_scores = (probs * (grad_probs - row_delta.transpose(0, 2, 1)[..., None])).astype(BF16)
    grad_queries = jnp.einsum(
        "mhtj,mjhd->mthd", grad_scores, memory[0], preferred_element_type=F32
    )
    grad_queries = scale * (grad_queries + grad_self_score * key_heads.astype(F32))
    grad_queries = grad_queries.reshape(micro * tok, width).astype(BF16)
    grad_memory = jnp.stack(
        [
            scale
            * jnp.einsum("mhtj,mthd->mjhd", grad_scores, query_heads, preferred_element_type=F32),
            jnp.einsum("mhtj,mthd->mjhd", probs_low, grad_attended, preferred_element_type=F32),
        ]
    ).astype(BF16)
    grad_memory = grad_memory.reshape(2, micro, seq, slots, width).transpose(2, 0, 1, 3, 4)
    grad_memory = lax.psum_scatter(grad_memory, "seq", scatter_dimension=0, tiled=False)
    grad_memory = grad_memory.reshape(2, micro * slots, width)
    grad_conv_key = dot(windows[0], grad_memory[0], TN)
    grad_conv_value = dot(windows[1], grad_memory[1], TN)
    grad_windows = jnp.stack(
        [dot(grad_memory[0], conv_key, NT), dot(grad_memory[1], conv_value, NT)]
    ).reshape(2, micro, tok, width)
    back = lax.ppermute(grad_windows[:, :, :2], "seq", [(i + 1, i) for i in range(seq - 1)])
    grad_kept = jnp.concatenate([grad_windows[:, :, 2:], back], axis=2).reshape(
        2, micro * tok, width
    )
    self_key_grad = (scale * grad_self_score * query_heads.astype(F32)).reshape(-1, width)
    self_value_grad = (self_weight[..., None] * grad_attended_f).reshape(-1, width)
    grad_keys = ((grad_kept[0] + self_key_grad) * valid_f).astype(BF16)
    grad_values = ((grad_kept[1] + self_value_grad) * valid_f).astype(BF16)
    grad_w_query = dot(normed, grad_queries, TN)
    grad_w_key = dot(normed, grad_keys, TN)
    grad_w_value = dot(normed, grad_values, TN)
    grad_normed = (
        dot(grad_queries, w_query, NT) + dot(grad_keys, w_key, NT) + dot(grad_values, w_value, NT)
    )
    grad_input_norm, grad_ln1_gain, grad_ln1_bias = norm1_pull(grad_normed)
    input_grad = (grad_middle + grad_input_norm).astype(BF16)

    vector_grads = jnp.concatenate(
        [
            v.reshape(count, -1)
            for v in (
                grad_ln1_gain,
                grad_ln1_bias,
                grad_ln2_gain,
                grad_ln2_bias,
                grad_b_down,
                grad_b_up,
            )
        ],
        axis=1,
    ).astype(BF16)
    vector_grads = jnp.pad(vector_grads, ((0, 0), (0, width - vector_grads.shape[1])))
    vector_grads = jnp.pad(vector_grads[:, None, :], ((0, 0), (0, 15), (0, 0)))
    late = jnp.concatenate(
        [tiles_of(grad_conv_key[width * i : width * (i + 1)]) for i in range(3)]
        + [tiles_of(grad_conv_value[width * i : width * (i + 1)]) for i in range(3)]
        + [tiles_of(g) for g in (grad_w_out, grad_w_query, grad_w_key, grad_w_value)]
        + [vector_grads],
        axis=1,
    )
    late = reduce_rows(late)

    def own(buffer, number):
        return buffer[share * number : share * (number + 1)]

    vector_row = late[10 * share]

    def own_vector(number, length=share):
        return vector_row[share * number : share * number + length]

    return (
        output.reshape(tokens.shape),
        input_grad.reshape(tokens.shape),
        own_vector(0),
        own_vector(1),
        own(late, 7),
        own(late, 8),
        own(late, 9),
        jnp.stack([own(late, i) for i in range(3)]),
        jnp.stack([own(late, i) for i in range(3, 6)]),
        own(late, 6),
        own_vector(2),
        own_vector(3),
        jnp.concatenate([own(feed_grads, i) for i in range(wide)], axis=1),
        own_vector(5, ff // count),
        feed_grads[share * wide :],
        own_vector(4),
    )


def solution(mesh):
    rows = P(AXES, None)
    vector = P(AXES)
    conv = P(None, AXES, None)
    part = P(None, "batch", "seq", None)
    weights = (vector, vector, rows, rows, rows, conv, conv, rows, vector, vector)
    weights = weights + (rows, vector, rows, vector)
    return jax.shard_map(
        per_device,
        mesh=mesh,
        in_specs=(part, P(None, "batch", None)) + weights + (part,),
        out_specs=(part, part) + weights,
        check_vma=False,
    )
```

```python
import functools

import jax
import jax.numpy as jnp
from jax import lax
from jax.experimental import pallas as pl
from jax.experimental.pallas import tpu as pltpu
from jax.sharding import PartitionSpec as P

HEADS = 8
HEAD_DIM = 64
SCALE = HEAD_DIM ** (-0.5)
EPSILON = 1e-06
AXES = ("batch", "seq")
GROUPS = 32
UNIT = 16
PAIR = 2 * HEAD_DIM
RIM = 8
MASKED = -1e30
F32 = jnp.float32
BF16 = jnp.bfloat16
TN = ((0,), (0,))
NT = ((1,), (1,))
ERF_TOP = (
    0.00022905065861350646,
    0.0034082910107109506,
    0.050955695062380861,
    0.18520832239976145,
    1.128379143519084,
)
ERF_LOW = (
    -1.1791602954361697e-7,
    0.000023547966471313185,
    0.0010179625278914885,
    0.014070470171167667,
    0.11098505178285362,
    0.49746925110067538,
    1.0,
)


def device_count():
    return lax.axis_size("batch") * lax.axis_size("seq")


def device_index():
    return lax.axis_index("batch") * lax.axis_size("seq") + lax.axis_index("seq")


def powers(low, high):
    masks = []
    while low < high:
        masks.append(low)
        low *= 2
    return masks


def bit_axis(mask):
    return device_count().bit_length() - 1 - mask.bit_length()


def swap(array, mask):
    return lax.ppermute(array, AXES, [(i, i ^ mask) for i in range(device_count())])


def gather_step(held, mask):
    other = swap(held, mask)
    upper = (device_index() & mask) != 0
    low, high = jnp.where(upper, other, held), jnp.where(upper, held, other)
    return jnp.concatenate([low, high], axis=bit_axis(mask))


def reduce_step(held, mask):
    axis = bit_axis(mask)
    upper = ((device_index() & mask) != 0).astype(jnp.int32)
    send = lax.dynamic_slice_in_dim(held, 1 - upper, 1, axis)
    keep = lax.dynamic_slice_in_dim(held, upper, 1, axis)
    return keep.astype(F32) + swap(send, mask).astype(F32)


def exchange_orders():
    seq, count = lax.axis_size("seq"), device_count()
    along = powers(2, seq)[::-1]
    across = powers(seq, count)
    return along, across, across[::-1]


def gather_rows(rows):
    along, one, two = exchange_orders()
    bits = device_count().bit_length() - 1
    held = rows.reshape((1,) * bits + rows.shape)
    for mask in along:
        held = gather_step(held, mask)
    half = rows.shape[0] // 2
    parts = [held[..., :half, :], held[..., half:, :]]
    for masks in zip(one, two):
        parts = [gather_step(part, mask) for part, mask in zip(parts, masks)]
    held = gather_step(jnp.concatenate(parts, axis=-2), 1)
    return held.reshape((device_count(),) + rows.shape)


def reduce_rows(blocks):
    along, one, two = exchange_orders()
    bits = device_count().bit_length() - 1
    held = blocks.reshape((2,) * bits + blocks.shape[1:])
    held = reduce_step(held, 1).astype(BF16)
    half = blocks.shape[1] // 2
    half = half // UNIT * UNIT or half
    parts = [held[..., :half, :], held[..., half:, :]]
    for masks in zip(one + along[::-1], two + along[::-1]):
        sums = [reduce_step(part, mask) for part, mask in zip(parts, masks)]
        parts = [part.astype(BF16) for part in sums]
    return [part.reshape((-1, blocks.shape[-1])) for part in sums]


def reduce_seq(blocks):
    seq = lax.axis_size("seq")
    shape = blocks.shape[1:]
    held = blocks
    for mask in [1] + powers(2, seq):
        size = held.shape[0] // 2
        pairs = [(i, i ^ mask) for i in range(seq)]
        held = held.reshape((size, 2) + shape)
        upper = ((lax.axis_index("seq") & mask) != 0).astype(jnp.int32)
        send = lax.dynamic_slice_in_dim(held, 1 - upper, 1, 1)
        keep = lax.dynamic_slice_in_dim(held, upper, 1, 1)
        other = lax.ppermute(send, "seq", pairs)
        held = (keep.astype(F32) + other.astype(F32)).astype(BF16).reshape((size,) + shape)
    return held.reshape(shape)


def grouped(buffer, sizes):
    count = buffer.shape[0]
    if count == GROUPS:
        return buffer
    width = buffer.shape[-1]
    share = width // count
    parts, start = [], 0
    for size in sizes:
        part = buffer[:, start : start + share * size]
        parts.append(part.reshape(GROUPS, UNIT * size, width))
        start += share * size
    return jnp.concatenate(parts, axis=1)


def scattered(buffer, sizes):
    count, width = device_count(), buffer.shape[-1]
    if count == GROUPS:
        return buffer
    parts, start = [], 0
    for size in sizes:
        part = buffer[:, start : start + UNIT * size]
        parts.append(part.reshape(count, width // count * size, width))
        start += UNIT * size
    return jnp.concatenate(parts, axis=1)


def vector_pack(vectors, rows, width):
    filled = jnp.pad(vectors, ((0, 0), (0, width - vectors.shape[1])))
    return jnp.pad(filled[:, None], ((0, 0), (0, rows - 1), (0, 0)))


def vector_regroup(vectors, parts, lengths):
    pieces, start = [], 0
    for length in lengths:
        pieces.append(vectors[:, start : start + length].reshape(parts, -1))
        start += length
    return jnp.concatenate(pieces, axis=1)


def dot(a, b, dims=((1,), (0,))):
    return lax.dot_general(a, b, (dims, ((), ())), preferred_element_type=F32)


def iota(shape, axis):
    return lax.broadcasted_iota(jnp.int32, shape, axis)


def tile(ref, place, size=1):
    rows = ref[:, UNIT * place : UNIT * (place + size), :]
    return rows.reshape(GROUPS * UNIT * size, rows.shape[-1])


def kernel(body, args, outs, flops, limit):
    spec = {jnp.dtype(jnp.int32): pltpu.SMEM}
    return pl.pallas_call(
        body,
        in_specs=[pl.BlockSpec(memory_space=spec.get(a.dtype, pltpu.VMEM)) for a in args],
        out_specs=[pl.BlockSpec(memory_space=pltpu.VMEM) for _ in outs],
        out_shape=[jax.ShapeDtypeStruct(shape, dtype) for shape, dtype in outs],
        compiler_params=pltpu.CompilerParams(vmem_limit_bytes=limit << 20),
        cost_estimate=pl.CostEstimate(
            flops=flops,
            bytes_accessed=sum(a.size * a.dtype.itemsize for a in args),
            transcendentals=0,
        ),
    )(*args)


def unit_norm(values):
    center = values - jnp.mean(values, axis=-1, keepdims=True)
    spread = jnp.mean(center * center, axis=-1, keepdims=True)
    inverse = lax.rsqrt(spread + EPSILON)
    return center * inverse, inverse


def norm_back(grad, unit, inverse, gain):
    e = grad * gain
    mean_e = jnp.mean(e, axis=-1, keepdims=True)
    mean_x = jnp.mean(e * unit, axis=-1, keepdims=True)
    return inverse * (e - mean_e - unit * mean_x)


def column_sum(values):
    return jnp.sum(values, axis=0, keepdims=True)


def valid_column(info, m, start, rows):
    place = start + iota((rows, 1), 0)
    first = (place >= 1) & (place < info[m, 0])
    second = (place >= info[m, 1]) & (place < info[m, 2])
    return jnp.where(first | second, 1.0, 0.0).astype(F32)


def segment_start(info, m, place):
    start = jnp.where(place >= 1, 1, 0)
    start = jnp.where(place >= info[m, 1], info[m, 1], start)
    return jnp.where(place >= info[m, 3], info[m, 3], start)


VECTORS = 5
BIAS_AT = VECTORS * UNIT


def vector_maps(width):
    lanes = width // 2
    fine = (iota((lanes, width), 0) & 15) == (iota((lanes, width), 1) & 15)
    wide = ((iota((lanes, width), 0) + 48) & 63) == (iota((lanes, width), 1) & 63)
    own_fine = iota((GROUPS, width), 1) >> 4 == iota((GROUPS, width), 0)
    own_wide = iota((GROUPS, width), 1) >> 6 == (iota((GROUPS, width), 0) & 7)
    as_bf16 = [jnp.where(m, 1.0, 0.0).astype(BF16) for m in (fine, wide)]
    as_f32 = [jnp.where(m, 1.0, 0.0).astype(F32) for m in (own_fine, own_wide)]
    return as_bf16 + as_f32


def lane_window(lanes, k):
    place = iota((GROUPS, lanes), 1)
    if k == VECTORS:
        return (place >= BIAS_AT) & (place < BIAS_AT + 64)
    return (place >= UNIT * k) & (place < UNIT * (k + 1))


def project_kernel(info, tok, halo, first, normed, query, kept, vec):
    width = tok.shape[-1]
    lanes = width // 2
    fine, wide, own_fine, own_wide = vector_maps(width)
    rows = jnp.sum(first[:, 3 * UNIT : 4 * UNIT, :lanes].astype(F32), axis=1)
    picked = [jnp.where(lane_window(lanes, k), rows, 0.0) for k in range(VECTORS + 1)]
    spread = dot(jnp.concatenate(picked[:VECTORS], axis=0).astype(BF16), fine)
    vectors = [
        column_sum(spread[GROUPS * k : GROUPS * (k + 1)] * own_fine) for k in range(VECTORS)
    ]
    bias = dot(picked[VECTORS].astype(BF16), wide) * own_wide
    bias = jnp.sum(bias.reshape(4, 8, width), axis=1)
    vec[...] = jnp.concatenate(vectors + [bias, jnp.zeros((7, width), F32)], axis=0)

    count = tok.shape[0]
    micro = info.shape[0]
    each = count // micro
    values = jnp.concatenate([tok[...], halo[...]], axis=0).astype(F32)
    unit, _ = unit_norm(values)
    low = (unit * vectors[0] + vectors[1]).astype(BF16)
    normed[...] = low[:count]
    query[...] = dot(low[:count], tile(first, 0)).astype(BF16)
    valid = [valid_column(info, m, info[m, 4], each) for m in range(micro)]
    valid += [valid_column(info, m, info[m, 4] - RIM, RIM) for m in range(micro)]
    valid = jnp.concatenate(valid, axis=0)
    kept[:, :width] = (dot(low, tile(first, 1)) * valid).astype(BF16)
    kept[:, width:] = (dot(low, tile(first, 2)) * valid).astype(BF16)


def window_map(micro, each, tap):
    slots = each // 3
    shape = (micro * slots, micro * (each + RIM))
    row, place = iota(shape, 0), iota(shape, 1)
    m = jnp.zeros(shape, jnp.int32)
    for i in range(1, micro):
        m = m + jnp.where(row >= slots * i, 1, 0)
    source = 3 * (row - slots * m) - 2 + tap
    rim = micro * each + RIM * m + RIM + source
    target = jnp.where(source >= 0, each * m + source, rim)
    return jnp.where(place == target, 1.0, 0.0).astype(BF16)


def compress_kernel(micro, kept, conv, window, memory):
    width = conv.shape[-1]
    each = kept.shape[0] // micro - RIM
    sums = [None, None]
    for tap in range(3):
        rows = dot(window_map(micro, each, tap), kept[...]).astype(BF16)
        window[tap] = rows
        for kind in range(2):
            part = dot(rows[:, width * kind : width * (kind + 1)], tile(conv, 3 * kind + tap))
            sums[kind] = part if sums[kind] is None else sums[kind] + part
    for kind in range(2):
        memory[kind] = sums[kind].astype(BF16)


def stacked(values, lower):
    zero = jnp.zeros_like(values)
    return jnp.concatenate(
        [jnp.where(lower, values, zero), jnp.where(lower, zero, values)], axis=0
    )


def merged(values, lower):
    half = values.shape[0] // 2
    return jnp.where(lower, values[:half], values[half:])


def memory_pair(memory, kind, m, pair, micro):
    slots = memory.shape[2] // micro
    rows = memory[:, kind, slots * m : slots * (m + 1), PAIR * pair : PAIR * (pair + 1)]
    return rows.reshape(memory.shape[0] * slots, PAIR)


def attend_kernel(info, query, kept, memory, attended, stats):
    micro = info.shape[0]
    count, width = query.shape
    each = count // micro
    slots = memory.shape[0] * memory.shape[2] // micro
    pairs = width // PAIR
    lower = iota((each, PAIR), 1) < HEAD_DIM
    lane = iota((2 * each, 128), 1)
    found = jnp.zeros((2 * each, 128), F32)
    for m in range(micro):
        rows = slice(each * m, each * (m + 1))
        place = info[m, 4] + iota((each, 1), 0)
        start = segment_start(info, m, place)
        end = 3 * iota((each, slots), 1)
        bias = jnp.where((end <= place) & (end >= start), 0.0, MASKED).astype(F32)
        bias = jnp.concatenate([bias, bias], axis=0)
        for pair in range(pairs):
            cols = slice(PAIR * pair, PAIR * (pair + 1))
            key = kept[rows, cols].astype(F32)
            value = kept[rows, width + PAIR * pair : width + PAIR * (pair + 1)].astype(F32)
            queries = stacked(query[rows, cols].astype(F32) * SCALE, lower)
            own = jnp.sum(queries * jnp.concatenate([key, key], axis=0), axis=1, keepdims=True)
            memory_key = memory_pair(memory, 0, m, pair, micro)
            memory_value = memory_pair(memory, 1, m, pair, micro)
            scores = dot(queries.astype(BF16), memory_key, NT) + bias
            top = jnp.maximum(jnp.max(scores, axis=1, keepdims=True), own)
            expos = jnp.exp(scores - top)
            own = jnp.exp(own - top)
            total = jnp.sum(expos, axis=1, keepdims=True) + own
            inverse = 1.0 / total
            mixed = dot(expos.astype(BF16), memory_value) * inverse
            weight = jnp.broadcast_to(own * inverse, mixed.shape)
            attended[rows, cols] = merged(mixed, lower) + merged(weight, lower) * value
            found = jnp.where(lane == m * pairs + pair, top + jnp.log(total), found)
    stats[...] = found


def erf(values):
    values = jnp.clip(values, -3.832506856900711, 3.832506856900711)
    square = values * values
    above, below = ERF_TOP[0], ERF_LOW[0]
    for c in ERF_TOP[1:]:
        above = above * square + c
    for c in ERF_LOW[1:]:
        below = below * square + c
    return values * above / below


def feed_kernel(tok, cot, attended, vec, rest, out, grad_mid, grad_att, grads, vec_grad):
    count, width = tok.shape
    wide = 4
    low_att = attended[...].astype(BF16)
    w_out = tile(rest, 0)
    middle = tok[...].astype(F32) + dot(low_att, w_out)
    unit, inverse = unit_norm(middle)
    gain = vec[2:3, :]
    low = (unit * gain + vec[3:4, :]).astype(BF16)
    low_t = low.T
    cots = cot[...]
    total = middle + vec[4:5, :]
    grad_low = jnp.zeros((count, width), F32)
    bias_rows = []
    eighth = GROUPS // wide
    for c in range(wide):
        w_up = tile(rest, 1 + c)
        down = slice(eighth * c, eighth * (c + 1))
        w_down = rest[down, UNIT * (1 + wide) :, :].reshape(width, width)
        hidden = dot(low, w_up) + vec[5 + c : 6 + c, :]
        share = 0.5 + 0.5 * erf(hidden * 0.7071067811865476)
        slope = share + hidden * (0.3989422804014327 * jnp.exp(-0.5 * hidden * hidden))
        active = (hidden * share).astype(BF16)
        total = total + dot(active, w_down)
        grad_hidden_f = dot(cots, w_down, NT) * slope
        grad_hidden = grad_hidden_f.astype(BF16)
        bias_rows.append(column_sum(grad_hidden.astype(F32)))
        grad_low = grad_low + dot(grad_hidden, w_up, NT)
        grad_up = dot(low_t, grad_hidden).astype(BF16)
        grads[:, UNIT * (1 + c) : UNIT * (2 + c), :] = grad_up.reshape(GROUPS, UNIT, width)
        grad_down = dot(active, cots, TN).astype(BF16)
        grads[down, UNIT * (1 + wide) :, :] = grad_down.reshape(eighth, UNIT * wide, width)
    out[...] = total.astype(BF16)
    cots_f = cots.astype(F32)
    grad_middle = cots_f + norm_back(grad_low, unit, inverse, gain)
    grad_mid[...] = grad_middle
    branch = grad_middle.astype(BF16)
    grads[:, :UNIT, :] = dot(low_att, branch, TN).astype(BF16).reshape(GROUPS, UNIT, width)
    grad_att[...] = dot(branch, w_out, NT).astype(BF16)
    rows = [jnp.zeros((2, width), F32), column_sum(grad_low * unit), column_sum(grad_low)]
    rows += [column_sum(cots_f)] + bias_rows + [jnp.zeros((7, width), F32)]
    vec_grad[...] = jnp.concatenate(rows, axis=0)


def attend_back_kernel(
    info, query, kept, memory, attended, stats, grad_att, grad_query, grad_memory, own_key, own_value
):
    micro = info.shape[0]
    count, width = query.shape
    each = count // micro
    slots = memory.shape[0] * memory.shape[2] // micro
    share = memory.shape[2] // micro
    pairs = width // PAIR
    lower = iota((each, PAIR), 1) < HEAD_DIM
    lane = iota((2 * each, 128), 1)
    found = stats[...]
    deltas = jnp.zeros((2 * each, 128), F32)
    parts = {}
    for m in range(micro):
        rows = slice(each * m, each * (m + 1))
        for pair in range(pairs):
            cols = slice(PAIR * pair, PAIR * (pair + 1))
            grad = grad_att[rows, cols].astype(F32)
            product = stacked(grad * attended[rows, cols], lower)
            delta = jnp.sum(product, axis=1, keepdims=True)
            deltas = jnp.where(lane == m * pairs + pair, delta, deltas)
            parts[m, pair] = delta
    found_t, deltas_t = found.T, deltas.T
    for m in range(micro):
        rows = slice(each * m, each * (m + 1))
        lanes = iota((1, 2 * each), 1)
        place = info[m, 4] + jnp.where(lanes >= each, lanes - each, lanes)
        start = segment_start(info, m, place)
        end = 3 * iota((slots, 2 * each), 0)
        bias = jnp.where((end <= place) & (end >= start), 0.0, MASKED).astype(F32)
        for pair in range(pairs):
            cols = slice(PAIR * pair, PAIR * (pair + 1))
            at = m * pairs + pair
            key = kept[rows, cols].astype(F32)
            value = kept[rows, width + PAIR * pair : width + PAIR * (pair + 1)].astype(F32)
            query_f = query[rows, cols].astype(F32) * SCALE
            grad_f = grad_att[rows, cols].astype(F32)
            queries = stacked(query_f, lower)
            grads = stacked(grad_f, lower)
            own = jnp.sum(queries * jnp.concatenate([key, key], axis=0), axis=1, keepdims=True)
            own = jnp.exp(own - found[:, at : at + 1])
            grad_own = jnp.sum(
                grads * jnp.concatenate([value, value], axis=0), axis=1, keepdims=True
            )
            grad_own = (own * (grad_own - parts[m, pair])).astype(BF16).astype(F32)
            queries, grads = queries.astype(BF16), grads.astype(BF16)
            memory_key = memory_pair(memory, 0, m, pair, micro)
            memory_value = memory_pair(memory, 1, m, pair, micro)
            scores = dot(memory_key, queries, NT) + bias
            probs = jnp.exp(scores - found_t[at : at + 1, :])
            grad_probs = dot(memory_value, grads, NT)
            grad_scores = (probs * (grad_probs - deltas_t[at : at + 1, :])).astype(BF16)
            into = (slice(None), slice(share * m, share * (m + 1)), cols)
            shape = (memory.shape[0], share, PAIR)
            grad_memory[(into[0], 0) + into[1:]] = (
                dot(grad_scores, queries).astype(BF16).reshape(shape)
            )
            grad_memory[(into[0], 1) + into[1:]] = (
                dot(probs.astype(BF16), grads).astype(BF16).reshape(shape)
            )
            turned = dot(memory_key.T, grad_scores).T
            own_grad = merged(jnp.broadcast_to(grad_own, (2 * each, PAIR)), lower)
            own_weight = merged(jnp.broadcast_to(own, (2 * each, PAIR)), lower)
            grad_query[rows, cols] = (
                SCALE * (merged(turned, lower) + own_grad * key)
            ).astype(BF16)
            own_key[rows, cols] = own_grad * query_f
            own_value[rows, cols] = own_weight * grad_f


def compress_back_kernel(micro, grad_memory, window, conv, grads, grad_kept, rim):
    width = conv.shape[-1]
    each = grad_kept.shape[0] // micro
    for kind in range(2):
        cols = slice(width * kind, width * (kind + 1))
        grad = grad_memory[kind]
        total = None
        for tap in range(3):
            at = 3 * kind + tap
            term = dot(window[tap, :, cols], grad, TN).astype(BF16)
            grads[:, UNIT * at : UNIT * (at + 1), :] = term.reshape(GROUPS, UNIT, width)
            part = dot(grad, tile(conv, at), NT)
            high = part.astype(BF16)
            rest = (part - high.astype(F32)).astype(BF16)
            places = window_map(micro, each, tap)
            part = dot(places, high, TN) + dot(places, rest, TN)
            total = part if total is None else total + part
        grad_kept[:, cols] = total[: micro * each]
        rim[:, cols] = total[micro * each :]


def input_kernel(
    info,
    tok,
    normed,
    grad_query,
    grad_kept,
    rim,
    own_key,
    own_value,
    first,
    vec,
    grad_mid,
    vec_grad,
    grad_in,
    grads,
    total,
):
    count, width = tok.shape
    micro = info.shape[0]
    each = count // micro
    total[...] = grad_kept[...]
    for m in range(micro):
        rows = slice(each * (m + 1) - RIM, each * (m + 1))
        total[rows, :] = total[rows, :] + rim[RIM * m : RIM * (m + 1), :]
    valid = [valid_column(info, m, info[m, 4], each) for m in range(micro)]
    valid = jnp.concatenate(valid, axis=0)
    grad_key = ((total[:, :width] + own_key[...]) * valid).astype(BF16)
    grad_value = ((total[:, width:] + own_value[...]) * valid).astype(BF16)
    low_t = normed[...].T
    grad_low = None
    for at, grad in enumerate((grad_query[...], grad_key, grad_value)):
        part = dot(grad, tile(first, at), NT)
        grad_low = part if grad_low is None else grad_low + part
        term = dot(low_t, grad).astype(BF16)
        grads[:, UNIT * at : UNIT * (at + 1), :] = term.reshape(GROUPS, UNIT, width)
    unit, inverse = unit_norm(tok[...].astype(F32))
    back = norm_back(grad_low, unit, inverse, vec[0:1, :])
    grad_in[...] = (grad_mid[...] + back).astype(BF16)

    lanes = width // 2
    fine, wide, own_fine, own_wide = vector_maps(width)
    vectors = [column_sum(grad_low * unit), column_sum(grad_low)]
    vectors += [vec_grad[k : k + 1, :] for k in range(2, VECTORS)]
    dealt = jnp.concatenate([own_fine * v for v in vectors], axis=0).astype(BF16)
    dealt = dot(dealt, fine, NT)
    bias = [
        jnp.broadcast_to(vec_grad[VECTORS + c : VECTORS + c + 1, :], (8, width)) for c in range(4)
    ]
    bias = (jnp.concatenate(bias, axis=0) * own_wide).astype(BF16)
    packed = jnp.where(lane_window(lanes, VECTORS), dot(bias, wide, NT), 0.0)
    for k in range(VECTORS):
        packed = jnp.where(lane_window(lanes, k), dealt[GROUPS * k : GROUPS * (k + 1)], packed)
    packed = jnp.concatenate([packed, jnp.zeros((GROUPS, width - lanes), F32)], axis=1)
    spot = iota((GROUPS, UNIT, width), 1) == 0
    spread = jnp.broadcast_to(packed[:, None, :], (GROUPS, UNIT, width))
    grads[:, 3 * UNIT :, :] = jnp.where(spot, spread, 0.0).astype(BF16)


def per_device(
    tokens,
    lengths,
    ln1_gain,
    ln1_bias,
    w_query,
    w_key,
    w_value,
    conv_key,
    conv_value,
    w_out,
    ln2_gain,
    ln2_bias,
    w_up,
    b_up,
    w_down,
    b_down,
    cotangent,
):
    count = device_count()
    micro, _, each, width = tokens.shape
    ff = w_up.shape[1]
    wide = ff // width
    share = width // count
    seq = lax.axis_size("seq")
    all_tokens = micro * each
    slots = micro * each // 3

    halo = lax.ppermute(
        tokens[:, 0, each - RIM :], "seq", [(i, i + 1) for i in range(seq - 1)]
    ).reshape(micro * RIM, width)

    vectors = jnp.concatenate([ln1_gain, ln1_bias, ln2_gain, ln2_bias, b_down, b_up])
    vector_lengths = [share] * VECTORS + [ff // count]
    vector_rows = UNIT if count == GROUPS else 2
    vector_tile = vector_pack(vectors[None], vector_rows, width)[0]
    first = gather_rows(jnp.concatenate([w_query, w_key, w_value, vector_tile], axis=0))
    if count != GROUPS:
        dealt = vector_regroup(first[:, 3 * share], GROUPS, vector_lengths)
        dealt = vector_pack(dealt, UNIT, width)
        first = jnp.concatenate([grouped(first, [1] * 3), dealt], axis=1)
    conv = jnp.concatenate([conv_key, conv_value], axis=0).reshape(6 * share, width)
    conv = grouped(lax.all_gather(conv, AXES, axis=0, tiled=False), [1] * 6)
    rest = [w_out] + [w_up[:, width * c : width * (c + 1)] for c in range(wide)] + [w_down]
    rest = lax.all_gather(jnp.concatenate(rest, axis=0), AXES, axis=0, tiled=False)
    rest_sizes = [1] * (1 + wide) + [wide]
    rest = grouped(rest, rest_sizes)

    lengths = lengths[:, 0]
    first_pad = 3 * ((lengths[:, 0] + 2) // 3)
    second_pad = 3 * ((lengths[:, 1] + 2) // 3)
    second = 1 + first_pad
    offset = jnp.full_like(second, lax.axis_index("seq") * each)
    info = jnp.stack(
        [1 + lengths[:, 0], second, second + lengths[:, 1], second + second_pad, offset], axis=1
    ).astype(jnp.int32)

    tok = tokens.reshape(all_tokens, width)
    cot = cotangent.reshape(all_tokens, width)
    rows = (all_tokens, width)
    matmul = 2 * all_tokens * width * width

    normed, query, kept, vec = kernel(
        project_kernel,
        (info, tok, halo, first),
        (
            (rows, BF16),
            (rows, BF16),
            ((all_tokens + micro * RIM, 2 * width), BF16),
            ((16, width), F32),
        ),
        3 * matmul,
        32,
    )
    window, memory_own = kernel(
        functools.partial(compress_kernel, micro),
        (kept, conv),
        (((3, slots, 2 * width), BF16), ((2, slots, width), BF16)),
        2 * matmul,
        32,
    )
    memory = lax.all_gather(memory_own, "seq", axis=0, tiled=False)
    attended, stats = kernel(
        attend_kernel,
        (info, query, kept, memory),
        ((rows, F32), ((2 * each, 128), F32)),
        4 * matmul,
        48,
    )
    output, grad_mid, grad_att, rest_grads, vec_grad = kernel(
        feed_kernel,
        (tok, cot, attended, vec, rest),
        (
            (rows, BF16),
            (rows, F32),
            (rows, BF16),
            ((GROUPS, UNIT * (1 + 2 * wide), width), BF16),
            ((16, width), F32),
        ),
        27 * matmul,
        48,
    )
    rest_grads = reduce_rows(scattered(rest_grads, rest_sizes))
    grad_query, grad_memory, own_key, own_value = kernel(
        attend_back_kernel,
        (info, query, kept, memory, attended, stats, grad_att),
        ((rows, BF16), (memory.shape, BF16), (rows, F32), (rows, F32)),
        10 * matmul,
        56,
    )
    grad_memory = reduce_seq(grad_memory)
    conv_grads, grad_kept, rim = kernel(
        functools.partial(compress_back_kernel, micro),
        (grad_memory, window, conv),
        (
            ((GROUPS, 6 * UNIT, width), BF16),
            ((all_tokens, 2 * width), F32),
            ((micro * RIM, 2 * width), F32),
        ),
        4 * matmul,
        40,
    )
    conv_grads = reduce_rows(scattered(conv_grads, [1] * 6))
    rim = lax.ppermute(rim, "seq", [(i + 1, i) for i in range(seq - 1)])
    grad_in, first_grads = pl.pallas_call(
        input_kernel,
        in_specs=[pl.BlockSpec(memory_space=pltpu.SMEM)]
        + [pl.BlockSpec(memory_space=pltpu.VMEM)] * 11,
        out_specs=[pl.BlockSpec(memory_space=pltpu.VMEM)] * 2,
        out_shape=[
            jax.ShapeDtypeStruct(rows, BF16),
            jax.ShapeDtypeStruct((GROUPS, 4 * UNIT, width), BF16),
        ],
        scratch_shapes=[pltpu.VMEM((all_tokens, 2 * width), F32)],
        compiler_params=pltpu.CompilerParams(vmem_limit_bytes=40 << 20),
        cost_estimate=pl.CostEstimate(
            flops=6 * matmul, bytes_accessed=8 << 20, transcendentals=0
        ),
    )(
        info,
        tok,
        normed,
        grad_query,
        grad_kept,
        rim,
        own_key,
        own_value,
        first,
        vec,
        grad_mid,
        vec_grad,
    )
    if count != GROUPS:
        dealt = first_grads[:, 3 * UNIT, : VECTORS * UNIT + ff // GROUPS]
        dealt = vector_regroup(dealt, count, [UNIT] * VECTORS + [ff // GROUPS])
        dealt = vector_pack(dealt, vector_rows, width)
        first_grads = jnp.concatenate([scattered(first_grads, [1] * 3), dealt], axis=1)
    first_grads = reduce_rows(first_grads)

    late = jnp.concatenate(first_grads, axis=0)
    convs = jnp.concatenate(conv_grads, axis=0).reshape(2, 3, share, width)
    rest = jnp.concatenate(rest_grads, axis=0)

    def own(buffer, number):
        return buffer[share * number : share * (number + 1)]

    vector_row = late[3 * share]

    def own_vector(number, length=share):
        return vector_row[share * number : share * number + length]

    return (
        output.reshape(tokens.shape),
        grad_in.reshape(tokens.shape),
        own_vector(0),
        own_vector(1),
        own(late, 0),
        own(late, 1),
        own(late, 2),
        convs[0],
        convs[1],
        own(rest, 0),
        own_vector(2),
        own_vector(3),
        jnp.concatenate([own(rest, 1 + c) for c in range(wide)], axis=1),
        own_vector(VECTORS, ff // count),
        rest[share * (1 + wide) :],
        own_vector(4),
    )


def solution(mesh):
    rows = P(AXES, None)
    vector = P(AXES)
    conv = P(None, AXES, None)
    part = P(None, "batch", "seq", None)
    weights = (vector, vector, rows, rows, rows, conv, conv, rows, vector, vector)
    weights = weights + (rows, vector, rows, vector)
    return jax.shard_map(
        per_device,
        mesh=mesh,
        in_specs=(part, P(None, "batch", None)) + weights + (part,),
        out_specs=(part, part) + weights,
        check_vma=False,
    )
```

```python
import functools

import jax
import jax.numpy as jnp
from jax import lax
from jax.experimental import pallas as pl
from jax.experimental.pallas import tpu as pltpu
from jax.sharding import PartitionSpec as P

HEADS = 8
HEAD_DIM = 64
SCALE = HEAD_DIM ** (-0.5)
EPSILON = 1e-06
AXES = ("batch", "seq")
GROUPS = 32
UNIT = 16
PAIR = 2 * HEAD_DIM
RIM = 8
MASKED = -1e30
F32 = jnp.float32
BF16 = jnp.bfloat16
TN = ((0,), (0,))
NT = ((1,), (1,))
ERF_TOP = (
    0.00022905065861350646,
    0.0034082910107109506,
    0.050955695062380861,
    0.18520832239976145,
    1.128379143519084,
)
ERF_LOW = (
    -1.1791602954361697e-7,
    0.000023547966471313185,
    0.0010179625278914885,
    0.014070470171167667,
    0.11098505178285362,
    0.49746925110067538,
    1.0,
)


def device_count():
    return lax.axis_size("batch") * lax.axis_size("seq")


def device_index():
    return lax.axis_index("batch") * lax.axis_size("seq") + lax.axis_index("seq")


def powers(low, high):
    masks = []
    while low < high:
        masks.append(low)
        low *= 2
    return masks


def swap(array, mask):
    return lax.ppermute(array, AXES, [(i, i ^ mask) for i in range(device_count())])


def gather_step(held, mask, axis):
    other = swap(held, mask)
    upper = (device_index() & mask) != 0
    low, high = jnp.where(upper, other, held), jnp.where(upper, held, other)
    return jnp.concatenate([low, high], axis=axis)


def reduce_step(held, mask, axis):
    upper = ((device_index() & mask) != 0).astype(jnp.int32)
    send = lax.dynamic_slice_in_dim(held, 1 - upper, 1, axis)
    keep = lax.dynamic_slice_in_dim(held, upper, 1, axis)
    return keep.astype(F32) + swap(send, mask).astype(F32)


def place_of(mask, count):
    return count.bit_length() - 1 - mask.bit_length()


def exchange_orders():
    seq, count = lax.axis_size("seq"), device_count()
    across = powers(seq, count)
    return powers(2, seq)[::-1], across, across[::-1]


def together(*moves):
    return lax.optimization_barrier(moves)


def spread(rows):
    return rows.reshape((1,) * (device_count().bit_length() - 1) + rows.shape)


def gather_one(held, mask):
    return gather_step(held, mask, place_of(mask, device_count()))


def gather_across(parts, step):
    _, one, two = exchange_orders()
    return [gather_one(p, m) for p, m in zip(parts, (one[step], two[step]))]


def gather_cores(parts):
    held = gather_one(jnp.concatenate(parts, axis=-2), 1)
    return held.reshape((device_count(),) + held.shape[-2:])


def halfway(rows):
    half = rows // 2
    return half // UNIT * UNIT or half


def reduce_cores(blocks):
    count = device_count()
    held = blocks.reshape((2,) * (count.bit_length() - 1) + blocks.shape[1:])
    return reduce_step(held, 1, place_of(1, count)).astype(BF16)


def halves(held):
    half = halfway(held.shape[-2])
    return [held[..., :half, :], held[..., half:, :]]


def reduce_across(parts, step):
    _, one, two = exchange_orders()
    count = device_count()
    masks = (one[step], two[step])
    return [reduce_step(p, m, place_of(m, count)).astype(BF16) for p, m in zip(parts, masks)]


def reduce_one(held, mask):
    return reduce_step(held, mask, place_of(mask, device_count()))


def grouped(buffer, sizes):
    count = buffer.shape[0]
    if count == GROUPS:
        return buffer
    width = buffer.shape[-1]
    share = width // count
    parts, start = [], 0
    for size in sizes:
        part = buffer[:, start : start + share * size]
        parts.append(part.reshape(GROUPS, UNIT * size, width))
        start += share * size
    return jnp.concatenate(parts, axis=1)


def scattered(buffer, sizes):
    count, width = device_count(), buffer.shape[-1]
    if count == GROUPS:
        return buffer
    parts, start = [], 0
    for size in sizes:
        part = buffer[:, start : start + UNIT * size]
        parts.append(part.reshape(count, width // count * size, width))
        start += UNIT * size
    return jnp.concatenate(parts, axis=1)


def vector_pack(vectors, rows, width):
    filled = jnp.pad(vectors, ((0, 0), (0, width - vectors.shape[1])))
    return jnp.pad(filled[:, None], ((0, 0), (0, rows - 1), (0, 0)))


def vector_regroup(vectors, parts, lengths):
    pieces, start = [], 0
    for length in lengths:
        pieces.append(vectors[:, start : start + length].reshape(parts, -1))
        start += length
    return jnp.concatenate(pieces, axis=1)


def dot(a, b, dims=((1,), (0,))):
    return lax.dot_general(a, b, (dims, ((), ())), preferred_element_type=F32)


def iota(shape, axis):
    return lax.broadcasted_iota(jnp.int32, shape, axis)


def tile(ref, place, size=1):
    rows = ref[:, UNIT * place : UNIT * (place + size), :]
    return rows.reshape(GROUPS * UNIT * size, rows.shape[-1])


def kernel(body, args, outs, flops, limit):
    spec = {jnp.dtype(jnp.int32): pltpu.SMEM}
    return pl.pallas_call(
        body,
        in_specs=[pl.BlockSpec(memory_space=spec.get(a.dtype, pltpu.VMEM)) for a in args],
        out_specs=[pl.BlockSpec(memory_space=pltpu.VMEM) for _ in outs],
        out_shape=[jax.ShapeDtypeStruct(shape, dtype) for shape, dtype in outs],
        compiler_params=pltpu.CompilerParams(vmem_limit_bytes=limit << 20),
        cost_estimate=pl.CostEstimate(
            flops=flops,
            bytes_accessed=sum(a.size * a.dtype.itemsize for a in args),
            transcendentals=0,
        ),
    )(*args)


def unit_norm(values):
    center = values - jnp.mean(values, axis=-1, keepdims=True)
    spread = jnp.mean(center * center, axis=-1, keepdims=True)
    inverse = lax.rsqrt(spread + EPSILON)
    return center * inverse, inverse


def norm_back(grad, unit, inverse, gain):
    e = grad * gain
    mean_e = jnp.mean(e, axis=-1, keepdims=True)
    mean_x = jnp.mean(e * unit, axis=-1, keepdims=True)
    return inverse * (e - mean_e - unit * mean_x)


def column_sum(values):
    return jnp.sum(values, axis=0, keepdims=True)


def valid_column(info, m, start, rows):
    place = start + iota((rows, 1), 0)
    first = (place >= 1) & (place < info[m, 0])
    second = (place >= info[m, 1]) & (place < info[m, 2])
    return jnp.where(first | second, 1.0, 0.0).astype(F32)


def segment_start(info, m, place):
    start = jnp.where(place >= 1, 1, 0)
    start = jnp.where(place >= info[m, 1], info[m, 1], start)
    return jnp.where(place >= info[m, 3], info[m, 3], start)


VECTORS = 5
BIAS_AT = VECTORS * UNIT


def vector_maps(width):
    lanes = width // 2
    fine = (iota((lanes, width), 0) & 15) == (iota((lanes, width), 1) & 15)
    wide = ((iota((lanes, width), 0) + 48) & 63) == (iota((lanes, width), 1) & 63)
    own_fine = iota((GROUPS, width), 1) >> 4 == iota((GROUPS, width), 0)
    own_wide = iota((GROUPS, width), 1) >> 6 == (iota((GROUPS, width), 0) & 7)
    as_bf16 = [jnp.where(m, 1.0, 0.0).astype(BF16) for m in (fine, wide)]
    as_f32 = [jnp.where(m, 1.0, 0.0).astype(F32) for m in (own_fine, own_wide)]
    return as_bf16 + as_f32


def lane_window(lanes, k):
    place = iota((GROUPS, lanes), 1)
    if k == VECTORS:
        return (place >= BIAS_AT) & (place < BIAS_AT + 64)
    return (place >= UNIT * k) & (place < UNIT * (k + 1))


def project_kernel(info, tok, halo, first, normed, query, kept, vec):
    width = tok.shape[-1]
    lanes = width // 2
    fine, wide, own_fine, own_wide = vector_maps(width)
    rows = jnp.sum(first[:, 9 * UNIT : 10 * UNIT, :lanes].astype(F32), axis=1)
    picked = [jnp.where(lane_window(lanes, k), rows, 0.0) for k in range(VECTORS + 1)]
    spread = dot(jnp.concatenate(picked[:VECTORS], axis=0).astype(BF16), fine)
    vectors = [
        column_sum(spread[GROUPS * k : GROUPS * (k + 1)] * own_fine) for k in range(VECTORS)
    ]
    bias = dot(picked[VECTORS].astype(BF16), wide) * own_wide
    bias = jnp.sum(bias.reshape(4, 8, width), axis=1)
    vec[...] = jnp.concatenate(vectors + [bias, jnp.zeros((7, width), F32)], axis=0)

    count = tok.shape[0]
    micro = info.shape[0]
    each = count // micro
    values = jnp.concatenate([tok[...], halo[...]], axis=0).astype(F32)
    unit, _ = unit_norm(values)
    low = (unit * vectors[0] + vectors[1]).astype(BF16)
    normed[...] = low[:count]
    query[...] = dot(low[:count], tile(first, 0)).astype(BF16)
    valid = [valid_column(info, m, info[m, 4], each) for m in range(micro)]
    valid += [valid_column(info, m, info[m, 4] - RIM, RIM) for m in range(micro)]
    valid = jnp.concatenate(valid, axis=0)
    kept[:, :width] = (dot(low, tile(first, 1)) * valid).astype(BF16)
    kept[:, width:] = (dot(low, tile(first, 2)) * valid).astype(BF16)


def window_map(micro, each, tap):
    slots = each // 3
    shape = (micro * slots, micro * (each + RIM))
    row, place = iota(shape, 0), iota(shape, 1)
    m = jnp.zeros(shape, jnp.int32)
    for i in range(1, micro):
        m = m + jnp.where(row >= slots * i, 1, 0)
    source = 3 * (row - slots * m) - 2 + tap
    rim = micro * each + RIM * m + RIM + source
    target = jnp.where(source >= 0, each * m + source, rim)
    return jnp.where(place == target, 1.0, 0.0).astype(BF16)


def compress_kernel(micro, kept, conv, window, memory):
    width = conv.shape[-1]
    each = kept.shape[0] // micro - RIM
    sums = [None, None]
    for tap in range(3):
        rows = dot(window_map(micro, each, tap), kept[...]).astype(BF16)
        window[tap] = rows
        for kind in range(2):
            part = dot(rows[:, width * kind : width * (kind + 1)], tile(conv, 3 + 3 * kind + tap))
            sums[kind] = part if sums[kind] is None else sums[kind] + part
    for kind in range(2):
        memory[kind] = sums[kind].astype(BF16)


def stacked(values, lower):
    zero = jnp.zeros_like(values)
    return jnp.concatenate(
        [jnp.where(lower, values, zero), jnp.where(lower, zero, values)], axis=0
    )


def merged(values, lower):
    half = values.shape[0] // 2
    return jnp.where(lower, values[:half], values[half:])


def memory_pair(memory, kind, m, pair, micro):
    slots = memory.shape[2] // micro
    rows = memory[:, kind, slots * m : slots * (m + 1), PAIR * pair : PAIR * (pair + 1)]
    return rows.reshape(memory.shape[0] * slots, PAIR)


def attend_kernel(info, query, kept, memory, attended, stats):
    micro = info.shape[0]
    count, width = query.shape
    each = count // micro
    slots = memory.shape[0] * memory.shape[2] // micro
    pairs = width // PAIR
    lower = iota((each, PAIR), 1) < HEAD_DIM
    lane = iota((2 * each, 128), 1)
    found = jnp.zeros((2 * each, 128), F32)
    for m in range(micro):
        rows = slice(each * m, each * (m + 1))
        place = info[m, 4] + iota((each, 1), 0)
        start = segment_start(info, m, place)
        end = 3 * iota((each, slots), 1)
        bias = jnp.where((end <= place) & (end >= start), 0.0, MASKED).astype(F32)
        bias = jnp.concatenate([bias, bias], axis=0)
        for pair in range(pairs):
            cols = slice(PAIR * pair, PAIR * (pair + 1))
            key = kept[rows, cols].astype(F32)
            value = kept[rows, width + PAIR * pair : width + PAIR * (pair + 1)].astype(F32)
            queries = stacked(query[rows, cols].astype(F32) * SCALE, lower)
            own = jnp.sum(queries * jnp.concatenate([key, key], axis=0), axis=1, keepdims=True)
            memory_key = memory_pair(memory, 0, m, pair, micro)
            memory_value = memory_pair(memory, 1, m, pair, micro)
            scores = dot(queries.astype(BF16), memory_key, NT) + bias
            top = jnp.maximum(jnp.max(scores, axis=1, keepdims=True), own)
            expos = jnp.exp(scores - top)
            own = jnp.exp(own - top)
            total = jnp.sum(expos, axis=1, keepdims=True) + own
            inverse = 1.0 / total
            mixed = dot(expos.astype(BF16), memory_value) * inverse
            weight = jnp.broadcast_to(own * inverse, mixed.shape)
            attended[rows, cols] = merged(mixed, lower) + merged(weight, lower) * value
            found = jnp.where(lane == m * pairs + pair, top + jnp.log(total), found)
    stats[...] = found


def erf(values):
    values = jnp.clip(values, -3.832506856900711, 3.832506856900711)
    square = values * values
    above, below = ERF_TOP[0], ERF_LOW[0]
    for c in ERF_TOP[1:]:
        above = above * square + c
    for c in ERF_LOW[1:]:
        below = below * square + c
    return values * above / below


def feed_kernel(tok, cot, attended, vec, rest, out, grad_mid, grad_att, grads, vec_grad):
    count, width = tok.shape
    wide = 4
    low_att = attended[...].astype(BF16)
    w_out = tile(rest, 0)
    middle = tok[...].astype(F32) + dot(low_att, w_out)
    unit, inverse = unit_norm(middle)
    gain = vec[2:3, :]
    low = (unit * gain + vec[3:4, :]).astype(BF16)
    low_t = low.T
    cots = cot[...]
    total = middle + vec[4:5, :]
    grad_low = jnp.zeros((count, width), F32)
    bias_rows = []
    eighth = GROUPS // wide
    for c in range(wide):
        w_up = tile(rest, 1 + c)
        down = slice(eighth * c, eighth * (c + 1))
        w_down = rest[down, UNIT * (1 + wide) :, :].reshape(width, width)
        hidden = dot(low, w_up) + vec[5 + c : 6 + c, :]
        share = 0.5 + 0.5 * erf(hidden * 0.7071067811865476)
        slope = share + hidden * (0.3989422804014327 * jnp.exp(-0.5 * hidden * hidden))
        active = (hidden * share).astype(BF16)
        total = total + dot(active, w_down)
        grad_hidden_f = dot(cots, w_down, NT) * slope
        grad_hidden = grad_hidden_f.astype(BF16)
        bias_rows.append(column_sum(grad_hidden.astype(F32)))
        grad_low = grad_low + dot(grad_hidden, w_up, NT)
        grad_up = dot(low_t, grad_hidden).astype(BF16)
        grads[:, UNIT * (1 + c) : UNIT * (2 + c), :] = grad_up.reshape(GROUPS, UNIT, width)
        grad_down = dot(active, cots, TN).astype(BF16)
        grads[down, UNIT * (1 + wide) :, :] = grad_down.reshape(eighth, UNIT * wide, width)
    out[...] = total.astype(BF16)
    cots_f = cots.astype(F32)
    grad_middle = cots_f + norm_back(grad_low, unit, inverse, gain)
    grad_mid[...] = grad_middle
    branch = grad_middle.astype(BF16)
    grads[:, :UNIT, :] = dot(low_att, branch, TN).astype(BF16).reshape(GROUPS, UNIT, width)
    grad_att[...] = dot(branch, w_out, NT).astype(BF16)
    rows = [jnp.zeros((2, width), F32), column_sum(grad_low * unit), column_sum(grad_low)]
    rows += [column_sum(cots_f)] + bias_rows + [jnp.zeros((7, width), F32)]
    vec_grad[...] = jnp.concatenate(rows, axis=0)


def attend_back_kernel(
    info, query, kept, memory, attended, stats, grad_att, grad_query, grad_memory, own_key, own_value
):
    micro = info.shape[0]
    count, width = query.shape
    each = count // micro
    slots = memory.shape[0] * memory.shape[2] // micro
    share = memory.shape[2] // micro
    pairs = width // PAIR
    lower = iota((each, PAIR), 1) < HEAD_DIM
    lane = iota((2 * each, 128), 1)
    found = stats[...]
    deltas = jnp.zeros((2 * each, 128), F32)
    parts = {}
    for m in range(micro):
        rows = slice(each * m, each * (m + 1))
        for pair in range(pairs):
            cols = slice(PAIR * pair, PAIR * (pair + 1))
            grad = grad_att[rows, cols].astype(F32)
            product = stacked(grad * attended[rows, cols], lower)
            delta = jnp.sum(product, axis=1, keepdims=True)
            deltas = jnp.where(lane == m * pairs + pair, delta, deltas)
            parts[m, pair] = delta
    found_t, deltas_t = found.T, deltas.T
    for m in range(micro):
        rows = slice(each * m, each * (m + 1))
        lanes = iota((1, 2 * each), 1)
        place = info[m, 4] + jnp.where(lanes >= each, lanes - each, lanes)
        start = segment_start(info, m, place)
        end = 3 * iota((slots, 2 * each), 0)
        bias = jnp.where((end <= place) & (end >= start), 0.0, MASKED).astype(F32)
        for pair in range(pairs):
            cols = slice(PAIR * pair, PAIR * (pair + 1))
            at = m * pairs + pair
            key = kept[rows, cols].astype(F32)
            value = kept[rows, width + PAIR * pair : width + PAIR * (pair + 1)].astype(F32)
            query_f = query[rows, cols].astype(F32) * SCALE
            grad_f = grad_att[rows, cols].astype(F32)
            queries = stacked(query_f, lower)
            grads = stacked(grad_f, lower)
            own = jnp.sum(queries * jnp.concatenate([key, key], axis=0), axis=1, keepdims=True)
            own = jnp.exp(own - found[:, at : at + 1])
            grad_own = jnp.sum(
                grads * jnp.concatenate([value, value], axis=0), axis=1, keepdims=True
            )
            grad_own = (own * (grad_own - parts[m, pair])).astype(BF16).astype(F32)
            queries, grads = queries.astype(BF16), grads.astype(BF16)
            memory_key = memory_pair(memory, 0, m, pair, micro)
            memory_value = memory_pair(memory, 1, m, pair, micro)
            scores = dot(memory_key, queries, NT) + bias
            probs = jnp.exp(scores - found_t[at : at + 1, :])
            grad_probs = dot(memory_value, grads, NT)
            grad_scores = (probs * (grad_probs - deltas_t[at : at + 1, :])).astype(BF16)
            into = (slice(None), slice(share * m, share * (m + 1)), cols)
            shape = (memory.shape[0], share, PAIR)
            grad_memory[(into[0], 0) + into[1:]] = (
                dot(grad_scores, queries).astype(BF16).reshape(shape)
            )
            grad_memory[(into[0], 1) + into[1:]] = (
                dot(probs.astype(BF16), grads).astype(BF16).reshape(shape)
            )
            turned = dot(memory_key.T, grad_scores).T
            own_grad = merged(jnp.broadcast_to(grad_own, (2 * each, PAIR)), lower)
            own_weight = merged(jnp.broadcast_to(own, (2 * each, PAIR)), lower)
            grad_query[rows, cols] = (
                SCALE * (merged(turned, lower) + own_grad * key)
            ).astype(BF16)
            own_key[rows, cols] = own_grad * query_f
            own_value[rows, cols] = own_weight * grad_f


def compress_back_kernel(micro, grad_memory, window, conv, grads, grad_kept, rim):
    width = conv.shape[-1]
    each = grad_kept.shape[0] // micro
    for kind in range(2):
        cols = slice(width * kind, width * (kind + 1))
        grad = grad_memory[kind]
        total = None
        for tap in range(3):
            at = 3 * kind + tap
            term = dot(window[tap, :, cols], grad, TN).astype(BF16)
            grads[:, UNIT * at : UNIT * (at + 1), :] = term.reshape(GROUPS, UNIT, width)
            part = dot(grad, tile(conv, 3 + at), NT)
            high = part.astype(BF16)
            rest = (part - high.astype(F32)).astype(BF16)
            places = window_map(micro, each, tap)
            part = dot(places, high, TN) + dot(places, rest, TN)
            total = part if total is None else total + part
        grad_kept[:, cols] = total[: micro * each]
        rim[:, cols] = total[micro * each :]


def input_kernel(
    info,
    tok,
    normed,
    grad_query,
    grad_kept,
    rim,
    own_key,
    own_value,
    first,
    vec,
    grad_mid,
    vec_grad,
    grad_in,
    grads,
    total,
):
    count, width = tok.shape
    micro = info.shape[0]
    each = count // micro
    total[...] = grad_kept[...]
    for m in range(micro):
        rows = slice(each * (m + 1) - RIM, each * (m + 1))
        total[rows, :] = total[rows, :] + rim[RIM * m : RIM * (m + 1), :]
    valid = [valid_column(info, m, info[m, 4], each) for m in range(micro)]
    valid = jnp.concatenate(valid, axis=0)
    grad_key = ((total[:, :width] + own_key[...]) * valid).astype(BF16)
    grad_value = ((total[:, width:] + own_value[...]) * valid).astype(BF16)
    low_t = normed[...].T
    grad_low = None
    for at, grad in enumerate((grad_query[...], grad_key, grad_value)):
        part = dot(grad, tile(first, at), NT)
        grad_low = part if grad_low is None else grad_low + part
        term = dot(low_t, grad).astype(BF16)
        grads[:, UNIT * at : UNIT * (at + 1), :] = term.reshape(GROUPS, UNIT, width)
    unit, inverse = unit_norm(tok[...].astype(F32))
    back = norm_back(grad_low, unit, inverse, vec[0:1, :])
    grad_in[...] = (grad_mid[...] + back).astype(BF16)

    lanes = width // 2
    fine, wide, own_fine, own_wide = vector_maps(width)
    vectors = [column_sum(grad_low * unit), column_sum(grad_low)]
    vectors += [vec_grad[k : k + 1, :] for k in range(2, VECTORS)]
    dealt = jnp.concatenate([own_fine * v for v in vectors], axis=0).astype(BF16)
    dealt = dot(dealt, fine, NT)
    bias = [
        jnp.broadcast_to(vec_grad[VECTORS + c : VECTORS + c + 1, :], (8, width)) for c in range(4)
    ]
    bias = (jnp.concatenate(bias, axis=0) * own_wide).astype(BF16)
    packed = jnp.where(lane_window(lanes, VECTORS), dot(bias, wide, NT), 0.0)
    for k in range(VECTORS):
        packed = jnp.where(lane_window(lanes, k), dealt[GROUPS * k : GROUPS * (k + 1)], packed)
    packed = jnp.concatenate([packed, jnp.zeros((GROUPS, width - lanes), F32)], axis=1)
    spot = iota((GROUPS, UNIT, width), 1) == 0
    spread = jnp.broadcast_to(packed[:, None, :], (GROUPS, UNIT, width))
    grads[:, 3 * UNIT :, :] = jnp.where(spot, spread, 0.0).astype(BF16)


def per_device(
    tokens,
    lengths,
    ln1_gain,
    ln1_bias,
    w_query,
    w_key,
    w_value,
    conv_key,
    conv_value,
    w_out,
    ln2_gain,
    ln2_bias,
    w_up,
    b_up,
    w_down,
    b_down,
    cotangent,
):
    count = device_count()
    micro, _, each, width = tokens.shape
    ff = w_up.shape[1]
    wide = ff // width
    share = width // count
    seq = lax.axis_size("seq")
    all_tokens = micro * each
    slots = micro * each // 3
    memory_bytes = 4 * seq * slots * width

    halo = lax.ppermute(
        tokens[:, 0, each - RIM :], "seq", [(i, i + 1) for i in range(seq - 1)]
    ).reshape(micro * RIM, width)

    vectors = jnp.concatenate([ln1_gain, ln1_bias, ln2_gain, ln2_bias, b_down, b_up])
    vector_lengths = [share] * VECTORS + [ff // count]
    vector_rows = UNIT if count == GROUPS else 2
    vector_tile = vector_pack(vectors[None], vector_rows, width)[0]
    rest = [w_out] + [w_up[:, width * c : width * (c + 1)] for c in range(wide)] + [w_down]
    rest = spread(jnp.concatenate(rest, axis=0))
    rest_sizes = [1] * (1 + wide) + [wide]
    taps = jnp.concatenate([conv_key, conv_value], axis=0).reshape(6 * share, width)
    first = spread(jnp.concatenate([w_query, w_key, w_value, taps, vector_tile], axis=0))
    along, across, _ = exchange_orders()
    steps = len(across)
    for mask in along:
        first = gather_one(first, mask)
    first_parts = halves(first)
    for at in range(max(steps, len(along))):
        if at < steps:
            first_parts = gather_across(first_parts, at)
        if at < len(along):
            rest = gather_one(rest, along[at])
        first_parts, rest = together(first_parts, rest)
    first = gather_cores(first_parts)
    first_sizes = [1] * 9
    if count != GROUPS:
        dealt = vector_regroup(first[:, 9 * share], GROUPS, vector_lengths)
        dealt = vector_pack(dealt, UNIT, width)
        first = jnp.concatenate([grouped(first, first_sizes), dealt], axis=1)

    lengths = lengths[:, 0]
    first_pad = 3 * ((lengths[:, 0] + 2) // 3)
    second_pad = 3 * ((lengths[:, 1] + 2) // 3)
    second = 1 + first_pad
    offset = jnp.full_like(second, lax.axis_index("seq") * each)
    info = jnp.stack(
        [1 + lengths[:, 0], second, second + lengths[:, 1], second + second_pad, offset], axis=1
    ).astype(jnp.int32)

    tok = tokens.reshape(all_tokens, width)
    cot = cotangent.reshape(all_tokens, width)
    rows = (all_tokens, width)
    grown = 4 * max(memory_bytes // (1 << 20) - 2, 0)
    limits = [16, 16, 16 + grown, 28, 28 + grown, 28, 28]
    matmul = 2 * all_tokens * width * width

    normed, query, kept, vec = kernel(
        project_kernel,
        (info, tok, halo, first),
        (
            (rows, BF16),
            (rows, BF16),
            ((all_tokens + micro * RIM, 2 * width), BF16),
            ((16, width), F32),
        ),
        3 * matmul,
        limits[0],
    )
    window, memory_own = kernel(
        functools.partial(compress_kernel, micro),
        (kept, first),
        (((3, slots, 2 * width), BF16), ((2, slots, width), BF16)),
        2 * matmul,
        limits[1],
    )
    memory = memory_own.reshape((1,) * (seq.bit_length() - 1) + memory_own.shape)
    rest_parts = halves(rest)
    for at, mask in enumerate(along + [1]):
        memory = gather_step(memory, mask, place_of(mask, seq))
        if at < steps:
            rest_parts = gather_across(rest_parts, at)
            memory, rest_parts = together(memory, rest_parts)
    memory = memory.reshape((seq,) + memory_own.shape)
    rest = grouped(gather_cores(rest_parts), rest_sizes)
    attended, stats = kernel(
        attend_kernel,
        (info, query, kept, memory),
        ((rows, F32), ((2 * each, 128), F32)),
        4 * matmul,
        limits[2],
    )
    output, grad_mid, grad_att, rest_grads, vec_grad = kernel(
        feed_kernel,
        (tok, cot, attended, vec, rest),
        (
            (rows, BF16),
            (rows, F32),
            (rows, BF16),
            ((GROUPS, UNIT * (1 + 2 * wide), width), BF16),
            ((16, width), F32),
        ),
        27 * matmul,
        limits[3],
    )
    rest_held = reduce_cores(scattered(rest_grads, rest_sizes))
    grad_query, grad_memory, own_key, own_value = kernel(
        attend_back_kernel,
        (info, query, kept, memory, attended, stats, grad_att),
        ((rows, BF16), (memory.shape, BF16), (rows, F32), (rows, F32)),
        10 * matmul,
        limits[4],
    )
    rest_parts = halves(rest_held)
    held = grad_memory
    for at, mask in enumerate([1] + powers(2, seq)):
        held = held.reshape((-1, 2) + memory.shape[1:])
        held = reduce_step(held, mask, 1).astype(BF16)
        if at < steps:
            rest_parts = reduce_across(rest_parts, at)
            held, rest_parts = together(held, rest_parts)
    grad_memory = held.reshape(memory.shape[1:])
    rest = jnp.concatenate(rest_parts, axis=-2)
    conv_grads, grad_kept, rim = kernel(
        functools.partial(compress_back_kernel, micro),
        (grad_memory, window, first),
        (
            ((GROUPS, 6 * UNIT, width), BF16),
            ((all_tokens, 2 * width), F32),
            ((micro * RIM, 2 * width), F32),
        ),
        4 * matmul,
        limits[5],
    )
    conv_held = reduce_cores(scattered(conv_grads, [1] * 6))
    rim = lax.ppermute(rim, "seq", [(i + 1, i) for i in range(seq - 1)])
    grad_in, first_grads = pl.pallas_call(
        input_kernel,
        in_specs=[pl.BlockSpec(memory_space=pltpu.SMEM)]
        + [pl.BlockSpec(memory_space=pltpu.VMEM)] * 11,
        out_specs=[pl.BlockSpec(memory_space=pltpu.VMEM)] * 2,
        out_shape=[
            jax.ShapeDtypeStruct(rows, BF16),
            jax.ShapeDtypeStruct((GROUPS, 4 * UNIT, width), BF16),
        ],
        scratch_shapes=[pltpu.VMEM((all_tokens, 2 * width), F32)],
        compiler_params=pltpu.CompilerParams(vmem_limit_bytes=limits[6] << 20),
        cost_estimate=pl.CostEstimate(
            flops=6 * matmul, bytes_accessed=8 << 20, transcendentals=0
        ),
    )(
        info,
        tok,
        normed,
        grad_query,
        grad_kept,
        rim,
        own_key,
        own_value,
        first,
        vec,
        grad_mid,
        vec_grad,
    )
    if count != GROUPS:
        dealt = first_grads[:, 3 * UNIT, : VECTORS * UNIT + ff // GROUPS]
        dealt = vector_regroup(dealt, count, [UNIT] * VECTORS + [ff // GROUPS])
        dealt = vector_pack(dealt, vector_rows, width)
        first_grads = jnp.concatenate([scattered(first_grads, [1] * 3), dealt], axis=1)
    late = jnp.concatenate([conv_held, reduce_cores(first_grads)], axis=-2)
    parts = halves(late)
    back = along[::-1]
    for at in range(max(steps, len(along))):
        if at < steps:
            parts = reduce_across(parts, at)
        if at < len(along):
            rest_sum = reduce_one(rest, back[at])
            rest = rest_sum.astype(BF16)
        parts, rest = together(parts, rest)
    late = jnp.concatenate(parts, axis=-2)
    for mask in back:
        late_sum = reduce_one(late, mask)
        late = late_sum.astype(BF16)
    rest = rest_sum.reshape(rest.shape[-2:])
    convs, late = jnp.split(late_sum.reshape(late.shape[-2:]), [share * 6])
    convs = convs.reshape(2, 3, share, width)

    def own(buffer, number):
        return buffer[share * number : share * (number + 1)]

    vector_row = late[3 * share]

    def own_vector(number, length=share):
        return vector_row[share * number : share * number + length]

    return (
        output.reshape(tokens.shape),
        grad_in.reshape(tokens.shape),
        own_vector(0),
        own_vector(1),
        own(late, 0),
        own(late, 1),
        own(late, 2),
        convs[0],
        convs[1],
        own(rest, 0),
        own_vector(2),
        own_vector(3),
        jnp.concatenate([own(rest, 1 + c) for c in range(wide)], axis=1),
        own_vector(VECTORS, ff // count),
        rest[share * (1 + wide) :],
        own_vector(4),
    )


def solution(mesh):
    rows = P(AXES, None)
    vector = P(AXES)
    conv = P(None, AXES, None)
    part = P(None, "batch", "seq", None)
    weights = (vector, vector, rows, rows, rows, conv, conv, rows, vector, vector)
    weights = weights + (rows, vector, rows, vector)
    return jax.shard_map(
        per_device,
        mesh=mesh,
        in_specs=(part, P(None, "batch", None)) + weights + (part,),
        out_specs=(part, part) + weights,
        check_vma=False,
    )
```

```python
import jax
import jax.numpy as jnp
from jax import lax
from jax.experimental import pallas as pl
from jax.experimental.pallas import tpu as pltpu
from jax.sharding import PartitionSpec as P

HEADS = 8
HEAD_DIM = 64
SCALE = HEAD_DIM ** (-0.5)
EPSILON = 1e-06
AXES = ("batch", "seq")
GROUPS = 32
UNIT = 16
PAIR = 2 * HEAD_DIM
RIM = 8
MASKED = -1e30
F32 = jnp.float32
BF16 = jnp.bfloat16
TN = ((0,), (0,))
NT = ((1,), (1,))
ERF_TOP = (
    0.00022905065861350646,
    0.0034082910107109506,
    0.050955695062380861,
    0.18520832239976145,
    1.128379143519084,
)
ERF_LOW = (
    -1.1791602954361697e-7,
    0.000023547966471313185,
    0.0010179625278914885,
    0.014070470171167667,
    0.11098505178285362,
    0.49746925110067538,
    1.0,
)


def device_count():
    return lax.axis_size("batch") * lax.axis_size("seq")


def device_index():
    return lax.axis_index("batch") * lax.axis_size("seq") + lax.axis_index("seq")


def powers(low, high):
    masks = []
    while low < high:
        masks.append(low)
        low *= 2
    return masks


def exchange_masks(turned):
    seq = lax.axis_size("seq")
    across = powers(seq, device_count())
    return powers(2, seq)[::-1] + (across[::-1] if turned else across) + [1]


def swap(array, mask):
    return lax.ppermute(array, AXES, [(i, i ^ mask) for i in range(device_count())])


def after(array, *others):
    return lax.optimization_barrier((array,) + others)[0]


def around(bits, mask):
    return 2 ** sum(b > mask for b in bits), 2 ** sum(b < mask for b in bits)


def upper_half(mask):
    return ((device_index() & mask) != 0).astype(jnp.int32)


def place_kernel(upper, mine, other, out):
    at = upper[0]
    out[:, pl.ds(at, 1)] = mine[...][:, None]
    out[:, pl.ds(1 - at, 1)] = other[...][:, None]


def gather_step(held, bits, mask):
    other = swap(held, mask)
    outer, inner = around(bits, mask)
    rows = held.shape[1:]
    shape = (outer, inner) + rows
    mine, other = held.reshape(shape), other.reshape(shape)
    upper = upper_half(mask)
    if device_count() == GROUPS:
        out = ((outer, 2, inner) + rows, held.dtype)
        (held,) = kernel(place_kernel, (upper.reshape(1), mine, other), (out,), 0, 16)
    else:
        low, high = jnp.where(upper, other, mine), jnp.where(upper, mine, other)
        held = jnp.stack([low, high], axis=1)
    return held.reshape((-1,) + rows), bits + [mask]


def add_kernel(upper, keep, other, next_keep, next_send):
    at = upper[0]
    next_keep[...] = (keep[:, pl.ds(at, 1)] + other[:, pl.ds(at, 1)])[:, 0]
    next_send[...] = (keep[:, pl.ds(1 - at, 1)] + other[:, pl.ds(1 - at, 1)])[:, 0]


def reduce_step(state, mask, following):
    keep, send, bits = state
    other = swap(send, mask)
    if following is None:
        return (keep.astype(F32) + other.astype(F32)).reshape(keep.shape[1:])
    outer, inner = around(bits, following)
    rows = keep.shape[1:]
    shape = (outer, 2, inner) + rows
    keep, other = keep.reshape(shape), other.reshape(shape)
    upper = upper_half(following)
    if device_count() == GROUPS:
        out = ((outer, inner) + rows, keep.dtype)
        keep, send = kernel(add_kernel, (upper.reshape(1), keep, other), (out, out), 0, 20)
    else:
        total = (keep.astype(F32) + other.astype(F32)).astype(BF16)
        keep = lax.dynamic_index_in_dim(total, upper, 1, keepdims=False)
        send = lax.dynamic_index_in_dim(total, 1 - upper, 1, keepdims=False)
    bits = [b for b in bits if b != following]
    return keep.reshape((-1,) + rows), send.reshape((-1,) + rows), bits


def split_cores(blocks):
    pairs = blocks.reshape((-1, 2) + blocks.shape[1:])
    upper = upper_half(1)
    keep = lax.dynamic_index_in_dim(pairs, upper, 1, keepdims=False)
    return keep, lax.dynamic_index_in_dim(pairs, 1 - upper, 1, keepdims=False)


def joined(keep, send):
    return jnp.stack([keep, send], axis=1).reshape((-1,) + keep.shape[1:])


def grouped(buffer, sizes):
    count = buffer.shape[0]
    if count == GROUPS:
        return buffer
    width = buffer.shape[-1]
    share = width // count
    parts, start = [], 0
    for size in sizes:
        part = buffer[:, start : start + share * size]
        parts.append(part.reshape(GROUPS, UNIT * size, width))
        start += share * size
    return jnp.concatenate(parts, axis=1)


def scattered(buffer, sizes):
    count, width = device_count(), buffer.shape[-1]
    if count == GROUPS:
        return buffer
    parts, start = [], 0
    for size in sizes:
        part = buffer[:, start : start + UNIT * size]
        parts.append(part.reshape(count, width // count * size, width))
        start += UNIT * size
    return jnp.concatenate(parts, axis=1)


def vector_pack(vectors, rows, width):
    filled = jnp.pad(vectors, ((0, 0), (0, width - vectors.shape[1])))
    return jnp.pad(filled[:, None], ((0, 0), (0, rows - 1), (0, 0)))


def vector_regroup(vectors, parts, lengths):
    pieces, start = [], 0
    for length in lengths:
        pieces.append(vectors[:, start : start + length].reshape(parts, -1))
        start += length
    return jnp.concatenate(pieces, axis=1)


def dot(a, b, dims=((1,), (0,))):
    return lax.dot_general(a, b, (dims, ((), ())), preferred_element_type=F32)


def iota(shape, axis):
    return lax.broadcasted_iota(jnp.int32, shape, axis)


def tile(ref, place, size=1):
    rows = ref[:, UNIT * place : UNIT * (place + size), :]
    return rows.reshape(GROUPS * UNIT * size, rows.shape[-1])


def pack_kernel(key, taps, vec, first):
    unit = key.shape[0]
    first[:unit] = key[...]
    for tap in range(3):
        first[unit * (1 + tap) : unit * (2 + tap)] = taps[tap]
    first[4 * unit :] = vec[...]


def pack_rest_kernel(value, query, taps, w_out, w_up, second, third):
    unit, width = value.shape
    second[:unit] = value[...]
    for tap in range(3):
        second[unit * (1 + tap) : unit * (2 + tap)] = taps[tap]
    second[4 * unit :] = query[...]
    third[:unit] = w_out[...]
    for c in range(4):
        third[unit * (1 + c) : unit * (2 + c)] = w_up[:, width * c : width * (c + 1)]


def kernel(body, args, outs, flops, limit, scratch=()):
    spec = {jnp.dtype(jnp.int32): pltpu.SMEM}
    return pl.pallas_call(
        body,
        in_specs=[pl.BlockSpec(memory_space=spec.get(a.dtype, pltpu.VMEM)) for a in args],
        out_specs=[pl.BlockSpec(memory_space=pltpu.VMEM) for _ in outs],
        out_shape=[jax.ShapeDtypeStruct(shape, dtype) for shape, dtype in outs],
        scratch_shapes=list(scratch),
        compiler_params=pltpu.CompilerParams(vmem_limit_bytes=limit << 20),
        cost_estimate=pl.CostEstimate(
            flops=flops,
            bytes_accessed=sum(a.size * a.dtype.itemsize for a in args),
            transcendentals=0,
        ),
    )(*args)


def unit_norm(values):
    center = values - jnp.mean(values, axis=-1, keepdims=True)
    spread = jnp.mean(center * center, axis=-1, keepdims=True)
    inverse = lax.rsqrt(spread + EPSILON)
    return center * inverse, inverse


def norm_back(grad, unit, inverse, gain):
    e = grad * gain
    mean_e = jnp.mean(e, axis=-1, keepdims=True)
    mean_x = jnp.mean(e * unit, axis=-1, keepdims=True)
    return inverse * (e - mean_e - unit * mean_x)


def column_sum(values):
    return jnp.sum(values, axis=0, keepdims=True)


def valid_column(info, m, start, rows):
    place = start + iota((rows, 1), 0)
    first = (place >= 1) & (place < info[m, 0])
    second = (place >= info[m, 1]) & (place < info[m, 2])
    return jnp.where(first | second, 1.0, 0.0).astype(F32)


def segment_start(info, m, place):
    start = jnp.where(place >= 1, 1, 0)
    start = jnp.where(place >= info[m, 1], info[m, 1], start)
    return jnp.where(place >= info[m, 3], info[m, 3], start)


VECTORS = 5
BIAS_AT = VECTORS * UNIT


def vector_maps(width):
    lanes = width // 2
    fine = (iota((lanes, width), 0) & 15) == (iota((lanes, width), 1) & 15)
    wide = ((iota((lanes, width), 0) + 48) & 63) == (iota((lanes, width), 1) & 63)
    own_fine = iota((GROUPS, width), 1) >> 4 == iota((GROUPS, width), 0)
    own_wide = iota((GROUPS, width), 1) >> 6 == (iota((GROUPS, width), 0) & 7)
    as_bf16 = [jnp.where(m, 1.0, 0.0).astype(BF16) for m in (fine, wide)]
    as_f32 = [jnp.where(m, 1.0, 0.0).astype(F32) for m in (own_fine, own_wide)]
    return as_bf16 + as_f32


def lane_window(lanes, k):
    place = iota((GROUPS, lanes), 1)
    if k == VECTORS:
        return (place >= BIAS_AT) & (place < BIAS_AT + 64)
    return (place >= UNIT * k) & (place < UNIT * (k + 1))


def window_map(micro, each, tap):
    slots = each // 3
    shape = (micro * slots, micro * (each + RIM))
    row, place = iota(shape, 0), iota(shape, 1)
    m = jnp.zeros(shape, jnp.int32)
    for i in range(1, micro):
        m = m + jnp.where(row >= slots * i, 1, 0)
    source = 3 * (row - slots * m) - 2 + tap
    rim = micro * each + RIM * m + RIM + source
    target = jnp.where(source >= 0, each * m + source, rim)
    return jnp.where(place == target, 1.0, 0.0).astype(BF16)


def keep_and_compress(info, low, weights, kept, window, memory):
    micro = info.shape[0]
    each = low.shape[0] // micro - RIM
    valid = [valid_column(info, m, info[m, 4], each) for m in range(micro)]
    valid += [valid_column(info, m, info[m, 4] - RIM, RIM) for m in range(micro)]
    rows = (dot(low, tile(weights, 0)) * jnp.concatenate(valid, axis=0)).astype(BF16)
    kept[...] = rows
    total = None
    for tap in range(3):
        taken = dot(window_map(micro, each, tap), rows).astype(BF16)
        window[tap] = taken
        part = dot(taken, tile(weights, 1 + tap))
        total = part if total is None else total + part
    memory[...] = total.astype(BF16)


def key_kernel(info, tok, halo, weights, normed, kept, window, memory, vec):
    width = tok.shape[-1]
    lanes = width // 2
    fine, wide, own_fine, own_wide = vector_maps(width)
    rows = jnp.sum(weights[:, 4 * UNIT : 5 * UNIT, :lanes].astype(F32), axis=1)
    picked = [jnp.where(lane_window(lanes, k), rows, 0.0) for k in range(VECTORS + 1)]
    spread = dot(jnp.concatenate(picked[:VECTORS], axis=0).astype(BF16), fine)
    vectors = [
        column_sum(spread[GROUPS * k : GROUPS * (k + 1)] * own_fine) for k in range(VECTORS)
    ]
    bias = dot(picked[VECTORS].astype(BF16), wide) * own_wide
    bias = jnp.sum(bias.reshape(4, 8, width), axis=1)
    vec[...] = jnp.concatenate(vectors + [bias, jnp.zeros((7, width), F32)], axis=0)
    values = jnp.concatenate([tok[...], halo[...]], axis=0).astype(F32)
    unit, _ = unit_norm(values)
    low = (unit * vectors[0] + vectors[1]).astype(BF16)
    normed[...] = low
    keep_and_compress(info, low, weights, kept, window, memory)


def value_kernel(info, normed, weights, query, kept, window, memory):
    low = normed[...]
    keep_and_compress(info, low, weights, kept, window, memory)
    query[...] = dot(low[: query.shape[0]], tile(weights, 4)).astype(BF16)


def stacked(values, lower):
    zero = jnp.zeros_like(values)
    return jnp.concatenate(
        [jnp.where(lower, values, zero), jnp.where(lower, zero, values)], axis=0
    )


def merged(values, lower):
    half = values.shape[0] // 2
    return jnp.where(lower, values[:half], values[half:])


def memory_pair(memory, m, pair, micro):
    slots = memory.shape[1] // micro
    rows = memory[:, slots * m : slots * (m + 1), PAIR * pair : PAIR * (pair + 1)]
    return rows.reshape(memory.shape[0] * slots, PAIR)


def attend_kernel(info, query, keys, values, memory_keys, memory_values, attended, stats):
    micro = info.shape[0]
    count, width = query.shape
    each = count // micro
    slots = memory_keys.shape[0] * memory_keys.shape[1] // micro
    pairs = width // PAIR
    lower = iota((each, PAIR), 1) < HEAD_DIM
    lane = iota((2 * each, 128), 1)
    found = jnp.zeros((2 * each, 128), F32)
    for m in range(micro):
        rows = slice(each * m, each * (m + 1))
        place = info[m, 4] + iota((each, 1), 0)
        start = segment_start(info, m, place)
        end = 3 * iota((each, slots), 1)
        bias = jnp.where((end <= place) & (end >= start), 0.0, MASKED).astype(F32)
        bias = jnp.concatenate([bias, bias], axis=0)
        for pair in range(pairs):
            cols = slice(PAIR * pair, PAIR * (pair + 1))
            key = keys[rows, cols].astype(F32)
            value = values[rows, cols].astype(F32)
            queries = stacked(query[rows, cols].astype(F32) * SCALE, lower)
            own = jnp.sum(queries * jnp.concatenate([key, key], axis=0), axis=1, keepdims=True)
            memory_key = memory_pair(memory_keys, m, pair, micro)
            memory_value = memory_pair(memory_values, m, pair, micro)
            scores = dot(queries.astype(BF16), memory_key, NT) + bias
            top = jnp.maximum(jnp.max(scores, axis=1, keepdims=True), own)
            expos = jnp.exp(scores - top)
            own = jnp.exp(own - top)
            total = jnp.sum(expos, axis=1, keepdims=True) + own
            inverse = 1.0 / total
            mixed = dot(expos.astype(BF16), memory_value) * inverse
            weight = jnp.broadcast_to(own * inverse, mixed.shape)
            attended[rows, cols] = merged(mixed, lower) + merged(weight, lower) * value
            found = jnp.where(lane == m * pairs + pair, top + jnp.log(total), found)
    stats[...] = found


def erf(values):
    values = jnp.clip(values, -3.832506856900711, 3.832506856900711)
    square = values * values
    above, below = ERF_TOP[0], ERF_LOW[0]
    for c in ERF_TOP[1:]:
        above = above * square + c
    for c in ERF_LOW[1:]:
        below = below * square + c
    return values * above / below


def deal_rows(info, value, rows, keep, send, where):
    pairs = value.astype(BF16).reshape(-1, 2, rows, value.shape[-1])

    @pl.when(info[0, 5] == 0)
    def _():
        keep[where] = pairs[:, 0]
        send[where] = pairs[:, 1]

    @pl.when(info[0, 5] != 0)
    def _():
        keep[where] = pairs[:, 1]
        send[where] = pairs[:, 0]


def deal_tile(info, value, place, keep, send):
    where = (slice(None), slice(UNIT * place, UNIT * (place + 1)), slice(None))
    deal_rows(info, value, UNIT, keep, send, where)


def feed_kernel(
    info,
    tok,
    cot,
    attended,
    vec,
    up,
    down,
    out,
    grad_mid,
    grad_att,
    up_keep,
    up_send,
    down_keep,
    down_send,
    vec_grad,
):
    count, width = tok.shape
    wide = 4
    low_att = attended[...].astype(BF16)
    w_out = tile(up, 0)
    middle = tok[...].astype(F32) + dot(low_att, w_out)
    unit, inverse = unit_norm(middle)
    gain = vec[2:3, :]
    low = (unit * gain + vec[3:4, :]).astype(BF16)
    low_t = low.T
    cots = cot[...]
    total = middle + vec[4:5, :]
    grad_low = jnp.zeros((count, width), F32)
    bias_rows = []
    eighth = GROUPS // wide
    for c in range(wide):
        w_up = tile(up, 1 + c)
        w_down = down[eighth * c : eighth * (c + 1)].reshape(width, width)
        hidden = dot(low, w_up) + vec[5 + c : 6 + c, :]
        share = 0.5 + 0.5 * erf(hidden * 0.7071067811865476)
        slope = share + hidden * (0.3989422804014327 * jnp.exp(-0.5 * hidden * hidden))
        active = (hidden * share).astype(BF16)
        total = total + dot(active, w_down)
        grad_hidden_f = dot(cots, w_down, NT) * slope
        grad_hidden = grad_hidden_f.astype(BF16)
        bias_rows.append(column_sum(grad_hidden.astype(F32)))
        grad_low = grad_low + dot(grad_hidden, w_up, NT)
        deal_tile(info, dot(low_t, grad_hidden), 1 + c, up_keep, up_send)
        where = slice(eighth // 2 * c, eighth // 2 * (c + 1))
        deal_rows(info, dot(active, cots, TN), UNIT * wide, down_keep, down_send, where)
    out[...] = total.astype(BF16)
    cots_f = cots.astype(F32)
    grad_middle = cots_f + norm_back(grad_low, unit, inverse, gain)
    grad_mid[...] = grad_middle
    branch = grad_middle.astype(BF16)
    deal_tile(info, dot(low_att, branch, TN), 0, up_keep, up_send)
    grad_att[...] = dot(branch, w_out, NT).astype(BF16)
    rows = [jnp.zeros((2, width), F32), column_sum(grad_low * unit), column_sum(grad_low)]
    rows += [column_sum(cots_f)] + bias_rows + [jnp.zeros((7, width), F32)]
    vec_grad[...] = jnp.concatenate(rows, axis=0)


def deal_memory(info, value, share, keep, send, into):
    pairs = value.astype(BF16).reshape(-1, 2, share, value.shape[-1])

    @pl.when(info[0, 6] == 0)
    def _():
        keep[into] = pairs[:, 0]
        send[into] = pairs[:, 1]

    @pl.when(info[0, 6] != 0)
    def _():
        keep[into] = pairs[:, 1]
        send[into] = pairs[:, 0]


def attend_back_kernel(
    info,
    query,
    keys,
    values,
    memory_keys,
    memory_values,
    attended,
    stats,
    grad_att,
    grad_query,
    key_keep,
    key_send,
    value_keep,
    value_send,
    own_key,
    own_value,
):
    micro = info.shape[0]
    count, width = query.shape
    each = count // micro
    slots = memory_keys.shape[0] * memory_keys.shape[1] // micro
    share = memory_keys.shape[1] // micro
    pairs = width // PAIR
    lower = iota((each, PAIR), 1) < HEAD_DIM
    lane = iota((2 * each, 128), 1)
    found = stats[...]
    deltas = jnp.zeros((2 * each, 128), F32)
    parts = {}
    for m in range(micro):
        rows = slice(each * m, each * (m + 1))
        for pair in range(pairs):
            cols = slice(PAIR * pair, PAIR * (pair + 1))
            grad = grad_att[rows, cols].astype(F32)
            product = stacked(grad * attended[rows, cols], lower)
            delta = jnp.sum(product, axis=1, keepdims=True)
            deltas = jnp.where(lane == m * pairs + pair, delta, deltas)
            parts[m, pair] = delta
    found_t, deltas_t = found.T, deltas.T
    for m in range(micro):
        rows = slice(each * m, each * (m + 1))
        lanes = iota((1, 2 * each), 1)
        place = info[m, 4] + jnp.where(lanes >= each, lanes - each, lanes)
        start = segment_start(info, m, place)
        end = 3 * iota((slots, 2 * each), 0)
        bias = jnp.where((end <= place) & (end >= start), 0.0, MASKED).astype(F32)
        for pair in range(pairs):
            cols = slice(PAIR * pair, PAIR * (pair + 1))
            at = m * pairs + pair
            key = keys[rows, cols].astype(F32)
            value = values[rows, cols].astype(F32)
            query_f = query[rows, cols].astype(F32) * SCALE
            grad_f = grad_att[rows, cols].astype(F32)
            queries = stacked(query_f, lower)
            grads = stacked(grad_f, lower)
            own = jnp.sum(queries * jnp.concatenate([key, key], axis=0), axis=1, keepdims=True)
            own = jnp.exp(own - found[:, at : at + 1])
            grad_own = jnp.sum(
                grads * jnp.concatenate([value, value], axis=0), axis=1, keepdims=True
            )
            grad_own = (own * (grad_own - parts[m, pair])).astype(BF16).astype(F32)
            queries, grads = queries.astype(BF16), grads.astype(BF16)
            memory_key = memory_pair(memory_keys, m, pair, micro)
            memory_value = memory_pair(memory_values, m, pair, micro)
            scores = dot(memory_key, queries, NT) + bias
            probs = jnp.exp(scores - found_t[at : at + 1, :])
            grad_probs = dot(memory_value, grads, NT)
            grad_scores = (probs * (grad_probs - deltas_t[at : at + 1, :])).astype(BF16)
            into = (slice(None), slice(share * m, share * (m + 1)), cols)
            deal_memory(info, dot(grad_scores, queries), share, key_keep, key_send, into)
            deal_memory(info, dot(probs.astype(BF16), grads), share, value_keep, value_send, into)
            turned = dot(memory_key.T, grad_scores).T
            own_grad = merged(jnp.broadcast_to(grad_own, (2 * each, PAIR)), lower)
            own_weight = merged(jnp.broadcast_to(own, (2 * each, PAIR)), lower)
            grad_query[rows, cols] = (
                SCALE * (merged(turned, lower) + own_grad * key)
            ).astype(BF16)
            own_key[rows, cols] = own_grad * query_f
            own_value[rows, cols] = own_weight * grad_f


def compress_back(info, grad_memory, window, weights, grad_kept, rim, keep, send):
    micro = info.shape[0]
    each = grad_kept.shape[0] // micro
    grad = grad_memory[...]
    total = None
    for tap in range(3):
        deal_tile(info, dot(window[tap], grad, TN), tap, keep, send)
        part = dot(grad, tile(weights, 1 + tap), NT)
        high = part.astype(BF16)
        rest = (part - high.astype(F32)).astype(BF16)
        places = window_map(micro, each, tap)
        part = dot(places, high, TN) + dot(places, rest, TN)
        total = part if total is None else total + part
    grad_kept[...] = total[: micro * each]
    rim[...] = total[micro * each :]


def key_back_kernel(
    info, grad_memory, window, weights, normed, grad_query, grad_kept, rim, keep, send
):
    compress_back(info, grad_memory, window, weights, grad_kept, rim, keep, send)
    low = normed[: grad_query.shape[0], :]
    deal_tile(info, dot(low, grad_query[...], TN), 3, keep, send)


def value_back_kernel(
    info, grad_memory, window, weights, key_rim, grad_kept, rims, keep, send
):
    width = key_rim.shape[-1]
    rims[:, :width] = key_rim[...]
    value_rim = rims.at[:, width:]
    compress_back(info, grad_memory, window, weights, grad_kept, value_rim, keep, send)


def input_kernel(
    info,
    tok,
    normed,
    grad_query,
    key_grad,
    value_grad,
    rims,
    own_key,
    own_value,
    key_weights,
    value_weights,
    vec,
    grad_mid,
    vec_grad,
    grad_in,
    keep,
    send,
    total,
):
    count, width = tok.shape
    micro = info.shape[0]
    each = count // micro
    valid = [valid_column(info, m, info[m, 4], each) for m in range(micro)]
    valid = jnp.concatenate(valid, axis=0)
    low_t = normed[:count, :].T
    grad_low = dot(grad_query[...], tile(value_weights, 4), NT)
    sides = ((key_grad, own_key, key_weights), (value_grad, own_value, value_weights))
    for kind, (grad, own, weights) in enumerate(sides):
        total[...] = grad[...] + own[...]
        for m in range(micro):
            rows = slice(each * (m + 1) - RIM, each * (m + 1))
            rim = rims[RIM * m : RIM * (m + 1), width * kind : width * (kind + 1)]
            total[rows, :] = total[rows, :] + rim
        low_grad = (total[...] * valid).astype(BF16)
        grad_low = grad_low + dot(low_grad, tile(weights, 0), NT)
        deal_tile(info, dot(low_t, low_grad), kind, keep, send)
    unit, inverse = unit_norm(tok[...].astype(F32))
    back = norm_back(grad_low, unit, inverse, vec[0:1, :])
    grad_in[...] = (grad_mid[...] + back).astype(BF16)

    lanes = width // 2
    fine, wide, own_fine, own_wide = vector_maps(width)
    vectors = [column_sum(grad_low * unit), column_sum(grad_low)]
    vectors += [vec_grad[k : k + 1, :] for k in range(2, VECTORS)]
    dealt = jnp.concatenate([own_fine * v for v in vectors], axis=0).astype(BF16)
    dealt = dot(dealt, fine, NT)
    bias = [
        jnp.broadcast_to(vec_grad[VECTORS + c : VECTORS + c + 1, :], (8, width)) for c in range(4)
    ]
    bias = (jnp.concatenate(bias, axis=0) * own_wide).astype(BF16)
    packed = jnp.where(lane_window(lanes, VECTORS), dot(bias, wide, NT), 0.0)
    for k in range(VECTORS):
        packed = jnp.where(lane_window(lanes, k), dealt[GROUPS * k : GROUPS * (k + 1)], packed)
    packed = jnp.concatenate([packed, jnp.zeros((GROUPS, width - lanes), F32)], axis=1)
    spot = iota((GROUPS, UNIT, width), 1) == 0
    spread = jnp.broadcast_to(packed[:, None, :], (GROUPS, UNIT, width))
    packed = jnp.where(spot, spread, 0.0).reshape(GROUPS * UNIT, width)
    deal_tile(info, packed, 2, keep, send)


def per_device(
    tokens,
    lengths,
    ln1_gain,
    ln1_bias,
    w_query,
    w_key,
    w_value,
    conv_key,
    conv_value,
    w_out,
    ln2_gain,
    ln2_bias,
    w_up,
    b_up,
    w_down,
    b_down,
    cotangent,
):
    count = device_count()
    micro, _, each, width = tokens.shape
    ff = w_up.shape[1]
    wide = ff // width
    share = width // count
    seq = lax.axis_size("seq")
    all_tokens = micro * each
    slots = micro * each // 3
    memory_bytes = 4 * seq * slots * width

    halo = lax.ppermute(
        tokens[:, 0, each - RIM :], "seq", [(i, i + 1) for i in range(seq - 1)]
    ).reshape(micro * RIM, width)

    whole = count == GROUPS
    vectors = jnp.concatenate([ln1_gain, ln1_bias, ln2_gain, ln2_bias, b_down, b_up])
    vector_lengths = [share] * VECTORS + [ff // count]
    vector_tile = vector_pack(vectors[None], UNIT if whole else 2, width)[0]
    if whole:
        chunk = ((5 * UNIT, width), BF16)
        (first,) = kernel(pack_kernel, (w_key, conv_key, vector_tile), (chunk,), 0, 16)
        second, third = kernel(
            pack_rest_kernel, (w_value, w_query, conv_value, w_out, w_up), (chunk, chunk), 0, 16
        )
    else:
        first = jnp.concatenate([w_key, *conv_key, vector_tile], axis=0)
        second = jnp.concatenate([w_value, *conv_value, w_query], axis=0)
        ups = [w_up[:, width * c : width * (c + 1)] for c in range(wide)]
        third = jnp.concatenate([w_out] + ups, axis=0)
    steps = range(len(exchange_masks(False)))
    chunks, previous = [], None
    for at, rows in enumerate((first, second, third, w_down)):
        held, bits = rows[None], []
        if previous is not None:
            held = after(held, previous)
        for step, mask in enumerate(exchange_masks(at % 2 == 1)):
            held, bits = gather_step(held, bits, mask)
            if step == 0:
                previous = held
        chunks.append(held)
    sizes = ([1] * 5, [1] * 5, [1] * (1 + wide), [wide])
    if not whole:
        dealt = vector_regroup(chunks[0][:, 4 * share], GROUPS, vector_lengths)
        dealt = vector_pack(dealt, UNIT, width)
        chunks[0] = jnp.concatenate([grouped(chunks[0], [1] * 4), dealt], axis=1)
        chunks[1:] = [grouped(c, z) for c, z in zip(chunks[1:], sizes[1:])]
    first, second, third, fourth = chunks

    lengths = lengths[:, 0]
    first_pad = 3 * ((lengths[:, 0] + 2) // 3)
    second_pad = 3 * ((lengths[:, 1] + 2) // 3)
    start = 1 + first_pad
    seats = [lax.axis_index("seq") * each, upper_half(1) if whole else 0, upper_half(1)]
    seats = [jnp.full_like(start, seat) for seat in seats]
    info = [1 + lengths[:, 0], start, start + lengths[:, 1], start + second_pad]
    info = jnp.stack(info + seats, axis=1).astype(jnp.int32)

    tok = tokens.reshape(all_tokens, width)
    cot = cotangent.reshape(all_tokens, width)
    rows = (all_tokens, width)
    grown = 4 * max(memory_bytes // (1 << 20) - 2, 0)
    limits = [16, 16, 16 + grown, 28, 28 + grown, 28, 28]
    matmul = 2 * all_tokens * width * width

    padded = (all_tokens + micro * RIM, width)
    windows = (3, slots, width)

    normed, keys, key_window, memory_key, vec = kernel(
        key_kernel,
        (info, tok, halo, first),
        ((padded, BF16), (padded, BF16), (windows, BF16), ((slots, width), BF16), ((16, width), F32)),
        2 * matmul,
        limits[0],
    )
    query, values, value_window, memory_value = kernel(
        value_kernel,
        (info, normed, second),
        ((rows, BF16), (padded, BF16), (windows, BF16), ((slots, width), BF16)),
        3 * matmul,
        limits[1],
    )
    memories = []
    for held in (memory_key, memory_value):
        held, bits = held[None], []
        for mask in powers(2, seq)[::-1] + [1]:
            held, bits = gather_step(held, bits, mask)
        memories.append(held)
    attended, stats = kernel(
        attend_kernel,
        (info, query, keys, values, *memories),
        ((rows, F32), ((2 * each, 128), F32)),
        4 * matmul,
        limits[2],
    )
    half = GROUPS // 2
    up_half = ((half, UNIT * (1 + wide), width), BF16)
    down_half = ((half, UNIT * wide, width), BF16)
    output, grad_mid, grad_att, *halves, vec_grad = kernel(
        feed_kernel,
        (info, tok, cot, attended, vec, third, fourth),
        (
            (rows, BF16),
            (rows, F32),
            (rows, BF16),
            up_half,
            up_half,
            down_half,
            down_half,
            ((16, width), F32),
        ),
        27 * matmul,
        limits[3],
    )
    all_bits = powers(2, count)

    def begin(keep, send, size):
        if not whole:
            keep, send = split_cores(scattered(joined(keep, send), size))
        return keep, send, all_bits

    def reduce_masks(turned):
        return exchange_masks(turned)[::-1]

    def advance(state, turned, step):
        masks = reduce_masks(turned) + [None]
        return reduce_step(state, masks[step], masks[step + 1])

    ups = advance(begin(*halves[:2], sizes[2]), False, 0)
    downs = advance(begin(*halves[2:], sizes[3]), True, 0)

    memory_half = ((seq // 2, slots, width), BF16)
    grad_query, *halves, own_key, own_value = kernel(
        attend_back_kernel,
        (info, query, keys, values, *memories, attended, stats, grad_att),
        ((rows, BF16),) + (memory_half,) * 4 + ((rows, F32), (rows, F32)),
        10 * matmul,
        limits[4],
    )
    memory_masks = [1] + powers(2, seq) + [None]
    memory_grads = [(*halves[:2], powers(2, seq)), (*halves[2:], powers(2, seq))]
    for now, following in zip(memory_masks, memory_masks[1:]):
        memory_grads = [reduce_step(state, now, following) for state in memory_grads]
        if now == 1:
            memory_grads = [
                (after(keep, ups[0], downs[0]), send, bits) for keep, send, bits in memory_grads
            ]
    key_grad, value_grad = (grad.astype(BF16) for grad in memory_grads)
    for step in range(1, 1 + len(powers(seq, count))):
        ups, downs = advance(ups, False, step), advance(downs, True, step)

    def pieces(size):
        return (((half, UNIT * size, width), BF16),) * 2

    key_kept, key_rim, *halves = kernel(
        key_back_kernel,
        (info, after(key_grad, ups[0], downs[0]), key_window, first, normed, grad_query),
        ((rows, F32), ((micro * RIM, width), F32)) + pieces(4),
        3 * matmul,
        limits[5],
    )
    late_keys = begin(*halves, [1] * 4)
    value_kept, rims, *halves = kernel(
        value_back_kernel,
        (info, value_grad, value_window, second, key_rim),
        ((rows, F32), ((micro * RIM, 2 * width), F32)) + pieces(3),
        3 * matmul,
        limits[5],
    )
    late_values = begin(*halves, [1] * 3)
    rims = lax.ppermute(rims, "seq", [(i + 1, i) for i in range(seq - 1)])
    grad_in, *halves = kernel(
        input_kernel,
        (
            info,
            tok,
            normed,
            grad_query,
            key_kept,
            value_kept,
            rims,
            own_key,
            own_value,
            first,
            second,
            vec,
            grad_mid,
            vec_grad,
        ),
        ((rows, BF16),) + pieces(3),
        6 * matmul,
        limits[6],
        (pltpu.VMEM(rows, F32),),
    )
    if whole:
        late_inputs = begin(*halves, [1] * 3)
    else:
        dealt = joined(*halves)
        vectors = dealt[:, 2 * UNIT, : VECTORS * UNIT + ff // GROUPS]
        vectors = vector_regroup(vectors, count, [UNIT] * VECTORS + [ff // GROUPS])
        dealt = [scattered(dealt, [1] * 2), vector_pack(vectors, 2, width)]
        late_inputs = (*split_cores(jnp.concatenate(dealt, axis=1)), all_bits)

    for step in steps:
        late_keys = advance(late_keys, False, step)
        late_values = advance(late_values, True, step)
        late_inputs = advance(late_inputs, False, step)
    for step in list(steps)[1 + len(powers(seq, count)) :]:
        ups, downs = advance(ups, False, step), advance(downs, True, step)
    conv_keys = late_keys[: 3 * share].reshape(3, share, width)
    conv_values = late_values.reshape(3, share, width)

    def own(buffer, number):
        return buffer[share * number : share * (number + 1)]

    vector_row = late_inputs[2 * share]

    def own_vector(number, length=share):
        return vector_row[share * number : share * number + length]

    return (
        output.reshape(tokens.shape),
        grad_in.reshape(tokens.shape),
        own_vector(0),
        own_vector(1),
        own(late_keys, 3),
        own(late_inputs, 0),
        own(late_inputs, 1),
        conv_keys,
        conv_values,
        own(ups, 0),
        own_vector(2),
        own_vector(3),
        jnp.concatenate([own(ups, 1 + c) for c in range(wide)], axis=1),
        own_vector(VECTORS, ff // count),
        downs,
        own_vector(4),
    )


def solution(mesh):
    rows = P(AXES, None)
    vector = P(AXES)
    conv = P(None, AXES, None)
    part = P(None, "batch", "seq", None)
    weights = (vector, vector, rows, rows, rows, conv, conv, rows, vector, vector)
    weights = weights + (rows, vector, rows, vector)
    return jax.shard_map(
        per_device,
        mesh=mesh,
        in_specs=(part, P(None, "batch", None)) + weights + (part,),
        out_specs=(part, part) + weights,
        check_vma=False,
    )
```

```python
import functools

import jax
import jax.numpy as jnp
from jax import lax
from jax.experimental import pallas as pl
from jax.experimental.pallas import tpu as pltpu
from jax.sharding import PartitionSpec as P

HEADS = 8
HEAD_DIM = 64
SCALE = HEAD_DIM ** (-0.5)
EPSILON = 1e-06
AXES = ("batch", "seq")
GROUPS = 32
UNIT = 16
PAIR = 2 * HEAD_DIM
RIM = 8
MASKED = -1e30
F32 = jnp.float32
BF16 = jnp.bfloat16
TN = ((0,), (0,))
NT = ((1,), (1,))
ERF_TOP = (
    0.00022905065861350646,
    0.0034082910107109506,
    0.050955695062380861,
    0.18520832239976145,
    1.128379143519084,
)
ERF_LOW = (
    -1.1791602954361697e-7,
    0.000023547966471313185,
    0.0010179625278914885,
    0.014070470171167667,
    0.11098505178285362,
    0.49746925110067538,
    1.0,
)


def device_count():
    return lax.axis_size("batch") * lax.axis_size("seq")


def device_index():
    return lax.axis_index("batch") * lax.axis_size("seq") + lax.axis_index("seq")


def powers(low, high):
    masks = []
    while low < high:
        masks.append(low)
        low *= 2
    return masks


def swap(array, mask):
    return lax.ppermute(array, AXES, [(i, i ^ mask) for i in range(device_count())])


def upper_half(mask):
    return ((device_index() & mask) != 0).astype(jnp.int32)


class Order:
    def __init__(self):
        self.last = None

    def turn(self, array):
        if self.last is not None:
            array, _ = lax.optimization_barrier((array, self.last))
        return array

    def done(self, array):
        self.last = array


def axis_of(bits, mask):
    return sum(b > mask for b in bits)


def bit_shape(bits, rows):
    return (2,) * len(bits) + tuple(rows)


def at_bit(rank, axis, index, rows):
    where = [slice(None)] * rank
    where[axis] = pl.ds(index, 1)
    where[-2] = rows
    return tuple(where)


def overlaps(lefts, rights):
    found, left_at = [], 0
    for i, left in enumerate(lefts):
        right_at = 0
        for j, right in enumerate(rights):
            low = max(left_at, right_at)
            high = min(left_at + left, right_at + right)
            if low < high:
                found.append(
                    (i, j, slice(low - left_at, high - left_at), slice(low - right_at, high - right_at))
                )
            right_at += right
        left_at += left
    return found


def place_kernel(axes, cuts, upper, *refs):
    count = len(axes)
    for i, j, inside, outside in cuts:
        mine, other, out = refs[2 * i], refs[2 * i + 1], refs[2 * count + j]
        rank, axis, at = len(out.shape), axes[i], upper[i]
        source = (slice(None),) * (rank - 3) + (inside, slice(None))
        out[at_bit(rank, axis, at, outside)] = jnp.expand_dims(mine[source], axis)
        out[at_bit(rank, axis, 1 - at, outside)] = jnp.expand_dims(other[source], axis)


def add_kernel(axes, cuts, count, upper, *refs):
    for i, j, inside, outside in cuts:
        keep, other = refs[2 * i], refs[2 * i + 1]
        next_keep, next_send = refs[2 * count + 2 * j], refs[2 * count + 2 * j + 1]
        rank, axis, at = len(keep.shape), axes[j], upper[j]
        into = (slice(None),) * (rank - 3) + (outside, slice(None))
        here, there = at_bit(rank, axis, at, inside), at_bit(rank, axis, 1 - at, inside)
        next_send[into] = jnp.squeeze(keep[there] + other[there], axis)
        next_keep[into] = jnp.squeeze(keep[here] + other[here], axis)


class Gather:
    def __init__(self, order, rows):
        self.order, self.parts, self.bits = order, [rows], [[]]

    def go(self, *masks, wait=False):
        self.masks = masks
        parts = [self.order.turn(p) for p in self.parts] if wait else self.parts
        self.others = [swap(p, m) for p, m in zip(parts, masks)]

    def place(self, *sizes):
        olds = [p.shape[-2] for p in self.parts]
        sizes = sizes or olds
        axes = [axis_of(b, m) for b, m in zip(self.bits, self.masks)]
        bits = [sorted(b + [m], reverse=True) for b, m in zip(self.bits, self.masks)]
        uppers = [upper_half(m) for m in self.masks]
        width = self.parts[0].shape[-1]
        out_bits = [bits[min(j, len(bits) - 1)] for j in range(len(sizes))]
        if device_count() == GROUPS:
            args = []
            for mine, other in zip(self.parts, self.others):
                args += [self.order.turn(mine), other]
            outs = [(bit_shape(b, (r, width)), BF16) for b, r in zip(out_bits, sizes)]
            body = functools.partial(place_kernel, axes, overlaps(olds, sizes))
            self.parts = kernel(body, (jnp.stack(uppers), *args), outs, 0, 20)
            self.order.done(self.parts[0])
        else:
            held = []
            for mine, other, axis, up in zip(self.parts, self.others, axes, uppers):
                low, high = jnp.where(up, other, mine), jnp.where(up, mine, other)
                held.append(jnp.stack([low, high], axis=axis))
            self.parts = cut_rows(held, olds, sizes)
        self.bits = out_bits
        return self

    def whole(self):
        held = self.parts[0]
        return held.reshape((-1,) + held.shape[-2:])


def cut_rows(arrays, olds, sizes):
    if list(olds) == list(sizes):
        return arrays
    joint = jnp.concatenate(arrays, axis=-2)
    ends = [sum(sizes[: j + 1]) for j in range(len(sizes) - 1)]
    return jnp.split(joint, ends, axis=-2)


class Reduce:
    def __init__(self, order, keep, send, bits):
        shape = bit_shape(bits, keep.shape[-2:])
        self.order, self.bits = order, [bits]
        self.keeps, self.sends = [keep.reshape(shape)], [send.reshape(shape)]

    def go(self, *masks, wait=False):
        sends = [self.order.turn(p) for p in self.sends] if wait else self.sends
        self.others = [swap(p, m) for p, m in zip(sends, masks)]

    def add(self, masks, *sizes):
        olds = [p.shape[-2] for p in self.keeps]
        sizes = sizes or olds
        bits = [self.bits[min(j, len(olds) - 1)] for j in range(len(sizes))]
        axes = [axis_of(b, m) for b, m in zip(bits, masks)]
        uppers = [upper_half(m) for m in masks]
        width = self.keeps[0].shape[-1]
        left = [[b for b in old if b != m] for old, m in zip(bits, masks)]
        if device_count() == GROUPS:
            args = []
            for keep, other in zip(self.keeps, self.others):
                args += [self.order.turn(keep), other]
            outs = []
            for b, r in zip(left, sizes):
                outs += [(bit_shape(b, (r, width)), BF16)] * 2
            body = functools.partial(add_kernel, axes, overlaps(olds, sizes), len(olds))
            both = kernel(body, (jnp.stack(uppers), *args), outs, 0, 20)
            self.keeps, self.sends = both[0::2], both[1::2]
            self.order.done(self.keeps[0])
        else:
            sums = [
                (k.astype(F32) + o.astype(F32)).astype(BF16)
                for k, o in zip(self.keeps, self.others)
            ]
            sums = cut_rows(sums, olds, sizes)
            take = lax.dynamic_index_in_dim
            self.keeps = [take(t, u, a, False) for t, u, a in zip(sums, uppers, axes)]
            self.sends = [take(t, 1 - u, a, False) for t, u, a in zip(sums, uppers, axes)]
        self.bits = left
        return self

    def total(self):
        keep, other = self.order.turn(self.keeps[0]), self.others[0]
        return (keep.astype(F32) + other.astype(F32)).reshape(keep.shape[-2:])


def split_cores(blocks):
    pairs = blocks.reshape((-1, 2) + blocks.shape[1:])
    upper = upper_half(1)
    keep = lax.dynamic_index_in_dim(pairs, upper, 1, keepdims=False)
    return keep, lax.dynamic_index_in_dim(pairs, 1 - upper, 1, keepdims=False)


def joined(keep, send):
    return jnp.stack([keep, send], axis=1).reshape((-1,) + keep.shape[1:])


def grouped(buffer, sizes):
    count = buffer.shape[0]
    if count == GROUPS:
        return buffer
    width = buffer.shape[-1]
    share = width // count
    parts, start = [], 0
    for size in sizes:
        part = buffer[:, start : start + share * size]
        parts.append(part.reshape(GROUPS, UNIT * size, width))
        start += share * size
    return jnp.concatenate(parts, axis=1)


def scattered(buffer, sizes):
    count, width = device_count(), buffer.shape[-1]
    if count == GROUPS:
        return buffer
    parts, start = [], 0
    for size in sizes:
        part = buffer[:, start : start + UNIT * size]
        parts.append(part.reshape(count, width // count * size, width))
        start += UNIT * size
    return jnp.concatenate(parts, axis=1)


def vector_pack(vectors, rows, width):
    filled = jnp.pad(vectors, ((0, 0), (0, width - vectors.shape[1])))
    return jnp.pad(filled[:, None], ((0, 0), (0, rows - 1), (0, 0)))


def vector_regroup(vectors, parts, lengths):
    pieces, start = [], 0
    for length in lengths:
        pieces.append(vectors[:, start : start + length].reshape(parts, -1))
        start += length
    return jnp.concatenate(pieces, axis=1)


def dot(a, b, dims=((1,), (0,))):
    return lax.dot_general(a, b, (dims, ((), ())), preferred_element_type=F32)


def iota(shape, axis):
    return lax.broadcasted_iota(jnp.int32, shape, axis)


def tile(ref, place, size=1):
    rows = ref[:, UNIT * place : UNIT * (place + size), :]
    return rows.reshape(GROUPS * UNIT * size, rows.shape[-1])


def pack_kernel(key, taps, *refs):
    vectors, first = refs[:-1], refs[-1]
    unit, width = key.shape
    first[:unit] = key[...]
    for tap in range(3):
        first[unit * (1 + tap) : unit * (2 + tap)] = taps[tap]
    row, start = jnp.zeros((UNIT, width), F32), 0
    for part in vectors:
        length = part.shape[-1]
        spots = iota((length, width), 1) == iota((length, width), 0) + start
        shown = jnp.broadcast_to(part[...].astype(F32), (UNIT, length)).astype(BF16)
        row = row + dot(shown, jnp.where(spots, 1.0, 0.0).astype(BF16))
        start += length
    first[4 * unit :] = jnp.where(iota((UNIT, width), 0) == 0, row, 0.0).astype(BF16)


def pack_second_kernel(value, query, taps, second):
    unit = value.shape[0]
    second[:unit] = value[...]
    for tap in range(3):
        second[unit * (1 + tap) : unit * (2 + tap)] = taps[tap]
    second[4 * unit :] = query[...]


def pack_rest_kernel(w_out, w_up, w_down, rest):
    unit, width = w_out.shape
    rest[:unit] = w_out[...]
    for c in range(4):
        rest[unit * (1 + c) : unit * (2 + c)] = w_up[:, width * c : width * (c + 1)]
    rest[5 * unit :] = w_down[...]


def kernel(body, args, outs, flops, limit, scratch=()):
    spec = {jnp.dtype(jnp.int32): pltpu.SMEM}
    return pl.pallas_call(
        body,
        in_specs=[pl.BlockSpec(memory_space=spec.get(a.dtype, pltpu.VMEM)) for a in args],
        out_specs=[pl.BlockSpec(memory_space=pltpu.VMEM) for _ in outs],
        out_shape=[jax.ShapeDtypeStruct(shape, dtype) for shape, dtype in outs],
        scratch_shapes=list(scratch),
        compiler_params=pltpu.CompilerParams(vmem_limit_bytes=limit << 20),
        cost_estimate=pl.CostEstimate(
            flops=flops,
            bytes_accessed=sum(a.size * a.dtype.itemsize for a in args),
            transcendentals=0,
        ),
    )(*args)


def unit_norm(values):
    center = values - jnp.mean(values, axis=-1, keepdims=True)
    spread = jnp.mean(center * center, axis=-1, keepdims=True)
    inverse = lax.rsqrt(spread + EPSILON)
    return center * inverse, inverse


def norm_back(grad, unit, inverse, gain):
    e = grad * gain
    mean_e = jnp.mean(e, axis=-1, keepdims=True)
    mean_x = jnp.mean(e * unit, axis=-1, keepdims=True)
    return inverse * (e - mean_e - unit * mean_x)


def column_sum(values):
    return jnp.sum(values, axis=0, keepdims=True)


def valid_column(info, m, start, rows):
    place = start + iota((rows, 1), 0)
    first = (place >= 1) & (place < info[m, 0])
    second = (place >= info[m, 1]) & (place < info[m, 2])
    return jnp.where(first | second, 1.0, 0.0).astype(F32)


def segment_start(info, m, place):
    start = jnp.where(place >= 1, 1, 0)
    start = jnp.where(place >= info[m, 1], info[m, 1], start)
    return jnp.where(place >= info[m, 3], info[m, 3], start)


VECTORS = 5
BIAS_AT = VECTORS * UNIT


def vector_maps(width):
    lanes = width // 2
    fine = (iota((lanes, width), 0) & 15) == (iota((lanes, width), 1) & 15)
    wide = ((iota((lanes, width), 0) + 48) & 63) == (iota((lanes, width), 1) & 63)
    own_fine = iota((GROUPS, width), 1) >> 4 == iota((GROUPS, width), 0)
    own_wide = iota((GROUPS, width), 1) >> 6 == (iota((GROUPS, width), 0) & 7)
    as_bf16 = [jnp.where(m, 1.0, 0.0).astype(BF16) for m in (fine, wide)]
    as_f32 = [jnp.where(m, 1.0, 0.0).astype(F32) for m in (own_fine, own_wide)]
    return as_bf16 + as_f32


def lane_window(lanes, k):
    place = iota((GROUPS, lanes), 1)
    if k == VECTORS:
        return (place >= BIAS_AT) & (place < BIAS_AT + 64)
    return (place >= UNIT * k) & (place < UNIT * (k + 1))


def window_map(micro, each, tap):
    slots = each // 3
    shape = (micro * slots, micro * (each + RIM))
    row, place = iota(shape, 0), iota(shape, 1)
    m = jnp.zeros(shape, jnp.int32)
    for i in range(1, micro):
        m = m + jnp.where(row >= slots * i, 1, 0)
    source = 3 * (row - slots * m) - 2 + tap
    rim = micro * each + RIM * m + RIM + source
    target = jnp.where(source >= 0, each * m + source, rim)
    return jnp.where(place == target, 1.0, 0.0).astype(BF16)


def keep_and_compress(info, low, weights, kept, window, memory):
    micro = info.shape[0]
    each = low.shape[0] // micro - RIM
    valid = [valid_column(info, m, info[m, 4], each) for m in range(micro)]
    valid += [valid_column(info, m, info[m, 4] - RIM, RIM) for m in range(micro)]
    rows = (dot(low, tile(weights, 0)) * jnp.concatenate(valid, axis=0)).astype(BF16)
    kept[...] = rows
    total = None
    for tap in range(3):
        taken = dot(window_map(micro, each, tap), rows).astype(BF16)
        window[tap] = taken
        part = dot(taken, tile(weights, 1 + tap))
        total = part if total is None else total + part
    memory[...] = total.astype(BF16)


def key_kernel(info, tok, halo, weights, normed, kept, window, memory, vec):
    width = tok.shape[-1]
    lanes = width // 2
    fine, wide, own_fine, own_wide = vector_maps(width)
    rows = jnp.sum(weights[:, 4 * UNIT : 5 * UNIT, :lanes].astype(F32), axis=1)
    picked = [jnp.where(lane_window(lanes, k), rows, 0.0) for k in range(VECTORS + 1)]
    spread = dot(jnp.concatenate(picked[:VECTORS], axis=0).astype(BF16), fine)
    vectors = [
        column_sum(spread[GROUPS * k : GROUPS * (k + 1)] * own_fine) for k in range(VECTORS)
    ]
    bias = dot(picked[VECTORS].astype(BF16), wide) * own_wide
    bias = jnp.sum(bias.reshape(4, 8, width), axis=1)
    vec[...] = jnp.concatenate(vectors + [bias, jnp.zeros((7, width), F32)], axis=0)
    values = jnp.concatenate([tok[...], halo[...]], axis=0).astype(F32)
    unit, _ = unit_norm(values)
    low = (unit * vectors[0] + vectors[1]).astype(BF16)
    normed[...] = low
    keep_and_compress(info, low, weights, kept, window, memory)


def value_kernel(info, normed, weights, query, kept, window, memory):
    low = normed[...]
    keep_and_compress(info, low, weights, kept, window, memory)
    query[...] = dot(low[: query.shape[0]], tile(weights, 4)).astype(BF16)


def stacked(values, lower):
    zero = jnp.zeros_like(values)
    return jnp.concatenate(
        [jnp.where(lower, values, zero), jnp.where(lower, zero, values)], axis=0
    )


def merged(values, lower):
    half = values.shape[0] // 2
    return jnp.where(lower, values[:half], values[half:])


def memory_pair(memory, m, pair, micro):
    slots = memory.shape[1] // micro
    rows = memory[:, slots * m : slots * (m + 1), PAIR * pair : PAIR * (pair + 1)]
    return rows.reshape(memory.shape[0] * slots, PAIR)


def attend_kernel(info, query, keys, values, memory_keys, memory_values, attended, stats):
    micro = info.shape[0]
    count, width = query.shape
    each = count // micro
    slots = memory_keys.shape[0] * memory_keys.shape[1] // micro
    pairs = width // PAIR
    lower = iota((each, PAIR), 1) < HEAD_DIM
    lane = iota((2 * each, 128), 1)
    found = jnp.zeros((2 * each, 128), F32)
    for m in range(micro):
        rows = slice(each * m, each * (m + 1))
        place = info[m, 4] + iota((each, 1), 0)
        start = segment_start(info, m, place)
        end = 3 * iota((each, slots), 1)
        bias = jnp.where((end <= place) & (end >= start), 0.0, MASKED).astype(F32)
        bias = jnp.concatenate([bias, bias], axis=0)
        for pair in range(pairs):
            cols = slice(PAIR * pair, PAIR * (pair + 1))
            key = keys[rows, cols].astype(F32)
            value = values[rows, cols].astype(F32)
            queries = stacked(query[rows, cols].astype(F32) * SCALE, lower)
            own = jnp.sum(queries * jnp.concatenate([key, key], axis=0), axis=1, keepdims=True)
            memory_key = memory_pair(memory_keys, m, pair, micro)
            memory_value = memory_pair(memory_values, m, pair, micro)
            scores = dot(queries.astype(BF16), memory_key, NT) + bias
            top = jnp.maximum(jnp.max(scores, axis=1, keepdims=True), own)
            expos = jnp.exp(scores - top)
            own = jnp.exp(own - top)
            total = jnp.sum(expos, axis=1, keepdims=True) + own
            inverse = 1.0 / total
            mixed = dot(expos.astype(BF16), memory_value) * inverse
            weight = jnp.broadcast_to(own * inverse, mixed.shape)
            attended[rows, cols] = merged(mixed, lower) + merged(weight, lower) * value
            found = jnp.where(lane == m * pairs + pair, top + jnp.log(total), found)
    stats[...] = found


def erf(values):
    values = jnp.clip(values, -3.832506856900711, 3.832506856900711)
    square = values * values
    above, below = ERF_TOP[0], ERF_LOW[0]
    for c in ERF_TOP[1:]:
        above = above * square + c
    for c in ERF_LOW[1:]:
        below = below * square + c
    return values * above / below


def even_first(flag, rows, size):
    pairs = rows.reshape(-1, 2, size, rows.shape[-1])
    even, odd = pairs[:, 0], pairs[:, 1]
    halves = [jnp.where(flag == 0, even, odd), jnp.where(flag == 0, odd, even)]
    return jnp.concatenate(halves, axis=0).reshape(rows.shape)


def deal(value, rows, keep, send, blocks, start):
    halves = value.astype(BF16).reshape(2, -1, rows, value.shape[-1])
    keep[blocks, start : start + rows, :] = halves[0]
    send[blocks, start : start + rows, :] = halves[1]


def deal_tile(value, place, keep, send):
    deal(value, UNIT, keep, send, slice(None), UNIT * place)


def feed_kernel(
    info,
    tok,
    cot,
    attended,
    vec,
    rest,
    out,
    grad_mid,
    grad_att,
    keep,
    send,
    vec_grad,
):
    count, width = tok.shape
    wide = 4
    low_att = attended[...].astype(BF16)
    w_out = tile(rest, 0)
    middle = tok[...].astype(F32) + dot(low_att, w_out)
    unit, inverse = unit_norm(middle)
    gain = vec[2:3, :]
    low = (unit * gain + vec[3:4, :]).astype(BF16)
    flag = info[0, 5]
    low_t = even_first(flag, low.T, UNIT)
    cots = cot[...]
    total = middle + vec[4:5, :]
    grad_low = jnp.zeros((count, width), F32)
    bias_rows = []
    eighth = GROUPS // wide
    for c in range(wide):
        w_up = tile(rest, 1 + c)
        down = slice(eighth * c, eighth * (c + 1))
        w_down = rest[down, UNIT * (1 + wide) :, :].reshape(width, width)
        hidden = dot(low, w_up) + vec[5 + c : 6 + c, :]
        share = 0.5 + 0.5 * erf(hidden * 0.7071067811865476)
        slope = share + hidden * (0.3989422804014327 * jnp.exp(-0.5 * hidden * hidden))
        active = (hidden * share).astype(BF16)
        total = total + dot(active, w_down)
        grad_hidden_f = dot(cots, w_down, NT) * slope
        grad_hidden = grad_hidden_f.astype(BF16)
        bias_rows.append(column_sum(grad_hidden.astype(F32)))
        grad_low = grad_low + dot(grad_hidden, w_up, NT)
        deal_tile(dot(low_t, grad_hidden), 1 + c, keep, send)
        where = slice(eighth // 2 * c, eighth // 2 * (c + 1))
        active_t = even_first(flag, active.T, UNIT * wide)
        deal(dot(active_t, cots), UNIT * wide, keep, send, where, UNIT * (1 + wide))
    out[...] = total.astype(BF16)
    cots_f = cots.astype(F32)
    grad_middle = cots_f + norm_back(grad_low, unit, inverse, gain)
    grad_mid[...] = grad_middle
    branch = grad_middle.astype(BF16)
    deal_tile(dot(even_first(flag, low_att.T, UNIT), branch), 0, keep, send)
    grad_att[...] = dot(branch, w_out, NT).astype(BF16)
    rows = [jnp.zeros((2, width), F32), column_sum(grad_low * unit), column_sum(grad_low)]
    rows += [column_sum(cots_f)] + bias_rows + [jnp.zeros((7, width), F32)]
    vec_grad[...] = jnp.concatenate(rows, axis=0)


def memory_turned(flag, memory, m, pair, micro):
    slots = memory.shape[2] // micro
    rows, cols = slice(slots * m, slots * (m + 1)), slice(PAIR * pair, PAIR * (pair + 1))
    halves = [memory[:, pl.ds(at, 1), rows, cols] for at in (flag, 1 - flag)]
    return jnp.concatenate([h.reshape(-1, PAIR) for h in halves], axis=0)


def attend_back_kernel(
    info,
    query,
    keys,
    values,
    memory_keys,
    memory_values,
    attended,
    stats,
    grad_att,
    grad_query,
    key_keep,
    key_send,
    value_keep,
    value_send,
    own_key,
    own_value,
):
    micro = info.shape[0]
    count, width = query.shape
    each = count // micro
    chips = memory_keys.shape[0]
    share = memory_keys.shape[2] // micro
    slots = 2 * chips * share
    flag = info[0, 6]
    pairs = width // PAIR
    lower = iota((each, PAIR), 1) < HEAD_DIM
    lane = iota((2 * each, 128), 1)
    found = stats[...]
    deltas = jnp.zeros((2 * each, 128), F32)
    parts = {}
    for m in range(micro):
        rows = slice(each * m, each * (m + 1))
        for pair in range(pairs):
            cols = slice(PAIR * pair, PAIR * (pair + 1))
            grad = grad_att[rows, cols].astype(F32)
            product = stacked(grad * attended[rows, cols], lower)
            delta = jnp.sum(product, axis=1, keepdims=True)
            deltas = jnp.where(lane == m * pairs + pair, delta, deltas)
            parts[m, pair] = delta
    found_t, deltas_t = found.T, deltas.T
    for m in range(micro):
        rows = slice(each * m, each * (m + 1))
        lanes = iota((1, 2 * each), 1)
        place = info[m, 4] + jnp.where(lanes >= each, lanes - each, lanes)
        start = segment_start(info, m, place)
        row = iota((slots, 1), 0)
        late = row >= chips * share
        row = jnp.where(late, row - chips * share, row)
        block = jnp.zeros((slots, 1), jnp.int32)
        for chip in range(1, chips):
            block = block + jnp.where(row >= share * chip, 1, 0)
        core = jnp.where(late, 1 - flag, flag)
        end = 3 * (row + share * (block + core))
        bias = jnp.where((end <= place) & (end >= start), 0.0, MASKED).astype(F32)
        for pair in range(pairs):
            cols = slice(PAIR * pair, PAIR * (pair + 1))
            at = m * pairs + pair
            key = keys[rows, cols].astype(F32)
            value = values[rows, cols].astype(F32)
            query_f = query[rows, cols].astype(F32) * SCALE
            grad_f = grad_att[rows, cols].astype(F32)
            queries = stacked(query_f, lower)
            grads = stacked(grad_f, lower)
            own = jnp.sum(queries * jnp.concatenate([key, key], axis=0), axis=1, keepdims=True)
            own = jnp.exp(own - found[:, at : at + 1])
            grad_own = jnp.sum(
                grads * jnp.concatenate([value, value], axis=0), axis=1, keepdims=True
            )
            grad_own = (own * (grad_own - parts[m, pair])).astype(BF16).astype(F32)
            queries, grads = queries.astype(BF16), grads.astype(BF16)
            memory_key = memory_turned(flag, memory_keys, m, pair, micro)
            memory_value = memory_turned(flag, memory_values, m, pair, micro)
            scores = dot(memory_key, queries, NT) + bias
            probs = jnp.exp(scores - found_t[at : at + 1, :])
            grad_probs = dot(memory_value, grads, NT)
            grad_scores = (probs * (grad_probs - deltas_t[at : at + 1, :])).astype(BF16)
            sides = (
                (dot(grad_scores, queries), key_keep, key_send),
                (dot(probs.astype(BF16), grads), value_keep, value_send),
            )
            for grad, keep, send in sides:
                halves = grad.astype(BF16).reshape(2, chips, share, PAIR)
                keep[:, share * m : share * (m + 1), cols] = halves[0]
                send[:, share * m : share * (m + 1), cols] = halves[1]
            turned = dot(memory_key.T, grad_scores).T
            own_grad = merged(jnp.broadcast_to(grad_own, (2 * each, PAIR)), lower)
            own_weight = merged(jnp.broadcast_to(own, (2 * each, PAIR)), lower)
            grad_query[rows, cols] = (
                SCALE * (merged(turned, lower) + own_grad * key)
            ).astype(BF16)
            own_key[rows, cols] = own_grad * query_f
            own_value[rows, cols] = own_weight * grad_f


def compress_back_kernel(
    info,
    key_memory,
    value_memory,
    key_window,
    value_window,
    key_weights,
    value_weights,
    normed,
    grad_query,
    key_grad,
    value_grad,
    rims,
    keep,
    send,
):
    micro = info.shape[0]
    count, width = key_grad.shape
    each = count // micro
    flag = info[0, 5]
    places = [window_map(micro, each, tap) for tap in range(3)]
    sides = (
        (key_memory, key_window, key_weights, key_grad),
        (value_memory, value_window, value_weights, value_grad),
    )
    for kind, (memory, window, weights, out) in enumerate(sides):
        grad = memory[...]
        total = None
        for tap in range(3):
            window_t = even_first(flag, window[tap].T, UNIT)
            deal_tile(dot(window_t, grad), 4 * kind + tap, keep, send)
            part = dot(grad, tile(weights, 1 + tap), NT)
            high = part.astype(BF16)
            rest = (part - high.astype(F32)).astype(BF16)
            part = dot(places[tap], high, TN) + dot(places[tap], rest, TN)
            total = part if total is None else total + part
        out[...] = total[:count]
        rims[:, width * kind : width * (kind + 1)] = total[count:]
    low_t = even_first(flag, normed[:count, :].T, UNIT)
    deal_tile(dot(low_t, grad_query[...]), 3, keep, send)


def input_kernel(
    info,
    tok,
    normed,
    grad_query,
    key_grad,
    value_grad,
    rims,
    own_key,
    own_value,
    key_weights,
    value_weights,
    vec,
    grad_mid,
    vec_grad,
    grad_in,
    keep,
    send,
    total,
):
    count, width = tok.shape
    micro = info.shape[0]
    each = count // micro
    valid = [valid_column(info, m, info[m, 4], each) for m in range(micro)]
    valid = jnp.concatenate(valid, axis=0)
    flag = info[0, 5]
    low_t = even_first(flag, normed[:count, :].T, UNIT)
    grad_low = dot(grad_query[...], tile(value_weights, 4), NT)
    sides = ((key_grad, own_key, key_weights), (value_grad, own_value, value_weights))
    for kind, (grad, own, weights) in enumerate(sides):
        total[...] = grad[...] + own[...]
        for m in range(micro):
            rows = slice(each * (m + 1) - RIM, each * (m + 1))
            rim = rims[RIM * m : RIM * (m + 1), width * kind : width * (kind + 1)]
            total[rows, :] = total[rows, :] + rim
        low_grad = (total[...] * valid).astype(BF16)
        grad_low = grad_low + dot(low_grad, tile(weights, 0), NT)
        deal_tile(dot(low_t, low_grad), kind, keep, send)
    unit, inverse = unit_norm(tok[...].astype(F32))
    back = norm_back(grad_low, unit, inverse, vec[0:1, :])
    grad_in[...] = (grad_mid[...] + back).astype(BF16)

    lanes = width // 2
    fine, wide, own_fine, own_wide = vector_maps(width)
    vectors = [column_sum(grad_low * unit), column_sum(grad_low)]
    vectors += [vec_grad[k : k + 1, :] for k in range(2, VECTORS)]
    dealt = jnp.concatenate([own_fine * v for v in vectors], axis=0).astype(BF16)
    dealt = dot(dealt, fine, NT)
    bias = [
        jnp.broadcast_to(vec_grad[VECTORS + c : VECTORS + c + 1, :], (8, width)) for c in range(4)
    ]
    bias = (jnp.concatenate(bias, axis=0) * own_wide).astype(BF16)
    packed = jnp.where(lane_window(lanes, VECTORS), dot(bias, wide, NT), 0.0)
    for k in range(VECTORS):
        packed = jnp.where(lane_window(lanes, k), dealt[GROUPS * k : GROUPS * (k + 1)], packed)
    packed = jnp.concatenate([packed, jnp.zeros((GROUPS, width - lanes), F32)], axis=1)
    spot = iota((GROUPS, UNIT, width), 1) == 0
    spread = jnp.broadcast_to(packed[:, None, :], (GROUPS, UNIT, width))
    packed = jnp.where(spot, spread, 0.0).reshape(GROUPS * UNIT, width)
    deal_tile(even_first(flag, packed, UNIT), 2, keep, send)


def per_device(
    tokens,
    lengths,
    ln1_gain,
    ln1_bias,
    w_query,
    w_key,
    w_value,
    conv_key,
    conv_value,
    w_out,
    ln2_gain,
    ln2_bias,
    w_up,
    b_up,
    w_down,
    b_down,
    cotangent,
):
    count = device_count()
    micro, _, each, width = tokens.shape
    ff = w_up.shape[1]
    wide = ff // width
    share = width // count
    seq = lax.axis_size("seq")
    all_tokens = micro * each
    slots = micro * each // 3
    memory_bytes = 4 * seq * slots * width

    halo = lax.ppermute(
        tokens[:, 0, each - RIM :], "seq", [(i, i + 1) for i in range(seq - 1)]
    ).reshape(micro * RIM, width)

    whole = count == GROUPS
    vectors = (ln1_gain, ln1_bias, ln2_gain, ln2_bias, b_down, b_up)
    vector_lengths = [share] * VECTORS + [ff // count]
    across = powers(seq, count)
    along = powers(2, seq)[::-1]
    order = Order()
    if whole:
        chunk = ((5 * UNIT, width), BF16)
        vectors = [v.reshape(1, -1) for v in vectors]
        (first,) = kernel(pack_kernel, (w_key, conv_key, *vectors), (chunk,), 0, 16)
        (second,) = kernel(pack_second_kernel, (w_value, w_query, conv_value), (chunk,), 0, 16)
        chunk = (((1 + 2 * wide) * UNIT, width), BF16)
        (rest,) = kernel(pack_rest_kernel, (w_out, w_up, w_down), (chunk,), 0, 16)
    else:
        vectors = vector_pack(jnp.concatenate(vectors)[None], 2, width)[0]
        first = jnp.concatenate([w_key, *conv_key, vectors], axis=0)
        second = jnp.concatenate([w_value, *conv_value, w_query], axis=0)
        ups = [w_up[:, width * c : width * (c + 1)] for c in range(wide)]
        rest = jnp.concatenate([w_out] + ups + [w_down], axis=0)
    one, two, both = Gather(order, first), Gather(order, second), Gather(order, rest)
    rest_rows = rest.shape[0]
    upper_rows = share * (1 + wide)
    one.go(along[0])
    two.go(along[0])
    one.place()
    for mask in along[1:]:
        one.go(mask)
        two.place()
        two.go(mask)
        one.place()
    one.go(across[0])
    both.go(along[0], wait=True)
    two.place()
    two.go(across[-1])
    for at, mask in enumerate(along[1:]):
        both.place()
        both.go(mask)
    for at in range(1, len(across)):
        one.place()
        one.go(across[at])
        two.place()
        two.go(across[-1 - at])
    both.place(upper_rows, rest_rows - upper_rows)
    one.place()
    one.go(1)
    both.go(across[0], across[-1], wait=True)
    two.place()
    two.go(1)
    first = one.place().whole()
    first_sizes, rest_sizes = [1] * 5, [1] * (1 + wide) + [wide]
    if not whole:
        dealt = vector_regroup(first[:, 4 * share], GROUPS, vector_lengths)
        dealt = vector_pack(dealt, UNIT, width)
        first = jnp.concatenate([grouped(first, [1] * 4), dealt], axis=1)

    lengths = lengths[:, 0]
    first_pad = 3 * ((lengths[:, 0] + 2) // 3)
    second_pad = 3 * ((lengths[:, 1] + 2) // 3)
    start = 1 + first_pad
    seats = [lax.axis_index("seq") * each, upper_half(1) if whole else 0, upper_half(1)]
    seats = [jnp.full_like(start, seat) for seat in seats]
    info = [1 + lengths[:, 0], start, start + lengths[:, 1], start + second_pad]
    info = jnp.stack(info + seats, axis=1).astype(jnp.int32)

    tok = tokens.reshape(all_tokens, width)
    cot = cotangent.reshape(all_tokens, width)
    rows = (all_tokens, width)
    grown = 4 * max(memory_bytes // (1 << 20) - 2, 0)
    limits = [16, 16, 16 + grown, 28, 28 + grown, 28, 28]
    matmul = 2 * all_tokens * width * width

    padded = (all_tokens + micro * RIM, width)
    windows = (3, slots, width)

    normed, keys, key_window, memory_key, vec = kernel(
        key_kernel,
        (info, order.turn(tok), halo, first),
        ((padded, BF16), (padded, BF16), (windows, BF16), ((slots, width), BF16), ((16, width), F32)),
        2 * matmul,
        limits[0],
    )
    order.done(memory_key)
    memories = [Gather(order, memory_key)]
    memories[0].go(along[0])
    second = grouped(two.place().whole(), first_sizes)
    query, values, value_window, memory_value = kernel(
        value_kernel,
        (info, normed, second),
        ((rows, BF16), (padded, BF16), (windows, BF16), ((slots, width), BF16)),
        3 * matmul,
        limits[1],
    )
    order.done(memory_value)
    memories.append(Gather(order, memory_value))
    memories[1].go(along[0])
    for mask in along[1:] + [1]:
        for held in memories:
            held.place()
            held.go(mask)
        if mask == along[1]:
            for at in range(1, len(across)):
                both.place()
                both.go(across[at], across[-1 - at])
    both.place(rest_rows)
    both.go(1)
    memories = [held.place().whole() for held in memories]
    attended, stats = kernel(
        attend_kernel,
        (info, order.turn(query), keys, values, *memories),
        ((rows, F32), ((2 * each, 128), F32)),
        4 * matmul,
        limits[2],
    )
    order.done(attended)
    rest = grouped(both.place().whole(), rest_sizes)
    half = GROUPS // 2

    def pieces(size):
        return (((half, UNIT * size, width), BF16),) * 2

    output, grad_mid, grad_att, *halves, vec_grad = kernel(
        feed_kernel,
        (info, order.turn(tok), cot, attended, vec, rest),
        ((rows, BF16), (rows, F32), (rows, BF16)) + pieces(1 + 2 * wide) + (((16, width), F32),),
        27 * matmul,
        limits[3],
    )
    order.done(halves[0])
    all_bits = powers(2, count)[::-1]

    def begin(keep, send, size):
        if not whole:
            keep, send = split_cores(scattered(joined(keep, send), size))
        return Reduce(order, keep, send, all_bits)

    feeds = begin(*halves, rest_sizes)
    feeds.go(1)
    memory_half = ((seq // 2, slots, width), BF16)
    chips = (seq // 2, 2, slots, width)
    grad_query, *halves, own_key, own_value = kernel(
        attend_back_kernel,
        (
            info,
            order.turn(query),
            keys,
            values,
            memories[0].reshape(chips),
            memories[1].reshape(chips),
            attended,
            stats,
            grad_att,
        ),
        ((rows, BF16),) + (memory_half,) * 4 + ((rows, F32), (rows, F32)),
        10 * matmul,
        limits[4],
    )
    order.done(grad_query)
    back = along[::-1]
    memories = [Reduce(order, *halves[:2], along), Reduce(order, *halves[2:], along)]
    for held in memories:
        held.go(1)
    cross = [(across[-1 - at], across[at]) for at in range(len(across))]
    for at, mask in enumerate(back):
        for held in memories:
            held.add((mask,))
            held.go(mask)
        if at == 0:
            feeds.add(cross[0], upper_rows, rest_rows - upper_rows)
            feeds.go(*cross[0])
    for masks in cross[1:]:
        feeds.add(masks)
        feeds.go(*masks)
    key_grad, value_grad = (held.total().astype(BF16) for held in memories)
    key_kept, value_kept, rims, *halves = kernel(
        compress_back_kernel,
        (
            info,
            key_grad,
            value_grad,
            key_window,
            value_window,
            first,
            second,
            normed,
            grad_query,
        ),
        ((rows, F32), (rows, F32), ((micro * RIM, 2 * width), F32)) + pieces(7),
        5 * matmul,
        limits[5],
    )
    order.done(rims)
    rims = lax.ppermute(rims, "seq", [(i + 1, i) for i in range(seq - 1)])
    convs = begin(*halves, [1] * 7)
    convs.go(1)
    feeds.add((back[0],), rest_rows)
    feeds.go(back[0])
    grad_in, *halves = kernel(
        input_kernel,
        (
            info,
            order.turn(tok),
            normed,
            grad_query,
            key_kept,
            value_kept,
            rims,
            own_key,
            own_value,
            first,
            second,
            vec,
            grad_mid,
            vec_grad,
        ),
        ((rows, BF16),) + pieces(3),
        6 * matmul,
        limits[6],
        (pltpu.VMEM(rows, F32),),
    )
    order.done(grad_in)
    if whole:
        inputs = begin(*halves, [1] * 3)
    else:
        dealt = joined(*halves)
        vectors = dealt[:, 2 * UNIT, : VECTORS * UNIT + ff // GROUPS]
        vectors = vector_regroup(vectors, count, [UNIT] * VECTORS + [ff // GROUPS])
        dealt = [scattered(dealt, [1] * 2), vector_pack(vectors, 2, width)]
        dealt = split_cores(jnp.concatenate(dealt, axis=1))
        inputs = Reduce(order, *dealt, all_bits)
    inputs.go(1)
    cut = 4 * share
    convs.add(cross[0], cut, 3 * share)
    convs.go(*cross[0])
    line = [masks[0] for masks in cross]
    inputs.add((line[0],))
    inputs.go(line[0])
    for mask in back[1:]:
        feeds.add((mask,))
        feeds.go(mask)
    for masks in cross[1:]:
        convs.add(masks)
        convs.go(*masks)
    for mask in line[1:]:
        inputs.add((mask,))
        inputs.go(mask)
    feeds = feeds.total()
    convs.add((back[0],), 7 * share)
    convs.go(back[0])
    inputs.add((back[0],))
    inputs.go(back[0])
    for mask in back[1:]:
        convs.add((mask,))
        convs.go(mask)
        inputs.add((mask,))
        inputs.go(mask)
    convs, late_inputs = convs.total(), inputs.total()
    conv_keys = convs[: 3 * share].reshape(3, share, width)
    conv_values = convs[4 * share :].reshape(3, share, width)

    def own(buffer, number):
        return buffer[share * number : share * (number + 1)]

    vector_row = late_inputs[2 * share]

    def own_vector(number, length=share):
        return vector_row[share * number : share * number + length]

    return (
        output.reshape(tokens.shape),
        grad_in.reshape(tokens.shape),
        own_vector(0),
        own_vector(1),
        own(convs, 3),
        own(late_inputs, 0),
        own(late_inputs, 1),
        conv_keys,
        conv_values,
        own(feeds, 0),
        own_vector(2),
        own_vector(3),
        jnp.concatenate([own(feeds, 1 + c) for c in range(wide)], axis=1),
        own_vector(VECTORS, ff // count),
        feeds[share * (1 + wide) :],
        own_vector(4),
    )


def solution(mesh):
    rows = P(AXES, None)
    vector = P(AXES)
    conv = P(None, AXES, None)
    part = P(None, "batch", "seq", None)
    weights = (vector, vector, rows, rows, rows, conv, conv, rows, vector, vector)
    weights = weights + (rows, vector, rows, vector)
    return jax.shard_map(
        per_device,
        mesh=mesh,
        in_specs=(part, P(None, "batch", None)) + weights + (part,),
        out_specs=(part, part) + weights,
        check_vma=False,
    )
```

```python
import functools

import jax
import jax.numpy as jnp
from jax import lax
from jax.experimental import pallas as pl
from jax.experimental.pallas import tpu as pltpu
from jax.sharding import PartitionSpec as P

HEADS = 8
HEAD_DIM = 64
SCALE = HEAD_DIM ** (-0.5)
EPSILON = 1e-06
AXES = ("batch", "seq")
GROUPS = 32
UNIT = 16
PAIR = 2 * HEAD_DIM
RIM = 8
MASKED = -1e30
F32 = jnp.float32
BF16 = jnp.bfloat16
TN = ((0,), (0,))
NT = ((1,), (1,))
ERF_TOP = (
    0.00022905065861350646,
    0.0034082910107109506,
    0.050955695062380861,
    0.18520832239976145,
    1.128379143519084,
)
ERF_LOW = (
    -1.1791602954361697e-7,
    0.000023547966471313185,
    0.0010179625278914885,
    0.014070470171167667,
    0.11098505178285362,
    0.49746925110067538,
    1.0,
)


def device_count():
    return lax.axis_size("batch") * lax.axis_size("seq")


def device_index():
    return lax.axis_index("batch") * lax.axis_size("seq") + lax.axis_index("seq")


def powers(low, high):
    masks = []
    while low < high:
        masks.append(low)
        low *= 2
    return masks


def swap(array, mask):
    return lax.ppermute(array, AXES, [(i, i ^ mask) for i in range(device_count())])


def upper_half(mask):
    return ((device_index() & mask) != 0).astype(jnp.int32)


class Order:
    def __init__(self):
        self.last = None

    def turn(self, array):
        if self.last is not None:
            array, _ = lax.optimization_barrier((array, self.last))
        return array

    def done(self, array):
        self.last = array


def axis_of(bits, mask):
    return sum(b > mask for b in bits)


def bit_shape(bits, rows):
    return (2,) * len(bits) + tuple(rows)


def at_bit(rank, axis, index, rows):
    where = [slice(None)] * rank
    where[axis] = pl.ds(index, 1)
    where[-2] = rows
    return tuple(where)


def overlaps(lefts, rights):
    found, left_at = [], 0
    for i, left in enumerate(lefts):
        right_at = 0
        for j, right in enumerate(rights):
            low = max(left_at, right_at)
            high = min(left_at + left, right_at + right)
            if low < high:
                found.append(
                    (i, j, slice(low - left_at, high - left_at), slice(low - right_at, high - right_at))
                )
            right_at += right
        left_at += left
    return found


def place_together(order, *jobs):
    axes, cuts, uppers, args, outs, plans = [], [], [], [], [], []
    for gather, sizes in jobs:
        olds = [p.shape[-2] for p in gather.parts]
        sizes = sizes or olds
        bits = [sorted(b + [m], reverse=True) for b, m in zip(gather.bits, gather.masks)]
        own_axes = [axis_of(b, m) for b, m in zip(gather.bits, gather.masks)]
        bits = [bits[min(j, len(bits) - 1)] for j in range(len(sizes))]
        own_uppers = [upper_half(m) for m in gather.masks]
        found = overlaps(olds, sizes)
        plans.append((gather, olds, sizes, bits, own_axes, own_uppers, len(outs)))
        cuts += [(len(axes) + i, len(outs) + j, x, y) for i, j, x, y in found]
        axes += own_axes
        uppers += own_uppers
        for mine, other in zip(gather.parts, gather.others):
            args += [order.turn(mine), other]
        width = gather.parts[0].shape[-1]
        outs += [(bit_shape(b, (r, width)), BF16) for b, r in zip(bits, sizes)]
    if device_count() == GROUPS:
        body = functools.partial(place_kernel, axes, cuts)
        placed = kernel(body, (jnp.stack(uppers), *args), outs, 0, 24)
        order.done(placed[0])
    for gather, olds, sizes, bits, own_axes, own_uppers, at in plans:
        if device_count() == GROUPS:
            parts = placed[at : at + len(sizes)]
        else:
            held = []
            sides = zip(gather.parts, gather.others, own_axes, own_uppers)
            for mine, other, axis, up in sides:
                low, high = jnp.where(up, other, mine), jnp.where(up, mine, other)
                held.append(jnp.stack([low, high], axis=axis))
            parts = cut_rows(held, olds, sizes)
        gather.parts, gather.bits = parts, bits


def place_kernel(axes, cuts, upper, *refs):
    count = len(axes)
    for i, j, inside, outside in cuts:
        mine, other, out = refs[2 * i], refs[2 * i + 1], refs[2 * count + j]
        rank, axis, at = len(out.shape), axes[i], upper[i]
        source = (slice(None),) * (rank - 3) + (inside, slice(None))
        out[at_bit(rank, axis, at, outside)] = jnp.expand_dims(mine[source], axis)
        out[at_bit(rank, axis, 1 - at, outside)] = jnp.expand_dims(other[source], axis)


def add_kernel(axes, cuts, count, upper, *refs):
    for i, j, inside, outside in cuts:
        keep, other = refs[2 * i], refs[2 * i + 1]
        next_keep, next_send = refs[2 * count + 2 * j], refs[2 * count + 2 * j + 1]
        rank, axis, at = len(keep.shape), axes[j], upper[j]
        into = (slice(None),) * (rank - 3) + (outside, slice(None))
        here, there = at_bit(rank, axis, at, inside), at_bit(rank, axis, 1 - at, inside)
        next_send[into] = jnp.squeeze(keep[there] + other[there], axis)
        next_keep[into] = jnp.squeeze(keep[here] + other[here], axis)


class Gather:
    def __init__(self, order, *parts):
        self.order, self.parts, self.bits = order, list(parts), [[] for _ in parts]

    def go(self, *masks, wait=False):
        self.masks = masks
        parts = [self.order.turn(p) for p in self.parts] if wait else self.parts
        self.others = [swap(p, m) for p, m in zip(parts, masks)]

    def place(self, *sizes):
        place_together(self.order, (self, sizes))
        return self

    def whole(self):
        held = self.parts[0]
        return held.reshape((-1,) + held.shape[-2:])


def cut_rows(arrays, olds, sizes):
    if list(olds) == list(sizes):
        return arrays
    joint = jnp.concatenate(arrays, axis=-2)
    ends = [sum(sizes[: j + 1]) for j in range(len(sizes) - 1)]
    return jnp.split(joint, ends, axis=-2)


def join_reduces(*chains):
    joint = Reduce.__new__(Reduce)
    joint.order = chains[0].order
    joint.keeps = [k for c in chains for k in c.keeps]
    joint.others = [o for c in chains for o in c.others]
    joint.bits = [b for c in chains for b in c.bits]
    return joint


class Reduce:
    def __init__(self, order, keep, send, bits):
        shape = bit_shape(bits, keep.shape[-2:])
        self.order, self.bits = order, [bits]
        self.keeps, self.sends = [keep.reshape(shape)], [send.reshape(shape)]

    def go(self, *masks, wait=False):
        sends = [self.order.turn(p) for p in self.sends] if wait else self.sends
        self.others = [swap(p, m) for p, m in zip(sends, masks)]

    def add(self, masks, *sizes):
        olds = [p.shape[-2] for p in self.keeps]
        sizes = sizes or olds
        bits = [self.bits[min(j, len(olds) - 1)] for j in range(len(sizes))]
        axes = [axis_of(b, m) for b, m in zip(bits, masks)]
        uppers = [upper_half(m) for m in masks]
        width = self.keeps[0].shape[-1]
        left = [[b for b in old if b != m] for old, m in zip(bits, masks)]
        if device_count() == GROUPS:
            args = []
            for keep, other in zip(self.keeps, self.others):
                args += [self.order.turn(keep), other]
            outs = []
            for b, r in zip(left, sizes):
                outs += [(bit_shape(b, (r, width)), BF16)] * 2
            body = functools.partial(add_kernel, axes, overlaps(olds, sizes), len(olds))
            both = kernel(body, (jnp.stack(uppers), *args), outs, 0, 20)
            self.keeps, self.sends = both[0::2], both[1::2]
            self.order.done(self.keeps[0])
        else:
            sums = [
                (k.astype(F32) + o.astype(F32)).astype(BF16)
                for k, o in zip(self.keeps, self.others)
            ]
            sums = cut_rows(sums, olds, sizes)
            take = lax.dynamic_index_in_dim
            self.keeps = [take(t, u, a, False) for t, u, a in zip(sums, uppers, axes)]
            self.sends = [take(t, 1 - u, a, False) for t, u, a in zip(sums, uppers, axes)]
        self.bits = left
        return self

    def totals(self):
        pairs = zip(self.keeps, self.others)
        return [(k.astype(F32) + o.astype(F32)).reshape(k.shape[-2:]) for k, o in pairs]


def split_cores(blocks):
    pairs = blocks.reshape((-1, 2) + blocks.shape[1:])
    upper = upper_half(1)
    keep = lax.dynamic_index_in_dim(pairs, upper, 1, keepdims=False)
    return keep, lax.dynamic_index_in_dim(pairs, 1 - upper, 1, keepdims=False)


def joined(keep, send):
    return jnp.stack([keep, send], axis=1).reshape((-1,) + keep.shape[1:])


def grouped(buffer, sizes):
    count = buffer.shape[0]
    if count == GROUPS:
        return buffer
    width = buffer.shape[-1]
    share = width // count
    parts, start = [], 0
    for size in sizes:
        part = buffer[:, start : start + share * size]
        parts.append(part.reshape(GROUPS, UNIT * size, width))
        start += share * size
    return jnp.concatenate(parts, axis=1)


def scattered(buffer, sizes):
    count, width = device_count(), buffer.shape[-1]
    if count == GROUPS:
        return buffer
    parts, start = [], 0
    for size in sizes:
        part = buffer[:, start : start + UNIT * size]
        parts.append(part.reshape(count, width // count * size, width))
        start += UNIT * size
    return jnp.concatenate(parts, axis=1)


def vector_pack(vectors, rows, width):
    filled = jnp.pad(vectors, ((0, 0), (0, width - vectors.shape[1])))
    return jnp.pad(filled[:, None], ((0, 0), (0, rows - 1), (0, 0)))


def vector_regroup(vectors, parts, lengths):
    pieces, start = [], 0
    for length in lengths:
        pieces.append(vectors[:, start : start + length].reshape(parts, -1))
        start += length
    return jnp.concatenate(pieces, axis=1)


def dot(a, b, dims=((1,), (0,))):
    return lax.dot_general(a, b, (dims, ((), ())), preferred_element_type=F32)


def iota(shape, axis):
    return lax.broadcasted_iota(jnp.int32, shape, axis)


def tile(ref, place, size=1):
    rows = ref[:, UNIT * place : UNIT * (place + size), :]
    return rows.reshape(GROUPS * UNIT * size, rows.shape[-1])


def pack_kernel(moves, counts, *refs):
    inputs, outs, sems = refs[: counts[0]], refs[counts[0] : -1], refs[-1]
    copies = []
    for at, (source, where, out, start, rows) in enumerate(moves):
        into = outs[out].at[pl.ds(start, rows)]
        piece = inputs[source] if where is None else inputs[source].at[where]
        copies.append(pltpu.make_async_copy(piece, into, sems.at[at]))
        copies[-1].start()
    for copy in copies:
        copy.wait()


def packed(args, moves, shapes):
    return pl.pallas_call(
        functools.partial(pack_kernel, moves, (len(args),)),
        in_specs=[pl.BlockSpec(memory_space=pl.ANY) for _ in args],
        out_specs=[pl.BlockSpec(memory_space=pltpu.VMEM) for _ in shapes],
        out_shape=[jax.ShapeDtypeStruct(shape, BF16) for shape in shapes],
        scratch_shapes=[pltpu.SemaphoreType.DMA((len(moves),))],
        compiler_params=pltpu.CompilerParams(vmem_limit_bytes=8 << 20),
    )(*args)


def kernel(body, args, outs, flops, limit, scratch=()):
    spec = {jnp.dtype(jnp.int32): pltpu.SMEM}
    return pl.pallas_call(
        body,
        in_specs=[pl.BlockSpec(memory_space=spec.get(a.dtype, pltpu.VMEM)) for a in args],
        out_specs=[pl.BlockSpec(memory_space=pltpu.VMEM) for _ in outs],
        out_shape=[jax.ShapeDtypeStruct(shape, dtype) for shape, dtype in outs],
        scratch_shapes=list(scratch),
        compiler_params=pltpu.CompilerParams(vmem_limit_bytes=limit << 20),
        cost_estimate=pl.CostEstimate(
            flops=flops,
            bytes_accessed=sum(a.size * a.dtype.itemsize for a in args),
            transcendentals=0,
        ),
    )(*args)


def unit_norm(values):
    center = values - jnp.mean(values, axis=-1, keepdims=True)
    spread = jnp.mean(center * center, axis=-1, keepdims=True)
    inverse = lax.rsqrt(spread + EPSILON)
    return center * inverse, inverse


def norm_back(grad, unit, inverse, gain):
    e = grad * gain
    mean_e = jnp.mean(e, axis=-1, keepdims=True)
    mean_x = jnp.mean(e * unit, axis=-1, keepdims=True)
    return inverse * (e - mean_e - unit * mean_x)


def column_sum(values):
    return jnp.sum(values, axis=0, keepdims=True)


def valid_column(info, m, start, rows):
    place = start + iota((rows, 1), 0)
    first = (place >= 1) & (place < info[m, 0])
    second = (place >= info[m, 1]) & (place < info[m, 2])
    return jnp.where(first | second, 1.0, 0.0).astype(F32)


def segment_start(info, m, place):
    start = jnp.where(place >= 1, 1, 0)
    start = jnp.where(place >= info[m, 1], info[m, 1], start)
    return jnp.where(place >= info[m, 3], info[m, 3], start)


VECTORS = 5
BIAS_AT = VECTORS * UNIT


def vector_maps(width):
    lanes = width // 2
    fine = (iota((lanes, width), 0) & 15) == (iota((lanes, width), 1) & 15)
    wide = ((iota((lanes, width), 0) + 48) & 63) == (iota((lanes, width), 1) & 63)
    own_fine = iota((GROUPS, width), 1) >> 4 == iota((GROUPS, width), 0)
    own_wide = iota((GROUPS, width), 1) >> 6 == (iota((GROUPS, width), 0) & 7)
    as_bf16 = [jnp.where(m, 1.0, 0.0).astype(BF16) for m in (fine, wide)]
    as_f32 = [jnp.where(m, 1.0, 0.0).astype(F32) for m in (own_fine, own_wide)]
    return as_bf16 + as_f32


def lane_window(lanes, k):
    place = iota((GROUPS, lanes), 1)
    if k == VECTORS:
        return (place >= BIAS_AT) & (place < BIAS_AT + 64)
    return (place >= UNIT * k) & (place < UNIT * (k + 1))


def window_map(micro, each, tap):
    slots = each // 3
    shape = (micro * slots, micro * (each + RIM))
    row, place = iota(shape, 0), iota(shape, 1)
    m = jnp.zeros(shape, jnp.int32)
    for i in range(1, micro):
        m = m + jnp.where(row >= slots * i, 1, 0)
    source = 3 * (row - slots * m) - 2 + tap
    rim = micro * each + RIM * m + RIM + source
    target = jnp.where(source >= 0, each * m + source, rim)
    return jnp.where(place == target, 1.0, 0.0).astype(BF16)


def project_kernel(
    info, tok, halo, weights, normed, query, keys, values, windows, key_memory, value_memory, vec
):
    width = tok.shape[-1]
    lanes = width // 2
    count = tok.shape[0]
    micro = info.shape[0]
    each = count // micro
    fine, wide, own_fine, own_wide = vector_maps(width)
    rows = jnp.sum(weights[:, 4 * UNIT : 5 * UNIT, :lanes].astype(F32), axis=1)
    picked = [jnp.where(lane_window(lanes, k), rows, 0.0) for k in range(VECTORS + 1)]
    spread = dot(jnp.concatenate(picked[:VECTORS], axis=0).astype(BF16), fine)
    vectors = [
        column_sum(spread[GROUPS * k : GROUPS * (k + 1)] * own_fine) for k in range(VECTORS)
    ]
    bias = dot(picked[VECTORS].astype(BF16), wide) * own_wide
    bias = jnp.sum(bias.reshape(4, 8, width), axis=1)
    vec[...] = jnp.concatenate(vectors + [bias, jnp.zeros((7, width), F32)], axis=0)
    inputs = jnp.concatenate([tok[...], halo[...]], axis=0).astype(F32)
    unit, _ = unit_norm(inputs)
    low = (unit * vectors[0] + vectors[1]).astype(BF16)
    normed[...] = low[:count]
    query[...] = dot(low[:count], tile(weights, 9)).astype(BF16)
    valid = [valid_column(info, m, info[m, 4], each) for m in range(micro)]
    valid += [valid_column(info, m, info[m, 4] - RIM, RIM) for m in range(micro)]
    valid = jnp.concatenate(valid, axis=0)
    places = [window_map(micro, each, tap) for tap in range(3)]
    for kind, (kept, memory) in enumerate(((keys, key_memory), (values, value_memory))):
        rows = (dot(low, tile(weights, 5 * kind)) * valid).astype(BF16)
        kept[...] = rows[:count]
        total = None
        for tap in range(3):
            taken = dot(places[tap], rows).astype(BF16)
            windows[tap, :, width * kind : width * (kind + 1)] = taken
            part = dot(taken, tile(weights, 5 * kind + 1 + tap))
            total = part if total is None else total + part
        memory[...] = total.astype(BF16)


def stacked(values, lower):
    zero = jnp.zeros_like(values)
    return jnp.concatenate(
        [jnp.where(lower, values, zero), jnp.where(lower, zero, values)], axis=0
    )


def merged(values, lower):
    half = values.shape[0] // 2
    return jnp.where(lower, values[:half], values[half:])


def memory_pair(memory, kind, m, pair, micro):
    slots = memory.shape[2] // micro
    rows = memory[:, kind, slots * m : slots * (m + 1), PAIR * pair : PAIR * (pair + 1)]
    return rows.reshape(memory.shape[0] * slots, PAIR)


def attend_kernel(info, query, keys, values, memory, attended, stats):
    micro = info.shape[0]
    count, width = query.shape
    each = count // micro
    slots = memory.shape[0] * memory.shape[2] // micro
    pairs = width // PAIR
    lower = iota((each, PAIR), 1) < HEAD_DIM
    lane = iota((2 * each, 128), 1)
    found = jnp.zeros((2 * each, 128), F32)
    for m in range(micro):
        rows = slice(each * m, each * (m + 1))
        place = info[m, 4] + iota((each, 1), 0)
        start = segment_start(info, m, place)
        end = 3 * iota((each, slots), 1)
        bias = jnp.where((end <= place) & (end >= start), 0.0, MASKED).astype(F32)
        bias = jnp.concatenate([bias, bias], axis=0)
        for pair in range(pairs):
            cols = slice(PAIR * pair, PAIR * (pair + 1))
            key = keys[rows, cols].astype(F32)
            value = values[rows, cols].astype(F32)
            queries = stacked(query[rows, cols].astype(F32) * SCALE, lower)
            own = jnp.sum(queries * jnp.concatenate([key, key], axis=0), axis=1, keepdims=True)
            memory_key = memory_pair(memory, 0, m, pair, micro)
            memory_value = memory_pair(memory, 1, m, pair, micro)
            scores = dot(queries.astype(BF16), memory_key, NT) + bias
            top = jnp.maximum(jnp.max(scores, axis=1, keepdims=True), own)
            expos = jnp.exp(scores - top)
            own = jnp.exp(own - top)
            total = jnp.sum(expos, axis=1, keepdims=True) + own
            inverse = 1.0 / total
            mixed = dot(expos.astype(BF16), memory_value) * inverse
            weight = jnp.broadcast_to(own * inverse, mixed.shape)
            attended[rows, cols] = merged(mixed, lower) + merged(weight, lower) * value
            found = jnp.where(lane == m * pairs + pair, top + jnp.log(total), found)
    stats[...] = found


def erf(values):
    values = jnp.clip(values, -3.832506856900711, 3.832506856900711)
    square = values * values
    above, below = ERF_TOP[0], ERF_LOW[0]
    for c in ERF_TOP[1:]:
        above = above * square + c
    for c in ERF_LOW[1:]:
        below = below * square + c
    return values * above / below


def even_first(flag, rows, size):
    pairs = rows.reshape(-1, 2, size, rows.shape[-1])
    even, odd = pairs[:, 0], pairs[:, 1]
    halves = [jnp.where(flag == 0, even, odd), jnp.where(flag == 0, odd, even)]
    return jnp.concatenate(halves, axis=0).reshape(rows.shape)


def deal(value, rows, keep, send, blocks, start):
    halves = value.astype(BF16).reshape(2, -1, rows, value.shape[-1])
    keep[blocks, start : start + rows, :] = halves[0]
    send[blocks, start : start + rows, :] = halves[1]


def deal_tile(value, place, keep, send):
    deal(value, UNIT, keep, send, slice(None), UNIT * place)


def feed_kernel(
    info,
    tok,
    cot,
    attended,
    vec,
    rest,
    out,
    grad_mid,
    grad_att,
    keep,
    send,
    vec_grad,
):
    count, width = tok.shape
    wide = 4
    low_att = attended[...].astype(BF16)
    w_out = tile(rest, 0)
    middle = tok[...].astype(F32) + dot(low_att, w_out)
    unit, inverse = unit_norm(middle)
    gain = vec[2:3, :]
    low = (unit * gain + vec[3:4, :]).astype(BF16)
    flag = info[0, 5]
    low_t = even_first(flag, low.T, UNIT)
    cots = cot[...]
    total = middle + vec[4:5, :]
    grad_low = jnp.zeros((count, width), F32)
    bias_rows = []
    eighth = GROUPS // wide
    for c in range(wide):
        w_up = tile(rest, 1 + c)
        down = slice(eighth * c, eighth * (c + 1))
        w_down = rest[down, UNIT * (1 + wide) :, :].reshape(width, width)
        hidden = dot(low, w_up) + vec[5 + c : 6 + c, :]
        share = 0.5 + 0.5 * erf(hidden * 0.7071067811865476)
        slope = share + hidden * (0.3989422804014327 * jnp.exp(-0.5 * hidden * hidden))
        active = (hidden * share).astype(BF16)
        total = total + dot(active, w_down)
        grad_hidden_f = dot(cots, w_down, NT) * slope
        grad_hidden = grad_hidden_f.astype(BF16)
        bias_rows.append(column_sum(grad_hidden.astype(F32)))
        grad_low = grad_low + dot(grad_hidden, w_up, NT)
        deal_tile(dot(low_t, grad_hidden), 1 + c, keep, send)
        where = slice(eighth // 2 * c, eighth // 2 * (c + 1))
        active_t = even_first(flag, active.T, UNIT * wide)
        deal(dot(active_t, cots), UNIT * wide, keep, send, where, UNIT * (1 + wide))
    out[...] = total.astype(BF16)
    cots_f = cots.astype(F32)
    grad_middle = cots_f + norm_back(grad_low, unit, inverse, gain)
    grad_mid[...] = grad_middle
    branch = grad_middle.astype(BF16)
    deal_tile(dot(even_first(flag, low_att.T, UNIT), branch), 0, keep, send)
    grad_att[...] = dot(branch, w_out, NT).astype(BF16)
    rows = [jnp.zeros((2, width), F32), column_sum(grad_low * unit), column_sum(grad_low)]
    rows += [column_sum(cots_f)] + bias_rows + [jnp.zeros((7, width), F32)]
    vec_grad[...] = jnp.concatenate(rows, axis=0)


def memory_turned(flag, memory, kind, m, pair, micro):
    slots = memory.shape[3] // micro
    rows, cols = slice(slots * m, slots * (m + 1)), slice(PAIR * pair, PAIR * (pair + 1))
    halves = [memory[:, pl.ds(at, 1), kind, rows, cols] for at in (flag, 1 - flag)]
    return jnp.concatenate([h.reshape(-1, PAIR) for h in halves], axis=0)


def attend_back_kernel(
    info,
    query,
    keys,
    values,
    memory,
    attended,
    stats,
    grad_att,
    grad_query,
    keep,
    send,
    own_key,
    own_value,
):
    micro = info.shape[0]
    count, width = query.shape
    each = count // micro
    chips = memory.shape[0]
    share = memory.shape[3] // micro
    slots = 2 * chips * share
    flag = info[0, 6]
    pairs = width // PAIR
    lower = iota((each, PAIR), 1) < HEAD_DIM
    lane = iota((2 * each, 128), 1)
    found = stats[...]
    deltas = jnp.zeros((2 * each, 128), F32)
    parts = {}
    for m in range(micro):
        rows = slice(each * m, each * (m + 1))
        for pair in range(pairs):
            cols = slice(PAIR * pair, PAIR * (pair + 1))
            grad = grad_att[rows, cols].astype(F32)
            product = stacked(grad * attended[rows, cols], lower)
            delta = jnp.sum(product, axis=1, keepdims=True)
            deltas = jnp.where(lane == m * pairs + pair, delta, deltas)
            parts[m, pair] = delta
    found_t, deltas_t = found.T, deltas.T
    for m in range(micro):
        rows = slice(each * m, each * (m + 1))
        lanes = iota((1, 2 * each), 1)
        place = info[m, 4] + jnp.where(lanes >= each, lanes - each, lanes)
        start = segment_start(info, m, place)
        row = iota((slots, 1), 0)
        late = row >= chips * share
        row = jnp.where(late, row - chips * share, row)
        block = jnp.zeros((slots, 1), jnp.int32)
        for chip in range(1, chips):
            block = block + jnp.where(row >= share * chip, 1, 0)
        core = jnp.where(late, 1 - flag, flag)
        end = 3 * (row + share * (block + core))
        bias = jnp.where((end <= place) & (end >= start), 0.0, MASKED).astype(F32)
        for pair in range(pairs):
            cols = slice(PAIR * pair, PAIR * (pair + 1))
            at = m * pairs + pair
            key = keys[rows, cols].astype(F32)
            value = values[rows, cols].astype(F32)
            query_f = query[rows, cols].astype(F32) * SCALE
            grad_f = grad_att[rows, cols].astype(F32)
            queries = stacked(query_f, lower)
            grads = stacked(grad_f, lower)
            own = jnp.sum(queries * jnp.concatenate([key, key], axis=0), axis=1, keepdims=True)
            own = jnp.exp(own - found[:, at : at + 1])
            grad_own = jnp.sum(
                grads * jnp.concatenate([value, value], axis=0), axis=1, keepdims=True
            )
            grad_own = (own * (grad_own - parts[m, pair])).astype(BF16).astype(F32)
            queries, grads = queries.astype(BF16), grads.astype(BF16)
            memory_key = memory_turned(flag, memory, 0, m, pair, micro)
            memory_value = memory_turned(flag, memory, 1, m, pair, micro)
            scores = dot(memory_key, queries, NT) + bias
            probs = jnp.exp(scores - found_t[at : at + 1, :])
            grad_probs = dot(memory_value, grads, NT)
            grad_scores = (probs * (grad_probs - deltas_t[at : at + 1, :])).astype(BF16)
            sides = (dot(grad_scores, queries), dot(probs.astype(BF16), grads))
            for kind, grad in enumerate(sides):
                halves = grad.astype(BF16).reshape(2, chips, share, PAIR)
                start = share * (micro * kind + m)
                keep[:, start : start + share, cols] = halves[0]
                send[:, start : start + share, cols] = halves[1]
            turned = dot(memory_key.T, grad_scores).T
            own_grad = merged(jnp.broadcast_to(grad_own, (2 * each, PAIR)), lower)
            own_weight = merged(jnp.broadcast_to(own, (2 * each, PAIR)), lower)
            grad_query[rows, cols] = (
                SCALE * (merged(turned, lower) + own_grad * key)
            ).astype(BF16)
            own_key[rows, cols] = own_grad * query_f
            own_value[rows, cols] = own_weight * grad_f


def compress_back_kernel(
    info,
    key_memory,
    value_memory,
    windows,
    weights,
    normed,
    grad_query,
    key_grad,
    value_grad,
    rims,
    keep,
    send,
):
    micro = info.shape[0]
    count, width = key_grad.shape
    each = count // micro
    flag = info[0, 5]
    places = [window_map(micro, each, tap) for tap in range(3)]
    sides = ((key_memory, key_grad), (value_memory, value_grad))
    for kind, (memory, out) in enumerate(sides):
        grad = memory[...]
        cols = slice(width * kind, width * (kind + 1))
        total = None
        for tap in range(3):
            window_t = even_first(flag, windows[tap, :, cols].T, UNIT)
            deal_tile(dot(window_t, grad), 4 * kind + tap, keep, send)
            part = dot(grad, tile(weights, 5 * kind + 1 + tap), NT)
            high = part.astype(BF16)
            rest = (part - high.astype(F32)).astype(BF16)
            part = dot(places[tap], high, TN) + dot(places[tap], rest, TN)
            total = part if total is None else total + part
        out[...] = total[:count]
        rims[:, cols] = total[count:]
    low_t = even_first(flag, normed[...].T, UNIT)
    deal_tile(dot(low_t, grad_query[...]), 3, keep, send)


def input_kernel(
    info,
    tok,
    normed,
    grad_query,
    key_grad,
    value_grad,
    rims,
    own_key,
    own_value,
    weights,
    vec,
    grad_mid,
    vec_grad,
    grad_in,
    keep,
    send,
    total,
):
    count, width = tok.shape
    micro = info.shape[0]
    each = count // micro
    valid = [valid_column(info, m, info[m, 4], each) for m in range(micro)]
    valid = jnp.concatenate(valid, axis=0)
    flag = info[0, 5]
    low_t = even_first(flag, normed[...].T, UNIT)
    grad_low = dot(grad_query[...], tile(weights, 9), NT)
    for kind, (grad, own) in enumerate(((key_grad, own_key), (value_grad, own_value))):
        total[...] = grad[...] + own[...]
        for m in range(micro):
            rows = slice(each * (m + 1) - RIM, each * (m + 1))
            rim = rims[RIM * m : RIM * (m + 1), width * kind : width * (kind + 1)]
            total[rows, :] = total[rows, :] + rim
        low_grad = (total[...] * valid).astype(BF16)
        grad_low = grad_low + dot(low_grad, tile(weights, 5 * kind), NT)
        deal_tile(dot(low_t, low_grad), kind, keep, send)
    unit, inverse = unit_norm(tok[...].astype(F32))
    back = norm_back(grad_low, unit, inverse, vec[0:1, :])
    grad_in[...] = (grad_mid[...] + back).astype(BF16)

    lanes = width // 2
    fine, wide, own_fine, own_wide = vector_maps(width)
    vectors = [column_sum(grad_low * unit), column_sum(grad_low)]
    vectors += [vec_grad[k : k + 1, :] for k in range(2, VECTORS)]
    dealt = jnp.concatenate([own_fine * v for v in vectors], axis=0).astype(BF16)
    dealt = dot(dealt, fine, NT)
    bias = [
        jnp.broadcast_to(vec_grad[VECTORS + c : VECTORS + c + 1, :], (8, width)) for c in range(4)
    ]
    bias = (jnp.concatenate(bias, axis=0) * own_wide).astype(BF16)
    packed = jnp.where(lane_window(lanes, VECTORS), dot(bias, wide, NT), 0.0)
    for k in range(VECTORS):
        packed = jnp.where(lane_window(lanes, k), dealt[GROUPS * k : GROUPS * (k + 1)], packed)
    packed = jnp.concatenate([packed, jnp.zeros((GROUPS, width - lanes), F32)], axis=1)
    spot = iota((GROUPS, UNIT, width), 1) == 0
    spread = jnp.broadcast_to(packed[:, None, :], (GROUPS, UNIT, width))
    packed = jnp.where(spot, spread, 0.0).reshape(GROUPS * UNIT, width)
    deal_tile(even_first(flag, packed, UNIT), 2, keep, send)


def per_device(
    tokens,
    lengths,
    ln1_gain,
    ln1_bias,
    w_query,
    w_key,
    w_value,
    conv_key,
    conv_value,
    w_out,
    ln2_gain,
    ln2_bias,
    w_up,
    b_up,
    w_down,
    b_down,
    cotangent,
):
    count = device_count()
    micro, _, each, width = tokens.shape
    ff = w_up.shape[1]
    wide = ff // width
    share = width // count
    seq = lax.axis_size("seq")
    all_tokens = micro * each
    slots = micro * each // 3
    memory_bytes = 4 * seq * slots * width

    whole = count == GROUPS
    vector_lengths = [share] * VECTORS + [ff // count]
    vectors, start = 0.0, 0
    for part in (ln1_gain, ln1_bias, ln2_gain, ln2_bias, b_down, b_up):
        end = start + part.shape[0]
        pad = ((0, (UNIT if whole else 2) - 1), (start, width - end))
        vectors, start = vectors + jnp.pad(part[None], pad), end
    vectors = vectors.astype(BF16)
    across = powers(seq, count)
    along = powers(2, seq)[::-1]
    back = along[::-1]
    order = Order()
    if whole:
        moves = [(kind, None, kind, 0, UNIT) for kind in range(2)]
        moves += [(2 + k, tap, k, UNIT * (1 + tap), UNIT) for k in range(2) for tap in range(3)]
        moves += [(4 + kind, None, kind, 4 * UNIT, UNIT) for kind in range(2)]
        keys_part, values_part = packed(
            (w_key, w_value, conv_key, conv_value, vectors, w_query),
            moves,
            ((5 * UNIT, width),) * 2,
        )
        moves = [(0, None, 0, 0, UNIT)]
        for c in range(wide):
            cols = (slice(None), pl.ds(width * c, width))
            moves.append((1, cols, 0, UNIT * (1 + c), UNIT))
        moves.append((2, None, 0, UNIT * (1 + wide), UNIT * wide))
        (rest,) = packed(
            (w_out, w_up, order.turn(w_down)), moves, (((1 + 2 * wide) * UNIT, width),)
        )
    else:
        keys_part = jnp.concatenate([w_key, *conv_key, vectors], axis=0)
        values_part = jnp.concatenate([w_value, *conv_value, w_query], axis=0)
        ups = [w_up[:, width * c : width * (c + 1)] for c in range(wide)]
        rest = jnp.concatenate([w_out] + ups + [w_down], axis=0)
    rest_rows = rest.shape[0]
    upper_rows = share * (1 + wide)
    first, both = Gather(order, keys_part, values_part), Gather(order, rest)
    first_rows = keys_part.shape[0] + values_part.shape[0]
    first.go(along[0], back[0])
    halo = lax.ppermute(
        tokens[:, 0, each - RIM :], "seq", [(i, i + 1) for i in range(seq - 1)]
    ).reshape(micro * RIM, width)
    order.done(halo)
    for at in range(1, len(along)):
        first.place()
        first.go(along[at], back[at])
    first.place()
    first.go(across[0], across[-1])
    both.go(along[0], wait=True)
    for at in range(1, max(len(along), len(across))):
        if at < len(along):
            both.place()
            both.go(along[at])
        if at < len(across):
            first.place()
            first.go(across[at], across[-1 - at])
    both.place(upper_rows, rest_rows - upper_rows)
    both.go(across[0], across[-1])
    first.place(first_rows)
    first.go(1)
    weights = first.place().whole()
    first_sizes, rest_sizes = [1] * 10, [1] * (1 + wide) + [wide]
    if not whole:
        dealt = vector_regroup(weights[:, 4 * share], GROUPS, vector_lengths)
        dealt = vector_pack(dealt, UNIT, width)
        front, tail = weights[:, : 4 * share], weights[:, 4 * share + 2 :]
        weights = jnp.concatenate(
            [grouped(front, [1] * 4), dealt, grouped(tail, [1] * 5)], axis=1
        )

    lengths = lengths[:, 0]
    first_pad = 3 * ((lengths[:, 0] + 2) // 3)
    second_pad = 3 * ((lengths[:, 1] + 2) // 3)
    start = 1 + first_pad
    seats = [lax.axis_index("seq") * each, upper_half(1) if whole else 0, upper_half(1)]
    seats = [jnp.full_like(start, seat) for seat in seats]
    info = [1 + lengths[:, 0], start, start + lengths[:, 1], start + second_pad]
    info = jnp.stack(info + seats, axis=1).astype(jnp.int32)

    tok = tokens.reshape(all_tokens, width)
    cot = cotangent.reshape(all_tokens, width)
    rows = (all_tokens, width)
    grown = 4 * max(memory_bytes // (1 << 20) - 2, 0)
    limits = [16, 16, 16 + grown, 28, 28 + grown, 28, 28]
    matmul = 2 * all_tokens * width * width

    normed, query, keys, values, windows, memory_key, memory_value, vec = kernel(
        project_kernel,
        (info, order.turn(tok), halo, weights),
        (
            (rows, BF16),
            (rows, BF16),
            (rows, BF16),
            (rows, BF16),
            ((3, slots, 2 * width), BF16),
            ((slots, width), BF16),
            ((slots, width), BF16),
            ((16, width), F32),
        ),
        5 * matmul,
        limits[0],
    )
    order.done(normed)
    memory = Gather(order, memory_key, memory_value)
    memory.go(along[0], back[0])
    for at in range(1, max(len(along), len(across))):
        if at < len(across):
            both.place()
            both.go(across[at], across[-1 - at])
        if at < len(along):
            memory.place()
            memory.go(along[at], back[at])
    place_together(order, (memory, [2 * slots]), (both, [rest_rows]))
    memory.go(1)
    both.go(1)
    memory = memory.place().whole().reshape(seq, 2, slots, width)
    attended, stats = kernel(
        attend_kernel,
        (info, order.turn(query), keys, values, memory),
        ((rows, F32), ((2 * each, 128), F32)),
        4 * matmul,
        limits[2],
    )
    order.done(attended)
    rest = grouped(both.place().whole(), rest_sizes)
    half = GROUPS // 2

    def pieces(size):
        return (((half, UNIT * size, width), BF16),) * 2

    output, grad_mid, grad_att, *halves, vec_grad = kernel(
        feed_kernel,
        (info, order.turn(tok), cot, attended, vec, rest),
        ((rows, BF16), (rows, F32), (rows, BF16)) + pieces(1 + 2 * wide) + (((16, width), F32),),
        27 * matmul,
        limits[3],
    )
    order.done(halves[0])
    all_bits = powers(2, count)[::-1]

    def begin(keep, send, size):
        if not whole:
            keep, send = split_cores(scattered(joined(keep, send), size))
        return Reduce(order, keep, send, all_bits)

    feeds = begin(*halves, rest_sizes)
    feeds.go(1)
    memory_half = ((seq // 2, 2 * slots, width), BF16)
    grad_query, *halves, own_key, own_value = kernel(
        attend_back_kernel,
        (
            info,
            order.turn(query),
            keys,
            values,
            memory.reshape(seq // 2, 2, 2, slots, width),
            attended,
            stats,
            grad_att,
        ),
        ((rows, BF16),) + (memory_half,) * 2 + ((rows, F32), (rows, F32)),
        10 * matmul,
        limits[4],
    )
    order.done(grad_query)
    memory_grads = Reduce(order, *halves, along)
    memory_grads.go(1)
    cross = [(across[-1 - at], across[at]) for at in range(len(across))]
    feeds.add(cross[0], upper_rows, rest_rows - upper_rows)
    feeds.go(*cross[0])
    memory_grads.add((back[0], along[0]), slots, slots)
    memory_grads.go(back[0], along[0])
    for at in range(1, max(len(along), len(cross))):
        if at < len(cross):
            feeds.add(cross[at])
            feeds.go(*cross[at])
        if at < len(along):
            memory_grads.add((back[at], along[at]))
            memory_grads.go(back[at], along[at])
    feeds.add((back[0],), rest_rows)
    key_grad, value_grad = (grad.astype(BF16) for grad in memory_grads.totals())
    key_kept, value_kept, rims, *halves = kernel(
        compress_back_kernel,
        (
            info,
            order.turn(key_grad),
            value_grad,
            windows,
            weights,
            normed,
            grad_query,
        ),
        ((rows, F32), (rows, F32), ((micro * RIM, 2 * width), F32)) + pieces(7),
        5 * matmul,
        limits[5],
    )
    order.done(rims)
    rims = lax.ppermute(rims, "seq", [(i + 1, i) for i in range(seq - 1)])
    convs = begin(*halves, [1] * 7)
    convs.go(1)
    feeds.go(back[0])
    grad_in, *halves = kernel(
        input_kernel,
        (
            info,
            order.turn(tok),
            normed,
            grad_query,
            key_kept,
            value_kept,
            rims,
            own_key,
            own_value,
            weights,
            vec,
            grad_mid,
            vec_grad,
        ),
        ((rows, BF16),) + pieces(3),
        6 * matmul,
        limits[6],
        (pltpu.VMEM(rows, F32),),
    )
    order.done(grad_in)
    if whole:
        inputs = begin(*halves, [1] * 3)
    else:
        dealt = joined(*halves)
        vectors = dealt[:, 2 * UNIT, : VECTORS * UNIT + ff // GROUPS]
        vectors = vector_regroup(vectors, count, [UNIT] * VECTORS + [ff // GROUPS])
        dealt = [scattered(dealt, [1] * 2), vector_pack(vectors, 2, width)]
        dealt = split_cores(jnp.concatenate(dealt, axis=1))
        inputs = Reduce(order, *dealt, all_bits)
    inputs.go(1)
    cut = 5 * share
    convs.add(cross[0], cut, 2 * share)
    convs.go(*cross[0])
    line = [masks[1] for masks in cross]
    inputs.add((line[0],))
    inputs.go(line[0])
    for mask in back[1:]:
        feeds.add((mask,))
        feeds.go(mask)
    late_rows = inputs.keeps[0].shape[-2]
    late = join_reduces(convs, inputs)
    for at in range(1, len(cross)):
        late.add((*cross[at], line[at]))
        late.go(*cross[at], line[at])
    (feeds,) = feeds.totals()
    for mask in back:
        late.add((mask,), 7 * share + late_rows)
        late.go(mask)
    (late,) = late.totals()
    convs, late_inputs = late[: 7 * share], late[7 * share :]
    conv_keys = convs[: 3 * share].reshape(3, share, width)
    conv_values = convs[4 * share :].reshape(3, share, width)

    def own(buffer, number):
        return buffer[share * number : share * (number + 1)]

    vector_row = late_inputs[2 * share]

    def own_vector(number, length=share):
        return vector_row[share * number : share * number + length]

    return (
        output.reshape(tokens.shape),
        grad_in.reshape(tokens.shape),
        own_vector(0),
        own_vector(1),
        own(convs, 3),
        own(late_inputs, 0),
        own(late_inputs, 1),
        conv_keys,
        conv_values,
        own(feeds, 0),
        own_vector(2),
        own_vector(3),
        jnp.concatenate([own(feeds, 1 + c) for c in range(wide)], axis=1),
        own_vector(VECTORS, ff // count),
        feeds[share * (1 + wide) :],
        own_vector(4),
    )


def solution(mesh):
    rows = P(AXES, None)
    vector = P(AXES)
    conv = P(None, AXES, None)
    part = P(None, "batch", "seq", None)
    weights = (vector, vector, rows, rows, rows, conv, conv, rows, vector, vector)
    weights = weights + (rows, vector, rows, vector)
    return jax.shard_map(
        per_device,
        mesh=mesh,
        in_specs=(part, P(None, "batch", None)) + weights + (part,),
        out_specs=(part, part) + weights,
        check_vma=False,
    )
```

```python
import functools

import jax
import jax.numpy as jnp
from jax import lax
from jax.experimental import pallas as pl
from jax.experimental.pallas import tpu as pltpu
from jax.sharding import PartitionSpec as P

HEADS = 8
HEAD_DIM = 64
SCALE = HEAD_DIM ** (-0.5)
EPSILON = 1e-06
AXES = ("batch", "seq")
GROUPS = 32
UNIT = 16
PAIR = 2 * HEAD_DIM
RIM = 8
MASKED = -1e30
F32 = jnp.float32
BF16 = jnp.bfloat16
TN = ((0,), (0,))
NT = ((1,), (1,))
ERF_TOP = (
    0.00022905065861350646,
    0.0034082910107109506,
    0.050955695062380861,
    0.18520832239976145,
    1.128379143519084,
)
ERF_LOW = (
    -1.1791602954361697e-7,
    0.000023547966471313185,
    0.0010179625278914885,
    0.014070470171167667,
    0.11098505178285362,
    0.49746925110067538,
    1.0,
)


def device_count():
    return lax.axis_size("batch") * lax.axis_size("seq")


def device_index():
    return lax.axis_index("batch") * lax.axis_size("seq") + lax.axis_index("seq")


def powers(low, high):
    masks = []
    while low < high:
        masks.append(low)
        low *= 2
    return masks


def swap(array, mask):
    return lax.ppermute(array, AXES, [(i, i ^ mask) for i in range(device_count())])


def upper_half(mask):
    return ((device_index() & mask) != 0).astype(jnp.int32)


class Order:
    def __init__(self):
        self.last = None
        bits = device_count().bit_length() - 1
        self.uppers = jnp.stack([upper_half(1 << bit) for bit in range(bits)])

    def turn(self, array):
        if self.last is not None:
            array = lax.optimization_barrier((array, self.last))[0]
        return array

    def done(self, array):
        self.last = array


def axis_of(bits, mask):
    return sum(b > mask for b in bits)


def bit_shape(bits, rows):
    return (2,) * len(bits) + tuple(rows)


def at_bit(rank, axis, index, rows):
    where = [slice(None)] * rank
    where[axis] = pl.ds(index, 1)
    where[-2] = rows
    return tuple(where)


def overlaps(lefts, rights):
    found, left_at = [], 0
    for i, left in enumerate(lefts):
        right_at = 0
        for j, right in enumerate(rights):
            low = max(left_at, right_at)
            high = min(left_at + left, right_at + right)
            if low < high:
                found.append(
                    (i, j, slice(low - left_at, high - left_at), slice(low - right_at, high - right_at))
                )
            right_at += right
        left_at += left
    return found


def place_kernel(axes, masks, cuts, uppers, *refs):
    count = len(axes)
    for i, j, inside, outside in cuts:
        mine, other, out = refs[2 * i], refs[2 * i + 1], refs[2 * count + j]
        rank, axis, at = len(out.shape), axes[i], uppers[masks[i].bit_length() - 1]
        source = (slice(None),) * (rank - 3) + (inside, slice(None))
        out[at_bit(rank, axis, at, outside)] = jnp.expand_dims(mine[source], axis)
        out[at_bit(rank, axis, 1 - at, outside)] = jnp.expand_dims(other[source], axis)


def add_kernel(axes, masks, cuts, count, uppers, *refs):
    for i, j, inside, outside in cuts:
        keep, other = refs[2 * i], refs[2 * i + 1]
        next_keep, next_send = refs[2 * count + 2 * j], refs[2 * count + 2 * j + 1]
        rank, axis, at = len(keep.shape), axes[j], uppers[masks[j].bit_length() - 1]
        into = (slice(None),) * (rank - 3) + (outside, slice(None))
        here, there = at_bit(rank, axis, at, inside), at_bit(rank, axis, 1 - at, inside)
        next_send[into] = jnp.squeeze(keep[there] + other[there], axis)
        next_keep[into] = jnp.squeeze(keep[here] + other[here], axis)


def place(order, *jobs):
    axes, masks, cuts, args, outs, plans = [], [], [], [], [], []
    for gather, sizes in jobs:
        olds = [p.shape[-2] for p in gather.parts]
        sizes = sizes or olds
        bits = [sorted(b + [m], reverse=True) for b, m in zip(gather.bits, gather.masks)]
        own_axes = [axis_of(b, m) for b, m in zip(gather.bits, gather.masks)]
        bits = [bits[min(j, len(bits) - 1)] for j in range(len(sizes))]
        found = overlaps(olds, sizes)
        plans.append((gather, olds, sizes, bits, own_axes, len(outs)))
        cuts += [(len(axes) + i, len(outs) + j, x, y) for i, j, x, y in found]
        axes += own_axes
        masks += gather.masks
        for mine, other in zip(gather.parts, gather.others):
            args += [order.turn(mine), other]
        width = gather.parts[0].shape[-1]
        outs += [(bit_shape(b, (r, width)), BF16) for b, r in zip(bits, sizes)]
    if device_count() == GROUPS:
        body = functools.partial(place_kernel, axes, masks, cuts)
        placed = kernel(body, (order.uppers, *args), outs, 0, 24)
        order.done(placed[0])
    for gather, olds, sizes, bits, own_axes, at in plans:
        if device_count() == GROUPS:
            parts = placed[at : at + len(sizes)]
        else:
            held = []
            sides = zip(gather.parts, gather.others, own_axes, gather.masks)
            for mine, other, axis, mask in sides:
                up = upper_half(mask)
                low, high = jnp.where(up, other, mine), jnp.where(up, mine, other)
                held.append(jnp.stack([low, high], axis=axis))
            parts = cut_rows(held, olds, sizes)
        gather.parts, gather.bits = parts, bits


def add(order, *jobs):
    axes, all_masks, cuts, args, outs, plans, count = [], [], [], [], [], [], 0
    for chain, masks, sizes in jobs:
        olds = [p.shape[-2] for p in chain.keeps]
        sizes = sizes or olds
        bits = [chain.bits[min(j, len(olds) - 1)] for j in range(len(sizes))]
        own_axes = [axis_of(b, m) for b, m in zip(bits, masks)]
        left = [[b for b in old if b != m] for old, m in zip(bits, masks)]
        plans.append((chain, masks, olds, sizes, own_axes, left, len(axes)))
        cuts += [(count + i, len(axes) + j, x, y) for i, j, x, y in overlaps(olds, sizes)]
        axes += own_axes
        all_masks += masks
        count += len(olds)
        for keep, other in zip(chain.keeps, chain.others):
            args += [order.turn(keep), other]
        width = chain.keeps[0].shape[-1]
        for b, r in zip(left, sizes):
            outs += [(bit_shape(b, (r, width)), BF16)] * 2
    if device_count() == GROUPS:
        body = functools.partial(add_kernel, axes, all_masks, cuts, count)
        both = kernel(body, (order.uppers, *args), outs, 0, 24)
        order.done(both[0])
    for chain, masks, olds, sizes, own_axes, left, at in plans:
        if device_count() == GROUPS:
            found = both[2 * at : 2 * (at + len(sizes))]
            chain.keeps, chain.sends = found[0::2], found[1::2]
        else:
            sums = [
                (k.astype(F32) + o.astype(F32)).astype(BF16)
                for k, o in zip(chain.keeps, chain.others)
            ]
            sums = cut_rows(sums, olds, sizes)
            sides = list(zip(sums, [upper_half(m) for m in masks], own_axes))
            take = lax.dynamic_index_in_dim
            chain.keeps = [take(t, u, axis, False) for t, u, axis in sides]
            chain.sends = [take(t, 1 - u, axis, False) for t, u, axis in sides]
        chain.bits = left


class Gather:
    def __init__(self, order, *parts):
        self.order, self.parts, self.bits = order, list(parts), [[] for _ in parts]

    def go(self, *masks, wait=False):
        self.masks = masks
        parts = [self.order.turn(p) for p in self.parts] if wait else self.parts
        self.others = [swap(p, m) for p, m in zip(parts, masks)]

    def place(self, *sizes):
        place(self.order, (self, sizes))
        return self

    def whole(self):
        held = self.parts[0]
        return held.reshape((-1,) + held.shape[-2:])


def cut_rows(arrays, olds, sizes):
    if list(olds) == list(sizes):
        return arrays
    joint = jnp.concatenate(arrays, axis=-2)
    ends = [sum(sizes[: j + 1]) for j in range(len(sizes) - 1)]
    return jnp.split(joint, ends, axis=-2)


class Reduce:
    def __init__(self, order, keep, send, bits):
        shape = bit_shape(bits, keep.shape[-2:])
        self.order, self.bits = order, [bits]
        self.keeps, self.sends = [keep.reshape(shape)], [send.reshape(shape)]

    def go(self, *masks, wait=False):
        sends = [self.order.turn(p) for p in self.sends] if wait else self.sends
        self.others = [swap(p, m) for p, m in zip(sends, masks)]

    def add(self, masks, *sizes):
        add(self.order, (self, masks, sizes))
        return self

    def total(self):
        keep, other = self.keeps[0], self.others[0]
        return (keep.astype(F32) + other.astype(F32)).reshape(keep.shape[-2:])


def split_cores(blocks):
    pairs = blocks.reshape((-1, 2) + blocks.shape[1:])
    upper = upper_half(1)
    keep = lax.dynamic_index_in_dim(pairs, upper, 1, keepdims=False)
    return keep, lax.dynamic_index_in_dim(pairs, 1 - upper, 1, keepdims=False)


def joined(keep, send):
    return jnp.stack([keep, send], axis=1).reshape((-1,) + keep.shape[1:])


def grouped(buffer, sizes):
    count = buffer.shape[0]
    if count == GROUPS:
        return buffer
    width = buffer.shape[-1]
    share = width // count
    parts, start = [], 0
    for size in sizes:
        part = buffer[:, start : start + share * size]
        parts.append(part.reshape(GROUPS, UNIT * size, width))
        start += share * size
    return jnp.concatenate(parts, axis=1)


def scattered(buffer, sizes):
    count, width = device_count(), buffer.shape[-1]
    if count == GROUPS:
        return buffer
    parts, start = [], 0
    for size in sizes:
        part = buffer[:, start : start + UNIT * size]
        parts.append(part.reshape(count, width // count * size, width))
        start += UNIT * size
    return jnp.concatenate(parts, axis=1)


def vector_pack(vectors, rows, width):
    filled = jnp.pad(vectors, ((0, 0), (0, width - vectors.shape[1])))
    return jnp.pad(filled[:, None], ((0, 0), (0, rows - 1), (0, 0)))


def vector_regroup(vectors, parts, lengths):
    pieces, start = [], 0
    for length in lengths:
        pieces.append(vectors[:, start : start + length].reshape(parts, -1))
        start += length
    return jnp.concatenate(pieces, axis=1)


def dot(a, b, dims=((1,), (0,))):
    return lax.dot_general(a, b, (dims, ((), ())), preferred_element_type=F32)


def iota(shape, axis):
    return lax.broadcasted_iota(jnp.int32, shape, axis)


def tile(ref, place, size=1):
    rows = ref[:, UNIT * place : UNIT * (place + size), :]
    return rows.reshape(GROUPS * UNIT * size, rows.shape[-1])


def pack_kernel(moves, counts, *refs):
    inputs, outs, sems = refs[: counts[0]], refs[counts[0] : -1], refs[-1]
    copies = []
    for at, (source, where, out, start, rows) in enumerate(moves):
        into = outs[out].at[pl.ds(start, rows)]
        piece = inputs[source] if where is None else inputs[source].at[where]
        copies.append(pltpu.make_async_copy(piece, into, sems.at[at]))
        copies[-1].start()
    for copy in copies:
        copy.wait()


def packed(args, moves, shapes):
    return pl.pallas_call(
        functools.partial(pack_kernel, moves, (len(args),)),
        in_specs=[pl.BlockSpec(memory_space=pltpu.HBM) for _ in args],
        out_specs=[pl.BlockSpec(memory_space=pltpu.VMEM) for _ in shapes],
        out_shape=[jax.ShapeDtypeStruct(shape, BF16) for shape in shapes],
        scratch_shapes=[pltpu.SemaphoreType.DMA((len(moves),))],
        compiler_params=pltpu.CompilerParams(vmem_limit_bytes=8 << 20),
    )(*args)


def kernel(body, args, outs, flops, limit, scratch=()):
    spec = {jnp.dtype(jnp.int32): pltpu.SMEM}
    return pl.pallas_call(
        body,
        in_specs=[pl.BlockSpec(memory_space=spec.get(a.dtype, pltpu.VMEM)) for a in args],
        out_specs=[pl.BlockSpec(memory_space=pltpu.VMEM) for _ in outs],
        out_shape=[jax.ShapeDtypeStruct(shape, dtype) for shape, dtype in outs],
        scratch_shapes=list(scratch),
        compiler_params=pltpu.CompilerParams(vmem_limit_bytes=limit << 20),
        cost_estimate=pl.CostEstimate(
            flops=flops,
            bytes_accessed=sum(a.size * a.dtype.itemsize for a in args),
            transcendentals=0,
        ),
    )(*args)


def unit_norm(values):
    center = values - jnp.mean(values, axis=-1, keepdims=True)
    spread = jnp.mean(center * center, axis=-1, keepdims=True)
    inverse = lax.rsqrt(spread + EPSILON)
    return center * inverse, inverse


def norm_back(grad, unit, inverse, gain):
    e = grad * gain
    mean_e = jnp.mean(e, axis=-1, keepdims=True)
    mean_x = jnp.mean(e * unit, axis=-1, keepdims=True)
    return inverse * (e - mean_e - unit * mean_x)


def column_sum(values):
    return jnp.sum(values, axis=0, keepdims=True)


def valid_column(info, m, start, rows):
    place = start + iota((rows, 1), 0)
    first = (place >= 1) & (place < info[m, 0])
    second = (place >= info[m, 1]) & (place < info[m, 2])
    return jnp.where(first | second, 1.0, 0.0).astype(F32)


def segment_start(info, m, place):
    start = jnp.where(place >= 1, 1, 0)
    start = jnp.where(place >= info[m, 1], info[m, 1], start)
    return jnp.where(place >= info[m, 3], info[m, 3], start)


VECTORS = 5
BIAS_AT = VECTORS * UNIT


def vector_maps(width):
    lanes = width // 2
    fine = (iota((lanes, width), 0) & 15) == (iota((lanes, width), 1) & 15)
    wide = ((iota((lanes, width), 0) + 48) & 63) == (iota((lanes, width), 1) & 63)
    own_fine = iota((GROUPS, width), 1) >> 4 == iota((GROUPS, width), 0)
    own_wide = iota((GROUPS, width), 1) >> 6 == (iota((GROUPS, width), 0) & 7)
    as_bf16 = [jnp.where(m, 1.0, 0.0).astype(BF16) for m in (fine, wide)]
    as_f32 = [jnp.where(m, 1.0, 0.0).astype(F32) for m in (own_fine, own_wide)]
    return as_bf16 + as_f32


def lane_window(lanes, k):
    place = iota((GROUPS, lanes), 1)
    if k == VECTORS:
        return (place >= BIAS_AT) & (place < BIAS_AT + 64)
    return (place >= UNIT * k) & (place < UNIT * (k + 1))


def window_map(micro, each, tap):
    slots = each // 3
    shape = (micro * slots, micro * (each + RIM))
    row, place = iota(shape, 0), iota(shape, 1)
    m = jnp.zeros(shape, jnp.int32)
    for i in range(1, micro):
        m = m + jnp.where(row >= slots * i, 1, 0)
    source = 3 * (row - slots * m) - 2 + tap
    rim = micro * each + RIM * m + RIM + source
    target = jnp.where(source >= 0, each * m + source, rim)
    return jnp.where(place == target, 1.0, 0.0).astype(BF16)


def keep_and_compress(info, low, weights, kept, window, memory):
    micro = info.shape[0]
    each = low.shape[0] // micro - RIM
    valid = [valid_column(info, m, info[m, 4], each) for m in range(micro)]
    valid += [valid_column(info, m, info[m, 4] - RIM, RIM) for m in range(micro)]
    rows = (dot(low, tile(weights, 0)) * jnp.concatenate(valid, axis=0)).astype(BF16)
    kept[...] = rows
    total = None
    for tap in range(3):
        taken = dot(window_map(micro, each, tap), rows).astype(BF16)
        window[tap] = taken
        part = dot(taken, tile(weights, 1 + tap))
        total = part if total is None else total + part
    memory[...] = total.astype(BF16)


def key_kernel(info, tok, halo, weights, normed, kept, window, memory, vec):
    width = tok.shape[-1]
    lanes = width // 2
    fine, wide, own_fine, own_wide = vector_maps(width)
    rows = jnp.sum(weights[:, 4 * UNIT : 5 * UNIT, :lanes].astype(F32), axis=1)
    picked = [jnp.where(lane_window(lanes, k), rows, 0.0) for k in range(VECTORS + 1)]
    spread = dot(jnp.concatenate(picked[:VECTORS], axis=0).astype(BF16), fine)
    vectors = [
        column_sum(spread[GROUPS * k : GROUPS * (k + 1)] * own_fine) for k in range(VECTORS)
    ]
    bias = dot(picked[VECTORS].astype(BF16), wide) * own_wide
    bias = jnp.sum(bias.reshape(4, 8, width), axis=1)
    vec[...] = jnp.concatenate(vectors + [bias, jnp.zeros((7, width), F32)], axis=0)
    values = jnp.concatenate([tok[...], halo[...]], axis=0).astype(F32)
    unit, _ = unit_norm(values)
    low = (unit * vectors[0] + vectors[1]).astype(BF16)
    normed[...] = low
    keep_and_compress(info, low, weights, kept, window, memory)


def value_kernel(info, normed, weights, query, kept, window, memory):
    low = normed[...]
    keep_and_compress(info, low, weights, kept, window, memory)
    query[...] = dot(low[: query.shape[0]], tile(weights, 4)).astype(BF16)


def stacked(values, lower):
    zero = jnp.zeros_like(values)
    return jnp.concatenate(
        [jnp.where(lower, values, zero), jnp.where(lower, zero, values)], axis=0
    )


def merged(values, lower):
    half = values.shape[0] // 2
    return jnp.where(lower, values[:half], values[half:])


def memory_pair(memory, m, pair, micro):
    slots = memory.shape[1] // micro
    rows = memory[:, slots * m : slots * (m + 1), PAIR * pair : PAIR * (pair + 1)]
    return rows.reshape(memory.shape[0] * slots, PAIR)


def attend_kernel(info, query, keys, values, memory_keys, memory_values, attended, stats):
    micro = info.shape[0]
    count, width = query.shape
    each = count // micro
    slots = memory_keys.shape[0] * memory_keys.shape[1] // micro
    pairs = width // PAIR
    lower = iota((each, PAIR), 1) < HEAD_DIM
    lane = iota((2 * each, 128), 1)
    found = jnp.zeros((2 * each, 128), F32)
    for m in range(micro):
        rows = slice(each * m, each * (m + 1))
        place = info[m, 4] + iota((each, 1), 0)
        start = segment_start(info, m, place)
        end = 3 * iota((each, slots), 1)
        bias = jnp.where((end <= place) & (end >= start), 0.0, MASKED).astype(F32)
        bias = jnp.concatenate([bias, bias], axis=0)
        for pair in range(pairs):
            cols = slice(PAIR * pair, PAIR * (pair + 1))
            key = keys[rows, cols].astype(F32)
            value = values[rows, cols].astype(F32)
            queries = stacked(query[rows, cols].astype(F32) * SCALE, lower)
            own = jnp.sum(queries * jnp.concatenate([key, key], axis=0), axis=1, keepdims=True)
            memory_key = memory_pair(memory_keys, m, pair, micro)
            memory_value = memory_pair(memory_values, m, pair, micro)
            scores = dot(queries.astype(BF16), memory_key, NT) + bias
            top = jnp.maximum(jnp.max(scores, axis=1, keepdims=True), own)
            expos = jnp.exp(scores - top)
            own = jnp.exp(own - top)
            total = jnp.sum(expos, axis=1, keepdims=True) + own
            inverse = 1.0 / total
            mixed = dot(expos.astype(BF16), memory_value) * inverse
            weight = jnp.broadcast_to(own * inverse, mixed.shape)
            attended[rows, cols] = merged(mixed, lower) + merged(weight, lower) * value
            found = jnp.where(lane == m * pairs + pair, top + jnp.log(total), found)
    stats[...] = found


def erf(values):
    values = jnp.clip(values, -3.832506856900711, 3.832506856900711)
    square = values * values
    above, below = ERF_TOP[0], ERF_LOW[0]
    for c in ERF_TOP[1:]:
        above = above * square + c
    for c in ERF_LOW[1:]:
        below = below * square + c
    return values * above / below


def even_first(flag, rows, size):
    pairs = rows.reshape(-1, 2, size, rows.shape[-1])
    even, odd = pairs[:, 0], pairs[:, 1]
    halves = [jnp.where(flag == 0, even, odd), jnp.where(flag == 0, odd, even)]
    return jnp.concatenate(halves, axis=0).reshape(rows.shape)


def deal(value, rows, keep, send, blocks, start):
    halves = value.astype(BF16).reshape(2, -1, rows, value.shape[-1])
    keep[blocks, start : start + rows, :] = halves[0]
    send[blocks, start : start + rows, :] = halves[1]


def deal_tile(value, place, keep, send):
    deal(value, UNIT, keep, send, slice(None), UNIT * place)


def feed_kernel(
    info,
    tok,
    cot,
    attended,
    vec,
    rest,
    out,
    grad_mid,
    grad_att,
    keep,
    send,
    vec_grad,
):
    count, width = tok.shape
    wide = 4
    low_att = attended[...].astype(BF16)
    w_out = tile(rest, 0)
    middle = tok[...].astype(F32) + dot(low_att, w_out)
    unit, inverse = unit_norm(middle)
    gain = vec[2:3, :]
    low = (unit * gain + vec[3:4, :]).astype(BF16)
    flag = info[0, 5]
    low_t = even_first(flag, low.T, UNIT)
    cots = cot[...]
    total = middle + vec[4:5, :]
    grad_low = jnp.zeros((count, width), F32)
    bias_rows = []
    eighth = GROUPS // wide
    for c in range(wide):
        w_up = tile(rest, 1 + c)
        down = slice(eighth * c, eighth * (c + 1))
        w_down = rest[down, UNIT * (1 + wide) :, :].reshape(width, width)
        hidden = dot(low, w_up) + vec[5 + c : 6 + c, :]
        share = 0.5 + 0.5 * erf(hidden * 0.7071067811865476)
        slope = share + hidden * (0.3989422804014327 * jnp.exp(-0.5 * hidden * hidden))
        active = (hidden * share).astype(BF16)
        total = total + dot(active, w_down)
        grad_hidden_f = dot(cots, w_down, NT) * slope
        grad_hidden = grad_hidden_f.astype(BF16)
        bias_rows.append(column_sum(grad_hidden.astype(F32)))
        grad_low = grad_low + dot(grad_hidden, w_up, NT)
        deal_tile(dot(low_t, grad_hidden), 1 + c, keep, send)
        where = slice(eighth // 2 * c, eighth // 2 * (c + 1))
        active_t = even_first(flag, active.T, UNIT * wide)
        deal(dot(active_t, cots), UNIT * wide, keep, send, where, UNIT * (1 + wide))
    out[...] = total.astype(BF16)
    cots_f = cots.astype(F32)
    grad_middle = cots_f + norm_back(grad_low, unit, inverse, gain)
    grad_mid[...] = grad_middle
    branch = grad_middle.astype(BF16)
    deal_tile(dot(even_first(flag, low_att.T, UNIT), branch), 0, keep, send)
    grad_att[...] = dot(branch, w_out, NT).astype(BF16)
    rows = [jnp.zeros((2, width), F32), column_sum(grad_low * unit), column_sum(grad_low)]
    rows += [column_sum(cots_f)] + bias_rows + [jnp.zeros((7, width), F32)]
    vec_grad[...] = jnp.concatenate(rows, axis=0)


def memory_turned(flag, memory, m, pair, micro):
    slots = memory.shape[2] // micro
    rows, cols = slice(slots * m, slots * (m + 1)), slice(PAIR * pair, PAIR * (pair + 1))
    halves = [memory[:, pl.ds(at, 1), rows, cols] for at in (flag, 1 - flag)]
    return jnp.concatenate([h.reshape(-1, PAIR) for h in halves], axis=0)


def attend_back_kernel(
    info,
    query,
    keys,
    values,
    memory_keys,
    memory_values,
    attended,
    stats,
    grad_att,
    grad_query,
    key_keep,
    key_send,
    value_keep,
    value_send,
    own_key,
    own_value,
):
    micro = info.shape[0]
    count, width = query.shape
    each = count // micro
    chips = memory_keys.shape[0]
    share = memory_keys.shape[2] // micro
    slots = 2 * chips * share
    flag = info[0, 6]
    pairs = width // PAIR
    lower = iota((each, PAIR), 1) < HEAD_DIM
    lane = iota((2 * each, 128), 1)
    found = stats[...]
    deltas = jnp.zeros((2 * each, 128), F32)
    parts = {}
    for m in range(micro):
        rows = slice(each * m, each * (m + 1))
        for pair in range(pairs):
            cols = slice(PAIR * pair, PAIR * (pair + 1))
            grad = grad_att[rows, cols].astype(F32)
            product = stacked(grad * attended[rows, cols], lower)
            delta = jnp.sum(product, axis=1, keepdims=True)
            deltas = jnp.where(lane == m * pairs + pair, delta, deltas)
            parts[m, pair] = delta
    found_t, deltas_t = found.T, deltas.T
    for m in range(micro):
        rows = slice(each * m, each * (m + 1))
        lanes = iota((1, 2 * each), 1)
        place = info[m, 4] + jnp.where(lanes >= each, lanes - each, lanes)
        start = segment_start(info, m, place)
        row = iota((slots, 1), 0)
        late = row >= chips * share
        row = jnp.where(late, row - chips * share, row)
        block = jnp.zeros((slots, 1), jnp.int32)
        for chip in range(1, chips):
            block = block + jnp.where(row >= share * chip, 1, 0)
        core = jnp.where(late, 1 - flag, flag)
        end = 3 * (row + share * (block + core))
        bias = jnp.where((end <= place) & (end >= start), 0.0, MASKED).astype(F32)
        for pair in range(pairs):
            cols = slice(PAIR * pair, PAIR * (pair + 1))
            at = m * pairs + pair
            key = keys[rows, cols].astype(F32)
            value = values[rows, cols].astype(F32)
            query_f = query[rows, cols].astype(F32) * SCALE
            grad_f = grad_att[rows, cols].astype(F32)
            queries = stacked(query_f, lower)
            grads = stacked(grad_f, lower)
            own = jnp.sum(queries * jnp.concatenate([key, key], axis=0), axis=1, keepdims=True)
            own = jnp.exp(own - found[:, at : at + 1])
            grad_own = jnp.sum(
                grads * jnp.concatenate([value, value], axis=0), axis=1, keepdims=True
            )
            grad_own = (own * (grad_own - parts[m, pair])).astype(BF16).astype(F32)
            queries, grads = queries.astype(BF16), grads.astype(BF16)
            memory_key = memory_turned(flag, memory_keys, m, pair, micro)
            memory_value = memory_turned(flag, memory_values, m, pair, micro)
            scores = dot(memory_key, queries, NT) + bias
            probs = jnp.exp(scores - found_t[at : at + 1, :])
            grad_probs = dot(memory_value, grads, NT)
            grad_scores = (probs * (grad_probs - deltas_t[at : at + 1, :])).astype(BF16)
            sides = (
                (dot(grad_scores, queries), key_keep, key_send),
                (dot(probs.astype(BF16), grads), value_keep, value_send),
            )
            for grad, keep, send in sides:
                halves = grad.astype(BF16).reshape(2, chips, share, PAIR)
                keep[:, share * m : share * (m + 1), cols] = halves[0]
                send[:, share * m : share * (m + 1), cols] = halves[1]
            turned = dot(memory_key.T, grad_scores).T
            own_grad = merged(jnp.broadcast_to(grad_own, (2 * each, PAIR)), lower)
            own_weight = merged(jnp.broadcast_to(own, (2 * each, PAIR)), lower)
            grad_query[rows, cols] = (
                SCALE * (merged(turned, lower) + own_grad * key)
            ).astype(BF16)
            own_key[rows, cols] = own_grad * query_f
            own_value[rows, cols] = own_weight * grad_f


def compress_back_kernel(
    info,
    key_memory,
    value_memory,
    key_window,
    value_window,
    key_weights,
    value_weights,
    normed,
    grad_query,
    key_grad,
    value_grad,
    rims,
    keep,
    send,
):
    micro = info.shape[0]
    count, width = key_grad.shape
    each = count // micro
    flag = info[0, 5]
    places = [window_map(micro, each, tap) for tap in range(3)]
    sides = (
        (key_memory, key_window, key_weights, key_grad),
        (value_memory, value_window, value_weights, value_grad),
    )
    for kind, (memory, window, weights, out) in enumerate(sides):
        grad = memory[...]
        total = None
        for tap in range(3):
            window_t = even_first(flag, window[tap].T, UNIT)
            deal_tile(dot(window_t, grad), 4 * kind + tap, keep, send)
            part = dot(grad, tile(weights, 1 + tap), NT)
            high = part.astype(BF16)
            rest = (part - high.astype(F32)).astype(BF16)
            part = dot(places[tap], high, TN) + dot(places[tap], rest, TN)
            total = part if total is None else total + part
        out[...] = total[:count]
        rims[:, width * kind : width * (kind + 1)] = total[count:]
    low_t = even_first(flag, normed[:count, :].T, UNIT)
    deal_tile(dot(low_t, grad_query[...]), 3, keep, send)


def input_kernel(
    info,
    tok,
    normed,
    grad_query,
    key_grad,
    value_grad,
    rims,
    own_key,
    own_value,
    key_weights,
    value_weights,
    vec,
    grad_mid,
    vec_grad,
    grad_in,
    keep,
    send,
    total,
):
    count, width = tok.shape
    micro = info.shape[0]
    each = count // micro
    valid = [valid_column(info, m, info[m, 4], each) for m in range(micro)]
    valid = jnp.concatenate(valid, axis=0)
    flag = info[0, 5]
    low_t = even_first(flag, normed[:count, :].T, UNIT)
    grad_low = dot(grad_query[...], tile(value_weights, 4), NT)
    sides = ((key_grad, own_key, key_weights), (value_grad, own_value, value_weights))
    for kind, (grad, own, weights) in enumerate(sides):
        total[...] = grad[...] + own[...]
        for m in range(micro):
            rows = slice(each * (m + 1) - RIM, each * (m + 1))
            rim = rims[RIM * m : RIM * (m + 1), width * kind : width * (kind + 1)]
            total[rows, :] = total[rows, :] + rim
        low_grad = (total[...] * valid).astype(BF16)
        grad_low = grad_low + dot(low_grad, tile(weights, 0), NT)
        deal_tile(dot(low_t, low_grad), kind, keep, send)
    unit, inverse = unit_norm(tok[...].astype(F32))
    back = norm_back(grad_low, unit, inverse, vec[0:1, :])
    grad_in[...] = (grad_mid[...] + back).astype(BF16)

    lanes = width // 2
    fine, wide, own_fine, own_wide = vector_maps(width)
    vectors = [column_sum(grad_low * unit), column_sum(grad_low)]
    vectors += [vec_grad[k : k + 1, :] for k in range(2, VECTORS)]
    dealt = jnp.concatenate([own_fine * v for v in vectors], axis=0).astype(BF16)
    dealt = dot(dealt, fine, NT)
    bias = [
        jnp.broadcast_to(vec_grad[VECTORS + c : VECTORS + c + 1, :], (8, width)) for c in range(4)
    ]
    bias = (jnp.concatenate(bias, axis=0) * own_wide).astype(BF16)
    packed = jnp.where(lane_window(lanes, VECTORS), dot(bias, wide, NT), 0.0)
    for k in range(VECTORS):
        packed = jnp.where(lane_window(lanes, k), dealt[GROUPS * k : GROUPS * (k + 1)], packed)
    packed = jnp.concatenate([packed, jnp.zeros((GROUPS, width - lanes), F32)], axis=1)
    spot = iota((GROUPS, UNIT, width), 1) == 0
    spread = jnp.broadcast_to(packed[:, None, :], (GROUPS, UNIT, width))
    packed = jnp.where(spot, spread, 0.0).reshape(GROUPS * UNIT, width)
    deal_tile(even_first(flag, packed, UNIT), 2, keep, send)


def per_device(
    tokens,
    lengths,
    ln1_gain,
    ln1_bias,
    w_query,
    w_key,
    w_value,
    conv_key,
    conv_value,
    w_out,
    ln2_gain,
    ln2_bias,
    w_up,
    b_up,
    w_down,
    b_down,
    cotangent,
):
    count = device_count()
    micro, _, each, width = tokens.shape
    ff = w_up.shape[1]
    wide = ff // width
    share = width // count
    seq = lax.axis_size("seq")
    all_tokens = micro * each
    slots = micro * each // 3
    memory_bytes = 4 * seq * slots * width

    whole = count == GROUPS
    vector_lengths = [share] * VECTORS + [ff // count]
    vectors, start = 0.0, 0
    for part in (ln1_gain, ln1_bias, ln2_gain, ln2_bias, b_down, b_up):
        end = start + part.shape[0]
        pad = ((0, (UNIT if whole else 2) - 1), (start, width - end))
        vectors, start = vectors + jnp.pad(part[None], pad), end
    vectors = vectors.astype(BF16)
    across = powers(seq, count)
    along = powers(2, seq)[::-1]
    back = along[::-1]
    order = Order()
    lengths = lengths[:, 0]
    first_pad = 3 * ((lengths[:, 0] + 2) // 3)
    second_pad = 3 * ((lengths[:, 1] + 2) // 3)
    start = 1 + first_pad
    seats = [lax.axis_index("seq") * each, upper_half(1) if whole else 0, upper_half(1)]
    seats = [jnp.full_like(start, seat) for seat in seats]
    info = [1 + lengths[:, 0], start, start + lengths[:, 1], start + second_pad]
    info = jnp.stack(info + seats, axis=1).astype(jnp.int32)
    if whole:
        moves = [(kind, None, kind, 0, UNIT) for kind in range(2)]
        moves += [(2 + k, tap, k, UNIT * (1 + tap), UNIT) for k in range(2) for tap in range(3)]
        moves += [(4 + kind, None, kind, 4 * UNIT, UNIT) for kind in range(2)]
        first, second = packed(
            (w_key, w_value, conv_key, conv_value, vectors, w_query),
            moves,
            ((5 * UNIT, width),) * 2,
        )
        moves = [(0, None, 0, 0, UNIT)]
        for c in range(wide):
            cols = (slice(None), pl.ds(width * c, width))
            moves.append((1, cols, 0, UNIT * (1 + c), UNIT))
        moves.append((2, None, 0, UNIT * (1 + wide), UNIT * wide))
        (rest,) = packed(
            (w_out, w_up, w_down), moves, (((1 + 2 * wide) * UNIT, width),)
        )
    else:
        first = jnp.concatenate([w_key, *conv_key, vectors], axis=0)
        second = jnp.concatenate([w_value, *conv_value, w_query], axis=0)
        ups = [w_up[:, width * c : width * (c + 1)] for c in range(wide)]
        rest = jnp.concatenate([w_out] + ups + [w_down], axis=0)
    rest_rows = rest.shape[0]
    upper_rows = share * (1 + wide)
    one, two, both = Gather(order, first), Gather(order, second), Gather(order, rest)
    one.go(along[0])
    two.go(back[0])
    halo = lax.ppermute(
        tokens[:, 0, each - RIM :], "seq", [(i, i + 1) for i in range(seq - 1)]
    ).reshape(micro * RIM, width)
    order.done((halo, info, rest))
    for at in range(1, len(along)):
        one.place()
        one.go(along[at])
        two.place()
        two.go(back[at])
    one.place()
    one.go(across[0])
    two.place()
    two.go(across[-1])
    both.go(along[0], wait=True)
    for at in range(1, max(len(across), len(along))):
        jobs = []
        if at < len(across):
            one.place()
            one.go(across[at])
            jobs.append((two, ()))
        if at < len(along):
            jobs.append((both, ()))
        place(order, *jobs)
        if at < len(across):
            two.go(across[-1 - at])
        if at < len(along):
            both.go(along[at])
    one.place()
    one.go(1)
    place(order, (two, ()), (both, (upper_rows, rest_rows - upper_rows)))
    two.go(1)
    both.go(across[0], across[-1])
    first = one.place().whole()
    first_sizes, rest_sizes = [1] * 5, [1] * (1 + wide) + [wide]
    if not whole:
        dealt = vector_regroup(first[:, 4 * share], GROUPS, vector_lengths)
        dealt = vector_pack(dealt, UNIT, width)
        first = jnp.concatenate([grouped(first, [1] * 4), dealt], axis=1)

    tok = tokens.reshape(all_tokens, width)
    cot = cotangent.reshape(all_tokens, width)
    rows = (all_tokens, width)
    grown = 4 * max(memory_bytes // (1 << 20) - 2, 0)
    limits = [16, 16, 16 + grown, 28, 28 + grown, 28, 28]
    matmul = 2 * all_tokens * width * width

    padded = (all_tokens + micro * RIM, width)
    windows = (3, slots, width)

    normed, keys, key_window, memory_key, vec = kernel(
        key_kernel,
        (info, order.turn(tok), halo, first),
        ((padded, BF16), (padded, BF16), (windows, BF16), ((slots, width), BF16), ((16, width), F32)),
        2 * matmul,
        limits[0],
    )
    order.done(memory_key)
    keys_side = Gather(order, memory_key)
    keys_side.go(along[0])
    second = grouped(two.place().whole(), first_sizes)
    query, values, value_window, memory_value = kernel(
        value_kernel,
        (info, normed, second),
        ((rows, BF16), (padded, BF16), (windows, BF16), ((slots, width), BF16)),
        3 * matmul,
        limits[1],
    )
    order.done(memory_value)
    values_side = Gather(order, memory_value)
    values_side.go(back[0])
    for at in range(1, max(len(across), len(along))):
        jobs = []
        if at < len(along):
            keys_side.place()
            keys_side.go(along[at])
            jobs.append((values_side, ()))
        if at < len(across):
            jobs.append((both, ()))
        place(order, *jobs)
        if at < len(along):
            values_side.go(back[at])
        if at < len(across):
            both.go(across[at], across[-1 - at])
    keys_side.place()
    keys_side.go(1)
    place(order, (values_side, ()), (both, (rest_rows,)))
    values_side.go(1)
    both.go(1)
    memories = [keys_side.place().whole(), values_side.place().whole()]
    attended, stats = kernel(
        attend_kernel,
        (info, order.turn(query), keys, values, *memories),
        ((rows, F32), ((2 * each, 128), F32)),
        4 * matmul,
        limits[2],
    )
    order.done(attended)
    rest = grouped(both.place().whole(), rest_sizes)
    half = GROUPS // 2

    def pieces(size):
        return (((half, UNIT * size, width), BF16),) * 2

    output, grad_mid, grad_att, *halves, vec_grad = kernel(
        feed_kernel,
        (info, order.turn(tok), cot, attended, vec, rest),
        ((rows, BF16), (rows, F32), (rows, BF16)) + pieces(1 + 2 * wide) + (((16, width), F32),),
        27 * matmul,
        limits[3],
    )
    order.done(halves[0])
    all_bits = powers(2, count)[::-1]

    def begin(keep, send, size):
        if not whole:
            keep, send = split_cores(scattered(joined(keep, send), size))
        return Reduce(order, keep, send, all_bits)

    feeds = begin(*halves, rest_sizes)
    feeds.go(1)
    memory_half = ((seq // 2, slots, width), BF16)
    chips = (seq // 2, 2, slots, width)
    grad_query, *halves, own_key, own_value = kernel(
        attend_back_kernel,
        (
            info,
            order.turn(query),
            keys,
            values,
            memories[0].reshape(chips),
            memories[1].reshape(chips),
            attended,
            stats,
            grad_att,
        ),
        ((rows, BF16),) + (memory_half,) * 4 + ((rows, F32), (rows, F32)),
        10 * matmul,
        limits[4],
    )
    order.done(grad_query)
    keys_side = Reduce(order, *halves[:2], along)
    values_side = Reduce(order, *halves[2:], along)
    keys_side.go(1)
    values_side.go(1)
    cross = [(across[-1 - at], across[at]) for at in range(len(across))]
    keys_side.add((back[0],))
    keys_side.go(back[0])
    cuts = (upper_rows, rest_rows - upper_rows)
    add(order, (values_side, (along[0],), ()), (feeds, cross[0], cuts))
    values_side.go(along[0])
    feeds.go(*cross[0])
    for at in range(1, max(len(along), len(cross))):
        jobs = []
        if at < len(along):
            keys_side.add((back[at],))
            keys_side.go(back[at])
            jobs.append((values_side, (along[at],), ()))
        if at < len(cross):
            jobs.append((feeds, cross[at], ()))
        add(order, *jobs)
        if at < len(along):
            values_side.go(along[at])
        if at < len(cross):
            feeds.go(*cross[at])
    feeds.add((back[0],), rest_rows)
    key_grad, value_grad = (held.total().astype(BF16) for held in (keys_side, values_side))
    key_kept, value_kept, rims, *halves = kernel(
        compress_back_kernel,
        (
            info,
            order.turn(key_grad),
            value_grad,
            key_window,
            value_window,
            first,
            second,
            normed,
            grad_query,
        ),
        ((rows, F32), (rows, F32), ((micro * RIM, 2 * width), F32)) + pieces(7),
        5 * matmul,
        limits[5],
    )
    order.done(rims)
    rims = lax.ppermute(rims, "seq", [(i + 1, i) for i in range(seq - 1)])
    convs = begin(*halves, [1] * 7)
    convs.go(1)
    grad_in, *halves = kernel(
        input_kernel,
        (
            info,
            order.turn(tok),
            normed,
            grad_query,
            key_kept,
            value_kept,
            rims,
            own_key,
            own_value,
            first,
            second,
            vec,
            grad_mid,
            vec_grad,
        ),
        ((rows, BF16),) + pieces(3),
        6 * matmul,
        limits[6],
        (pltpu.VMEM(rows, F32),),
    )
    order.done(grad_in)
    if whole:
        inputs = begin(*halves, [1] * 3)
    else:
        dealt = joined(*halves)
        vectors = dealt[:, 2 * UNIT, : VECTORS * UNIT + ff // GROUPS]
        vectors = vector_regroup(vectors, count, [UNIT] * VECTORS + [ff // GROUPS])
        dealt = [scattered(dealt, [1] * 2), vector_pack(vectors, 2, width)]
        dealt = split_cores(jnp.concatenate(dealt, axis=1))
        inputs = Reduce(order, *dealt, all_bits)
    inputs.go(1)
    line = [masks[1] for masks in cross]
    cuts = (5 * share, 2 * share)
    convs.add(cross[0], *cuts)
    convs.go(*cross[0])
    feeds.go(back[0])
    inputs.add((line[0],))
    inputs.go(line[0])
    for at in range(1, max(len(along), len(cross))):
        jobs = []
        if at < len(cross):
            jobs.append((convs, cross[at], ()))
        if at < len(along):
            jobs.append((feeds, (back[at],), ()))
        add(order, *jobs)
        if at < len(cross):
            convs.go(*cross[at])
        if at < len(along):
            feeds.go(back[at])
        if at < len(cross):
            inputs.add((line[at],))
            inputs.go(line[at])
    for at in range(len(along)):
        convs.add((back[at],), 7 * share)
        convs.go(back[at])
        inputs.add((along[at],))
        inputs.go(along[at])
    feeds, convs, late_inputs = feeds.total(), convs.total(), inputs.total()
    conv_keys = convs[: 3 * share].reshape(3, share, width)
    conv_values = convs[4 * share :].reshape(3, share, width)

    def own(buffer, number):
        return buffer[share * number : share * (number + 1)]

    vector_row = late_inputs[2 * share]

    def own_vector(number, length=share):
        return vector_row[share * number : share * number + length]

    return (
        output.reshape(tokens.shape),
        grad_in.reshape(tokens.shape),
        own_vector(0),
        own_vector(1),
        own(convs, 3),
        own(late_inputs, 0),
        own(late_inputs, 1),
        conv_keys,
        conv_values,
        own(feeds, 0),
        own_vector(2),
        own_vector(3),
        jnp.concatenate([own(feeds, 1 + c) for c in range(wide)], axis=1),
        own_vector(VECTORS, ff // count),
        feeds[share * (1 + wide) :],
        own_vector(4),
    )


def solution(mesh):
    rows = P(AXES, None)
    vector = P(AXES)
    conv = P(None, AXES, None)
    part = P(None, "batch", "seq", None)
    weights = (vector, vector, rows, rows, rows, conv, conv, rows, vector, vector)
    weights = weights + (rows, vector, rows, vector)
    return jax.shard_map(
        per_device,
        mesh=mesh,
        in_specs=(part, P(None, "batch", None)) + weights + (part,),
        out_specs=(part, part) + weights,
        check_vma=False,
    )
```

```python
import functools

import jax
import jax.numpy as jnp
from jax import lax
from jax.experimental import pallas as pl
from jax.experimental.pallas import tpu as pltpu
from jax.sharding import PartitionSpec as P

HEADS = 8
HEAD_DIM = 64
SCALE = HEAD_DIM ** (-0.5)
EPSILON = 1e-06
AXES = ("batch", "seq")
GROUPS = 32
UNIT = 16
PAIR = 2 * HEAD_DIM
RIM = 8
MASKED = -1e30
F32 = jnp.float32
BF16 = jnp.bfloat16
TN = ((0,), (0,))
NT = ((1,), (1,))
ERF_STEP = 0.3275911
ERF_TERMS = (1.061405429, -1.453152027, 1.421413741, -0.284496736, 0.254829592)


def device_count():
    return lax.axis_size("batch") * lax.axis_size("seq")


def device_index():
    return lax.axis_index("batch") * lax.axis_size("seq") + lax.axis_index("seq")


def powers(low, high):
    masks = []
    while low < high:
        masks.append(low)
        low *= 2
    return masks


def swap(array, mask):
    return lax.ppermute(array, AXES, [(i, i ^ mask) for i in range(device_count())])


def upper_half(mask):
    return ((device_index() & mask) != 0).astype(jnp.int32)


class Order:
    def __init__(self):
        self.last = None
        bits = device_count().bit_length() - 1
        self.uppers = jnp.stack([upper_half(1 << bit) for bit in range(bits)])

    def turn(self, array):
        if self.last is not None:
            array = lax.optimization_barrier((array, self.last))[0]
        return array

    def done(self, array):
        self.last = array


def axis_of(bits, mask):
    return sum(b > mask for b in bits)


def bit_shape(bits, rows):
    return (2,) * len(bits) + tuple(rows)


def at_bit(rank, axis, index, rows):
    where = [slice(None)] * rank
    where[axis] = pl.ds(index, 1)
    where[-2] = rows
    return tuple(where)


def overlaps(lefts, rights):
    found, left_at = [], 0
    for i, left in enumerate(lefts):
        right_at = 0
        for j, right in enumerate(rights):
            low = max(left_at, right_at)
            high = min(left_at + left, right_at + right)
            if low < high:
                found.append(
                    (i, j, slice(low - left_at, high - left_at), slice(low - right_at, high - right_at))
                )
            right_at += right
        left_at += left
    return found


def place_kernel(axes, masks, cuts, uppers, *refs):
    count = len(axes)
    for i, j, inside, outside in cuts:
        mine, other, out = refs[2 * i], refs[2 * i + 1], refs[2 * count + j]
        rank, axis, at = len(out.shape), axes[i], uppers[masks[i].bit_length() - 1]
        source = (slice(None),) * (rank - 3) + (inside, slice(None))
        out[at_bit(rank, axis, at, outside)] = jnp.expand_dims(mine[source], axis)
        out[at_bit(rank, axis, 1 - at, outside)] = jnp.expand_dims(other[source], axis)


def add_kernel(axes, masks, cuts, count, uppers, *refs):
    for i, j, inside, outside in cuts:
        keep, other = refs[2 * i], refs[2 * i + 1]
        next_keep, next_send = refs[2 * count + 2 * j], refs[2 * count + 2 * j + 1]
        rank, axis, at = len(keep.shape), axes[j], uppers[masks[j].bit_length() - 1]
        into = (slice(None),) * (rank - 3) + (outside, slice(None))
        here, there = at_bit(rank, axis, at, inside), at_bit(rank, axis, 1 - at, inside)
        next_send[into] = jnp.squeeze(keep[there] + other[there], axis)
        next_keep[into] = jnp.squeeze(keep[here] + other[here], axis)


def place(order, *jobs):
    axes, masks, cuts, args, outs, plans = [], [], [], [], [], []
    for gather, sizes in jobs:
        olds = [p.shape[-2] for p in gather.parts]
        sizes = sizes or olds
        bits = [sorted(b + [m], reverse=True) for b, m in zip(gather.bits, gather.masks)]
        own_axes = [axis_of(b, m) for b, m in zip(gather.bits, gather.masks)]
        bits = [bits[min(j, len(bits) - 1)] for j in range(len(sizes))]
        found = overlaps(olds, sizes)
        plans.append((gather, olds, sizes, bits, own_axes, len(outs)))
        cuts += [(len(axes) + i, len(outs) + j, x, y) for i, j, x, y in found]
        axes += own_axes
        masks += gather.masks
        for mine, other in zip(gather.parts, gather.others):
            args += [order.turn(mine), other]
        width = gather.parts[0].shape[-1]
        outs += [(bit_shape(b, (r, width)), BF16) for b, r in zip(bits, sizes)]
    if device_count() == GROUPS:
        body = functools.partial(place_kernel, axes, masks, cuts)
        placed = kernel(body, (order.uppers, *args), outs, 0, 24)
        order.done(placed[0])
    for gather, olds, sizes, bits, own_axes, at in plans:
        if device_count() == GROUPS:
            parts = placed[at : at + len(sizes)]
        else:
            held = []
            sides = zip(gather.parts, gather.others, own_axes, gather.masks)
            for mine, other, axis, mask in sides:
                up = upper_half(mask)
                low, high = jnp.where(up, other, mine), jnp.where(up, mine, other)
                held.append(jnp.stack([low, high], axis=axis))
            parts = cut_rows(held, olds, sizes)
        gather.parts, gather.bits = parts, bits


def add(order, *jobs):
    axes, all_masks, cuts, args, outs, plans, count = [], [], [], [], [], [], 0
    for chain, masks, sizes in jobs:
        olds = [p.shape[-2] for p in chain.keeps]
        sizes = sizes or olds
        bits = [chain.bits[min(j, len(olds) - 1)] for j in range(len(sizes))]
        own_axes = [axis_of(b, m) for b, m in zip(bits, masks)]
        left = [[b for b in old if b != m] for old, m in zip(bits, masks)]
        plans.append((chain, masks, olds, sizes, own_axes, left, len(axes)))
        cuts += [(count + i, len(axes) + j, x, y) for i, j, x, y in overlaps(olds, sizes)]
        axes += own_axes
        all_masks += masks
        count += len(olds)
        for keep, other in zip(chain.keeps, chain.others):
            args += [order.turn(keep), other]
        width = chain.keeps[0].shape[-1]
        for b, r in zip(left, sizes):
            outs += [(bit_shape(b, (r, width)), BF16)] * 2
    if device_count() == GROUPS:
        body = functools.partial(add_kernel, axes, all_masks, cuts, count)
        both = kernel(body, (order.uppers, *args), outs, 0, 24)
        order.done(both[0])
    for chain, masks, olds, sizes, own_axes, left, at in plans:
        if device_count() == GROUPS:
            found = both[2 * at : 2 * (at + len(sizes))]
            chain.keeps, chain.sends = found[0::2], found[1::2]
        else:
            sums = [
                (k.astype(F32) + o.astype(F32)).astype(BF16)
                for k, o in zip(chain.keeps, chain.others)
            ]
            sums = cut_rows(sums, olds, sizes)
            sides = list(zip(sums, [upper_half(m) for m in masks], own_axes))
            take = lax.dynamic_index_in_dim
            chain.keeps = [take(t, u, axis, False) for t, u, axis in sides]
            chain.sends = [take(t, 1 - u, axis, False) for t, u, axis in sides]
        chain.bits = left


class Gather:
    def __init__(self, order, *parts):
        self.order, self.parts, self.bits = order, list(parts), [[] for _ in parts]

    def go(self, *masks, wait=False):
        self.masks = masks
        parts = [self.order.turn(p) for p in self.parts] if wait else self.parts
        self.others = [swap(p, m) for p, m in zip(parts, masks)]

    def place(self, *sizes):
        place(self.order, (self, sizes))
        return self

    def whole(self):
        held = self.parts[0]
        return held.reshape((-1,) + held.shape[-2:])


def cut_rows(arrays, olds, sizes):
    if list(olds) == list(sizes):
        return arrays
    joint = jnp.concatenate(arrays, axis=-2)
    ends = [sum(sizes[: j + 1]) for j in range(len(sizes) - 1)]
    return jnp.split(joint, ends, axis=-2)


class Reduce:
    def __init__(self, order, keep, send, bits):
        shape = bit_shape(bits, keep.shape[-2:])
        self.order, self.bits = order, [bits]
        self.keeps, self.sends = [keep.reshape(shape)], [send.reshape(shape)]

    def go(self, *masks, wait=False):
        sends = [self.order.turn(p) for p in self.sends] if wait else self.sends
        self.others = [swap(p, m) for p, m in zip(sends, masks)]

    def add(self, masks, *sizes):
        add(self.order, (self, masks, sizes))
        return self

    def total(self):
        keep, other = self.keeps[0], self.others[0]
        return (keep.astype(F32) + other.astype(F32)).reshape(keep.shape[-2:])


def split_cores(blocks):
    pairs = blocks.reshape((-1, 2) + blocks.shape[1:])
    upper = upper_half(1)
    keep = lax.dynamic_index_in_dim(pairs, upper, 1, keepdims=False)
    return keep, lax.dynamic_index_in_dim(pairs, 1 - upper, 1, keepdims=False)


def joined(keep, send):
    return jnp.stack([keep, send], axis=1).reshape((-1,) + keep.shape[1:])


def grouped(buffer, sizes):
    count = buffer.shape[0]
    if count == GROUPS:
        return buffer
    width = buffer.shape[-1]
    share = width // count
    parts, start = [], 0
    for size in sizes:
        part = buffer[:, start : start + share * size]
        parts.append(part.reshape(GROUPS, UNIT * size, width))
        start += share * size
    return jnp.concatenate(parts, axis=1)


def scattered(buffer, sizes):
    count, width = device_count(), buffer.shape[-1]
    if count == GROUPS:
        return buffer
    parts, start = [], 0
    for size in sizes:
        part = buffer[:, start : start + UNIT * size]
        parts.append(part.reshape(count, width // count * size, width))
        start += UNIT * size
    return jnp.concatenate(parts, axis=1)


def vector_pack(vectors, rows, width):
    filled = jnp.pad(vectors, ((0, 0), (0, width - vectors.shape[1])))
    return jnp.pad(filled[:, None], ((0, 0), (0, rows - 1), (0, 0)))


def vector_regroup(vectors, parts, lengths):
    pieces, start = [], 0
    for length in lengths:
        pieces.append(vectors[:, start : start + length].reshape(parts, -1))
        start += length
    return jnp.concatenate(pieces, axis=1)


def dot(a, b, dims=((1,), (0,))):
    return lax.dot_general(a, b, (dims, ((), ())), preferred_element_type=F32)


def iota(shape, axis):
    return lax.broadcasted_iota(jnp.int32, shape, axis)


def tile(ref, place, size=1):
    rows = ref[:, UNIT * place : UNIT * (place + size), :]
    return rows.reshape(GROUPS * UNIT * size, rows.shape[-1])


def kernel(body, args, outs, flops, limit, scratch=()):
    spec = {jnp.dtype(jnp.int32): pltpu.SMEM}
    return pl.pallas_call(
        body,
        in_specs=[pl.BlockSpec(memory_space=spec.get(a.dtype, pltpu.VMEM)) for a in args],
        out_specs=[pl.BlockSpec(memory_space=pltpu.VMEM) for _ in outs],
        out_shape=[jax.ShapeDtypeStruct(shape, dtype) for shape, dtype in outs],
        scratch_shapes=list(scratch),
        compiler_params=pltpu.CompilerParams(vmem_limit_bytes=limit << 20),
        cost_estimate=pl.CostEstimate(
            flops=flops,
            bytes_accessed=sum(a.size * a.dtype.itemsize for a in args),
            transcendentals=0,
        ),
    )(*args)


def unit_norm(values):
    center = values - jnp.mean(values, axis=-1, keepdims=True)
    spread = jnp.mean(center * center, axis=-1, keepdims=True)
    inverse = lax.rsqrt(spread + EPSILON)
    return center * inverse, inverse


def norm_back(grad, unit, inverse, gain):
    e = grad * gain
    mean_e = jnp.mean(e, axis=-1, keepdims=True)
    mean_x = jnp.mean(e * unit, axis=-1, keepdims=True)
    return inverse * (e - mean_e - unit * mean_x)


def column_sum(values):
    return jnp.sum(values, axis=0, keepdims=True)


def valid_column(info, m, start, rows):
    place = start + iota((rows, 1), 0)
    first = (place >= 1) & (place < info[m, 0])
    second = (place >= info[m, 1]) & (place < info[m, 2])
    return jnp.where(first | second, 1.0, 0.0).astype(F32)


def segment_start(info, m, place):
    start = jnp.where(place >= 1, 1, 0)
    start = jnp.where(place >= info[m, 1], info[m, 1], start)
    return jnp.where(place >= info[m, 3], info[m, 3], start)


VECTORS = 5
BIAS_AT = VECTORS * UNIT


def vector_maps(width):
    lanes = width // 2
    fine = (iota((lanes, width), 0) & 15) == (iota((lanes, width), 1) & 15)
    wide = ((iota((lanes, width), 0) + 48) & 63) == (iota((lanes, width), 1) & 63)
    own_fine = iota((GROUPS, width), 1) >> 4 == iota((GROUPS, width), 0)
    own_wide = iota((GROUPS, width), 1) >> 6 == (iota((GROUPS, width), 0) & 7)
    as_bf16 = [jnp.where(m, 1.0, 0.0).astype(BF16) for m in (fine, wide)]
    as_f32 = [jnp.where(m, 1.0, 0.0).astype(F32) for m in (own_fine, own_wide)]
    return as_bf16 + as_f32


def lane_window(lanes, k):
    place = iota((GROUPS, lanes), 1)
    if k == VECTORS:
        return (place >= BIAS_AT) & (place < BIAS_AT + 64)
    return (place >= UNIT * k) & (place < UNIT * (k + 1))


def window_map(micro, each, tap):
    slots = each // 3
    shape = (micro * slots, micro * (each + RIM))
    row, place = iota(shape, 0), iota(shape, 1)
    m = jnp.zeros(shape, jnp.int32)
    for i in range(1, micro):
        m = m + jnp.where(row >= slots * i, 1, 0)
    source = 3 * (row - slots * m) - 2 + tap
    rim = micro * each + RIM * m + RIM + source
    target = jnp.where(source >= 0, each * m + source, rim)
    return jnp.where(place == target, 1.0, 0.0).astype(BF16)


def keep_and_compress(info, low, weights, kept, window, memory):
    micro = info.shape[0]
    each = low.shape[0] // micro - RIM
    valid = [valid_column(info, m, info[m, 4], each) for m in range(micro)]
    valid += [valid_column(info, m, info[m, 4] - RIM, RIM) for m in range(micro)]
    rows = (dot(low, tile(weights, 0)) * jnp.concatenate(valid, axis=0)).astype(BF16)
    kept[...] = rows
    total = None
    for tap in range(3):
        taken = dot(window_map(micro, each, tap), rows).astype(BF16)
        window[tap] = taken
        part = dot(taken, tile(weights, 1 + tap))
        total = part if total is None else total + part
    memory[...] = total.astype(BF16)


def key_kernel(info, tok, halo, weights, normed, kept, window, memory, vec):
    width = tok.shape[-1]
    lanes = width // 2
    fine, wide, own_fine, own_wide = vector_maps(width)
    rows = jnp.sum(weights[:, 4 * UNIT : 5 * UNIT, :lanes].astype(F32), axis=1)
    picked = [jnp.where(lane_window(lanes, k), rows, 0.0) for k in range(VECTORS + 1)]
    spread = dot(jnp.concatenate(picked[:VECTORS], axis=0).astype(BF16), fine)
    vectors = [
        column_sum(spread[GROUPS * k : GROUPS * (k + 1)] * own_fine) for k in range(VECTORS)
    ]
    bias = dot(picked[VECTORS].astype(BF16), wide) * own_wide
    bias = jnp.sum(bias.reshape(4, 8, width), axis=1)
    vec[...] = jnp.concatenate(vectors + [bias, jnp.zeros((7, width), F32)], axis=0)
    values = jnp.concatenate([tok[...], halo[...]], axis=0).astype(F32)
    unit, _ = unit_norm(values)
    low = (unit * vectors[0] + vectors[1]).astype(BF16)
    normed[...] = low
    keep_and_compress(info, low, weights, kept, window, memory)


def value_kernel(info, normed, weights, query, kept, window, memory):
    low = normed[...]
    keep_and_compress(info, low, weights, kept, window, memory)
    query[...] = dot(low[: query.shape[0]], tile(weights, 4)).astype(BF16)


def stacked(values, lower):
    zero = jnp.zeros_like(values)
    return jnp.concatenate(
        [jnp.where(lower, values, zero), jnp.where(lower, zero, values)], axis=0
    )


def merged(values, lower):
    half = values.shape[0] // 2
    return jnp.where(lower, values[:half], values[half:])


def memory_pair(memory, m, pair, micro):
    slots = memory.shape[1] // micro
    rows = memory[:, slots * m : slots * (m + 1), PAIR * pair : PAIR * (pair + 1)]
    return rows.reshape(memory.shape[0] * slots, PAIR)


def attend_kernel(info, query, keys, values, memory_keys, memory_values, attended, stats):
    micro = info.shape[0]
    count, width = query.shape
    each = count // micro
    slots = memory_keys.shape[0] * memory_keys.shape[1] // micro
    pairs = width // PAIR
    lower = iota((each, PAIR), 1) < HEAD_DIM
    lane = iota((2 * each, 128), 1)
    found = jnp.zeros((2 * each, 128), F32)
    for m in range(micro):
        rows = slice(each * m, each * (m + 1))
        place = info[m, 4] + iota((each, 1), 0)
        start = segment_start(info, m, place)
        end = 3 * iota((each, slots), 1)
        bias = jnp.where((end <= place) & (end >= start), 0.0, MASKED).astype(F32)
        bias = jnp.concatenate([bias, bias], axis=0)
        for pair in range(pairs):
            cols = slice(PAIR * pair, PAIR * (pair + 1))
            key = keys[rows, cols].astype(F32)
            value = values[rows, cols].astype(F32)
            queries = stacked(query[rows, cols].astype(F32) * SCALE, lower)
            own = jnp.sum(queries * jnp.concatenate([key, key], axis=0), axis=1, keepdims=True)
            memory_key = memory_pair(memory_keys, m, pair, micro)
            memory_value = memory_pair(memory_values, m, pair, micro)
            scores = dot(queries.astype(BF16), memory_key, NT) + bias
            top = jnp.maximum(jnp.max(scores, axis=1, keepdims=True), own)
            expos = jnp.exp(scores - top)
            own = jnp.exp(own - top)
            total = jnp.sum(expos, axis=1, keepdims=True) + own
            inverse = 1.0 / total
            mixed = dot(expos.astype(BF16), memory_value) * inverse
            weight = jnp.broadcast_to(own * inverse, mixed.shape)
            attended[rows, cols] = merged(mixed, lower) + merged(weight, lower) * value
            found = jnp.where(lane == m * pairs + pair, top + jnp.log(total), found)
    stats[...] = found


def gelu_parts(hidden):
    falling = jnp.exp(hidden * hidden * -0.5)
    step = 1.0 / (1.0 + (ERF_STEP * 0.7071067811865476) * jnp.abs(hidden))
    tail = 0.5 * ERF_TERMS[0]
    for term in ERF_TERMS[1:]:
        tail = tail * step + 0.5 * term
    tail = tail * step * falling
    return jnp.where(hidden >= 0.0, 1.0 - tail, tail), falling


def even_first(flag, rows, size):
    pairs = rows.reshape(-1, 2, size, rows.shape[-1])
    even, odd = pairs[:, 0], pairs[:, 1]
    halves = [jnp.where(flag == 0, even, odd), jnp.where(flag == 0, odd, even)]
    return jnp.concatenate(halves, axis=0).reshape(rows.shape)


def deal(value, rows, keep, send, blocks, start):
    halves = value.astype(BF16).reshape(2, -1, rows, value.shape[-1])
    keep[blocks, start : start + rows, :] = halves[0]
    send[blocks, start : start + rows, :] = halves[1]


def deal_tile(value, place, keep, send):
    deal(value, UNIT, keep, send, slice(None), UNIT * place)


def feed_kernel(
    info,
    tok,
    cot,
    attended,
    vec,
    rest,
    out,
    grad_mid,
    grad_att,
    keep,
    send,
    vec_grad,
):
    count, width = tok.shape
    wide = 4
    low_att = attended[...].astype(BF16)
    w_out = tile(rest, 0)
    middle = tok[...].astype(F32) + dot(low_att, w_out)
    unit, inverse = unit_norm(middle)
    gain = vec[2:3, :]
    low = (unit * gain + vec[3:4, :]).astype(BF16)
    flag = info[0, 5]
    low_t = even_first(flag, low.T, UNIT)
    cots = cot[...]
    total = middle + vec[4:5, :]
    grad_low = jnp.zeros((count, width), F32)
    bias_rows = []
    eighth = GROUPS // wide
    for c in range(wide):
        w_up = tile(rest, 1 + c)
        down = slice(eighth * c, eighth * (c + 1))
        w_down = rest[down, UNIT * (1 + wide) :, :].reshape(width, width)
        hidden = dot(low, w_up) + vec[5 + c : 6 + c, :]
        share, falling = gelu_parts(hidden)
        slope = share + (0.3989422804014327 * hidden) * falling
        active = (hidden * share).astype(BF16)
        total = total + dot(active, w_down)
        grad_hidden_f = dot(cots, w_down, NT) * slope
        grad_hidden = grad_hidden_f.astype(BF16)
        bias_rows.append(column_sum(grad_hidden.astype(F32)))
        grad_low = grad_low + dot(grad_hidden, w_up, NT)
        deal_tile(dot(low_t, grad_hidden), 1 + c, keep, send)
        where = slice(eighth // 2 * c, eighth // 2 * (c + 1))
        active_t = even_first(flag, active.T, UNIT * wide)
        deal(dot(active_t, cots), UNIT * wide, keep, send, where, UNIT * (1 + wide))
    out[...] = total.astype(BF16)
    cots_f = cots.astype(F32)
    grad_middle = cots_f + norm_back(grad_low, unit, inverse, gain)
    grad_mid[...] = grad_middle
    branch = grad_middle.astype(BF16)
    deal_tile(dot(even_first(flag, low_att.T, UNIT), branch), 0, keep, send)
    grad_att[...] = dot(branch, w_out, NT).astype(BF16)
    rows = [jnp.zeros((2, width), F32), column_sum(grad_low * unit), column_sum(grad_low)]
    rows += [column_sum(cots_f)] + bias_rows + [jnp.zeros((7, width), F32)]
    vec_grad[...] = jnp.concatenate(rows, axis=0)


def memory_turned(flag, memory, m, pair, micro):
    slots = memory.shape[2] // micro
    rows, cols = slice(slots * m, slots * (m + 1)), slice(PAIR * pair, PAIR * (pair + 1))
    halves = [memory[:, pl.ds(at, 1), rows, cols] for at in (flag, 1 - flag)]
    return jnp.concatenate([h.reshape(-1, PAIR) for h in halves], axis=0)


def attend_back_kernel(
    info,
    query,
    keys,
    values,
    memory_keys,
    memory_values,
    attended,
    stats,
    grad_att,
    grad_query,
    key_keep,
    key_send,
    value_keep,
    value_send,
    own_key,
    own_value,
):
    micro = info.shape[0]
    count, width = query.shape
    each = count // micro
    chips = memory_keys.shape[0]
    share = memory_keys.shape[2] // micro
    slots = 2 * chips * share
    flag = info[0, 6]
    pairs = width // PAIR
    lower = iota((each, PAIR), 1) < HEAD_DIM
    lane = iota((2 * each, 128), 1)
    found = stats[...]
    deltas = jnp.zeros((2 * each, 128), F32)
    parts = {}
    for m in range(micro):
        rows = slice(each * m, each * (m + 1))
        for pair in range(pairs):
            cols = slice(PAIR * pair, PAIR * (pair + 1))
            grad = grad_att[rows, cols].astype(F32)
            product = stacked(grad * attended[rows, cols], lower)
            delta = jnp.sum(product, axis=1, keepdims=True)
            deltas = jnp.where(lane == m * pairs + pair, delta, deltas)
            parts[m, pair] = delta
    found_t, deltas_t = found.T, deltas.T
    for m in range(micro):
        rows = slice(each * m, each * (m + 1))
        lanes = iota((1, 2 * each), 1)
        place = info[m, 4] + jnp.where(lanes >= each, lanes - each, lanes)
        start = segment_start(info, m, place)
        row = iota((slots, 1), 0)
        late = row >= chips * share
        row = jnp.where(late, row - chips * share, row)
        block = jnp.zeros((slots, 1), jnp.int32)
        for chip in range(1, chips):
            block = block + jnp.where(row >= share * chip, 1, 0)
        core = jnp.where(late, 1 - flag, flag)
        end = 3 * (row + share * (block + core))
        bias = jnp.where((end <= place) & (end >= start), 0.0, MASKED).astype(F32)
        for pair in range(pairs):
            cols = slice(PAIR * pair, PAIR * (pair + 1))
            at = m * pairs + pair
            key = keys[rows, cols].astype(F32)
            value = values[rows, cols].astype(F32)
            query_f = query[rows, cols].astype(F32) * SCALE
            grad_f = grad_att[rows, cols].astype(F32)
            queries = stacked(query_f, lower)
            grads = stacked(grad_f, lower)
            own = jnp.sum(queries * jnp.concatenate([key, key], axis=0), axis=1, keepdims=True)
            own = jnp.exp(own - found[:, at : at + 1])
            grad_own = jnp.sum(
                grads * jnp.concatenate([value, value], axis=0), axis=1, keepdims=True
            )
            grad_own = (own * (grad_own - parts[m, pair])).astype(BF16).astype(F32)
            queries, grads = queries.astype(BF16), grads.astype(BF16)
            memory_key = memory_turned(flag, memory_keys, m, pair, micro)
            memory_value = memory_turned(flag, memory_values, m, pair, micro)
            scores = dot(memory_key, queries, NT) + bias
            probs = jnp.exp(scores - found_t[at : at + 1, :])
            grad_probs = dot(memory_value, grads, NT)
            grad_scores = (probs * (grad_probs - deltas_t[at : at + 1, :])).astype(BF16)
            sides = (
                (dot(grad_scores, queries), key_keep, key_send),
                (dot(probs.astype(BF16), grads), value_keep, value_send),
            )
            for grad, keep, send in sides:
                halves = grad.astype(BF16).reshape(2, chips, share, PAIR)
                keep[:, share * m : share * (m + 1), cols] = halves[0]
                send[:, share * m : share * (m + 1), cols] = halves[1]
            turned = dot(memory_key.T, grad_scores).T
            own_grad = merged(jnp.broadcast_to(grad_own, (2 * each, PAIR)), lower)
            own_weight = merged(jnp.broadcast_to(own, (2 * each, PAIR)), lower)
            grad_query[rows, cols] = (
                SCALE * (merged(turned, lower) + own_grad * key)
            ).astype(BF16)
            own_key[rows, cols] = own_grad * query_f
            own_value[rows, cols] = own_weight * grad_f


def compress_back_kernel(
    info,
    key_memory,
    value_memory,
    key_window,
    value_window,
    key_weights,
    value_weights,
    normed,
    grad_query,
    key_grad,
    value_grad,
    rims,
    keep,
    send,
):
    micro = info.shape[0]
    count, width = key_grad.shape
    each = count // micro
    flag = info[0, 5]
    places = [window_map(micro, each, tap) for tap in range(3)]
    sides = (
        (key_memory, key_window, key_weights, key_grad),
        (value_memory, value_window, value_weights, value_grad),
    )
    for kind, (memory, window, weights, out) in enumerate(sides):
        grad = memory[...]
        total = None
        for tap in range(3):
            window_t = even_first(flag, window[tap].T, UNIT)
            deal_tile(dot(window_t, grad), 4 * kind + tap, keep, send)
            part = dot(grad, tile(weights, 1 + tap), NT)
            high = part.astype(BF16)
            rest = (part - high.astype(F32)).astype(BF16)
            part = dot(places[tap], high, TN) + dot(places[tap], rest, TN)
            total = part if total is None else total + part
        out[...] = total[:count]
        rims[:, width * kind : width * (kind + 1)] = total[count:]
    low_t = even_first(flag, normed[:count, :].T, UNIT)
    deal_tile(dot(low_t, grad_query[...]), 3, keep, send)


def input_kernel(
    info,
    tok,
    normed,
    grad_query,
    key_grad,
    value_grad,
    rims,
    own_key,
    own_value,
    key_weights,
    value_weights,
    vec,
    grad_mid,
    vec_grad,
    grad_in,
    keep,
    send,
    total,
):
    count, width = tok.shape
    micro = info.shape[0]
    each = count // micro
    valid = [valid_column(info, m, info[m, 4], each) for m in range(micro)]
    valid = jnp.concatenate(valid, axis=0)
    flag = info[0, 5]
    low_t = even_first(flag, normed[:count, :].T, UNIT)
    grad_low = dot(grad_query[...], tile(value_weights, 4), NT)
    sides = ((key_grad, own_key, key_weights), (value_grad, own_value, value_weights))
    for kind, (grad, own, weights) in enumerate(sides):
        total[...] = grad[...] + own[...]
        for m in range(micro):
            rows = slice(each * (m + 1) - RIM, each * (m + 1))
            rim = rims[RIM * m : RIM * (m + 1), width * kind : width * (kind + 1)]
            total[rows, :] = total[rows, :] + rim
        low_grad = (total[...] * valid).astype(BF16)
        grad_low = grad_low + dot(low_grad, tile(weights, 0), NT)
        deal_tile(dot(low_t, low_grad), kind, keep, send)
    unit, inverse = unit_norm(tok[...].astype(F32))
    back = norm_back(grad_low, unit, inverse, vec[0:1, :])
    grad_in[...] = (grad_mid[...] + back).astype(BF16)

    lanes = width // 2
    fine, wide, own_fine, own_wide = vector_maps(width)
    vectors = [column_sum(grad_low * unit), column_sum(grad_low)]
    vectors += [vec_grad[k : k + 1, :] for k in range(2, VECTORS)]
    dealt = jnp.concatenate([own_fine * v for v in vectors], axis=0).astype(BF16)
    dealt = dot(dealt, fine, NT)
    bias = [
        jnp.broadcast_to(vec_grad[VECTORS + c : VECTORS + c + 1, :], (8, width)) for c in range(4)
    ]
    bias = (jnp.concatenate(bias, axis=0) * own_wide).astype(BF16)
    packed = jnp.where(lane_window(lanes, VECTORS), dot(bias, wide, NT), 0.0)
    for k in range(VECTORS):
        packed = jnp.where(lane_window(lanes, k), dealt[GROUPS * k : GROUPS * (k + 1)], packed)
    packed = jnp.concatenate([packed, jnp.zeros((GROUPS, width - lanes), F32)], axis=1)
    spot = iota((GROUPS, UNIT, width), 1) == 0
    spread = jnp.broadcast_to(packed[:, None, :], (GROUPS, UNIT, width))
    packed = jnp.where(spot, spread, 0.0).reshape(GROUPS * UNIT, width)
    deal_tile(even_first(flag, packed, UNIT), 2, keep, send)


def per_device(
    tokens,
    lengths,
    ln1_gain,
    ln1_bias,
    w_query,
    w_key,
    w_value,
    conv_key,
    conv_value,
    w_out,
    ln2_gain,
    ln2_bias,
    w_up,
    b_up,
    w_down,
    b_down,
    cotangent,
):
    count = device_count()
    micro, _, each, width = tokens.shape
    ff = w_up.shape[1]
    wide = ff // width
    share = width // count
    seq = lax.axis_size("seq")
    all_tokens = micro * each
    slots = micro * each // 3
    memory_bytes = 4 * seq * slots * width

    whole = count == GROUPS
    vector_lengths = [share] * VECTORS + [ff // count]
    vectors, start = 0.0, 0
    for part in (ln1_gain, ln1_bias, ln2_gain, ln2_bias, b_down, b_up):
        end = start + part.shape[0]
        pad = ((0, (UNIT if whole else 2) - 1), (start, width - end))
        vectors, start = vectors + jnp.pad(part[None], pad), end
    vectors = vectors.astype(BF16)
    across = powers(seq, count)
    along = powers(2, seq)[::-1]
    back = along[::-1]
    order = Order()
    lengths = lengths[:, 0]
    first_pad = 3 * ((lengths[:, 0] + 2) // 3)
    second_pad = 3 * ((lengths[:, 1] + 2) // 3)
    start = 1 + first_pad
    seats = [lax.axis_index("seq") * each, upper_half(1) if whole else 0, upper_half(1)]
    seats = [jnp.full_like(start, seat) for seat in seats]
    info = [1 + lengths[:, 0], start, start + lengths[:, 1], start + second_pad]
    info = jnp.stack(info + seats, axis=1).astype(jnp.int32)
    first = jnp.concatenate([w_key, *conv_key, vectors], axis=0)
    second = jnp.concatenate([w_value, *conv_value, w_query], axis=0)
    ups = [w_up[:, width * c : width * (c + 1)] for c in range(wide)]
    rest = jnp.concatenate([w_out] + ups + [w_down], axis=0)
    rest_rows = rest.shape[0]
    upper_rows = share * (1 + wide)
    one, two, both = Gather(order, first), Gather(order, second), Gather(order, rest)
    one.go(along[0])
    two.go(back[0])
    last_rows = lax.optimization_barrier((tokens[:, 0, each - RIM :], first))[0]
    halo = lax.ppermute(last_rows, "seq", [(i, i + 1) for i in range(seq - 1)])
    halo = halo.reshape(micro * RIM, width)
    for at in range(1, len(along)):
        one.place()
        one.go(along[at])
        two.place()
        two.go(back[at])
    order.done((halo, info, rest))
    one.place()
    one.go(across[0])
    two.place()
    two.go(across[-1])
    both.go(along[0], wait=True)
    for at in range(1, max(len(across), len(along))):
        jobs = []
        if at < len(across):
            one.place()
            one.go(across[at])
            jobs.append((two, ()))
        if at < len(along):
            jobs.append((both, ()))
        place(order, *jobs)
        if at < len(across):
            two.go(across[-1 - at])
        if at < len(along):
            both.go(along[at])
    one.place()
    one.go(1)
    place(order, (two, ()), (both, (upper_rows, rest_rows - upper_rows)))
    two.go(1)
    both.go(across[0], across[-1])
    first = one.place().whole()
    first_sizes, rest_sizes = [1] * 5, [1] * (1 + wide) + [wide]
    if not whole:
        dealt = vector_regroup(first[:, 4 * share], GROUPS, vector_lengths)
        dealt = vector_pack(dealt, UNIT, width)
        first = jnp.concatenate([grouped(first, [1] * 4), dealt], axis=1)

    tok = tokens.reshape(all_tokens, width)
    cot = cotangent.reshape(all_tokens, width)
    rows = (all_tokens, width)
    grown = 4 * max(memory_bytes // (1 << 20) - 2, 0)
    limits = [16, 16, 16 + grown, 28, 28 + grown, 28, 28]
    matmul = 2 * all_tokens * width * width

    padded = (all_tokens + micro * RIM, width)
    windows = (3, slots, width)

    normed, keys, key_window, memory_key, vec = kernel(
        key_kernel,
        (info, order.turn(tok), halo, first),
        ((padded, BF16), (padded, BF16), (windows, BF16), ((slots, width), BF16), ((16, width), F32)),
        2 * matmul,
        limits[0],
    )
    order.done(memory_key)
    keys_side = Gather(order, memory_key)
    keys_side.go(along[0])
    second = grouped(two.place().whole(), first_sizes)
    query, values, value_window, memory_value = kernel(
        value_kernel,
        (info, normed, second),
        ((rows, BF16), (padded, BF16), (windows, BF16), ((slots, width), BF16)),
        3 * matmul,
        limits[1],
    )
    order.done(memory_value)
    values_side = Gather(order, memory_value)
    values_side.go(back[0])
    for at in range(1, max(len(across), len(along))):
        jobs = []
        if at < len(along):
            keys_side.place()
            keys_side.go(along[at])
            jobs.append((values_side, ()))
        if at < len(across):
            jobs.append((both, ()))
        place(order, *jobs)
        if at < len(along):
            values_side.go(back[at])
        if at < len(across):
            both.go(across[at], across[-1 - at])
    keys_side.place()
    keys_side.go(1)
    place(order, (values_side, ()), (both, (rest_rows,)))
    values_side.go(1)
    both.go(1)
    memories = [keys_side.place().whole(), values_side.place().whole()]
    attended, stats = kernel(
        attend_kernel,
        (info, order.turn(query), keys, values, *memories),
        ((rows, F32), ((2 * each, 128), F32)),
        4 * matmul,
        limits[2],
    )
    order.done(attended)
    rest = grouped(both.place().whole(), rest_sizes)
    half = GROUPS // 2

    def pieces(size):
        return (((half, UNIT * size, width), BF16),) * 2

    output, grad_mid, grad_att, *halves, vec_grad = kernel(
        feed_kernel,
        (info, order.turn(tok), cot, attended, vec, rest),
        ((rows, BF16), (rows, F32), (rows, BF16)) + pieces(1 + 2 * wide) + (((16, width), F32),),
        27 * matmul,
        limits[3],
    )
    order.done(halves[0])
    all_bits = powers(2, count)[::-1]

    def begin(keep, send, size):
        if not whole:
            keep, send = split_cores(scattered(joined(keep, send), size))
        return Reduce(order, keep, send, all_bits)

    feeds = begin(*halves, rest_sizes)
    feeds.go(1)
    memory_half = ((seq // 2, slots, width), BF16)
    chips = (seq // 2, 2, slots, width)
    grad_query, *halves, own_key, own_value = kernel(
        attend_back_kernel,
        (
            info,
            order.turn(query),
            keys,
            values,
            memories[0].reshape(chips),
            memories[1].reshape(chips),
            attended,
            stats,
            grad_att,
        ),
        ((rows, BF16),) + (memory_half,) * 4 + ((rows, F32), (rows, F32)),
        10 * matmul,
        limits[4],
    )
    order.done(grad_query)
    keys_side = Reduce(order, *halves[:2], along)
    values_side = Reduce(order, *halves[2:], along)
    keys_side.go(1)
    values_side.go(1)
    cross = [(across[-1 - at], across[at]) for at in range(len(across))]
    keys_side.add((back[0],))
    keys_side.go(back[0])
    cuts = (upper_rows, rest_rows - upper_rows)
    add(order, (values_side, (along[0],), ()), (feeds, cross[0], cuts))
    values_side.go(along[0])
    feeds.go(*cross[0])
    for at in range(1, max(len(along), len(cross))):
        jobs = []
        if at < len(along):
            keys_side.add((back[at],))
            keys_side.go(back[at])
            jobs.append((values_side, (along[at],), ()))
        if at < len(cross):
            jobs.append((feeds, cross[at], ()))
        add(order, *jobs)
        if at < len(along):
            values_side.go(along[at])
        if at < len(cross):
            feeds.go(*cross[at])
    feeds.add((back[0],), rest_rows)
    key_grad, value_grad = (held.total().astype(BF16) for held in (keys_side, values_side))
    key_kept, value_kept, rims, *halves = kernel(
        compress_back_kernel,
        (
            info,
            order.turn(key_grad),
            value_grad,
            key_window,
            value_window,
            first,
            second,
            normed,
            grad_query,
        ),
        ((rows, F32), (rows, F32), ((micro * RIM, 2 * width), F32)) + pieces(7),
        5 * matmul,
        limits[5],
    )
    order.done(rims)
    rims = lax.ppermute(rims, "seq", [(i + 1, i) for i in range(seq - 1)])
    convs = begin(*halves, [1] * 7)
    convs.go(1)
    grad_in, *halves = kernel(
        input_kernel,
        (
            info,
            order.turn(tok),
            normed,
            grad_query,
            key_kept,
            value_kept,
            rims,
            own_key,
            own_value,
            first,
            second,
            vec,
            grad_mid,
            vec_grad,
        ),
        ((rows, BF16),) + pieces(3),
        6 * matmul,
        limits[6],
        (pltpu.VMEM(rows, F32),),
    )
    order.done(grad_in)
    if whole:
        inputs = begin(*halves, [1] * 3)
    else:
        dealt = joined(*halves)
        vectors = dealt[:, 2 * UNIT, : VECTORS * UNIT + ff // GROUPS]
        vectors = vector_regroup(vectors, count, [UNIT] * VECTORS + [ff // GROUPS])
        dealt = [scattered(dealt, [1] * 2), vector_pack(vectors, 2, width)]
        dealt = split_cores(jnp.concatenate(dealt, axis=1))
        inputs = Reduce(order, *dealt, all_bits)
    inputs.go(1)
    line = [masks[1] for masks in cross]
    cuts = (5 * share, 2 * share)
    convs.add(cross[0], *cuts)
    convs.go(*cross[0])
    feeds.go(back[0])
    inputs.add((line[0],))
    inputs.go(line[0])
    for at in range(1, max(len(along), len(cross))):
        jobs = []
        if at < len(cross):
            jobs.append((convs, cross[at], ()))
        if at < len(along):
            jobs.append((feeds, (back[at],), ()))
        add(order, *jobs)
        if at < len(cross):
            convs.go(*cross[at])
        if at < len(along):
            feeds.go(back[at])
        if at < len(cross):
            inputs.add((line[at],))
            inputs.go(line[at])
    for at in range(len(along)):
        convs.add((back[at],), 7 * share)
        convs.go(back[at])
        inputs.add((along[at],))
        inputs.go(along[at])
    feeds, convs, late_inputs = feeds.total(), convs.total(), inputs.total()
    conv_keys = convs[: 3 * share].reshape(3, share, width)
    conv_values = convs[4 * share :].reshape(3, share, width)

    def own(buffer, number):
        return buffer[share * number : share * (number + 1)]

    vector_row = late_inputs[2 * share]

    def own_vector(number, length=share):
        return vector_row[share * number : share * number + length]

    return (
        output.reshape(tokens.shape),
        grad_in.reshape(tokens.shape),
        own_vector(0),
        own_vector(1),
        own(convs, 3),
        own(late_inputs, 0),
        own(late_inputs, 1),
        conv_keys,
        conv_values,
        own(feeds, 0),
        own_vector(2),
        own_vector(3),
        jnp.concatenate([own(feeds, 1 + c) for c in range(wide)], axis=1),
        own_vector(VECTORS, ff // count),
        feeds[share * (1 + wide) :],
        own_vector(4),
    )


def solution(mesh):
    rows = P(AXES, None)
    vector = P(AXES)
    conv = P(None, AXES, None)
    part = P(None, "batch", "seq", None)
    weights = (vector, vector, rows, rows, rows, conv, conv, rows, vector, vector)
    weights = weights + (rows, vector, rows, vector)
    return jax.shard_map(
        per_device,
        mesh=mesh,
        in_specs=(part, P(None, "batch", None)) + weights + (part,),
        out_specs=(part, part) + weights,
        check_vma=False,
    )
```

```python
import functools

import jax
import jax.numpy as jnp
from jax import lax
from jax.experimental import pallas as pl
from jax.experimental.pallas import tpu as pltpu
from jax.sharding import PartitionSpec as P

HEADS = 8
HEAD_DIM = 64
SCALE = HEAD_DIM ** (-0.5)
EPSILON = 1e-06
AXES = ("batch", "seq")
GROUPS = 32
UNIT = 16
PAIR = 2 * HEAD_DIM
RIM = 8
MASKED = -1e30
F32 = jnp.float32
BF16 = jnp.bfloat16
TN = ((0,), (0,))
NT = ((1,), (1,))
ERF_STEP = 0.3275911
ERF_TERMS = (1.061405429, -1.453152027, 1.421413741, -0.284496736, 0.254829592)


def device_count():
    return lax.axis_size("batch") * lax.axis_size("seq")


def device_index():
    return lax.axis_index("batch") * lax.axis_size("seq") + lax.axis_index("seq")


def powers(low, high):
    masks = []
    while low < high:
        masks.append(low)
        low *= 2
    return masks


def swap(array, mask):
    return lax.ppermute(array, AXES, [(i, i ^ mask) for i in range(device_count())])


def upper_half(mask):
    return ((device_index() & mask) != 0).astype(jnp.int32)


class Order:
    def __init__(self):
        self.last = None
        bits = device_count().bit_length() - 1
        self.uppers = jnp.stack([upper_half(1 << bit) for bit in range(bits)])

    def turn(self, array):
        if self.last is not None:
            array = lax.optimization_barrier((array, self.last))[0]
        return array

    def done(self, array):
        self.last = array


def axis_of(bits, mask):
    return sum(b > mask for b in bits)


def bit_shape(bits, rows):
    return (2,) * len(bits) + tuple(rows)


def at_bit(rank, axis, index, rows):
    where = [slice(None)] * rank
    where[axis] = pl.ds(index, 1)
    where[-2] = rows
    return tuple(where)


def overlaps(lefts, rights):
    found, left_at = [], 0
    for i, left in enumerate(lefts):
        right_at = 0
        for j, right in enumerate(rights):
            low = max(left_at, right_at)
            high = min(left_at + left, right_at + right)
            if low < high:
                found.append(
                    (i, j, slice(low - left_at, high - left_at), slice(low - right_at, high - right_at))
                )
            right_at += right
        left_at += left
    return found


def place_kernel(axes, masks, cuts, uppers, *refs):
    count = len(axes)
    for i, j, inside, outside in cuts:
        mine, other, out = refs[2 * i], refs[2 * i + 1], refs[2 * count + j]
        rank, axis, at = len(out.shape), axes[i], uppers[masks[i].bit_length() - 1]
        source = (slice(None),) * (rank - 3) + (inside, slice(None))
        out[at_bit(rank, axis, at, outside)] = jnp.expand_dims(mine[source], axis)
        out[at_bit(rank, axis, 1 - at, outside)] = jnp.expand_dims(other[source], axis)


def add_kernel(axes, masks, cuts, count, uppers, *refs):
    for i, j, inside, outside in cuts:
        keep, other = refs[2 * i], refs[2 * i + 1]
        next_keep, next_send = refs[2 * count + 2 * j], refs[2 * count + 2 * j + 1]
        rank, axis, at = len(keep.shape), axes[j], uppers[masks[j].bit_length() - 1]
        into = (slice(None),) * (rank - 3) + (outside, slice(None))
        here, there = at_bit(rank, axis, at, inside), at_bit(rank, axis, 1 - at, inside)
        next_send[into] = jnp.squeeze(keep[there] + other[there], axis)
        next_keep[into] = jnp.squeeze(keep[here] + other[here], axis)


def place(order, *jobs):
    axes, masks, cuts, args, outs, plans = [], [], [], [], [], []
    for gather, sizes in jobs:
        olds = [p.shape[-2] for p in gather.parts]
        sizes = sizes or olds
        bits = [sorted(b + [m], reverse=True) for b, m in zip(gather.bits, gather.masks)]
        own_axes = [axis_of(b, m) for b, m in zip(gather.bits, gather.masks)]
        bits = [bits[min(j, len(bits) - 1)] for j in range(len(sizes))]
        found = overlaps(olds, sizes)
        plans.append((gather, olds, sizes, bits, own_axes, len(outs)))
        cuts += [(len(axes) + i, len(outs) + j, x, y) for i, j, x, y in found]
        axes += own_axes
        masks += gather.masks
        for mine, other in zip(gather.parts, gather.others):
            args += [order.turn(mine), other]
        width = gather.parts[0].shape[-1]
        outs += [(bit_shape(b, (r, width)), BF16) for b, r in zip(bits, sizes)]
    if device_count() == GROUPS:
        body = functools.partial(place_kernel, axes, masks, cuts)
        placed = kernel(body, (order.uppers, *args), outs, 0, 24)
        order.done(placed[0])
    for gather, olds, sizes, bits, own_axes, at in plans:
        if device_count() == GROUPS:
            parts = placed[at : at + len(sizes)]
        else:
            held = []
            sides = zip(gather.parts, gather.others, own_axes, gather.masks)
            for mine, other, axis, mask in sides:
                up = upper_half(mask)
                low, high = jnp.where(up, other, mine), jnp.where(up, mine, other)
                held.append(jnp.stack([low, high], axis=axis))
            parts = cut_rows(held, olds, sizes)
        gather.parts, gather.bits = parts, bits


def add(order, *jobs):
    axes, all_masks, cuts, args, outs, plans, count = [], [], [], [], [], [], 0
    for chain, masks, sizes in jobs:
        olds = [p.shape[-2] for p in chain.keeps]
        sizes = sizes or olds
        bits = [chain.bits[min(j, len(olds) - 1)] for j in range(len(sizes))]
        own_axes = [axis_of(b, m) for b, m in zip(bits, masks)]
        left = [[b for b in old if b != m] for old, m in zip(bits, masks)]
        plans.append((chain, masks, olds, sizes, own_axes, left, len(axes)))
        cuts += [(count + i, len(axes) + j, x, y) for i, j, x, y in overlaps(olds, sizes)]
        axes += own_axes
        all_masks += masks
        count += len(olds)
        for keep, other in zip(chain.keeps, chain.others):
            args += [order.turn(keep), other]
        width = chain.keeps[0].shape[-1]
        for b, r in zip(left, sizes):
            outs += [(bit_shape(b, (r, width)), BF16)] * 2
    if device_count() == GROUPS:
        body = functools.partial(add_kernel, axes, all_masks, cuts, count)
        both = kernel(body, (order.uppers, *args), outs, 0, 24)
        order.done(both[0])
    for chain, masks, olds, sizes, own_axes, left, at in plans:
        if device_count() == GROUPS:
            found = both[2 * at : 2 * (at + len(sizes))]
            chain.keeps, chain.sends = found[0::2], found[1::2]
        else:
            sums = [
                (k.astype(F32) + o.astype(F32)).astype(BF16)
                for k, o in zip(chain.keeps, chain.others)
            ]
            sums = cut_rows(sums, olds, sizes)
            sides = list(zip(sums, [upper_half(m) for m in masks], own_axes))
            take = lax.dynamic_index_in_dim
            chain.keeps = [take(t, u, axis, False) for t, u, axis in sides]
            chain.sends = [take(t, 1 - u, axis, False) for t, u, axis in sides]
        chain.bits = left


class Gather:
    def __init__(self, order, *parts):
        self.order, self.parts, self.bits = order, list(parts), [[] for _ in parts]

    def go(self, *masks, wait=False):
        self.masks = masks
        parts = [self.order.turn(p) for p in self.parts] if wait else self.parts
        self.others = [swap(p, m) for p, m in zip(parts, masks)]

    def place(self, *sizes):
        place(self.order, (self, sizes))
        return self

    def whole(self):
        held = self.parts[0]
        return held.reshape((-1,) + held.shape[-2:])


def cut_rows(arrays, olds, sizes):
    if list(olds) == list(sizes):
        return arrays
    joint = jnp.concatenate(arrays, axis=-2)
    ends = [sum(sizes[: j + 1]) for j in range(len(sizes) - 1)]
    return jnp.split(joint, ends, axis=-2)


class Reduce:
    def __init__(self, order, keep, send, bits):
        shape = bit_shape(bits, keep.shape[-2:])
        self.order, self.bits = order, [bits]
        self.keeps, self.sends = [keep.reshape(shape)], [send.reshape(shape)]

    def go(self, *masks, wait=False):
        sends = [self.order.turn(p) for p in self.sends] if wait else self.sends
        self.others = [swap(p, m) for p, m in zip(sends, masks)]

    def add(self, masks, *sizes):
        add(self.order, (self, masks, sizes))
        return self

    def total(self):
        keep, other = self.keeps[0], self.others[0]
        return (keep.astype(F32) + other.astype(F32)).reshape(keep.shape[-2:])


def split_cores(blocks):
    pairs = blocks.reshape((-1, 2) + blocks.shape[1:])
    upper = upper_half(1)
    keep = lax.dynamic_index_in_dim(pairs, upper, 1, keepdims=False)
    return keep, lax.dynamic_index_in_dim(pairs, 1 - upper, 1, keepdims=False)


def joined(keep, send):
    return jnp.stack([keep, send], axis=1).reshape((-1,) + keep.shape[1:])


def grouped(buffer, sizes):
    count = buffer.shape[0]
    if count == GROUPS:
        return buffer
    width = buffer.shape[-1]
    share = width // count
    parts, start = [], 0
    for size in sizes:
        part = buffer[:, start : start + share * size]
        parts.append(part.reshape(GROUPS, UNIT * size, width))
        start += share * size
    return jnp.concatenate(parts, axis=1)


def scattered(buffer, sizes):
    count, width = device_count(), buffer.shape[-1]
    if count == GROUPS:
        return buffer
    parts, start = [], 0
    for size in sizes:
        part = buffer[:, start : start + UNIT * size]
        parts.append(part.reshape(count, width // count * size, width))
        start += UNIT * size
    return jnp.concatenate(parts, axis=1)


def vector_pack(vectors, rows, width):
    filled = jnp.pad(vectors, ((0, 0), (0, width - vectors.shape[1])))
    return jnp.pad(filled[:, None], ((0, 0), (0, rows - 1), (0, 0)))


def vector_regroup(vectors, parts, lengths):
    pieces, start = [], 0
    for length in lengths:
        pieces.append(vectors[:, start : start + length].reshape(parts, -1))
        start += length
    return jnp.concatenate(pieces, axis=1)


def dot(a, b, dims=((1,), (0,))):
    return lax.dot_general(a, b, (dims, ((), ())), preferred_element_type=F32)


def iota(shape, axis):
    return lax.broadcasted_iota(jnp.int32, shape, axis)


def tile(ref, place, size=1):
    rows = ref[:, UNIT * place : UNIT * (place + size), :]
    return rows.reshape(GROUPS * UNIT * size, rows.shape[-1])


def pack_kernel(moves, counts, *refs):
    inputs, outs, sems = refs[: counts[0]], refs[counts[0] : -1], refs[-1]
    copies = []
    for at, (source, where, out, start, rows) in enumerate(moves):
        into = outs[out].at[pl.ds(start, rows)]
        piece = inputs[source] if where is None else inputs[source].at[where]
        copies.append(pltpu.make_async_copy(piece, into, sems.at[at]))
        copies[-1].start()
    for copy in copies:
        copy.wait()


def packed(args, moves, shapes):
    return pl.pallas_call(
        functools.partial(pack_kernel, moves, (len(args),)),
        in_specs=[pl.BlockSpec(memory_space=pltpu.HBM) for _ in args],
        out_specs=[pl.BlockSpec(memory_space=pltpu.VMEM) for _ in shapes],
        out_shape=[jax.ShapeDtypeStruct(shape, BF16) for shape in shapes],
        scratch_shapes=[pltpu.SemaphoreType.DMA((len(moves),))],
        compiler_params=pltpu.CompilerParams(vmem_limit_bytes=62 << 20),
    )(*args)


def kernel(body, args, outs, flops, limit, scratch=()):
    spec = {jnp.dtype(jnp.int32): pltpu.SMEM}
    return pl.pallas_call(
        body,
        in_specs=[pl.BlockSpec(memory_space=spec.get(a.dtype, pltpu.VMEM)) for a in args],
        out_specs=[pl.BlockSpec(memory_space=pltpu.VMEM) for _ in outs],
        out_shape=[jax.ShapeDtypeStruct(shape, dtype) for shape, dtype in outs],
        scratch_shapes=list(scratch),
        compiler_params=pltpu.CompilerParams(vmem_limit_bytes=limit << 20),
        cost_estimate=pl.CostEstimate(
            flops=flops,
            bytes_accessed=sum(a.size * a.dtype.itemsize for a in args),
            transcendentals=0,
        ),
    )(*args)


def unit_norm(values):
    center = values - jnp.mean(values, axis=-1, keepdims=True)
    spread = jnp.mean(center * center, axis=-1, keepdims=True)
    inverse = lax.rsqrt(spread + EPSILON)
    return center * inverse, inverse


def norm_back(grad, unit, inverse, gain):
    e = grad * gain
    mean_e = jnp.mean(e, axis=-1, keepdims=True)
    mean_x = jnp.mean(e * unit, axis=-1, keepdims=True)
    return inverse * (e - mean_e - unit * mean_x)


def column_sum(values):
    return jnp.sum(values, axis=0, keepdims=True)


def valid_column(info, m, start, rows):
    place = start + iota((rows, 1), 0)
    first = (place >= 1) & (place < info[m, 0])
    second = (place >= info[m, 1]) & (place < info[m, 2])
    return jnp.where(first | second, 1.0, 0.0).astype(F32)


def segment_start(info, m, place):
    start = jnp.where(place >= 1, 1, 0)
    start = jnp.where(place >= info[m, 1], info[m, 1], start)
    return jnp.where(place >= info[m, 3], info[m, 3], start)


VECTORS = 5
BIAS_AT = VECTORS * UNIT


def vector_maps(width):
    lanes = width // 2
    fine = (iota((lanes, width), 0) & 15) == (iota((lanes, width), 1) & 15)
    wide = ((iota((lanes, width), 0) + 48) & 63) == (iota((lanes, width), 1) & 63)
    own_fine = iota((GROUPS, width), 1) >> 4 == iota((GROUPS, width), 0)
    own_wide = iota((GROUPS, width), 1) >> 6 == (iota((GROUPS, width), 0) & 7)
    as_bf16 = [jnp.where(m, 1.0, 0.0).astype(BF16) for m in (fine, wide)]
    as_f32 = [jnp.where(m, 1.0, 0.0).astype(F32) for m in (own_fine, own_wide)]
    return as_bf16 + as_f32


def lane_window(lanes, k):
    place = iota((GROUPS, lanes), 1)
    if k == VECTORS:
        return (place >= BIAS_AT) & (place < BIAS_AT + 64)
    return (place >= UNIT * k) & (place < UNIT * (k + 1))


def line_cuts(line):
    micro, cuts = line.shape[:2]
    found = [(m, c) for m in range(micro) for c in range(cuts)]
    return [(m, c, slice(128 * c, 128 * (c + 1))) for m, c in found]


def keep_and_compress(info, low, weights, kept, window, memory, line):
    micro = info.shape[0]
    each = low.shape[0] // micro - RIM
    slots = each // 3
    count = micro * each
    valid = [valid_column(info, m, info[m, 4], each) for m in range(micro)]
    valid += [valid_column(info, m, info[m, 4] - RIM, RIM) for m in range(micro)]
    rows = (dot(low, tile(weights, 0)) * jnp.concatenate(valid, axis=0)).astype(BF16)
    kept[...] = rows[:count]
    rows = rows.astype(F32)
    for m, cut, cols in line_cuts(line):
        line[m, cut, :RIM] = rows[count + RIM * m : count + RIM * (m + 1), cols]
        line[m, cut, RIM:] = rows[each * m : each * (m + 1), cols]
    total = None
    for tap in range(3):
        start = RIM - 2 + tap
        for m, cut, cols in line_cuts(line):
            taken = line[m, cut, pl.ds(start, slots, stride=3), :]
            window[tap, slots * m : slots * (m + 1), cols] = taken.astype(BF16)
        part = dot(window[tap], tile(weights, 1 + tap))
        total = part if total is None else total + part
    memory[...] = total.astype(BF16)


def key_kernel(info, tok, halo, weights, normed, kept, window, memory, vec, line):
    width = tok.shape[-1]
    lanes = width // 2
    fine, wide, own_fine, own_wide = vector_maps(width)
    rows = jnp.sum(weights[:, 4 * UNIT : 5 * UNIT, :lanes].astype(F32), axis=1)
    picked = [jnp.where(lane_window(lanes, k), rows, 0.0) for k in range(VECTORS + 1)]
    spread = dot(jnp.concatenate(picked[:VECTORS], axis=0).astype(BF16), fine)
    vectors = [
        column_sum(spread[GROUPS * k : GROUPS * (k + 1)] * own_fine) for k in range(VECTORS)
    ]
    bias = dot(picked[VECTORS].astype(BF16), wide) * own_wide
    bias = jnp.sum(bias.reshape(4, 8, width), axis=1)
    vec[...] = jnp.concatenate(vectors + [bias, jnp.zeros((7, width), F32)], axis=0)
    values = jnp.concatenate([tok[...], halo[...]], axis=0).astype(F32)
    unit, _ = unit_norm(values)
    low = (unit * vectors[0] + vectors[1]).astype(BF16)
    normed[...] = low
    keep_and_compress(info, low, weights, kept, window, memory, line)


def value_kernel(info, normed, weights, query, kept, window, memory, line):
    low = normed[...]
    keep_and_compress(info, low, weights, kept, window, memory, line)
    query[...] = dot(low[: query.shape[0]], tile(weights, 4)).astype(BF16)


def stacked(values, lower):
    zero = jnp.zeros_like(values)
    return jnp.concatenate(
        [jnp.where(lower, values, zero), jnp.where(lower, zero, values)], axis=0
    )


def merged(values, lower):
    half = values.shape[0] // 2
    return jnp.where(lower, values[:half], values[half:])


def memory_pair(memory, m, pair, micro):
    slots = memory.shape[1] // micro
    rows = memory[:, slots * m : slots * (m + 1), PAIR * pair : PAIR * (pair + 1)]
    return rows.reshape(memory.shape[0] * slots, PAIR)


def attend_kernel(info, query, keys, values, memory_keys, memory_values, attended, stats):
    micro = info.shape[0]
    count, width = query.shape
    each = count // micro
    slots = memory_keys.shape[0] * memory_keys.shape[1] // micro
    pairs = width // PAIR
    lower = iota((each, PAIR), 1) < HEAD_DIM
    lane = iota((2 * each, 128), 1)
    found = jnp.zeros((2 * each, 128), F32)
    for m in range(micro):
        rows = slice(each * m, each * (m + 1))
        place = info[m, 4] + iota((each, 1), 0)
        start = segment_start(info, m, place)
        end = 3 * iota((each, slots), 1)
        bias = jnp.where((end <= place) & (end >= start), 0.0, MASKED).astype(F32)
        bias = jnp.concatenate([bias, bias], axis=0)
        for pair in range(pairs):
            cols = slice(PAIR * pair, PAIR * (pair + 1))
            key = keys[rows, cols].astype(F32)
            value = values[rows, cols].astype(F32)
            queries = stacked(query[rows, cols].astype(F32) * SCALE, lower)
            own = jnp.sum(queries * jnp.concatenate([key, key], axis=0), axis=1, keepdims=True)
            memory_key = memory_pair(memory_keys, m, pair, micro)
            memory_value = memory_pair(memory_values, m, pair, micro)
            scores = dot(queries.astype(BF16), memory_key, NT) + bias
            top = jnp.maximum(jnp.max(scores, axis=1, keepdims=True), own)
            expos = jnp.exp(scores - top)
            own = jnp.exp(own - top)
            total = jnp.sum(expos, axis=1, keepdims=True) + own
            inverse = 1.0 / total
            mixed = dot(expos.astype(BF16), memory_value) * inverse
            weight = jnp.broadcast_to(own * inverse, mixed.shape)
            attended[rows, cols] = merged(mixed, lower) + merged(weight, lower) * value
            found = jnp.where(lane == m * pairs + pair, top + jnp.log(total), found)
    stats[...] = found


def gelu_parts(hidden):
    falling = jnp.exp(hidden * hidden * -0.5)
    step = 1.0 / (1.0 + (ERF_STEP * 0.7071067811865476) * jnp.abs(hidden))
    tail = 0.5 * ERF_TERMS[0]
    for term in ERF_TERMS[1:]:
        tail = tail * step + 0.5 * term
    tail = tail * step * falling
    return jnp.where(hidden >= 0.0, 1.0 - tail, tail), falling


def even_first(flag, rows, size):
    pairs = rows.reshape(-1, 2, size, rows.shape[-1])
    even, odd = pairs[:, 0], pairs[:, 1]
    halves = [jnp.where(flag == 0, even, odd), jnp.where(flag == 0, odd, even)]
    return jnp.concatenate(halves, axis=0).reshape(rows.shape)


def deal(value, rows, keep, send, blocks, start):
    halves = value.astype(BF16).reshape(2, -1, rows, value.shape[-1])
    keep[blocks, start : start + rows, :] = halves[0]
    send[blocks, start : start + rows, :] = halves[1]


def deal_tile(value, place, keep, send):
    deal(value, UNIT, keep, send, slice(None), UNIT * place)


def feed_kernel(
    info,
    tok,
    cot,
    attended,
    vec,
    rest,
    out,
    grad_mid,
    grad_att,
    keep,
    send,
    vec_grad,
):
    count, width = tok.shape
    wide = 4
    low_att = attended[...].astype(BF16)
    w_out = tile(rest, 0)
    middle = tok[...].astype(F32) + dot(low_att, w_out)
    unit, inverse = unit_norm(middle)
    gain = vec[2:3, :]
    low = (unit * gain + vec[3:4, :]).astype(BF16)
    flag = info[0, 5]
    low_t = even_first(flag, low.T, UNIT)
    cots = cot[...]
    total = middle + vec[4:5, :]
    grad_low = jnp.zeros((count, width), F32)
    bias_rows = []
    eighth = GROUPS // wide
    for c in range(wide):
        w_up = tile(rest, 1 + c)
        down = slice(eighth * c, eighth * (c + 1))
        w_down = rest[down, UNIT * (1 + wide) :, :].reshape(width, width)
        hidden = dot(low, w_up) + vec[5 + c : 6 + c, :]
        share, falling = gelu_parts(hidden)
        slope = share + (0.3989422804014327 * hidden) * falling
        active = (hidden * share).astype(BF16)
        total = total + dot(active, w_down)
        grad_hidden_f = dot(cots, w_down, NT) * slope
        grad_hidden = grad_hidden_f.astype(BF16)
        bias_rows.append(column_sum(grad_hidden.astype(F32)))
        grad_low = grad_low + dot(grad_hidden, w_up, NT)
        deal_tile(dot(low_t, grad_hidden), 1 + c, keep, send)
        where = slice(eighth // 2 * c, eighth // 2 * (c + 1))
        active_t = even_first(flag, active.T, UNIT * wide)
        deal(dot(active_t, cots), UNIT * wide, keep, send, where, UNIT * (1 + wide))
    out[...] = total.astype(BF16)
    cots_f = cots.astype(F32)
    grad_middle = cots_f + norm_back(grad_low, unit, inverse, gain)
    grad_mid[...] = grad_middle
    branch = grad_middle.astype(BF16)
    deal_tile(dot(even_first(flag, low_att.T, UNIT), branch), 0, keep, send)
    grad_att[...] = dot(branch, w_out, NT).astype(BF16)
    rows = [jnp.zeros((2, width), F32), column_sum(grad_low * unit), column_sum(grad_low)]
    rows += [column_sum(cots_f)] + bias_rows + [jnp.zeros((7, width), F32)]
    vec_grad[...] = jnp.concatenate(rows, axis=0)


def memory_turned(flag, memory, m, pair, micro):
    slots = memory.shape[2] // micro
    rows, cols = slice(slots * m, slots * (m + 1)), slice(PAIR * pair, PAIR * (pair + 1))
    halves = [memory[:, pl.ds(at, 1), rows, cols] for at in (flag, 1 - flag)]
    return jnp.concatenate([h.reshape(-1, PAIR) for h in halves], axis=0)


def attend_back_kernel(
    info,
    query,
    keys,
    values,
    memory_keys,
    memory_values,
    attended,
    stats,
    grad_att,
    grad_query,
    key_keep,
    key_send,
    value_keep,
    value_send,
    own_key,
    own_value,
):
    micro = info.shape[0]
    count, width = query.shape
    each = count // micro
    chips = memory_keys.shape[0]
    share = memory_keys.shape[2] // micro
    slots = 2 * chips * share
    flag = info[0, 6]
    pairs = width // PAIR
    lower = iota((each, PAIR), 1) < HEAD_DIM
    lane = iota((2 * each, 128), 1)
    found = stats[...]
    deltas = jnp.zeros((2 * each, 128), F32)
    parts = {}
    for m in range(micro):
        rows = slice(each * m, each * (m + 1))
        for pair in range(pairs):
            cols = slice(PAIR * pair, PAIR * (pair + 1))
            grad = grad_att[rows, cols].astype(F32)
            product = stacked(grad * attended[rows, cols], lower)
            delta = jnp.sum(product, axis=1, keepdims=True)
            deltas = jnp.where(lane == m * pairs + pair, delta, deltas)
            parts[m, pair] = delta
    found_t, deltas_t = found.T, deltas.T
    for m in range(micro):
        rows = slice(each * m, each * (m + 1))
        lanes = iota((1, 2 * each), 1)
        place = info[m, 4] + jnp.where(lanes >= each, lanes - each, lanes)
        start = segment_start(info, m, place)
        row = iota((slots, 1), 0)
        late = row >= chips * share
        row = jnp.where(late, row - chips * share, row)
        block = jnp.zeros((slots, 1), jnp.int32)
        for chip in range(1, chips):
            block = block + jnp.where(row >= share * chip, 1, 0)
        core = jnp.where(late, 1 - flag, flag)
        end = 3 * (row + share * (block + core))
        bias = jnp.where((end <= place) & (end >= start), 0.0, MASKED).astype(F32)
        for pair in range(pairs):
            cols = slice(PAIR * pair, PAIR * (pair + 1))
            at = m * pairs + pair
            key = keys[rows, cols].astype(F32)
            value = values[rows, cols].astype(F32)
            query_f = query[rows, cols].astype(F32) * SCALE
            grad_f = grad_att[rows, cols].astype(F32)
            queries = stacked(query_f, lower)
            grads = stacked(grad_f, lower)
            own = jnp.sum(queries * jnp.concatenate([key, key], axis=0), axis=1, keepdims=True)
            own = jnp.exp(own - found[:, at : at + 1])
            grad_own = jnp.sum(
                grads * jnp.concatenate([value, value], axis=0), axis=1, keepdims=True
            )
            grad_own = (own * (grad_own - parts[m, pair])).astype(BF16).astype(F32)
            queries, grads = queries.astype(BF16), grads.astype(BF16)
            memory_key = memory_turned(flag, memory_keys, m, pair, micro)
            memory_value = memory_turned(flag, memory_values, m, pair, micro)
            scores = dot(memory_key, queries, NT) + bias
            probs = jnp.exp(scores - found_t[at : at + 1, :])
            grad_probs = dot(memory_value, grads, NT)
            grad_scores = (probs * (grad_probs - deltas_t[at : at + 1, :])).astype(BF16)
            sides = (
                (dot(grad_scores, queries), key_keep, key_send),
                (dot(probs.astype(BF16), grads), value_keep, value_send),
            )
            for grad, keep, send in sides:
                halves = grad.astype(BF16).reshape(2, chips, share, PAIR)
                keep[:, share * m : share * (m + 1), cols] = halves[0]
                send[:, share * m : share * (m + 1), cols] = halves[1]
            turned = dot(memory_key.T, grad_scores).T
            own_grad = merged(jnp.broadcast_to(grad_own, (2 * each, PAIR)), lower)
            own_weight = merged(jnp.broadcast_to(own, (2 * each, PAIR)), lower)
            grad_query[rows, cols] = (
                SCALE * (merged(turned, lower) + own_grad * key)
            ).astype(BF16)
            own_key[rows, cols] = own_grad * query_f
            own_value[rows, cols] = own_weight * grad_f


def compress_back_kernel(
    info,
    key_memory,
    value_memory,
    key_window,
    value_window,
    key_weights,
    value_weights,
    normed,
    grad_query,
    key_grad,
    value_grad,
    rims,
    keep,
    send,
    line,
):
    micro = info.shape[0]
    count, width = key_grad.shape
    each = count // micro
    flag = info[0, 5]
    own_slots = each // 3
    edge = iota((RIM, width), 0) >= RIM - 2
    sides = (
        (key_memory, key_window, key_weights, key_grad),
        (value_memory, value_window, value_weights, value_grad),
    )
    for kind, (memory, window, weights, out) in enumerate(sides):
        grad = memory[...]
        for tap in range(3):
            window_t = even_first(flag, window[tap].T, UNIT)
            deal_tile(dot(window_t, grad), 4 * kind + tap, keep, send)
            part = dot(grad, tile(weights, 1 + tap), NT)
            for m, cut, cols in line_cuts(line):
                rows = slice(own_slots * m, own_slots * (m + 1))
                line[m, cut, pl.ds(tap, own_slots, stride=3), :] = part[rows, cols]
        for m, cut, cols in line_cuts(line):
            out[each * m : each * (m + 1), cols] = line[m, cut]
        for m in range(micro):
            first = pltpu.roll(out[each * m : each * m + RIM, :], RIM - 2, 0)
            into = (slice(RIM * m, RIM * (m + 1)), slice(width * kind, width * (kind + 1)))
            rims[into] = jnp.where(edge, first, 0.0)
    low_t = even_first(flag, normed[:count, :].T, UNIT)
    deal_tile(dot(low_t, grad_query[...]), 3, keep, send)


def input_kernel(
    info,
    tok,
    normed,
    grad_query,
    key_grad,
    value_grad,
    rims,
    own_key,
    own_value,
    key_weights,
    value_weights,
    vec,
    grad_mid,
    vec_grad,
    grad_in,
    keep,
    send,
    total,
):
    count, width = tok.shape
    micro = info.shape[0]
    each = count // micro
    valid = [valid_column(info, m, info[m, 4], each) for m in range(micro)]
    valid = jnp.concatenate(valid, axis=0)
    flag = info[0, 5]
    low_t = even_first(flag, normed[:count, :].T, UNIT)
    grad_low = dot(grad_query[...], tile(value_weights, 4), NT)
    inner = iota((each, width), 0) < each - 2
    sides = ((key_grad, own_key, key_weights), (value_grad, own_value, value_weights))
    for kind, (grad, own, weights) in enumerate(sides):
        for m in range(micro):
            rows = slice(each * m, each * (m + 1))
            moved = pltpu.roll(grad[rows, :], each - 2, 0)
            total[rows, :] = jnp.where(inner, moved, 0.0) + own[rows, :]
            rows = slice(each * (m + 1) - RIM, each * (m + 1))
            rim = rims[RIM * m : RIM * (m + 1), width * kind : width * (kind + 1)]
            total[rows, :] = total[rows, :] + rim
        low_grad = (total[...] * valid).astype(BF16)
        grad_low = grad_low + dot(low_grad, tile(weights, 0), NT)
        deal_tile(dot(low_t, low_grad), kind, keep, send)
    unit, inverse = unit_norm(tok[...].astype(F32))
    back = norm_back(grad_low, unit, inverse, vec[0:1, :])
    grad_in[...] = (grad_mid[...] + back).astype(BF16)

    lanes = width // 2
    fine, wide, own_fine, own_wide = vector_maps(width)
    vectors = [column_sum(grad_low * unit), column_sum(grad_low)]
    vectors += [vec_grad[k : k + 1, :] for k in range(2, VECTORS)]
    dealt = jnp.concatenate([own_fine * v for v in vectors], axis=0).astype(BF16)
    dealt = dot(dealt, fine, NT)
    bias = [
        jnp.broadcast_to(vec_grad[VECTORS + c : VECTORS + c + 1, :], (8, width)) for c in range(4)
    ]
    bias = (jnp.concatenate(bias, axis=0) * own_wide).astype(BF16)
    packed = jnp.where(lane_window(lanes, VECTORS), dot(bias, wide, NT), 0.0)
    for k in range(VECTORS):
        packed = jnp.where(lane_window(lanes, k), dealt[GROUPS * k : GROUPS * (k + 1)], packed)
    packed = jnp.concatenate([packed, jnp.zeros((GROUPS, width - lanes), F32)], axis=1)
    spot = iota((GROUPS, UNIT, width), 1) == 0
    spread = jnp.broadcast_to(packed[:, None, :], (GROUPS, UNIT, width))
    packed = jnp.where(spot, spread, 0.0).reshape(GROUPS * UNIT, width)
    deal_tile(even_first(flag, packed, UNIT), 2, keep, send)


def per_device(
    tokens,
    lengths,
    ln1_gain,
    ln1_bias,
    w_query,
    w_key,
    w_value,
    conv_key,
    conv_value,
    w_out,
    ln2_gain,
    ln2_bias,
    w_up,
    b_up,
    w_down,
    b_down,
    cotangent,
):
    count = device_count()
    micro, _, each, width = tokens.shape
    ff = w_up.shape[1]
    wide = ff // width
    share = width // count
    seq = lax.axis_size("seq")
    all_tokens = micro * each
    slots = micro * each // 3
    memory_bytes = 4 * seq * slots * width

    whole = count == GROUPS
    vector_lengths = [share] * VECTORS + [ff // count]
    vectors, start = 0.0, 0
    for part in (ln1_gain, ln1_bias, ln2_gain, ln2_bias, b_down, b_up):
        end = start + part.shape[0]
        pad = ((0, (UNIT if whole else 2) - 1), (start, width - end))
        vectors, start = vectors + jnp.pad(part[None], pad), end
    vectors = vectors.astype(BF16)
    across = powers(seq, count)
    along = powers(2, seq)[::-1]
    back = along[::-1]
    order = Order()
    lengths = lengths[:, 0]
    first_pad = 3 * ((lengths[:, 0] + 2) // 3)
    second_pad = 3 * ((lengths[:, 1] + 2) // 3)
    start = 1 + first_pad
    seats = [lax.axis_index("seq") * each, upper_half(1) if whole else 0, upper_half(1)]
    seats = [jnp.full_like(start, seat) for seat in seats]
    info = [1 + lengths[:, 0], start, start + lengths[:, 1], start + second_pad]
    info = jnp.stack(info + seats, axis=1).astype(jnp.int32)
    if whole:
        moves = [(kind, None, kind, 0, UNIT) for kind in range(2)]
        moves += [(2 + k, tap, k, UNIT * (1 + tap), UNIT) for k in range(2) for tap in range(3)]
        moves += [(4 + kind, None, kind, 4 * UNIT, UNIT) for kind in range(2)]
        moves += [(6, None, 2, 0, UNIT)]
        for c in range(wide):
            cols = (slice(None), pl.ds(width * c, width))
            moves.append((7, cols, 2, UNIT * (1 + c), UNIT))
        moves.append((8, None, 2, UNIT * (1 + wide), UNIT * wide))
        rows = (5 * UNIT, 5 * UNIT, (1 + 2 * wide) * UNIT)
        args = (w_key, w_value, conv_key, conv_value, vectors, w_query, w_out, w_up, w_down)
        first, second, rest = packed(args, moves, [(r, width) for r in rows])
    else:
        first = jnp.concatenate([w_key, *conv_key, vectors], axis=0)
        second = jnp.concatenate([w_value, *conv_value, w_query], axis=0)
        ups = [w_up[:, width * c : width * (c + 1)] for c in range(wide)]
        rest = jnp.concatenate([w_out] + ups + [w_down], axis=0)
    rest_rows = rest.shape[0]
    upper_rows = share * (1 + wide)
    one, two, both = Gather(order, first), Gather(order, second), Gather(order, rest)
    one.go(along[0])
    two.go(back[0])
    last_rows = lax.optimization_barrier((tokens[:, 0, each - RIM :], first))[0]
    halo = lax.ppermute(last_rows, "seq", [(i, i + 1) for i in range(seq - 1)])
    halo = halo.reshape(micro * RIM, width)
    for at in range(1, len(along)):
        one.place()
        one.go(along[at])
        two.place()
        two.go(back[at])
    order.done((halo, info, rest))
    one.place()
    one.go(across[0])
    two.place()
    two.go(across[-1])
    both.go(along[0], wait=True)
    for at in range(1, max(len(across), len(along))):
        jobs = []
        if at < len(across):
            one.place()
            one.go(across[at])
            jobs.append((two, ()))
        if at < len(along):
            jobs.append((both, ()))
        place(order, *jobs)
        if at < len(across):
            two.go(across[-1 - at])
        if at < len(along):
            both.go(along[at])
    one.place()
    one.go(1)
    place(order, (two, ()), (both, (upper_rows, rest_rows - upper_rows)))
    two.go(1)
    both.go(across[0], across[-1])
    first = one.place().whole()
    first_sizes, rest_sizes = [1] * 5, [1] * (1 + wide) + [wide]
    if not whole:
        dealt = vector_regroup(first[:, 4 * share], GROUPS, vector_lengths)
        dealt = vector_pack(dealt, UNIT, width)
        first = jnp.concatenate([grouped(first, [1] * 4), dealt], axis=1)

    tok = tokens.reshape(all_tokens, width)
    cot = cotangent.reshape(all_tokens, width)
    rows = (all_tokens, width)
    grown = 4 * max(memory_bytes // (1 << 20) - 2, 0)
    limits = [16, 16, 16 + grown, 28, 28 + grown, 28, 28]
    matmul = 2 * all_tokens * width * width

    padded = (all_tokens + micro * RIM, width)
    windows = (3, slots, width)
    line = (pltpu.VMEM((micro, width // 128, RIM + each, 128), F32),)

    normed, keys, key_window, memory_key, vec = kernel(
        key_kernel,
        (info, order.turn(tok), halo, first),
        ((padded, BF16), (rows, BF16), (windows, BF16), ((slots, width), BF16), ((16, width), F32)),
        2 * matmul,
        limits[0],
        line,
    )
    order.done(memory_key)
    keys_side = Gather(order, memory_key)
    keys_side.go(along[0])
    second = grouped(two.place().whole(), first_sizes)
    query, values, value_window, memory_value = kernel(
        value_kernel,
        (info, normed, second),
        ((rows, BF16), (rows, BF16), (windows, BF16), ((slots, width), BF16)),
        3 * matmul,
        limits[1],
        line,
    )
    order.done(memory_value)
    values_side = Gather(order, memory_value)
    values_side.go(back[0])
    for at in range(1, max(len(across), len(along))):
        jobs = []
        if at < len(along):
            jobs += [(keys_side, ()), (values_side, ())]
        if at < len(across):
            jobs.append((both, ()))
        place(order, *jobs)
        if at < len(along):
            keys_side.go(along[at])
            values_side.go(back[at])
        if at < len(across):
            both.go(across[at], across[-1 - at])
    place(order, (keys_side, ()), (values_side, ()), (both, (rest_rows,)))
    keys_side.go(1)
    values_side.go(1)
    both.go(1)
    memories = [keys_side.place().whole(), values_side.place().whole()]
    attended, stats = kernel(
        attend_kernel,
        (info, order.turn(query), keys, values, *memories),
        ((rows, F32), ((2 * each, 128), F32)),
        4 * matmul,
        limits[2],
    )
    order.done(attended)
    rest = grouped(both.place().whole(), rest_sizes)
    half = GROUPS // 2

    def pieces(size):
        return (((half, UNIT * size, width), BF16),) * 2

    output, grad_mid, grad_att, *halves, vec_grad = kernel(
        feed_kernel,
        (info, order.turn(tok), cot, attended, vec, rest),
        ((rows, BF16), (rows, F32), (rows, BF16)) + pieces(1 + 2 * wide) + (((16, width), F32),),
        27 * matmul,
        limits[3],
    )
    order.done(halves[0])
    all_bits = powers(2, count)[::-1]

    def begin(keep, send, size):
        if not whole:
            keep, send = split_cores(scattered(joined(keep, send), size))
        return Reduce(order, keep, send, all_bits)

    feeds = begin(*halves, rest_sizes)
    feeds.go(1)
    memory_half = ((seq // 2, slots, width), BF16)
    chips = (seq // 2, 2, slots, width)
    grad_query, *halves, own_key, own_value = kernel(
        attend_back_kernel,
        (
            info,
            order.turn(query),
            keys,
            values,
            memories[0].reshape(chips),
            memories[1].reshape(chips),
            attended,
            stats,
            grad_att,
        ),
        ((rows, BF16),) + (memory_half,) * 4 + ((rows, F32), (rows, F32)),
        10 * matmul,
        limits[4],
    )
    order.done(grad_query)
    keys_side = Reduce(order, *halves[:2], along)
    values_side = Reduce(order, *halves[2:], along)
    keys_side.go(1)
    values_side.go(1)
    cross = [(across[-1 - at], across[at]) for at in range(len(across))]
    keys_side.add((back[0],))
    keys_side.go(back[0])
    cuts = (upper_rows, rest_rows - upper_rows)
    add(order, (values_side, (along[0],), ()), (feeds, cross[0], cuts))
    values_side.go(along[0])
    feeds.go(*cross[0])
    for at in range(1, max(len(along), len(cross))):
        jobs = []
        if at < len(along):
            keys_side.add((back[at],))
            keys_side.go(back[at])
            jobs.append((values_side, (along[at],), ()))
        if at < len(cross):
            jobs.append((feeds, cross[at], ()))
        add(order, *jobs)
        if at < len(along):
            values_side.go(along[at])
        if at < len(cross):
            feeds.go(*cross[at])
    feeds.add((back[0],), rest_rows)
    key_grad, value_grad = (held.total().astype(BF16) for held in (keys_side, values_side))
    key_kept, value_kept, rims, *halves = kernel(
        compress_back_kernel,
        (
            info,
            order.turn(key_grad),
            value_grad,
            key_window,
            value_window,
            first,
            second,
            normed,
            grad_query,
        ),
        ((rows, F32), (rows, F32), ((micro * RIM, 2 * width), F32)) + pieces(7),
        5 * matmul,
        limits[5],
        (pltpu.VMEM((micro, width // 128, each, 128), F32),),
    )
    order.done(rims)
    rims = lax.ppermute(rims, "seq", [(i + 1, i) for i in range(seq - 1)])
    convs = begin(*halves, [1] * 7)
    convs.go(1)
    grad_in, *halves = kernel(
        input_kernel,
        (
            info,
            order.turn(tok),
            normed,
            grad_query,
            key_kept,
            value_kept,
            rims,
            own_key,
            own_value,
            first,
            second,
            vec,
            grad_mid,
            vec_grad,
        ),
        ((rows, BF16),) + pieces(3),
        6 * matmul,
        limits[6],
        (pltpu.VMEM(rows, F32),),
    )
    order.done(grad_in)
    if whole:
        inputs = begin(*halves, [1] * 3)
    else:
        dealt = joined(*halves)
        vectors = dealt[:, 2 * UNIT, : VECTORS * UNIT + ff // GROUPS]
        vectors = vector_regroup(vectors, count, [UNIT] * VECTORS + [ff // GROUPS])
        dealt = [scattered(dealt, [1] * 2), vector_pack(vectors, 2, width)]
        dealt = split_cores(jnp.concatenate(dealt, axis=1))
        inputs = Reduce(order, *dealt, all_bits)
    inputs.go(1)
    line = [masks[1] for masks in cross]
    cuts = (5 * share, 2 * share)
    convs.add(cross[0], *cuts)
    convs.go(*cross[0])
    feeds.go(back[0])
    inputs.add((line[0],))
    inputs.go(line[0])
    for at in range(1, max(len(along), len(cross))):
        jobs = []
        if at < len(cross):
            jobs.append((convs, cross[at], ()))
        if at < len(along):
            jobs.append((feeds, (back[at],), ()))
        add(order, *jobs)
        if at < len(cross):
            convs.go(*cross[at])
        if at < len(along):
            feeds.go(back[at])
        if at < len(cross):
            inputs.add((line[at],))
            inputs.go(line[at])
    for at in range(len(along)):
        convs.add((back[at],), 7 * share)
        convs.go(back[at])
        inputs.add((along[at],))
        inputs.go(along[at])
    feeds, convs, late_inputs = feeds.total(), convs.total(), inputs.total()
    conv_keys = convs[: 3 * share].reshape(3, share, width)
    conv_values = convs[4 * share :].reshape(3, share, width)

    def own(buffer, number):
        return buffer[share * number : share * (number + 1)]

    vector_row = late_inputs[2 * share]

    def own_vector(number, length=share):
        return vector_row[share * number : share * number + length]

    return (
        output.reshape(tokens.shape),
        grad_in.reshape(tokens.shape),
        own_vector(0),
        own_vector(1),
        own(convs, 3),
        own(late_inputs, 0),
        own(late_inputs, 1),
        conv_keys,
        conv_values,
        own(feeds, 0),
        own_vector(2),
        own_vector(3),
        jnp.concatenate([own(feeds, 1 + c) for c in range(wide)], axis=1),
        own_vector(VECTORS, ff // count),
        feeds[share * (1 + wide) :],
        own_vector(4),
    )


def solution(mesh):
    rows = P(AXES, None)
    vector = P(AXES)
    conv = P(None, AXES, None)
    part = P(None, "batch", "seq", None)
    weights = (vector, vector, rows, rows, rows, conv, conv, rows, vector, vector)
    weights = weights + (rows, vector, rows, vector)
    return jax.shard_map(
        per_device,
        mesh=mesh,
        in_specs=(part, P(None, "batch", None)) + weights + (part,),
        out_specs=(part, part) + weights,
        check_vma=False,
    )
```

```python
import functools

import jax
import jax.numpy as jnp
from jax import lax
from jax.experimental import pallas as pl
from jax.experimental.pallas import tpu as pltpu
from jax.sharding import PartitionSpec as P

HEADS = 8
HEAD_DIM = 64
SCALE = HEAD_DIM ** (-0.5)
EPSILON = 1e-06
AXES = ("batch", "seq")
GROUPS = 32
UNIT = 16
PAIR = 2 * HEAD_DIM
RIM = 8
MASKED = -1e30
LEAST_ITEM = 501
F32 = jnp.float32
BF16 = jnp.bfloat16
TN = ((0,), (0,))
NT = ((1,), (1,))
ERF_STEP = 0.3275911
ERF_TERMS = (1.061405429, -1.453152027, 1.421413741, -0.284496736, 0.254829592)


def device_count():
    return lax.axis_size("batch") * lax.axis_size("seq")


def device_index():
    return lax.axis_index("batch") * lax.axis_size("seq") + lax.axis_index("seq")


def powers(low, high):
    masks = []
    while low < high:
        masks.append(low)
        low *= 2
    return masks


def swap(array, mask):
    return lax.ppermute(array, AXES, [(i, i ^ mask) for i in range(device_count())])


def upper_half(mask):
    return ((device_index() & mask) != 0).astype(jnp.int32)


class Order:
    def __init__(self):
        self.last = None
        bits = device_count().bit_length() - 1
        self.uppers = jnp.stack([upper_half(1 << bit) for bit in range(bits)])

    def turn(self, array):
        if self.last is not None:
            array = lax.optimization_barrier((array, self.last))[0]
        return array

    def done(self, array):
        self.last = array


def axis_of(bits, mask):
    return sum(b > mask for b in bits)


def bit_shape(bits, rows):
    return (2,) * len(bits) + tuple(rows)


def at_bit(rank, axis, index, rows):
    where = [slice(None)] * rank
    where[axis] = pl.ds(index, 1)
    where[-2] = rows
    return tuple(where)


def overlaps(lefts, rights):
    found, left_at = [], 0
    for i, left in enumerate(lefts):
        right_at = 0
        for j, right in enumerate(rights):
            low = max(left_at, right_at)
            high = min(left_at + left, right_at + right)
            if low < high:
                found.append(
                    (i, j, slice(low - left_at, high - left_at), slice(low - right_at, high - right_at))
                )
            right_at += right
        left_at += left
    return found


def place_kernel(axes, masks, cuts, uppers, *refs):
    count = len(axes)
    for i, j, inside, outside in cuts:
        mine, other, out = refs[2 * i], refs[2 * i + 1], refs[2 * count + j]
        rank, axis, at = len(out.shape), axes[i], uppers[masks[i].bit_length() - 1]
        source = (slice(None),) * (rank - 3) + (inside, slice(None))
        out[at_bit(rank, axis, at, outside)] = jnp.expand_dims(mine[source], axis)
        out[at_bit(rank, axis, 1 - at, outside)] = jnp.expand_dims(other[source], axis)


def add_kernel(axes, masks, cuts, count, uppers, *refs):
    for i, j, inside, outside in cuts:
        keep, other = refs[2 * i], refs[2 * i + 1]
        next_keep, next_send = refs[2 * count + 2 * j], refs[2 * count + 2 * j + 1]
        rank, axis, at = len(keep.shape), axes[j], uppers[masks[j].bit_length() - 1]
        into = (slice(None),) * (rank - 3) + (outside, slice(None))
        here, there = at_bit(rank, axis, at, inside), at_bit(rank, axis, 1 - at, inside)
        next_send[into] = jnp.squeeze(keep[there] + other[there], axis)
        next_keep[into] = jnp.squeeze(keep[here] + other[here], axis)


def place(order, *jobs):
    axes, masks, cuts, args, outs, plans = [], [], [], [], [], []
    for gather, sizes in jobs:
        olds = [p.shape[-2] for p in gather.parts]
        sizes = sizes or olds
        bits = [sorted(b + [m], reverse=True) for b, m in zip(gather.bits, gather.masks)]
        own_axes = [axis_of(b, m) for b, m in zip(gather.bits, gather.masks)]
        bits = [bits[min(j, len(bits) - 1)] for j in range(len(sizes))]
        found = overlaps(olds, sizes)
        plans.append((gather, olds, sizes, bits, own_axes, len(outs)))
        cuts += [(len(axes) + i, len(outs) + j, x, y) for i, j, x, y in found]
        axes += own_axes
        masks += gather.masks
        for mine, other in zip(gather.parts, gather.others):
            args += [order.turn(mine), other]
        width = gather.parts[0].shape[-1]
        outs += [(bit_shape(b, (r, width)), BF16) for b, r in zip(bits, sizes)]
    if device_count() == GROUPS:
        body = functools.partial(place_kernel, axes, masks, cuts)
        placed = kernel(body, (order.uppers, *args), outs, 0, 24)
        order.done(placed[0])
    for gather, olds, sizes, bits, own_axes, at in plans:
        if device_count() == GROUPS:
            parts = placed[at : at + len(sizes)]
        else:
            held = []
            sides = zip(gather.parts, gather.others, own_axes, gather.masks)
            for mine, other, axis, mask in sides:
                up = upper_half(mask)
                low, high = jnp.where(up, other, mine), jnp.where(up, mine, other)
                held.append(jnp.stack([low, high], axis=axis))
            parts = cut_rows(held, olds, sizes)
        gather.parts, gather.bits = parts, bits


def add(order, *jobs):
    axes, all_masks, cuts, args, outs, plans, count = [], [], [], [], [], [], 0
    for chain, masks, sizes in jobs:
        olds = [p.shape[-2] for p in chain.keeps]
        sizes = sizes or olds
        bits = [chain.bits[min(j, len(olds) - 1)] for j in range(len(sizes))]
        own_axes = [axis_of(b, m) for b, m in zip(bits, masks)]
        left = [[b for b in old if b != m] for old, m in zip(bits, masks)]
        plans.append((chain, masks, olds, sizes, own_axes, left, len(axes)))
        cuts += [(count + i, len(axes) + j, x, y) for i, j, x, y in overlaps(olds, sizes)]
        axes += own_axes
        all_masks += masks
        count += len(olds)
        for keep, other in zip(chain.keeps, chain.others):
            args += [order.turn(keep), other]
        width = chain.keeps[0].shape[-1]
        for b, r in zip(left, sizes):
            outs += [(bit_shape(b, (r, width)), BF16)] * 2
    if device_count() == GROUPS:
        body = functools.partial(add_kernel, axes, all_masks, cuts, count)
        both = kernel(body, (order.uppers, *args), outs, 0, 24)
        order.done(both[0])
    for chain, masks, olds, sizes, own_axes, left, at in plans:
        if device_count() == GROUPS:
            found = both[2 * at : 2 * (at + len(sizes))]
            chain.keeps, chain.sends = found[0::2], found[1::2]
        else:
            sums = [
                (k.astype(F32) + o.astype(F32)).astype(BF16)
                for k, o in zip(chain.keeps, chain.others)
            ]
            sums = cut_rows(sums, olds, sizes)
            sides = list(zip(sums, [upper_half(m) for m in masks], own_axes))
            take = lax.dynamic_index_in_dim
            chain.keeps = [take(t, u, axis, False) for t, u, axis in sides]
            chain.sends = [take(t, 1 - u, axis, False) for t, u, axis in sides]
        chain.bits = left


class Gather:
    def __init__(self, order, *parts):
        self.order, self.parts, self.bits = order, list(parts), [[] for _ in parts]

    def go(self, *masks, wait=False):
        self.masks = masks
        parts = [self.order.turn(p) for p in self.parts] if wait else self.parts
        self.others = [swap(p, m) for p, m in zip(parts, masks)]

    def place(self, *sizes):
        place(self.order, (self, sizes))
        return self

    def whole(self):
        held = self.parts[0]
        return held.reshape((-1,) + held.shape[-2:])


def cut_rows(arrays, olds, sizes):
    if list(olds) == list(sizes):
        return arrays
    joint = jnp.concatenate(arrays, axis=-2)
    ends = [sum(sizes[: j + 1]) for j in range(len(sizes) - 1)]
    return jnp.split(joint, ends, axis=-2)


class Reduce:
    def __init__(self, order, keep, send, bits):
        shape = bit_shape(bits, keep.shape[-2:])
        self.order, self.bits = order, [bits]
        self.keeps, self.sends = [keep.reshape(shape)], [send.reshape(shape)]

    def go(self, *masks, wait=False):
        sends = [self.order.turn(p) for p in self.sends] if wait else self.sends
        self.others = [swap(p, m) for p, m in zip(sends, masks)]

    def add(self, masks, *sizes):
        add(self.order, (self, masks, sizes))
        return self

    def total(self):
        keep, other = self.keeps[0], self.others[0]
        return (keep.astype(F32) + other.astype(F32)).reshape(keep.shape[-2:])


def split_cores(blocks):
    pairs = blocks.reshape((-1, 2) + blocks.shape[1:])
    upper = upper_half(1)
    keep = lax.dynamic_index_in_dim(pairs, upper, 1, keepdims=False)
    return keep, lax.dynamic_index_in_dim(pairs, 1 - upper, 1, keepdims=False)


def joined(keep, send):
    return jnp.stack([keep, send], axis=1).reshape((-1,) + keep.shape[1:])


def grouped(buffer, sizes):
    count = buffer.shape[0]
    if count == GROUPS:
        return buffer
    width = buffer.shape[-1]
    share = width // count
    parts, start = [], 0
    for size in sizes:
        part = buffer[:, start : start + share * size]
        parts.append(part.reshape(GROUPS, UNIT * size, width))
        start += share * size
    return jnp.concatenate(parts, axis=1)


def scattered(buffer, sizes):
    count, width = device_count(), buffer.shape[-1]
    if count == GROUPS:
        return buffer
    parts, start = [], 0
    for size in sizes:
        part = buffer[:, start : start + UNIT * size]
        parts.append(part.reshape(count, width // count * size, width))
        start += UNIT * size
    return jnp.concatenate(parts, axis=1)


def vector_pack(vectors, rows, width):
    filled = jnp.pad(vectors, ((0, 0), (0, width - vectors.shape[1])))
    return jnp.pad(filled[:, None], ((0, 0), (0, rows - 1), (0, 0)))


def vector_regroup(vectors, parts, lengths):
    pieces, start = [], 0
    for length in lengths:
        pieces.append(vectors[:, start : start + length].reshape(parts, -1))
        start += length
    return jnp.concatenate(pieces, axis=1)


def dot(a, b, dims=((1,), (0,))):
    return lax.dot_general(a, b, (dims, ((), ())), preferred_element_type=F32)


def iota(shape, axis):
    return lax.broadcasted_iota(jnp.int32, shape, axis)


def tile(ref, place, size=1):
    rows = ref[:, UNIT * place : UNIT * (place + size), :]
    return rows.reshape(GROUPS * UNIT * size, rows.shape[-1])


def pack_kernel(moves, counts, *refs):
    inputs, outs, sems = refs[: counts[0]], refs[counts[0] : -1], refs[-1]
    copies = []
    for at, (source, where, out, start, rows) in enumerate(moves):
        into = outs[out].at[pl.ds(start, rows)]
        piece = inputs[source] if where is None else inputs[source].at[where]
        copies.append(pltpu.make_async_copy(piece, into, sems.at[at]))
        copies[-1].start()
    for copy in copies:
        copy.wait()


def packed(args, moves, shapes):
    return pl.pallas_call(
        functools.partial(pack_kernel, moves, (len(args),)),
        in_specs=[pl.BlockSpec(memory_space=pltpu.HBM) for _ in args],
        out_specs=[pl.BlockSpec(memory_space=pltpu.VMEM) for _ in shapes],
        out_shape=[jax.ShapeDtypeStruct(shape, BF16) for shape in shapes],
        scratch_shapes=[pltpu.SemaphoreType.DMA((len(moves),))],
        compiler_params=pltpu.CompilerParams(vmem_limit_bytes=62 << 20),
    )(*args)


def kernel(body, args, outs, flops, limit, scratch=()):
    spec = {jnp.dtype(jnp.int32): pltpu.SMEM}
    return pl.pallas_call(
        body,
        in_specs=[pl.BlockSpec(memory_space=spec.get(a.dtype, pltpu.VMEM)) for a in args],
        out_specs=[pl.BlockSpec(memory_space=pltpu.VMEM) for _ in outs],
        out_shape=[jax.ShapeDtypeStruct(shape, dtype) for shape, dtype in outs],
        scratch_shapes=list(scratch),
        compiler_params=pltpu.CompilerParams(vmem_limit_bytes=limit << 20),
        cost_estimate=pl.CostEstimate(
            flops=flops,
            bytes_accessed=sum(a.size * a.dtype.itemsize for a in args),
            transcendentals=0,
        ),
    )(*args)


def unit_norm(values):
    center = values - jnp.mean(values, axis=-1, keepdims=True)
    spread = jnp.mean(center * center, axis=-1, keepdims=True)
    inverse = lax.rsqrt(spread + EPSILON)
    return center * inverse, inverse


def norm_back(grad, unit, inverse, gain):
    e = grad * gain
    mean_e = jnp.mean(e, axis=-1, keepdims=True)
    mean_x = jnp.mean(e * unit, axis=-1, keepdims=True)
    return inverse * (e - mean_e - unit * mean_x)


def column_sum(values):
    return jnp.sum(values, axis=0, keepdims=True)


def valid_column(info, m, start, rows):
    place = start + iota((rows, 1), 0)
    first = (place >= 1) & (place < info[m, 0])
    second = (place >= info[m, 1]) & (place < info[m, 2])
    return jnp.where(first | second, 1.0, 0.0).astype(F32)


def segment_start(info, m, place):
    start = jnp.where(place >= 1, 1, 0)
    start = jnp.where(place >= info[m, 1], info[m, 1], start)
    return jnp.where(place >= info[m, 3], info[m, 3], start)


VECTORS = 5
BIAS_AT = VECTORS * UNIT


def vector_maps(width):
    lanes = width // 2
    fine = (iota((lanes, width), 0) & 15) == (iota((lanes, width), 1) & 15)
    wide = ((iota((lanes, width), 0) + 48) & 63) == (iota((lanes, width), 1) & 63)
    own_fine = iota((GROUPS, width), 1) >> 4 == iota((GROUPS, width), 0)
    own_wide = iota((GROUPS, width), 1) >> 6 == (iota((GROUPS, width), 0) & 7)
    as_bf16 = [jnp.where(m, 1.0, 0.0).astype(BF16) for m in (fine, wide)]
    as_f32 = [jnp.where(m, 1.0, 0.0).astype(F32) for m in (own_fine, own_wide)]
    return as_bf16 + as_f32


def lane_window(lanes, k):
    place = iota((GROUPS, lanes), 1)
    if k == VECTORS:
        return (place >= BIAS_AT) & (place < BIAS_AT + 64)
    return (place >= UNIT * k) & (place < UNIT * (k + 1))


def line_cuts(line):
    micro, cuts = line.shape[:2]
    found = [(m, c) for m in range(micro) for c in range(cuts)]
    return [(m, c, slice(128 * c, 128 * (c + 1))) for m, c in found]


def keep_and_compress(info, low, weights, kept, window, memory, line):
    micro = info.shape[0]
    each = low.shape[0] // micro - RIM
    slots = each // 3
    count = micro * each
    valid = [valid_column(info, m, info[m, 4], each) for m in range(micro)]
    valid += [valid_column(info, m, info[m, 4] - RIM, RIM) for m in range(micro)]
    rows = (dot(low, tile(weights, 0)) * jnp.concatenate(valid, axis=0)).astype(BF16)
    kept[...] = rows[:count]
    rows = rows.astype(F32)
    for m, cut, cols in line_cuts(line):
        line[m, cut, :RIM] = rows[count + RIM * m : count + RIM * (m + 1), cols]
        line[m, cut, RIM:] = rows[each * m : each * (m + 1), cols]
    total = None
    for tap in range(3):
        start = RIM - 2 + tap
        for m, cut, cols in line_cuts(line):
            taken = line[m, cut, pl.ds(start, slots, stride=3), :]
            window[tap, slots * m : slots * (m + 1), cols] = taken.astype(BF16)
        part = dot(window[tap], tile(weights, 1 + tap))
        total = part if total is None else total + part
    memory[...] = total.astype(BF16)


def key_kernel(info, tok, halo, weights, normed, kept, window, memory, vec, line):
    width = tok.shape[-1]
    lanes = width // 2
    fine, wide, own_fine, own_wide = vector_maps(width)
    rows = jnp.sum(weights[:, 4 * UNIT : 5 * UNIT, :lanes].astype(F32), axis=1)
    picked = [jnp.where(lane_window(lanes, k), rows, 0.0) for k in range(VECTORS + 1)]
    spread = dot(jnp.concatenate(picked[:VECTORS], axis=0).astype(BF16), fine)
    vectors = [
        column_sum(spread[GROUPS * k : GROUPS * (k + 1)] * own_fine) for k in range(VECTORS)
    ]
    bias = dot(picked[VECTORS].astype(BF16), wide) * own_wide
    bias = jnp.sum(bias.reshape(4, 8, width), axis=1)
    vec[...] = jnp.concatenate(vectors + [bias, jnp.zeros((7, width), F32)], axis=0)
    values = jnp.concatenate([tok[...], halo[...]], axis=0).astype(F32)
    unit, _ = unit_norm(values)
    low = (unit * vectors[0] + vectors[1]).astype(BF16)
    normed[...] = low
    keep_and_compress(info, low, weights, kept, window, memory, line)


def value_kernel(info, normed, weights, query, kept, window, memory, line):
    low = normed[...]
    keep_and_compress(info, low, weights, kept, window, memory, line)
    query[...] = dot(low[: query.shape[0]], tile(weights, 4)).astype(BF16)


def stacked(values, lower):
    zero = jnp.zeros_like(values)
    return jnp.concatenate(
        [jnp.where(lower, values, zero), jnp.where(lower, zero, values)], axis=0
    )


def merged(values, lower):
    half = values.shape[0] // 2
    return jnp.where(lower, values[:half], values[half:])


def reach(blocks, each):
    row = blocks * each
    size = (row - 2 - LEAST_ITEM) // each + 1
    size = min(size + size % 2, blocks)
    skipped = (LEAST_ITEM + 3) // 3 // (each // 3)
    return size if blocks - size <= skipped else blocks


def memory_pair(memory, first, size, m, pair, micro):
    slots = memory.shape[1] // micro
    rows, cols = slice(slots * m, slots * (m + 1)), slice(PAIR * pair, PAIR * (pair + 1))
    return memory[pl.ds(first, size), rows, cols].reshape(size * slots, PAIR)


def attend_kernel(info, query, keys, values, memory_keys, memory_values, attended, stats):
    micro = info.shape[0]
    count, width = query.shape
    each = count // micro
    blocks, share = memory_keys.shape[0], memory_keys.shape[1] // micro
    size = reach(blocks, each)
    slots = size * share
    pairs = width // PAIR
    lower = iota((each, PAIR), 1) < HEAD_DIM
    lane = iota((2 * each, 128), 1)
    found = jnp.zeros((2 * each, 128), F32)
    for m in range(micro):
        rows = slice(each * m, each * (m + 1))
        place = info[m, 4] + iota((each, 1), 0)
        start = segment_start(info, m, place)
        begin = jnp.where(info[m, 4] < info[m, 1], 0, blocks - size)
        end = 3 * (share * begin + iota((each, slots), 1))
        bias = jnp.where((end <= place) & (end >= start), 0.0, MASKED).astype(F32)
        bias = jnp.concatenate([bias, bias], axis=0)
        for pair in range(pairs):
            cols = slice(PAIR * pair, PAIR * (pair + 1))
            key = keys[rows, cols].astype(F32)
            value = values[rows, cols].astype(F32)
            queries = stacked(query[rows, cols].astype(F32) * SCALE, lower)
            own = jnp.sum(queries * jnp.concatenate([key, key], axis=0), axis=1, keepdims=True)
            memory_key = memory_pair(memory_keys, begin, size, m, pair, micro)
            memory_value = memory_pair(memory_values, begin, size, m, pair, micro)
            scores = dot(queries.astype(BF16), memory_key, NT) + bias
            top = jnp.maximum(jnp.max(scores, axis=1, keepdims=True), own)
            expos = jnp.exp(scores - top)
            own = jnp.exp(own - top)
            total = jnp.sum(expos, axis=1, keepdims=True) + own
            inverse = 1.0 / total
            mixed = dot(expos.astype(BF16), memory_value) * inverse
            weight = jnp.broadcast_to(own * inverse, mixed.shape)
            attended[rows, cols] = merged(mixed, lower) + merged(weight, lower) * value
            found = jnp.where(lane == m * pairs + pair, top + jnp.log(total), found)
    stats[...] = found


def gelu_parts(hidden):
    falling = jnp.exp(hidden * hidden * -0.5)
    step = 1.0 / (1.0 + (ERF_STEP * 0.7071067811865476) * jnp.abs(hidden))
    tail = 0.5 * ERF_TERMS[0]
    for term in ERF_TERMS[1:]:
        tail = tail * step + 0.5 * term
    tail = tail * step * falling
    return jnp.where(hidden >= 0.0, 1.0 - tail, tail), falling


def even_first(flag, rows, size):
    pairs = rows.reshape(-1, 2, size, rows.shape[-1])
    even, odd = pairs[:, 0], pairs[:, 1]
    halves = [jnp.where(flag == 0, even, odd), jnp.where(flag == 0, odd, even)]
    return jnp.concatenate(halves, axis=0).reshape(rows.shape)


def deal(value, rows, keep, send, blocks, start):
    halves = value.astype(BF16).reshape(2, -1, rows, value.shape[-1])
    keep[blocks, start : start + rows, :] = halves[0]
    send[blocks, start : start + rows, :] = halves[1]


def deal_tile(value, place, keep, send):
    deal(value, UNIT, keep, send, slice(None), UNIT * place)


def feed_kernel(
    info,
    tok,
    cot,
    attended,
    vec,
    rest,
    out,
    grad_mid,
    grad_att,
    keep,
    send,
    vec_grad,
):
    count, width = tok.shape
    wide = 4
    low_att = attended[...].astype(BF16)
    w_out = tile(rest, 0)
    middle = tok[...].astype(F32) + dot(low_att, w_out)
    unit, inverse = unit_norm(middle)
    gain = vec[2:3, :]
    low = (unit * gain + vec[3:4, :]).astype(BF16)
    flag = info[0, 5]
    low_t = even_first(flag, low.T, UNIT)
    cots = cot[...]
    total = middle + vec[4:5, :]
    grad_low = jnp.zeros((count, width), F32)
    bias_rows = []
    eighth = GROUPS // wide
    for c in range(wide):
        w_up = tile(rest, 1 + c)
        down = slice(eighth * c, eighth * (c + 1))
        w_down = rest[down, UNIT * (1 + wide) :, :].reshape(width, width)
        hidden = dot(low, w_up) + vec[5 + c : 6 + c, :]
        share, falling = gelu_parts(hidden)
        slope = share + (0.3989422804014327 * hidden) * falling
        active = (hidden * share).astype(BF16)
        total = total + dot(active, w_down)
        grad_hidden_f = dot(cots, w_down, NT) * slope
        grad_hidden = grad_hidden_f.astype(BF16)
        bias_rows.append(column_sum(grad_hidden.astype(F32)))
        grad_low = grad_low + dot(grad_hidden, w_up, NT)
        deal_tile(dot(low_t, grad_hidden), 1 + c, keep, send)
        where = slice(eighth // 2 * c, eighth // 2 * (c + 1))
        active_t = even_first(flag, active.T, UNIT * wide)
        deal(dot(active_t, cots), UNIT * wide, keep, send, where, UNIT * (1 + wide))
    out[...] = total.astype(BF16)
    cots_f = cots.astype(F32)
    grad_middle = cots_f + norm_back(grad_low, unit, inverse, gain)
    grad_mid[...] = grad_middle
    branch = grad_middle.astype(BF16)
    deal_tile(dot(even_first(flag, low_att.T, UNIT), branch), 0, keep, send)
    grad_att[...] = dot(branch, w_out, NT).astype(BF16)
    rows = [jnp.zeros((2, width), F32), column_sum(grad_low * unit), column_sum(grad_low)]
    rows += [column_sum(cots_f)] + bias_rows + [jnp.zeros((7, width), F32)]
    vec_grad[...] = jnp.concatenate(rows, axis=0)


def memory_turned(flag, memory, first, size, m, pair, micro):
    slots = memory.shape[2] // micro
    rows, cols = slice(slots * m, slots * (m + 1)), slice(PAIR * pair, PAIR * (pair + 1))
    halves = [memory[pl.ds(first, size), pl.ds(at, 1), rows, cols] for at in (flag, 1 - flag)]
    return jnp.concatenate([h.reshape(-1, PAIR) for h in halves], axis=0)


def attend_back_kernel(
    info,
    query,
    keys,
    values,
    memory_keys,
    memory_values,
    attended,
    stats,
    grad_att,
    grad_query,
    key_keep,
    key_send,
    value_keep,
    value_send,
    own_key,
    own_value,
):
    micro = info.shape[0]
    count, width = query.shape
    each = count // micro
    chips = memory_keys.shape[0]
    share = memory_keys.shape[2] // micro
    size = reach(2 * chips, each) // 2
    slots = 2 * size * share
    flag = info[0, 6]
    pairs = width // PAIR
    lower = iota((each, PAIR), 1) < HEAD_DIM
    lane = iota((2 * each, 128), 1)
    found = stats[...]
    deltas = jnp.zeros((2 * each, 128), F32)
    parts = {}
    for m in range(micro):
        rows = slice(each * m, each * (m + 1))
        for pair in range(pairs):
            cols = slice(PAIR * pair, PAIR * (pair + 1))
            grad = grad_att[rows, cols].astype(F32)
            product = stacked(grad * attended[rows, cols], lower)
            delta = jnp.sum(product, axis=1, keepdims=True)
            deltas = jnp.where(lane == m * pairs + pair, delta, deltas)
            parts[m, pair] = delta
    found_t, deltas_t = found.T, deltas.T
    for m in range(micro):
        rows = slice(each * m, each * (m + 1))
        lanes = iota((1, 2 * each), 1)
        place = info[m, 4] + jnp.where(lanes >= each, lanes - each, lanes)
        start = segment_start(info, m, place)
        row = iota((slots, 1), 0)
        late = row >= size * share
        row = jnp.where(late, row - size * share, row)
        front = info[m, 4] < info[m, 1]
        begin = jnp.where(front, 0, chips - size)
        block = jnp.zeros((slots, 1), jnp.int32) + 2 * begin
        for chip in range(1, size):
            block = block + jnp.where(row >= share * chip, 1, 0)
        core = jnp.where(late, 1 - flag, flag)
        end = 3 * (row + share * (block + core))
        bias = jnp.where((end <= place) & (end >= start), 0.0, MASKED).astype(F32)
        if size < chips:
            empty = pl.ds(jnp.where(front, size, 0), chips - size)
            zeros = jnp.zeros((chips - size, share, width), BF16)
            for half in (key_keep, key_send, value_keep, value_send):
                half[empty, share * m : share * (m + 1), :] = zeros
        for pair in range(pairs):
            cols = slice(PAIR * pair, PAIR * (pair + 1))
            at = m * pairs + pair
            key = keys[rows, cols].astype(F32)
            value = values[rows, cols].astype(F32)
            query_f = query[rows, cols].astype(F32) * SCALE
            grad_f = grad_att[rows, cols].astype(F32)
            queries = stacked(query_f, lower)
            grads = stacked(grad_f, lower)
            own = jnp.sum(queries * jnp.concatenate([key, key], axis=0), axis=1, keepdims=True)
            own = jnp.exp(own - found[:, at : at + 1])
            grad_own = jnp.sum(
                grads * jnp.concatenate([value, value], axis=0), axis=1, keepdims=True
            )
            grad_own = (own * (grad_own - parts[m, pair])).astype(BF16).astype(F32)
            queries, grads = queries.astype(BF16), grads.astype(BF16)
            memory_key = memory_turned(flag, memory_keys, begin, size, m, pair, micro)
            memory_value = memory_turned(flag, memory_values, begin, size, m, pair, micro)
            scores = dot(memory_key, queries, NT) + bias
            probs = jnp.exp(scores - found_t[at : at + 1, :])
            grad_probs = dot(memory_value, grads, NT)
            grad_scores = (probs * (grad_probs - deltas_t[at : at + 1, :])).astype(BF16)
            sides = (
                (dot(grad_scores, queries), key_keep, key_send),
                (dot(probs.astype(BF16), grads), value_keep, value_send),
            )
            for grad, keep, send in sides:
                halves = grad.astype(BF16).reshape(2, size, share, PAIR)
                into = (pl.ds(begin, size), slice(share * m, share * (m + 1)), cols)
                keep[into] = halves[0]
                send[into] = halves[1]
            turned = dot(memory_key.T, grad_scores).T
            own_grad = merged(jnp.broadcast_to(grad_own, (2 * each, PAIR)), lower)
            own_weight = merged(jnp.broadcast_to(own, (2 * each, PAIR)), lower)
            grad_query[rows, cols] = (
                SCALE * (merged(turned, lower) + own_grad * key)
            ).astype(BF16)
            own_key[rows, cols] = own_grad * query_f
            own_value[rows, cols] = own_weight * grad_f


def compress_back_kernel(
    info,
    key_memory,
    value_memory,
    key_window,
    value_window,
    key_weights,
    value_weights,
    normed,
    grad_query,
    key_grad,
    value_grad,
    rims,
    keep,
    send,
    line,
):
    micro = info.shape[0]
    count, width = key_grad.shape
    each = count // micro
    flag = info[0, 5]
    own_slots = each // 3
    edge = iota((RIM, width), 0) >= RIM - 2
    sides = (
        (key_memory, key_window, key_weights, key_grad),
        (value_memory, value_window, value_weights, value_grad),
    )
    for kind, (memory, window, weights, out) in enumerate(sides):
        grad = memory[...]
        for tap in range(3):
            window_t = even_first(flag, window[tap].T, UNIT)
            deal_tile(dot(window_t, grad), 4 * kind + tap, keep, send)
            part = dot(grad, tile(weights, 1 + tap), NT)
            for m, cut, cols in line_cuts(line):
                rows = slice(own_slots * m, own_slots * (m + 1))
                line[m, cut, pl.ds(tap, own_slots, stride=3), :] = part[rows, cols]
        for m, cut, cols in line_cuts(line):
            out[each * m : each * (m + 1), cols] = line[m, cut]
        for m in range(micro):
            first = pltpu.roll(out[each * m : each * m + RIM, :], RIM - 2, 0)
            into = (slice(RIM * m, RIM * (m + 1)), slice(width * kind, width * (kind + 1)))
            rims[into] = jnp.where(edge, first, 0.0)
    low_t = even_first(flag, normed[:count, :].T, UNIT)
    deal_tile(dot(low_t, grad_query[...]), 3, keep, send)


def input_kernel(
    info,
    tok,
    normed,
    grad_query,
    key_grad,
    value_grad,
    rims,
    own_key,
    own_value,
    key_weights,
    value_weights,
    vec,
    grad_mid,
    vec_grad,
    grad_in,
    keep,
    send,
    total,
):
    count, width = tok.shape
    micro = info.shape[0]
    each = count // micro
    valid = [valid_column(info, m, info[m, 4], each) for m in range(micro)]
    valid = jnp.concatenate(valid, axis=0)
    flag = info[0, 5]
    low_t = even_first(flag, normed[:count, :].T, UNIT)
    grad_low = dot(grad_query[...], tile(value_weights, 4), NT)
    inner = iota((each, width), 0) < each - 2
    sides = ((key_grad, own_key, key_weights), (value_grad, own_value, value_weights))
    for kind, (grad, own, weights) in enumerate(sides):
        for m in range(micro):
            rows = slice(each * m, each * (m + 1))
            moved = pltpu.roll(grad[rows, :], each - 2, 0)
            total[rows, :] = jnp.where(inner, moved, 0.0) + own[rows, :]
            rows = slice(each * (m + 1) - RIM, each * (m + 1))
            rim = rims[RIM * m : RIM * (m + 1), width * kind : width * (kind + 1)]
            total[rows, :] = total[rows, :] + rim
        low_grad = (total[...] * valid).astype(BF16)
        grad_low = grad_low + dot(low_grad, tile(weights, 0), NT)
        deal_tile(dot(low_t, low_grad), kind, keep, send)
    unit, inverse = unit_norm(tok[...].astype(F32))
    back = norm_back(grad_low, unit, inverse, vec[0:1, :])
    grad_in[...] = (grad_mid[...] + back).astype(BF16)

    lanes = width // 2
    fine, wide, own_fine, own_wide = vector_maps(width)
    vectors = [column_sum(grad_low * unit), column_sum(grad_low)]
    vectors += [vec_grad[k : k + 1, :] for k in range(2, VECTORS)]
    dealt = jnp.concatenate([own_fine * v for v in vectors], axis=0).astype(BF16)
    dealt = dot(dealt, fine, NT)
    bias = [
        jnp.broadcast_to(vec_grad[VECTORS + c : VECTORS + c + 1, :], (8, width)) for c in range(4)
    ]
    bias = (jnp.concatenate(bias, axis=0) * own_wide).astype(BF16)
    packed = jnp.where(lane_window(lanes, VECTORS), dot(bias, wide, NT), 0.0)
    for k in range(VECTORS):
        packed = jnp.where(lane_window(lanes, k), dealt[GROUPS * k : GROUPS * (k + 1)], packed)
    packed = jnp.concatenate([packed, jnp.zeros((GROUPS, width - lanes), F32)], axis=1)
    spot = iota((GROUPS, UNIT, width), 1) == 0
    spread = jnp.broadcast_to(packed[:, None, :], (GROUPS, UNIT, width))
    packed = jnp.where(spot, spread, 0.0).reshape(GROUPS * UNIT, width)
    deal_tile(even_first(flag, packed, UNIT), 2, keep, send)


def per_device(
    tokens,
    lengths,
    ln1_gain,
    ln1_bias,
    w_query,
    w_key,
    w_value,
    conv_key,
    conv_value,
    w_out,
    ln2_gain,
    ln2_bias,
    w_up,
    b_up,
    w_down,
    b_down,
    cotangent,
):
    count = device_count()
    micro, _, each, width = tokens.shape
    ff = w_up.shape[1]
    wide = ff // width
    share = width // count
    seq = lax.axis_size("seq")
    all_tokens = micro * each
    slots = micro * each // 3
    memory_bytes = 4 * seq * slots * width

    whole = count == GROUPS
    vector_lengths = [share] * VECTORS + [ff // count]
    vectors, start = 0.0, 0
    for part in (ln1_gain, ln1_bias, ln2_gain, ln2_bias, b_down, b_up):
        end = start + part.shape[0]
        pad = ((0, (UNIT if whole else 2) - 1), (start, width - end))
        vectors, start = vectors + jnp.pad(part[None], pad), end
    vectors = vectors.astype(BF16)
    across = powers(seq, count)
    along = powers(2, seq)[::-1]
    back = along[::-1]
    order = Order()
    if whole:
        moves = [(kind, None, kind, 0, UNIT) for kind in range(2)]
        moves += [(2 + k, tap, k, UNIT * (1 + tap), UNIT) for k in range(2) for tap in range(3)]
        moves += [(4 + kind, None, kind, 4 * UNIT, UNIT) for kind in range(2)]
        moves += [(6, None, 2, 0, UNIT)]
        for c in range(wide):
            cols = (slice(None), pl.ds(width * c, width))
            moves.append((7, cols, 2, UNIT * (1 + c), UNIT))
        moves.append((8, None, 2, UNIT * (1 + wide), UNIT * wide))
        rows = (5 * UNIT, 5 * UNIT, (1 + 2 * wide) * UNIT)
        args = (w_key, w_value, conv_key, conv_value, vectors, w_query, w_out, w_up, w_down)
        first, second, rest = packed(args, moves, [(r, width) for r in rows])
    else:
        first = jnp.concatenate([w_key, *conv_key, vectors], axis=0)
        second = jnp.concatenate([w_value, *conv_value, w_query], axis=0)
        ups = [w_up[:, width * c : width * (c + 1)] for c in range(wide)]
        rest = jnp.concatenate([w_out] + ups + [w_down], axis=0)
    rest_rows = rest.shape[0]
    upper_rows = share * (1 + wide)
    one, two, both = Gather(order, first), Gather(order, second), Gather(order, rest)
    one.go(along[0])
    two.go(back[0])
    last_rows = lax.optimization_barrier((tokens[:, 0, each - RIM :], first))[0]
    halo = lax.ppermute(last_rows, "seq", [(i, i + 1) for i in range(seq - 1)])
    halo = halo.reshape(micro * RIM, width)
    for at in range(1, len(along)):
        one.place()
        if at == 1:
            lengths = order.turn(lengths[:, 0])
            first_pad = 3 * ((lengths[:, 0] + 2) // 3)
            second_pad = 3 * ((lengths[:, 1] + 2) // 3)
            start = 1 + first_pad
            seats = [lax.axis_index("seq") * each, upper_half(1) if whole else 0, upper_half(1)]
            seats = [jnp.full_like(start, seat) for seat in seats]
            info = [1 + lengths[:, 0], start, start + lengths[:, 1], start + second_pad]
            info = jnp.stack(info + seats, axis=1).astype(jnp.int32)
        one.go(along[at])
        two.place()
        two.go(back[at])
    order.done((halo, info, rest))
    one.place()
    one.go(across[0])
    two.place()
    two.go(across[-1])
    both.go(along[0], wait=True)
    for at in range(1, max(len(across), len(along))):
        jobs = []
        if at < len(across):
            one.place()
            one.go(across[at])
            jobs.append((two, ()))
        if at < len(along):
            jobs.append((both, ()))
        place(order, *jobs)
        if at < len(across):
            two.go(across[-1 - at])
        if at < len(along):
            both.go(along[at])
    one.place()
    one.go(1)
    place(order, (two, ()), (both, (upper_rows, rest_rows - upper_rows)))
    two.go(1)
    both.go(across[0], across[-1])
    first = one.place().whole()
    first_sizes, rest_sizes = [1] * 5, [1] * (1 + wide) + [wide]
    if not whole:
        dealt = vector_regroup(first[:, 4 * share], GROUPS, vector_lengths)
        dealt = vector_pack(dealt, UNIT, width)
        first = jnp.concatenate([grouped(first, [1] * 4), dealt], axis=1)

    tok = tokens.reshape(all_tokens, width)
    cot = cotangent.reshape(all_tokens, width)
    rows = (all_tokens, width)
    grown = 4 * max(memory_bytes // (1 << 20) - 2, 0)
    limits = [16, 16, 16 + grown, 28, 28 + grown, 28, 28]
    matmul = 2 * all_tokens * width * width

    padded = (all_tokens + micro * RIM, width)
    windows = (3, slots, width)
    line = (pltpu.VMEM((micro, width // 128, RIM + each, 128), F32),)

    normed, keys, key_window, memory_key, vec = kernel(
        key_kernel,
        (info, order.turn(tok), halo, first),
        ((padded, BF16), (rows, BF16), (windows, BF16), ((slots, width), BF16), ((16, width), F32)),
        2 * matmul,
        limits[0],
        line,
    )
    order.done(memory_key)
    keys_side = Gather(order, memory_key)
    keys_side.go(along[0])
    second = grouped(two.place().whole(), first_sizes)
    query, values, value_window, memory_value = kernel(
        value_kernel,
        (info, normed, second),
        ((rows, BF16), (rows, BF16), (windows, BF16), ((slots, width), BF16)),
        3 * matmul,
        limits[1],
        line,
    )
    order.done(memory_value)
    values_side = Gather(order, memory_value)
    values_side.go(back[0])
    for at in range(1, max(len(across), len(along))):
        jobs = []
        if at < len(along):
            jobs += [(keys_side, ()), (values_side, ())]
        if at < len(across):
            jobs.append((both, ()))
        place(order, *jobs)
        if at < len(along):
            keys_side.go(along[at])
            values_side.go(back[at])
        if at < len(across):
            both.go(across[at], across[-1 - at])
    place(order, (keys_side, ()), (values_side, ()), (both, (rest_rows,)))
    keys_side.go(1)
    values_side.go(1)
    both.go(1)
    memories = [keys_side.place().whole(), values_side.place().whole()]
    attended, stats = kernel(
        attend_kernel,
        (info, order.turn(query), keys, values, *memories),
        ((rows, F32), ((2 * each, 128), F32)),
        4 * matmul,
        limits[2],
    )
    order.done(attended)
    rest = grouped(both.place().whole(), rest_sizes)
    half = GROUPS // 2

    def pieces(size):
        return (((half, UNIT * size, width), BF16),) * 2

    output, grad_mid, grad_att, *halves, vec_grad = kernel(
        feed_kernel,
        (info, order.turn(tok), cot, attended, vec, rest),
        ((rows, BF16), (rows, F32), (rows, BF16)) + pieces(1 + 2 * wide) + (((16, width), F32),),
        27 * matmul,
        limits[3],
    )
    order.done(halves[0])
    all_bits = powers(2, count)[::-1]

    def begin(keep, send, size):
        if not whole:
            keep, send = split_cores(scattered(joined(keep, send), size))
        return Reduce(order, keep, send, all_bits)

    feeds = begin(*halves, rest_sizes)
    feeds.go(1)
    memory_half = ((seq // 2, slots, width), BF16)
    chips = (seq // 2, 2, slots, width)
    grad_query, *halves, own_key, own_value = kernel(
        attend_back_kernel,
        (
            info,
            order.turn(query),
            keys,
            values,
            memories[0].reshape(chips),
            memories[1].reshape(chips),
            attended,
            stats,
            grad_att,
        ),
        ((rows, BF16),) + (memory_half,) * 4 + ((rows, F32), (rows, F32)),
        10 * matmul,
        limits[4],
    )
    order.done(grad_query)
    keys_side = Reduce(order, *halves[:2], along)
    values_side = Reduce(order, *halves[2:], along)
    keys_side.go(1)
    values_side.go(1)
    cross = [(across[-1 - at], across[at]) for at in range(len(across))]
    keys_side.add((back[0],))
    keys_side.go(back[0])
    cuts = (upper_rows, rest_rows - upper_rows)
    add(order, (values_side, (along[0],), ()), (feeds, cross[0], cuts))
    values_side.go(along[0])
    feeds.go(*cross[0])
    for at in range(1, max(len(along), len(cross))):
        jobs = []
        if at < len(along):
            keys_side.add((back[at],))
            keys_side.go(back[at])
            jobs.append((values_side, (along[at],), ()))
        if at < len(cross):
            jobs.append((feeds, cross[at], ()))
        add(order, *jobs)
        if at < len(along):
            values_side.go(along[at])
        if at < len(cross):
            feeds.go(*cross[at])
    feeds.add((back[0],), rest_rows)
    key_grad, value_grad = (held.total().astype(BF16) for held in (keys_side, values_side))
    key_kept, value_kept, rims, *halves = kernel(
        compress_back_kernel,
        (
            info,
            order.turn(key_grad),
            value_grad,
            key_window,
            value_window,
            first,
            second,
            normed,
            grad_query,
        ),
        ((rows, F32), (rows, F32), ((micro * RIM, 2 * width), F32)) + pieces(7),
        5 * matmul,
        limits[5],
        (pltpu.VMEM((micro, width // 128, each, 128), F32),),
    )
    order.done(rims)
    rims = lax.ppermute(rims, "seq", [(i + 1, i) for i in range(seq - 1)])
    convs = begin(*halves, [1] * 7)
    convs.go(1)
    grad_in, *halves = kernel(
        input_kernel,
        (
            info,
            order.turn(tok),
            normed,
            grad_query,
            key_kept,
            value_kept,
            rims,
            own_key,
            own_value,
            first,
            second,
            vec,
            grad_mid,
            vec_grad,
        ),
        ((rows, BF16),) + pieces(3),
        6 * matmul,
        limits[6],
        (pltpu.VMEM(rows, F32),),
    )
    order.done(grad_in)
    if whole:
        inputs = begin(*halves, [1] * 3)
    else:
        dealt = joined(*halves)
        vectors = dealt[:, 2 * UNIT, : VECTORS * UNIT + ff // GROUPS]
        vectors = vector_regroup(vectors, count, [UNIT] * VECTORS + [ff // GROUPS])
        dealt = [scattered(dealt, [1] * 2), vector_pack(vectors, 2, width)]
        dealt = split_cores(jnp.concatenate(dealt, axis=1))
        inputs = Reduce(order, *dealt, all_bits)
    inputs.go(1)
    line = [masks[1] for masks in cross]
    cuts = (5 * share, 2 * share)
    convs.add(cross[0], *cuts)
    convs.go(*cross[0])
    feeds.go(back[0])
    inputs.add((line[0],))
    inputs.go(line[0])
    for at in range(1, max(len(along), len(cross))):
        jobs = []
        if at < len(cross):
            jobs.append((convs, cross[at], ()))
        if at < len(along):
            jobs.append((feeds, (back[at],), ()))
        add(order, *jobs)
        if at < len(cross):
            convs.go(*cross[at])
        if at < len(along):
            feeds.go(back[at])
        if at < len(cross):
            inputs.add((line[at],))
            inputs.go(line[at])
    rest_total = feeds.total()
    for at in range(len(along)):
        if at == len(along) - 1:
            ups = [rest_total[share * c : share * (c + 1)] for c in range(1, 1 + wide)]
            rest_outs = (rest_total[:share], jnp.concatenate(ups, axis=1))
            rest_outs = rest_outs + (rest_total[share * (1 + wide) :],)
            rest_outs = lax.optimization_barrier(rest_outs)
            order.done(rest_outs)
        convs.add((back[at],), 7 * share)
        convs.go(back[at])
        inputs.add((along[at],))
        inputs.go(along[at])
    convs, late_inputs = convs.total(), inputs.total()
    conv_keys = convs[: 3 * share].reshape(3, share, width)
    conv_values = convs[4 * share :].reshape(3, share, width)

    def own(buffer, number):
        return buffer[share * number : share * (number + 1)]

    vector_row = late_inputs[2 * share]

    def own_vector(number, length=share):
        return vector_row[share * number : share * number + length]

    return (
        output.reshape(tokens.shape),
        grad_in.reshape(tokens.shape),
        own_vector(0),
        own_vector(1),
        own(convs, 3),
        own(late_inputs, 0),
        own(late_inputs, 1),
        conv_keys,
        conv_values,
        rest_outs[0],
        own_vector(2),
        own_vector(3),
        rest_outs[1],
        own_vector(VECTORS, ff // count),
        rest_outs[2],
        own_vector(4),
    )


def solution(mesh):
    rows = P(AXES, None)
    vector = P(AXES)
    conv = P(None, AXES, None)
    part = P(None, "batch", "seq", None)
    weights = (vector, vector, rows, rows, rows, conv, conv, rows, vector, vector)
    weights = weights + (rows, vector, rows, vector)
    return jax.shard_map(
        per_device,
        mesh=mesh,
        in_specs=(part, P(None, "batch", None)) + weights + (part,),
        out_specs=(part, part) + weights,
        check_vma=False,
    )
```

```python
import functools

import jax
import jax.numpy as jnp
from jax import lax
from jax.experimental import pallas as pl
from jax.experimental.pallas import tpu as pltpu
from jax.sharding import PartitionSpec as P

HEADS = 8
HEAD_DIM = 64
SCALE = HEAD_DIM ** (-0.5)
EPSILON = 1e-06
AXES = ("batch", "seq")
GROUPS = 32
UNIT = 16
PAIR = 2 * HEAD_DIM
RIM = 8
MASKED = -1e30
LEAST_ITEM = 501
F32 = jnp.float32
BF16 = jnp.bfloat16
TN = ((0,), (0,))
NT = ((1,), (1,))
ERF_STEP = 0.3275911
ERF_TERMS = (1.061405429, -1.453152027, 1.421413741, -0.284496736, 0.254829592)


def device_count():
    return lax.axis_size("batch") * lax.axis_size("seq")


def device_index():
    return lax.axis_index("batch") * lax.axis_size("seq") + lax.axis_index("seq")


def powers(low, high):
    masks = []
    while low < high:
        masks.append(low)
        low *= 2
    return masks


def swap(array, mask):
    return lax.ppermute(array, AXES, [(i, i ^ mask) for i in range(device_count())])


def upper_half(mask):
    return ((device_index() & mask) != 0).astype(jnp.int32)


class Order:
    def __init__(self):
        self.last = None
        bits = device_count().bit_length() - 1
        self.uppers = jnp.stack([upper_half(1 << bit) for bit in range(bits)])

    def turn(self, array):
        if self.last is not None:
            array = lax.optimization_barrier((array, self.last))[0]
        return array

    def done(self, array):
        self.last = array


def axis_of(bits, mask):
    return sum(b > mask for b in bits)


def bit_shape(bits, rows):
    return (2,) * len(bits) + tuple(rows)


def cut_of(rank, cut):
    by_lanes, part = cut
    last = (slice(None), part) if by_lanes else (part, slice(None))
    return (slice(None),) * (rank - 2) + last


def at_bit(rank, axis, index, cut):
    where = list(cut_of(rank, cut))
    where[axis] = pl.ds(index, 1)
    return tuple(where)


def cut_shape(shape, by_lanes, size):
    return (shape[0], size) if by_lanes else (size, shape[1])


def overlaps(lefts, rights):
    found, left_at = [], 0
    for i, left in enumerate(lefts):
        right_at = 0
        for j, right in enumerate(rights):
            low = max(left_at, right_at)
            high = min(left_at + left, right_at + right)
            if low < high:
                found.append(
                    (i, j, slice(low - left_at, high - left_at), slice(low - right_at, high - right_at))
                )
            right_at += right
        left_at += left
    return found


def place_kernel(axes, masks, cuts, uppers, *refs):
    count = len(axes)
    for i, j, inside, outside in cuts:
        mine, other, out = refs[2 * i], refs[2 * i + 1], refs[2 * count + j]
        rank, axis, at = len(out.shape), axes[i], uppers[masks[i].bit_length() - 1]
        source = cut_of(rank - 1, inside)
        out[at_bit(rank, axis, at, outside)] = jnp.expand_dims(mine[source], axis)
        out[at_bit(rank, axis, 1 - at, outside)] = jnp.expand_dims(other[source], axis)


def add_kernel(axes, masks, cuts, count, uppers, *refs):
    for i, j, inside, outside in cuts:
        keep, other = refs[2 * i], refs[2 * i + 1]
        next_keep, next_send = refs[2 * count + 2 * j], refs[2 * count + 2 * j + 1]
        rank, axis, at = len(keep.shape), axes[j], uppers[masks[j].bit_length() - 1]
        into = cut_of(rank - 1, outside)
        here, there = at_bit(rank, axis, at, inside), at_bit(rank, axis, 1 - at, inside)
        next_send[into] = jnp.squeeze(keep[there] + other[there], axis)
        next_keep[into] = jnp.squeeze(keep[here] + other[here], axis)


def place(order, *jobs):
    axes, masks, cuts, args, outs, plans = [], [], [], [], [], []
    for gather, sizes in jobs:
        lanes = gather.by_lanes
        whole = (gather.rows, gather.width)
        olds = [p.shape[-1 if lanes else -2] for p in gather.parts]
        sizes = sizes or olds
        bits = [sorted(b + [m], reverse=True) for b, m in zip(gather.bits, gather.masks)]
        own_axes = [axis_of(b, m) for b, m in zip(gather.bits, gather.masks)]
        bits = [bits[min(j, len(bits) - 1)] for j in range(len(sizes))]
        found = overlaps(olds, sizes)
        plans.append((gather, olds, sizes, bits, own_axes, len(outs)))
        cuts += [(len(axes) + i, len(outs) + j, (lanes, x), (lanes, y)) for i, j, x, y in found]
        axes += own_axes
        masks += gather.masks
        for mine, other in zip(gather.parts, gather.others):
            args += [order.turn(mine), other]
        outs += [(bit_shape(b, cut_shape(whole, lanes, r)), BF16) for b, r in zip(bits, sizes)]
    if device_count() == GROUPS:
        body = functools.partial(place_kernel, axes, masks, cuts)
        placed = kernel(body, (order.uppers, *args), outs, 0, 24)
        order.done(placed[0])
    for gather, olds, sizes, bits, own_axes, at in plans:
        if device_count() == GROUPS:
            parts = placed[at : at + len(sizes)]
        else:
            held = []
            sides = zip(gather.parts, gather.others, own_axes, gather.masks)
            for mine, other, axis, mask in sides:
                up = upper_half(mask)
                low, high = jnp.where(up, other, mine), jnp.where(up, mine, other)
                held.append(jnp.stack([low, high], axis=axis))
            parts = cut_parts(held, olds, sizes, gather.by_lanes)
        gather.parts, gather.bits = parts, bits


def add(order, *jobs):
    axes, all_masks, cuts, args, outs, plans, count = [], [], [], [], [], [], 0
    for chain, masks, sizes in jobs:
        lanes = chain.by_lanes
        whole = (chain.rows, chain.width)
        olds = [p.shape[-1 if lanes else -2] for p in chain.keeps]
        sizes = sizes or olds
        bits = [chain.bits[min(j, len(olds) - 1)] for j in range(len(sizes))]
        own_axes = [axis_of(b, m) for b, m in zip(bits, masks)]
        left = [[b for b in old if b != m] for old, m in zip(bits, masks)]
        plans.append((chain, masks, olds, sizes, own_axes, left, len(axes)))
        found = overlaps(olds, sizes)
        cuts += [(count + i, len(axes) + j, (lanes, x), (lanes, y)) for i, j, x, y in found]
        axes += own_axes
        all_masks += masks
        count += len(olds)
        for keep, other in zip(chain.keeps, chain.others):
            args += [order.turn(keep), other]
        for b, r in zip(left, sizes):
            outs += [(bit_shape(b, cut_shape(whole, lanes, r)), BF16)] * 2
    if device_count() == GROUPS:
        body = functools.partial(add_kernel, axes, all_masks, cuts, count)
        both = kernel(body, (order.uppers, *args), outs, 0, 24)
        order.done(both[0])
    for chain, masks, olds, sizes, own_axes, left, at in plans:
        if device_count() == GROUPS:
            found = both[2 * at : 2 * (at + len(sizes))]
            chain.keeps, chain.sends = found[0::2], found[1::2]
        else:
            sums = [
                (k.astype(F32) + o.astype(F32)).astype(BF16)
                for k, o in zip(chain.keeps, chain.others)
            ]
            sums = cut_parts(sums, olds, sizes, chain.by_lanes)
            sides = list(zip(sums, [upper_half(m) for m in masks], own_axes))
            take = lax.dynamic_index_in_dim
            chain.keeps = [take(t, u, axis, False) for t, u, axis in sides]
            chain.sends = [take(t, 1 - u, axis, False) for t, u, axis in sides]
        chain.bits = left


class Gather:
    def __init__(self, order, part, by_lanes=False):
        self.order, self.parts, self.bits = order, [part], [[]]
        self.by_lanes, (self.rows, self.width) = by_lanes, part.shape

    def go(self, *masks, wait=False):
        self.masks = masks
        parts = [self.order.turn(p) for p in self.parts] if wait else self.parts
        self.others = [swap(p, m) for p, m in zip(parts, masks)]

    def place(self, *sizes):
        place(self.order, (self, sizes))
        return self

    def whole(self):
        held = self.parts[0]
        return held.reshape((-1,) + held.shape[-2:])


def cut_parts(arrays, olds, sizes, by_lanes):
    if list(olds) == list(sizes):
        return arrays
    axis = -1 if by_lanes else -2
    joint = jnp.concatenate(arrays, axis=axis)
    ends = [sum(sizes[: j + 1]) for j in range(len(sizes) - 1)]
    return jnp.split(joint, ends, axis=axis)


class Reduce:
    def __init__(self, order, keep, send, bits, by_lanes=False):
        shape = bit_shape(bits, keep.shape[-2:])
        self.order, self.bits = order, [bits]
        self.by_lanes, (self.rows, self.width) = by_lanes, keep.shape[-2:]
        self.keeps, self.sends = [keep.reshape(shape)], [send.reshape(shape)]

    def go(self, *masks, wait=False):
        sends = [self.order.turn(p) for p in self.sends] if wait else self.sends
        self.others = [swap(p, m) for p, m in zip(sends, masks)]

    def add(self, masks, *sizes):
        add(self.order, (self, masks, sizes))
        return self

    def total(self):
        keep, other = self.keeps[0], self.others[0]
        return (keep.astype(F32) + other.astype(F32)).reshape(keep.shape[-2:])


def split_cores(blocks):
    pairs = blocks.reshape((-1, 2) + blocks.shape[1:])
    upper = upper_half(1)
    keep = lax.dynamic_index_in_dim(pairs, upper, 1, keepdims=False)
    return keep, lax.dynamic_index_in_dim(pairs, 1 - upper, 1, keepdims=False)


def joined(keep, send):
    return jnp.stack([keep, send], axis=1).reshape((-1,) + keep.shape[1:])


def grouped(buffer, sizes):
    count = buffer.shape[0]
    if count == GROUPS:
        return buffer
    width = buffer.shape[-1]
    share = width // count
    parts, start = [], 0
    for size in sizes:
        part = buffer[:, start : start + share * size]
        parts.append(part.reshape(GROUPS, UNIT * size, width))
        start += share * size
    return jnp.concatenate(parts, axis=1)


def scattered(buffer, sizes):
    count, width = device_count(), buffer.shape[-1]
    if count == GROUPS:
        return buffer
    parts, start = [], 0
    for size in sizes:
        part = buffer[:, start : start + UNIT * size]
        parts.append(part.reshape(count, width // count * size, width))
        start += UNIT * size
    return jnp.concatenate(parts, axis=1)


def vector_pack(vectors, rows, width):
    filled = jnp.pad(vectors, ((0, 0), (0, width - vectors.shape[1])))
    return jnp.pad(filled[:, None], ((0, 0), (0, rows - 1), (0, 0)))


def vector_regroup(vectors, parts, lengths):
    pieces, start = [], 0
    for length in lengths:
        pieces.append(vectors[:, start : start + length].reshape(parts, -1))
        start += length
    return jnp.concatenate(pieces, axis=1)


def dot(a, b, dims=((1,), (0,))):
    return lax.dot_general(a, b, (dims, ((), ())), preferred_element_type=F32)


def iota(shape, axis):
    return lax.broadcasted_iota(jnp.int32, shape, axis)


def tile(ref, place, size=1):
    rows = ref[:, UNIT * place : UNIT * (place + size), :]
    return rows.reshape(GROUPS * UNIT * size, rows.shape[-1])


def pack_kernel(moves, counts, *refs):
    inputs, outs, sems = refs[: counts[0]], refs[counts[0] : -1], refs[-1]
    copies = []
    for at, (source, where, out, start, rows) in enumerate(moves):
        into = outs[out].at[pl.ds(start, rows)]
        piece = inputs[source] if where is None else inputs[source].at[where]
        copies.append(pltpu.make_async_copy(piece, into, sems.at[at]))
        copies[-1].start()
    for copy in copies:
        copy.wait()


def packed(args, moves, shapes):
    return pl.pallas_call(
        functools.partial(pack_kernel, moves, (len(args),)),
        in_specs=[pl.BlockSpec(memory_space=pltpu.HBM) for _ in args],
        out_specs=[pl.BlockSpec(memory_space=pltpu.VMEM) for _ in shapes],
        out_shape=[jax.ShapeDtypeStruct(shape, BF16) for shape in shapes],
        scratch_shapes=[pltpu.SemaphoreType.DMA((len(moves),))],
        compiler_params=pltpu.CompilerParams(vmem_limit_bytes=62 << 20),
    )(*args)


def kernel(body, args, outs, flops, limit, scratch=()):
    spec = {jnp.dtype(jnp.int32): pltpu.SMEM}
    return pl.pallas_call(
        body,
        in_specs=[pl.BlockSpec(memory_space=spec.get(a.dtype, pltpu.VMEM)) for a in args],
        out_specs=[pl.BlockSpec(memory_space=pltpu.VMEM) for _ in outs],
        out_shape=[jax.ShapeDtypeStruct(shape, dtype) for shape, dtype in outs],
        scratch_shapes=list(scratch),
        compiler_params=pltpu.CompilerParams(vmem_limit_bytes=limit << 20),
        cost_estimate=pl.CostEstimate(
            flops=flops,
            bytes_accessed=sum(a.size * a.dtype.itemsize for a in args),
            transcendentals=0,
        ),
    )(*args)


def unit_norm(values):
    center = values - jnp.mean(values, axis=-1, keepdims=True)
    spread = jnp.mean(center * center, axis=-1, keepdims=True)
    inverse = lax.rsqrt(spread + EPSILON)
    return center * inverse, inverse


def norm_back(grad, unit, inverse, gain):
    e = grad * gain
    mean_e = jnp.mean(e, axis=-1, keepdims=True)
    mean_x = jnp.mean(e * unit, axis=-1, keepdims=True)
    return inverse * (e - mean_e - unit * mean_x)


def column_sum(values):
    return jnp.sum(values, axis=0, keepdims=True)


def valid_column(info, m, start, rows):
    place = start + iota((rows, 1), 0)
    first = (place >= 1) & (place < info[m, 0])
    second = (place >= info[m, 1]) & (place < info[m, 2])
    return jnp.where(first | second, 1.0, 0.0).astype(F32)


def segment_start(info, m, place):
    start = jnp.where(place >= 1, 1, 0)
    start = jnp.where(place >= info[m, 1], info[m, 1], start)
    return jnp.where(place >= info[m, 3], info[m, 3], start)


VECTORS = 5
BIAS_AT = VECTORS * UNIT


def vector_maps(width):
    lanes = width // 2
    fine = (iota((lanes, width), 0) & 15) == (iota((lanes, width), 1) & 15)
    wide = ((iota((lanes, width), 0) + 48) & 63) == (iota((lanes, width), 1) & 63)
    own_fine = iota((GROUPS, width), 1) >> 4 == iota((GROUPS, width), 0)
    own_wide = iota((GROUPS, width), 1) >> 6 == (iota((GROUPS, width), 0) & 7)
    as_bf16 = [jnp.where(m, 1.0, 0.0).astype(BF16) for m in (fine, wide)]
    as_f32 = [jnp.where(m, 1.0, 0.0).astype(F32) for m in (own_fine, own_wide)]
    return as_bf16 + as_f32


def lane_window(lanes, k):
    place = iota((GROUPS, lanes), 1)
    if k == VECTORS:
        return (place >= BIAS_AT) & (place < BIAS_AT + 64)
    return (place >= UNIT * k) & (place < UNIT * (k + 1))


def line_cuts(line):
    micro, cuts = line.shape[:2]
    found = [(m, c) for m in range(micro) for c in range(cuts)]
    return [(m, c, slice(128 * c, 128 * (c + 1))) for m, c in found]


def keep_and_compress(info, low, weights, kept, window, memory, line):
    micro = info.shape[0]
    each = low.shape[0] // micro - RIM
    slots = each // 3
    count = micro * each
    valid = [valid_column(info, m, info[m, 4], each) for m in range(micro)]
    valid += [valid_column(info, m, info[m, 4] - RIM, RIM) for m in range(micro)]
    rows = (dot(low, tile(weights, 0)) * jnp.concatenate(valid, axis=0)).astype(BF16)
    kept[...] = rows[:count]
    rows = rows.astype(F32)
    for m, cut, cols in line_cuts(line):
        line[m, cut, :RIM] = rows[count + RIM * m : count + RIM * (m + 1), cols]
        line[m, cut, RIM:] = rows[each * m : each * (m + 1), cols]
    total = None
    for tap in range(3):
        start = RIM - 2 + tap
        for m, cut, cols in line_cuts(line):
            taken = line[m, cut, pl.ds(start, slots, stride=3), :]
            window[tap, slots * m : slots * (m + 1), cols] = taken.astype(BF16)
        part = dot(window[tap], tile(weights, 1 + tap))
        total = part if total is None else total + part
    memory[...] = total.astype(BF16)


def key_kernel(info, tok, halo, weights, normed, kept, window, memory, vec, line):
    width = tok.shape[-1]
    lanes = width // 2
    fine, wide, own_fine, own_wide = vector_maps(width)
    rows = jnp.sum(weights[:, 4 * UNIT : 5 * UNIT, :lanes].astype(F32), axis=1)
    picked = [jnp.where(lane_window(lanes, k), rows, 0.0) for k in range(VECTORS + 1)]
    spread = dot(jnp.concatenate(picked[:VECTORS], axis=0).astype(BF16), fine)
    vectors = [
        column_sum(spread[GROUPS * k : GROUPS * (k + 1)] * own_fine) for k in range(VECTORS)
    ]
    bias = dot(picked[VECTORS].astype(BF16), wide) * own_wide
    bias = jnp.sum(bias.reshape(4, 8, width), axis=1)
    vec[...] = jnp.concatenate(vectors + [bias, jnp.zeros((7, width), F32)], axis=0)
    values = jnp.concatenate([tok[...], halo[...]], axis=0).astype(F32)
    unit, _ = unit_norm(values)
    low = (unit * vectors[0] + vectors[1]).astype(BF16)
    normed[...] = low
    keep_and_compress(info, low, weights, kept, window, memory, line)


def value_kernel(info, normed, weights, query, kept, window, memory, line):
    low = normed[...]
    keep_and_compress(info, low, weights, kept, window, memory, line)
    query[...] = dot(low[: query.shape[0]], tile(weights, 4)).astype(BF16)


def stacked(values, lower):
    zero = jnp.zeros_like(values)
    return jnp.concatenate(
        [jnp.where(lower, values, zero), jnp.where(lower, zero, values)], axis=0
    )


def merged(values, lower):
    half = values.shape[0] // 2
    return jnp.where(lower, values[:half], values[half:])


def reach(blocks, each):
    row = blocks * each
    size = (row - 2 - LEAST_ITEM) // each + 1
    size = min(size + size % 2, blocks)
    skipped = (LEAST_ITEM + 3) // 3 // (each // 3)
    return size if blocks - size <= skipped else blocks


def memory_pair(memory, first, size, m, pair, micro):
    slots = memory.shape[1] // micro
    rows, cols = slice(slots * m, slots * (m + 1)), slice(PAIR * pair, PAIR * (pair + 1))
    return memory[pl.ds(first, size), rows, cols].reshape(size * slots, PAIR)


def attend_kernel(info, query, keys, values, memory_keys, memory_values, attended, stats):
    micro = info.shape[0]
    count, width = query.shape
    each = count // micro
    blocks, share = memory_keys.shape[0], memory_keys.shape[1] // micro
    size = reach(blocks, each)
    slots = size * share
    pairs = width // PAIR
    lower = iota((each, PAIR), 1) < HEAD_DIM
    lane = iota((2 * each, 128), 1)
    found = jnp.zeros((2 * each, 128), F32)
    for m in range(micro):
        rows = slice(each * m, each * (m + 1))
        place = info[m, 4] + iota((each, 1), 0)
        start = segment_start(info, m, place)
        begin = jnp.where(info[m, 4] < info[m, 1], 0, blocks - size)
        end = 3 * (share * begin + iota((each, slots), 1))
        bias = jnp.where((end <= place) & (end >= start), 0.0, MASKED).astype(F32)
        bias = jnp.concatenate([bias, bias], axis=0)
        for pair in range(pairs):
            cols = slice(PAIR * pair, PAIR * (pair + 1))
            key = keys[rows, cols].astype(F32)
            value = values[rows, cols].astype(F32)
            queries = stacked(query[rows, cols].astype(F32) * SCALE, lower)
            own = jnp.sum(queries * jnp.concatenate([key, key], axis=0), axis=1, keepdims=True)
            memory_key = memory_pair(memory_keys, begin, size, m, pair, micro)
            memory_value = memory_pair(memory_values, begin, size, m, pair, micro)
            scores = dot(queries.astype(BF16), memory_key, NT) + bias
            top = jnp.maximum(jnp.max(scores, axis=1, keepdims=True), own)
            expos = jnp.exp(scores - top)
            own = jnp.exp(own - top)
            total = jnp.sum(expos, axis=1, keepdims=True) + own
            inverse = 1.0 / total
            mixed = dot(expos.astype(BF16), memory_value) * inverse
            weight = jnp.broadcast_to(own * inverse, mixed.shape)
            attended[rows, cols] = merged(mixed, lower) + merged(weight, lower) * value
            found = jnp.where(lane == m * pairs + pair, top + jnp.log(total), found)
    stats[...] = found


def gelu_parts(hidden):
    falling = jnp.exp(hidden * hidden * -0.5)
    step = 1.0 / (1.0 + (ERF_STEP * 0.7071067811865476) * jnp.abs(hidden))
    tail = 0.5 * ERF_TERMS[0]
    for term in ERF_TERMS[1:]:
        tail = tail * step + 0.5 * term
    tail = tail * step * falling
    return jnp.where(hidden >= 0.0, 1.0 - tail, tail), falling


def even_first(flag, rows, size):
    pairs = rows.reshape(-1, 2, size, rows.shape[-1])
    even, odd = pairs[:, 0], pairs[:, 1]
    halves = [jnp.where(flag == 0, even, odd), jnp.where(flag == 0, odd, even)]
    return jnp.concatenate(halves, axis=0).reshape(rows.shape)


def deal(value, rows, keep, send, blocks, start):
    halves = value.astype(BF16).reshape(2, -1, rows, value.shape[-1])
    keep[blocks, start : start + rows, :] = halves[0]
    send[blocks, start : start + rows, :] = halves[1]


def deal_tile(value, place, keep, send):
    deal(value, UNIT, keep, send, slice(None), UNIT * place)


def feed_kernel(
    info,
    tok,
    cot,
    attended,
    vec,
    rest,
    out,
    grad_mid,
    grad_att,
    keep,
    send,
    vec_grad,
):
    count, width = tok.shape
    wide = 4
    low_att = attended[...].astype(BF16)
    w_out = tile(rest, 0)
    middle = tok[...].astype(F32) + dot(low_att, w_out)
    unit, inverse = unit_norm(middle)
    gain = vec[2:3, :]
    low = (unit * gain + vec[3:4, :]).astype(BF16)
    flag = info[0, 5]
    low_t = even_first(flag, low.T, UNIT)
    cots = cot[...]
    total = middle + vec[4:5, :]
    grad_low = jnp.zeros((count, width), F32)
    bias_rows = []
    eighth = GROUPS // wide
    for c in range(wide):
        w_up = tile(rest, 1 + c)
        down = slice(eighth * c, eighth * (c + 1))
        w_down = rest[down, UNIT * (1 + wide) :, :].reshape(width, width)
        hidden = dot(low, w_up) + vec[5 + c : 6 + c, :]
        share, falling = gelu_parts(hidden)
        slope = share + (0.3989422804014327 * hidden) * falling
        active = (hidden * share).astype(BF16)
        total = total + dot(active, w_down)
        grad_hidden_f = dot(cots, w_down, NT) * slope
        grad_hidden = grad_hidden_f.astype(BF16)
        bias_rows.append(column_sum(grad_hidden.astype(F32)))
        grad_low = grad_low + dot(grad_hidden, w_up, NT)
        deal_tile(dot(low_t, grad_hidden), 1 + c, keep, send)
        where = slice(eighth // 2 * c, eighth // 2 * (c + 1))
        active_t = even_first(flag, active.T, UNIT * wide)
        deal(dot(active_t, cots), UNIT * wide, keep, send, where, UNIT * (1 + wide))
    out[...] = total.astype(BF16)
    cots_f = cots.astype(F32)
    grad_middle = cots_f + norm_back(grad_low, unit, inverse, gain)
    grad_mid[...] = grad_middle
    branch = grad_middle.astype(BF16)
    deal_tile(dot(even_first(flag, low_att.T, UNIT), branch), 0, keep, send)
    grad_att[...] = dot(branch, w_out, NT).astype(BF16)
    rows = [jnp.zeros((2, width), F32), column_sum(grad_low * unit), column_sum(grad_low)]
    rows += [column_sum(cots_f)] + bias_rows + [jnp.zeros((7, width), F32)]
    vec_grad[...] = jnp.concatenate(rows, axis=0)


def memory_turned(flag, memory, first, size, m, pair, micro):
    slots = memory.shape[2] // micro
    rows, cols = slice(slots * m, slots * (m + 1)), slice(PAIR * pair, PAIR * (pair + 1))
    halves = [memory[pl.ds(first, size), pl.ds(at, 1), rows, cols] for at in (flag, 1 - flag)]
    return jnp.concatenate([h.reshape(-1, PAIR) for h in halves], axis=0)


def attend_back_kernel(
    info,
    query,
    keys,
    values,
    memory_keys,
    memory_values,
    attended,
    stats,
    grad_att,
    grad_query,
    key_keep,
    key_send,
    value_keep,
    value_send,
    own_key,
    own_value,
):
    micro = info.shape[0]
    count, width = query.shape
    each = count // micro
    chips = memory_keys.shape[0]
    share = memory_keys.shape[2] // micro
    size = reach(2 * chips, each) // 2
    slots = 2 * size * share
    flag = info[0, 6]
    pairs = width // PAIR
    lower = iota((each, PAIR), 1) < HEAD_DIM
    lane = iota((2 * each, 128), 1)
    found = stats[...]
    deltas = jnp.zeros((2 * each, 128), F32)
    parts = {}
    for m in range(micro):
        rows = slice(each * m, each * (m + 1))
        for pair in range(pairs):
            cols = slice(PAIR * pair, PAIR * (pair + 1))
            grad = grad_att[rows, cols].astype(F32)
            product = stacked(grad * attended[rows, cols], lower)
            delta = jnp.sum(product, axis=1, keepdims=True)
            deltas = jnp.where(lane == m * pairs + pair, delta, deltas)
            parts[m, pair] = delta
    found_t, deltas_t = found.T, deltas.T
    for m in range(micro):
        rows = slice(each * m, each * (m + 1))
        lanes = iota((1, 2 * each), 1)
        place = info[m, 4] + jnp.where(lanes >= each, lanes - each, lanes)
        start = segment_start(info, m, place)
        row = iota((slots, 1), 0)
        late = row >= size * share
        row = jnp.where(late, row - size * share, row)
        front = info[m, 4] < info[m, 1]
        begin = jnp.where(front, 0, chips - size)
        block = jnp.zeros((slots, 1), jnp.int32) + 2 * begin
        for chip in range(1, size):
            block = block + jnp.where(row >= share * chip, 1, 0)
        core = jnp.where(late, 1 - flag, flag)
        end = 3 * (row + share * (block + core))
        bias = jnp.where((end <= place) & (end >= start), 0.0, MASKED).astype(F32)
        if size < chips:
            empty = pl.ds(jnp.where(front, size, 0), chips - size)
            zeros = jnp.zeros((chips - size, share, width), BF16)
            for half in (key_keep, key_send, value_keep, value_send):
                half[empty, share * m : share * (m + 1), :] = zeros
        for pair in range(pairs):
            cols = slice(PAIR * pair, PAIR * (pair + 1))
            at = m * pairs + pair
            key = keys[rows, cols].astype(F32)
            value = values[rows, cols].astype(F32)
            query_f = query[rows, cols].astype(F32) * SCALE
            grad_f = grad_att[rows, cols].astype(F32)
            queries = stacked(query_f, lower)
            grads = stacked(grad_f, lower)
            own = jnp.sum(queries * jnp.concatenate([key, key], axis=0), axis=1, keepdims=True)
            own = jnp.exp(own - found[:, at : at + 1])
            grad_own = jnp.sum(
                grads * jnp.concatenate([value, value], axis=0), axis=1, keepdims=True
            )
            grad_own = (own * (grad_own - parts[m, pair])).astype(BF16).astype(F32)
            queries, grads = queries.astype(BF16), grads.astype(BF16)
            memory_key = memory_turned(flag, memory_keys, begin, size, m, pair, micro)
            memory_value = memory_turned(flag, memory_values, begin, size, m, pair, micro)
            scores = dot(memory_key, queries, NT) + bias
            probs = jnp.exp(scores - found_t[at : at + 1, :])
            grad_probs = dot(memory_value, grads, NT)
            grad_scores = (probs * (grad_probs - deltas_t[at : at + 1, :])).astype(BF16)
            sides = (
                (dot(grad_scores, queries), key_keep, key_send),
                (dot(probs.astype(BF16), grads), value_keep, value_send),
            )
            for grad, keep, send in sides:
                halves = grad.astype(BF16).reshape(2, size, share, PAIR)
                into = (pl.ds(begin, size), slice(share * m, share * (m + 1)), cols)
                keep[into] = halves[0]
                send[into] = halves[1]
            turned = dot(memory_key.T, grad_scores).T
            own_grad = merged(jnp.broadcast_to(grad_own, (2 * each, PAIR)), lower)
            own_weight = merged(jnp.broadcast_to(own, (2 * each, PAIR)), lower)
            grad_query[rows, cols] = (
                SCALE * (merged(turned, lower) + own_grad * key)
            ).astype(BF16)
            own_key[rows, cols] = own_grad * query_f
            own_value[rows, cols] = own_weight * grad_f


def compress_back_kernel(
    info,
    key_memory,
    value_memory,
    key_window,
    value_window,
    key_weights,
    value_weights,
    normed,
    grad_query,
    key_grad,
    value_grad,
    rims,
    keep,
    send,
    line,
):
    micro = info.shape[0]
    count, width = key_grad.shape
    each = count // micro
    flag = info[0, 5]
    own_slots = each // 3
    edge = iota((RIM, width), 0) >= RIM - 2
    sides = (
        (key_memory, key_window, key_weights, key_grad),
        (value_memory, value_window, value_weights, value_grad),
    )
    for kind, (memory, window, weights, out) in enumerate(sides):
        grad = memory[...]
        for tap in range(3):
            window_t = even_first(flag, window[tap].T, UNIT)
            deal_tile(dot(window_t, grad), 4 * kind + tap, keep, send)
            part = dot(grad, tile(weights, 1 + tap), NT)
            for m, cut, cols in line_cuts(line):
                rows = slice(own_slots * m, own_slots * (m + 1))
                line[m, cut, pl.ds(tap, own_slots, stride=3), :] = part[rows, cols]
        for m, cut, cols in line_cuts(line):
            out[each * m : each * (m + 1), cols] = line[m, cut]
        for m in range(micro):
            first = pltpu.roll(out[each * m : each * m + RIM, :], RIM - 2, 0)
            into = (slice(RIM * m, RIM * (m + 1)), slice(width * kind, width * (kind + 1)))
            rims[into] = jnp.where(edge, first, 0.0)
    low_t = even_first(flag, normed[:count, :].T, UNIT)
    deal_tile(dot(low_t, grad_query[...]), 3, keep, send)


def input_kernel(
    info,
    tok,
    normed,
    grad_query,
    key_grad,
    value_grad,
    rims,
    own_key,
    own_value,
    key_weights,
    value_weights,
    vec,
    grad_mid,
    vec_grad,
    grad_in,
    keep,
    send,
    total,
):
    count, width = tok.shape
    micro = info.shape[0]
    each = count // micro
    valid = [valid_column(info, m, info[m, 4], each) for m in range(micro)]
    valid = jnp.concatenate(valid, axis=0)
    flag = info[0, 5]
    low_t = even_first(flag, normed[:count, :].T, UNIT)
    grad_low = dot(grad_query[...], tile(value_weights, 4), NT)
    inner = iota((each, width), 0) < each - 2
    sides = ((key_grad, own_key, key_weights), (value_grad, own_value, value_weights))
    for kind, (grad, own, weights) in enumerate(sides):
        for m in range(micro):
            rows = slice(each * m, each * (m + 1))
            moved = pltpu.roll(grad[rows, :], each - 2, 0)
            total[rows, :] = jnp.where(inner, moved, 0.0) + own[rows, :]
            rows = slice(each * (m + 1) - RIM, each * (m + 1))
            rim = rims[RIM * m : RIM * (m + 1), width * kind : width * (kind + 1)]
            total[rows, :] = total[rows, :] + rim
        low_grad = (total[...] * valid).astype(BF16)
        grad_low = grad_low + dot(low_grad, tile(weights, 0), NT)
        deal_tile(dot(low_t, low_grad), kind, keep, send)
    unit, inverse = unit_norm(tok[...].astype(F32))
    back = norm_back(grad_low, unit, inverse, vec[0:1, :])
    grad_in[...] = (grad_mid[...] + back).astype(BF16)

    lanes = width // 2
    fine, wide, own_fine, own_wide = vector_maps(width)
    vectors = [column_sum(grad_low * unit), column_sum(grad_low)]
    vectors += [vec_grad[k : k + 1, :] for k in range(2, VECTORS)]
    dealt = jnp.concatenate([own_fine * v for v in vectors], axis=0).astype(BF16)
    dealt = dot(dealt, fine, NT)
    bias = [
        jnp.broadcast_to(vec_grad[VECTORS + c : VECTORS + c + 1, :], (8, width)) for c in range(4)
    ]
    bias = (jnp.concatenate(bias, axis=0) * own_wide).astype(BF16)
    packed = jnp.where(lane_window(lanes, VECTORS), dot(bias, wide, NT), 0.0)
    for k in range(VECTORS):
        packed = jnp.where(lane_window(lanes, k), dealt[GROUPS * k : GROUPS * (k + 1)], packed)
    packed = jnp.concatenate([packed, jnp.zeros((GROUPS, width - lanes), F32)], axis=1)
    spot = iota((GROUPS, UNIT, width), 1) == 0
    spread = jnp.broadcast_to(packed[:, None, :], (GROUPS, UNIT, width))
    packed = jnp.where(spot, spread, 0.0).reshape(GROUPS * UNIT, width)
    deal_tile(even_first(flag, packed, UNIT), 2, keep, send)


def per_device(
    tokens,
    lengths,
    ln1_gain,
    ln1_bias,
    w_query,
    w_key,
    w_value,
    conv_key,
    conv_value,
    w_out,
    ln2_gain,
    ln2_bias,
    w_up,
    b_up,
    w_down,
    b_down,
    cotangent,
):
    count = device_count()
    micro, _, each, width = tokens.shape
    ff = w_up.shape[1]
    wide = ff // width
    share = width // count
    seq = lax.axis_size("seq")
    all_tokens = micro * each
    slots = micro * each // 3
    memory_bytes = 4 * seq * slots * width

    whole = count == GROUPS
    vector_lengths = [share] * VECTORS + [ff // count]
    vectors, start = 0.0, 0
    for part in (ln1_gain, ln1_bias, ln2_gain, ln2_bias, b_down, b_up):
        end = start + part.shape[0]
        pad = ((0, (UNIT if whole else 2) - 1), (start, width - end))
        vectors, start = vectors + jnp.pad(part[None], pad), end
    vectors = vectors.astype(BF16)
    across = powers(seq, count)
    along = powers(2, seq)[::-1]
    back = along[::-1]
    order = Order()
    if whole:
        moves = [(kind, None, kind, 0, UNIT) for kind in range(2)]
        moves += [(2 + k, tap, k, UNIT * (1 + tap), UNIT) for k in range(2) for tap in range(3)]
        moves += [(4 + kind, None, kind, 4 * UNIT, UNIT) for kind in range(2)]
        moves += [(6, None, 2, 0, UNIT)]
        for c in range(wide):
            cols = (slice(None), pl.ds(width * c, width))
            moves.append((7, cols, 2, UNIT * (1 + c), UNIT))
        moves.append((8, None, 2, UNIT * (1 + wide), UNIT * wide))
        rows = (5 * UNIT, 5 * UNIT, (1 + 2 * wide) * UNIT)
        args = (w_key, w_value, conv_key, conv_value, vectors, w_query, w_out, w_up, w_down)
        first, second, rest = packed(args, moves, [(r, width) for r in rows])
    else:
        first = jnp.concatenate([w_key, *conv_key, vectors], axis=0)
        second = jnp.concatenate([w_value, *conv_value, w_query], axis=0)
        ups = [w_up[:, width * c : width * (c + 1)] for c in range(wide)]
        rest = jnp.concatenate([w_out] + ups + [w_down], axis=0)
    one, two, both = Gather(order, first), Gather(order, second), Gather(order, rest, True)
    one.go(along[0])
    two.go(back[0])
    for at in range(1, len(along)):
        one.place()
        if at == 1:
            last_rows = order.turn(tokens[:, 0, each - RIM :])
            halo = lax.ppermute(last_rows, "seq", [(i, i + 1) for i in range(seq - 1)])
            halo = halo.reshape(micro * RIM, width)
        one.go(along[at])
        two.place()
        two.go(back[at])
    order.done((halo, rest))
    one.place()
    one.go(across[0])
    two.place()
    two.go(across[-1])
    both.go(along[0], wait=True)
    for at in range(1, max(len(across), len(along))):
        jobs = []
        if at < len(across):
            one.place()
            one.go(across[at])
            jobs.append((two, ()))
        if at < len(along):
            jobs.append((both, ()))
        place(order, *jobs)
        if at < len(across):
            two.go(across[-1 - at])
        if at < len(along):
            both.go(along[at])
    lengths = order.turn(lengths[:, 0])
    first_pad = 3 * ((lengths[:, 0] + 2) // 3)
    second_pad = 3 * ((lengths[:, 1] + 2) // 3)
    start = 1 + first_pad
    seats = [lax.axis_index("seq") * each, upper_half(1) if whole else 0, upper_half(1)]
    seats = [jnp.full_like(start, seat) for seat in seats]
    info = [1 + lengths[:, 0], start, start + lengths[:, 1], start + second_pad]
    info = jnp.stack(info + seats, axis=1).astype(jnp.int32)
    order.done((order.last, info))
    one.place()
    one.go(1)
    place(order, (two, ()), (both, (width // 2, width // 2)))
    two.go(1)
    both.go(across[0], across[-1])
    first = one.place().whole()
    first_sizes, rest_sizes = [1] * 5, [1] * (1 + wide) + [wide]
    if not whole:
        dealt = vector_regroup(first[:, 4 * share], GROUPS, vector_lengths)
        dealt = vector_pack(dealt, UNIT, width)
        first = jnp.concatenate([grouped(first, [1] * 4), dealt], axis=1)

    tok = tokens.reshape(all_tokens, width)
    cot = cotangent.reshape(all_tokens, width)
    rows = (all_tokens, width)
    grown = 4 * max(memory_bytes // (1 << 20) - 2, 0)
    limits = [16, 16, 16 + grown, 28, 28 + grown, 28, 28]
    matmul = 2 * all_tokens * width * width

    padded = (all_tokens + micro * RIM, width)
    windows = (3, slots, width)
    line = (pltpu.VMEM((micro, width // 128, RIM + each, 128), F32),)

    normed, keys, key_window, memory_key, vec = kernel(
        key_kernel,
        (info, order.turn(tok), halo, first),
        ((padded, BF16), (rows, BF16), (windows, BF16), ((slots, width), BF16), ((16, width), F32)),
        2 * matmul,
        limits[0],
        line,
    )
    order.done(memory_key)
    keys_side = Gather(order, memory_key)
    keys_side.go(along[0])
    second = grouped(two.place().whole(), first_sizes)
    query, values, value_window, memory_value = kernel(
        value_kernel,
        (info, normed, second),
        ((rows, BF16), (rows, BF16), (windows, BF16), ((slots, width), BF16)),
        3 * matmul,
        limits[1],
        line,
    )
    order.done(memory_value)
    values_side = Gather(order, memory_value)
    values_side.go(back[0])
    for at in range(1, max(len(across), len(along))):
        jobs = []
        if at < len(along):
            jobs += [(keys_side, ()), (values_side, ())]
        if at < len(across):
            jobs.append((both, ()))
        place(order, *jobs)
        if at < len(along):
            keys_side.go(along[at])
            values_side.go(back[at])
        if at < len(across):
            both.go(across[at], across[-1 - at])
    place(order, (keys_side, ()), (values_side, ()), (both, (width,)))
    keys_side.go(1)
    values_side.go(1)
    both.go(1)
    memories = [keys_side.place().whole(), values_side.place().whole()]
    attended, stats = kernel(
        attend_kernel,
        (info, order.turn(query), keys, values, *memories),
        ((rows, F32), ((2 * each, 128), F32)),
        4 * matmul,
        limits[2],
    )
    order.done(attended)
    rest = grouped(both.place().whole(), rest_sizes)
    half = GROUPS // 2

    def pieces(size):
        return (((half, UNIT * size, width), BF16),) * 2

    output, grad_mid, grad_att, *halves, vec_grad = kernel(
        feed_kernel,
        (info, order.turn(tok), cot, attended, vec, rest),
        ((rows, BF16), (rows, F32), (rows, BF16)) + pieces(1 + 2 * wide) + (((16, width), F32),),
        27 * matmul,
        limits[3],
    )
    order.done(halves[0])
    all_bits = powers(2, count)[::-1]

    def begin(keep, send, size, by_lanes=False):
        if not whole:
            keep, send = split_cores(scattered(joined(keep, send), size))
        return Reduce(order, keep, send, all_bits, by_lanes)

    feeds = begin(*halves, rest_sizes, True)
    feeds.go(1)
    memory_half = ((seq // 2, slots, width), BF16)
    chips = (seq // 2, 2, slots, width)
    grad_query, *halves, own_key, own_value = kernel(
        attend_back_kernel,
        (
            info,
            order.turn(query),
            keys,
            values,
            memories[0].reshape(chips),
            memories[1].reshape(chips),
            attended,
            stats,
            grad_att,
        ),
        ((rows, BF16),) + (memory_half,) * 4 + ((rows, F32), (rows, F32)),
        10 * matmul,
        limits[4],
    )
    order.done(grad_query)
    keys_side = Reduce(order, *halves[:2], along)
    values_side = Reduce(order, *halves[2:], along)
    keys_side.go(1)
    values_side.go(1)
    cross = [(across[-1 - at], across[at]) for at in range(len(across))]
    keys_side.add((back[0],))
    keys_side.go(back[0])
    cuts = (width // 2, width // 2)
    add(order, (values_side, (along[0],), ()), (feeds, cross[0], cuts))
    values_side.go(along[0])
    feeds.go(*cross[0])
    for at in range(1, max(len(along), len(cross))):
        jobs = []
        if at < len(along):
            keys_side.add((back[at],))
            keys_side.go(back[at])
            jobs.append((values_side, (along[at],), ()))
        if at < len(cross):
            jobs.append((feeds, cross[at], ()))
        add(order, *jobs)
        if at < len(along):
            values_side.go(along[at])
        if at < len(cross):
            feeds.go(*cross[at])
    feeds.add((back[0],), width)
    key_grad, value_grad = (held.total().astype(BF16) for held in (keys_side, values_side))
    key_kept, value_kept, rims, *halves = kernel(
        compress_back_kernel,
        (
            info,
            order.turn(key_grad),
            value_grad,
            key_window,
            value_window,
            first,
            second,
            normed,
            grad_query,
        ),
        ((rows, F32), (rows, F32), ((micro * RIM, 2 * width), F32)) + pieces(7),
        5 * matmul,
        limits[5],
        (pltpu.VMEM((micro, width // 128, each, 128), F32),),
    )
    order.done(rims)
    rims = lax.ppermute(rims, "seq", [(i + 1, i) for i in range(seq - 1)])
    convs = begin(*halves, [1] * 7)
    convs.go(1)
    grad_in, *halves = kernel(
        input_kernel,
        (
            info,
            order.turn(tok),
            normed,
            grad_query,
            key_kept,
            value_kept,
            rims,
            own_key,
            own_value,
            first,
            second,
            vec,
            grad_mid,
            vec_grad,
        ),
        ((rows, BF16),) + pieces(3),
        6 * matmul,
        limits[6],
        (pltpu.VMEM(rows, F32),),
    )
    order.done(grad_in)
    if whole:
        inputs = begin(*halves, [1] * 3)
    else:
        dealt = joined(*halves)
        vectors = dealt[:, 2 * UNIT, : VECTORS * UNIT + ff // GROUPS]
        vectors = vector_regroup(vectors, count, [UNIT] * VECTORS + [ff // GROUPS])
        dealt = [scattered(dealt, [1] * 2), vector_pack(vectors, 2, width)]
        dealt = split_cores(jnp.concatenate(dealt, axis=1))
        inputs = Reduce(order, *dealt, all_bits)
    inputs.go(1)
    line = [masks[1] for masks in cross]
    cuts = (5 * share, 2 * share)
    convs.add(cross[0], *cuts)
    convs.go(*cross[0])
    feeds.go(back[0])
    inputs.add((line[0],))
    inputs.go(line[0])
    for at in range(1, max(len(along), len(cross))):
        jobs = []
        if at < len(cross):
            jobs.append((convs, cross[at], ()))
        if at < len(along):
            jobs.append((feeds, (back[at],), ()))
        add(order, *jobs)
        if at < len(cross):
            convs.go(*cross[at])
        if at < len(along):
            feeds.go(back[at])
        if at < len(cross):
            inputs.add((line[at],))
            inputs.go(line[at])
    rest_total = feeds.total()
    for at in range(len(along)):
        if at == len(along) - 1:
            ups = [rest_total[share * c : share * (c + 1)] for c in range(1, 1 + wide)]
            rest_outs = (rest_total[:share], jnp.concatenate(ups, axis=1))
            rest_outs = rest_outs + (rest_total[share * (1 + wide) :],)
            rest_outs = lax.optimization_barrier(rest_outs)
            order.done(rest_outs)
        convs.add((back[at],), 7 * share)
        convs.go(back[at])
        inputs.add((along[at],))
        inputs.go(along[at])
    convs, late_inputs = convs.total(), inputs.total()
    conv_keys = convs[: 3 * share].reshape(3, share, width)
    conv_values = convs[4 * share :].reshape(3, share, width)

    def own(buffer, number):
        return buffer[share * number : share * (number + 1)]

    vector_row = late_inputs[2 * share]

    def own_vector(number, length=share):
        return vector_row[share * number : share * number + length]

    return (
        output.reshape(tokens.shape),
        grad_in.reshape(tokens.shape),
        own_vector(0),
        own_vector(1),
        own(convs, 3),
        own(late_inputs, 0),
        own(late_inputs, 1),
        conv_keys,
        conv_values,
        rest_outs[0],
        own_vector(2),
        own_vector(3),
        rest_outs[1],
        own_vector(VECTORS, ff // count),
        rest_outs[2],
        own_vector(4),
    )


def solution(mesh):
    rows = P(AXES, None)
    vector = P(AXES)
    conv = P(None, AXES, None)
    part = P(None, "batch", "seq", None)
    weights = (vector, vector, rows, rows, rows, conv, conv, rows, vector, vector)
    weights = weights + (rows, vector, rows, vector)
    return jax.shard_map(
        per_device,
        mesh=mesh,
        in_specs=(part, P(None, "batch", None)) + weights + (part,),
        out_specs=(part, part) + weights,
        check_vma=False,
    )
```

```python
import functools

import jax
import jax.numpy as jnp
from jax import lax
from jax.experimental import pallas as pl
from jax.experimental.pallas import tpu as pltpu
from jax.sharding import PartitionSpec as P

HEADS = 8
HEAD_DIM = 64
SCALE = HEAD_DIM ** (-0.5)
EPSILON = 1e-06
AXES = ("batch", "seq")
GROUPS = 32
UNIT = 16
PAIR = 2 * HEAD_DIM
RIM = 8
MASKED = -1e30
LEAST_ITEM = 501
F32 = jnp.float32
BF16 = jnp.bfloat16
TN = ((0,), (0,))
NT = ((1,), (1,))
ERF_STEP = 0.3275911
ERF_TERMS = (1.061405429, -1.453152027, 1.421413741, -0.284496736, 0.254829592)


def device_count():
    return lax.axis_size("batch") * lax.axis_size("seq")


def device_index():
    return lax.axis_index("batch") * lax.axis_size("seq") + lax.axis_index("seq")


def powers(low, high):
    masks = []
    while low < high:
        masks.append(low)
        low *= 2
    return masks


def swap(array, mask):
    return lax.ppermute(array, AXES, [(i, i ^ mask) for i in range(device_count())])


def upper_half(mask):
    return ((device_index() & mask) != 0).astype(jnp.int32)


class Order:
    def __init__(self):
        self.last = None
        bits = device_count().bit_length() - 1
        self.uppers = jnp.stack([upper_half(1 << bit) for bit in range(bits)])

    def turn(self, array):
        if self.last is not None:
            array = lax.optimization_barrier((array, self.last))[0]
        return array

    def done(self, array):
        self.last = array


def axis_of(bits, mask):
    return sum(b > mask for b in bits)


def bit_shape(bits, rows):
    return (2,) * len(bits) + tuple(rows)


def cut_of(rank, cut):
    by_lanes, part = cut
    last = (slice(None), part) if by_lanes else (part, slice(None))
    return (slice(None),) * (rank - 2) + last


def at_bit(rank, axis, index, cut):
    where = list(cut_of(rank, cut))
    where[axis] = pl.ds(index, 1)
    return tuple(where)


def cut_shape(shape, by_lanes, size):
    return (shape[0], size) if by_lanes else (size, shape[1])


def overlaps(lefts, rights):
    found, left_at = [], 0
    for i, left in enumerate(lefts):
        right_at = 0
        for j, right in enumerate(rights):
            low = max(left_at, right_at)
            high = min(left_at + left, right_at + right)
            if low < high:
                found.append(
                    (i, j, slice(low - left_at, high - left_at), slice(low - right_at, high - right_at))
                )
            right_at += right
        left_at += left
    return found


def place_kernel(axes, masks, cuts, uppers, *refs):
    count = len(axes)
    for i, j, inside, outside in cuts:
        mine, other, out = refs[2 * i], refs[2 * i + 1], refs[2 * count + j]
        rank, axis, at = len(out.shape), axes[i], uppers[masks[i].bit_length() - 1]
        source = cut_of(rank - 1, inside)
        out[at_bit(rank, axis, at, outside)] = jnp.expand_dims(mine[source], axis)
        out[at_bit(rank, axis, 1 - at, outside)] = jnp.expand_dims(other[source], axis)


def add_kernel(axes, masks, cuts, count, uppers, *refs):
    for i, j, inside, outside in cuts:
        keep, other = refs[2 * i], refs[2 * i + 1]
        next_keep, next_send = refs[2 * count + 2 * j], refs[2 * count + 2 * j + 1]
        rank, axis, at = len(keep.shape), axes[j], uppers[masks[j].bit_length() - 1]
        into = cut_of(rank - 1, outside)
        here, there = at_bit(rank, axis, at, inside), at_bit(rank, axis, 1 - at, inside)
        next_send[into] = jnp.squeeze(keep[there] + other[there], axis)
        next_keep[into] = jnp.squeeze(keep[here] + other[here], axis)


def place(order, *jobs):
    axes, masks, cuts, args, outs, plans = [], [], [], [], [], []
    for gather, sizes in jobs:
        lanes = gather.by_lanes
        whole = (gather.rows, gather.width)
        olds = [p.shape[-1 if lanes else -2] for p in gather.parts]
        sizes = sizes or olds
        bits = [sorted(b + [m], reverse=True) for b, m in zip(gather.bits, gather.masks)]
        own_axes = [axis_of(b, m) for b, m in zip(gather.bits, gather.masks)]
        bits = [bits[min(j, len(bits) - 1)] for j in range(len(sizes))]
        found = overlaps(olds, sizes)
        plans.append((gather, olds, sizes, bits, own_axes, len(outs)))
        cuts += [(len(axes) + i, len(outs) + j, (lanes, x), (lanes, y)) for i, j, x, y in found]
        axes += own_axes
        masks += gather.masks
        for mine, other in zip(gather.parts, gather.others):
            args += [order.turn(mine), other]
        outs += [(bit_shape(b, cut_shape(whole, lanes, r)), BF16) for b, r in zip(bits, sizes)]
    if device_count() == GROUPS:
        body = functools.partial(place_kernel, axes, masks, cuts)
        placed = kernel(body, (order.uppers, *args), outs, 0, 24)
        order.done(placed[0])
    for gather, olds, sizes, bits, own_axes, at in plans:
        if device_count() == GROUPS:
            parts = placed[at : at + len(sizes)]
        else:
            held = []
            sides = zip(gather.parts, gather.others, own_axes, gather.masks)
            for mine, other, axis, mask in sides:
                up = upper_half(mask)
                low, high = jnp.where(up, other, mine), jnp.where(up, mine, other)
                held.append(jnp.stack([low, high], axis=axis))
            parts = cut_parts(held, olds, sizes, gather.by_lanes)
        gather.parts, gather.bits = parts, bits


def add(order, *jobs):
    axes, all_masks, cuts, args, outs, plans, count = [], [], [], [], [], [], 0
    for chain, masks, sizes in jobs:
        lanes = chain.by_lanes
        whole = (chain.rows, chain.width)
        olds = [p.shape[-1 if lanes else -2] for p in chain.keeps]
        sizes = sizes or olds
        bits = [chain.bits[min(j, len(olds) - 1)] for j in range(len(sizes))]
        own_axes = [axis_of(b, m) for b, m in zip(bits, masks)]
        left = [[b for b in old if b != m] for old, m in zip(bits, masks)]
        plans.append((chain, masks, olds, sizes, own_axes, left, len(axes)))
        found = overlaps(olds, sizes)
        cuts += [(count + i, len(axes) + j, (lanes, x), (lanes, y)) for i, j, x, y in found]
        axes += own_axes
        all_masks += masks
        count += len(olds)
        for keep, other in zip(chain.keeps, chain.others):
            args += [order.turn(keep), other]
        for b, r in zip(left, sizes):
            outs += [(bit_shape(b, cut_shape(whole, lanes, r)), BF16)] * 2
    if device_count() == GROUPS:
        body = functools.partial(add_kernel, axes, all_masks, cuts, count)
        both = kernel(body, (order.uppers, *args), outs, 0, 24)
        order.done(both[0])
    for chain, masks, olds, sizes, own_axes, left, at in plans:
        if device_count() == GROUPS:
            found = both[2 * at : 2 * (at + len(sizes))]
            chain.keeps, chain.sends = found[0::2], found[1::2]
        else:
            sums = [
                (k.astype(F32) + o.astype(F32)).astype(BF16)
                for k, o in zip(chain.keeps, chain.others)
            ]
            sums = cut_parts(sums, olds, sizes, chain.by_lanes)
            sides = list(zip(sums, [upper_half(m) for m in masks], own_axes))
            take = lax.dynamic_index_in_dim
            chain.keeps = [take(t, u, axis, False) for t, u, axis in sides]
            chain.sends = [take(t, 1 - u, axis, False) for t, u, axis in sides]
        chain.bits = left


class Gather:
    def __init__(self, order, part, by_lanes=False):
        self.order, self.parts, self.bits = order, [part], [[]]
        self.by_lanes, (self.rows, self.width) = by_lanes, part.shape

    def go(self, *masks, wait=False):
        self.masks = masks
        parts = [self.order.turn(p) for p in self.parts] if wait else self.parts
        self.others = [swap(p, m) for p, m in zip(parts, masks)]

    def place(self, *sizes):
        place(self.order, (self, sizes))
        return self

    def whole(self):
        held = self.parts[0]
        return held.reshape((-1,) + held.shape[-2:])


def cut_parts(arrays, olds, sizes, by_lanes):
    if list(olds) == list(sizes):
        return arrays
    axis = -1 if by_lanes else -2
    joint = jnp.concatenate(arrays, axis=axis)
    ends = [sum(sizes[: j + 1]) for j in range(len(sizes) - 1)]
    return jnp.split(joint, ends, axis=axis)


class Reduce:
    def __init__(self, order, keep, send, bits, by_lanes=False):
        shape = bit_shape(bits, keep.shape[-2:])
        self.order, self.bits = order, [bits]
        self.by_lanes, (self.rows, self.width) = by_lanes, keep.shape[-2:]
        self.keeps, self.sends = [keep.reshape(shape)], [send.reshape(shape)]

    def go(self, *masks, wait=False):
        sends = [self.order.turn(p) for p in self.sends] if wait else self.sends
        self.others = [swap(p, m) for p, m in zip(sends, masks)]

    def add(self, masks, *sizes):
        add(self.order, (self, masks, sizes))
        return self

    def total(self):
        keep, other = self.keeps[0], self.others[0]
        return (keep.astype(F32) + other.astype(F32)).reshape(keep.shape[-2:])


def split_cores(blocks):
    pairs = blocks.reshape((-1, 2) + blocks.shape[1:])
    upper = upper_half(1)
    keep = lax.dynamic_index_in_dim(pairs, upper, 1, keepdims=False)
    return keep, lax.dynamic_index_in_dim(pairs, 1 - upper, 1, keepdims=False)


def joined(keep, send):
    return jnp.stack([keep, send], axis=1).reshape((-1,) + keep.shape[1:])


def grouped(buffer, sizes):
    count = buffer.shape[0]
    if count == GROUPS:
        return buffer
    width = buffer.shape[-1]
    share = width // count
    parts, start = [], 0
    for size in sizes:
        part = buffer[:, start : start + share * size]
        parts.append(part.reshape(GROUPS, UNIT * size, width))
        start += share * size
    return jnp.concatenate(parts, axis=1)


def scattered(buffer, sizes):
    count, width = device_count(), buffer.shape[-1]
    if count == GROUPS:
        return buffer
    parts, start = [], 0
    for size in sizes:
        part = buffer[:, start : start + UNIT * size]
        parts.append(part.reshape(count, width // count * size, width))
        start += UNIT * size
    return jnp.concatenate(parts, axis=1)


def vector_pack(vectors, rows, width):
    filled = jnp.pad(vectors, ((0, 0), (0, width - vectors.shape[1])))
    return jnp.pad(filled[:, None], ((0, 0), (0, rows - 1), (0, 0)))


def vector_regroup(vectors, parts, lengths):
    pieces, start = [], 0
    for length in lengths:
        pieces.append(vectors[:, start : start + length].reshape(parts, -1))
        start += length
    return jnp.concatenate(pieces, axis=1)


def dot(a, b, dims=((1,), (0,))):
    return lax.dot_general(a, b, (dims, ((), ())), preferred_element_type=F32)


def iota(shape, axis):
    return lax.broadcasted_iota(jnp.int32, shape, axis)


def tile(ref, place, size=1):
    rows = ref[:, UNIT * place : UNIT * (place + size), :]
    return rows.reshape(GROUPS * UNIT * size, rows.shape[-1])


def pack_kernel(moves, counts, *refs):
    inputs, outs, sems = refs[: counts[0]], refs[counts[0] : -1], refs[-1]
    copies = []
    for at, (source, where, out, start, rows) in enumerate(moves):
        into = outs[out].at[pl.ds(start, rows)]
        piece = inputs[source] if where is None else inputs[source].at[where]
        copies.append(pltpu.make_async_copy(piece, into, sems.at[at]))
        copies[-1].start()
    for copy in copies:
        copy.wait()


def packed(args, moves, shapes):
    return pl.pallas_call(
        functools.partial(pack_kernel, moves, (len(args),)),
        in_specs=[pl.BlockSpec(memory_space=pltpu.HBM) for _ in args],
        out_specs=[pl.BlockSpec(memory_space=pltpu.VMEM) for _ in shapes],
        out_shape=[jax.ShapeDtypeStruct(shape, BF16) for shape in shapes],
        scratch_shapes=[pltpu.SemaphoreType.DMA((len(moves),))],
        compiler_params=pltpu.CompilerParams(vmem_limit_bytes=62 << 20),
    )(*args)


def kernel(body, args, outs, flops, limit, scratch=()):
    spec = {jnp.dtype(jnp.int32): pltpu.SMEM}
    return pl.pallas_call(
        body,
        in_specs=[pl.BlockSpec(memory_space=spec.get(a.dtype, pltpu.VMEM)) for a in args],
        out_specs=[pl.BlockSpec(memory_space=pltpu.VMEM) for _ in outs],
        out_shape=[jax.ShapeDtypeStruct(shape, dtype) for shape, dtype in outs],
        scratch_shapes=list(scratch),
        compiler_params=pltpu.CompilerParams(vmem_limit_bytes=limit << 20),
        cost_estimate=pl.CostEstimate(
            flops=flops,
            bytes_accessed=sum(a.size * a.dtype.itemsize for a in args),
            transcendentals=0,
        ),
    )(*args)


def unit_norm(values):
    center = values - jnp.mean(values, axis=-1, keepdims=True)
    spread = jnp.mean(center * center, axis=-1, keepdims=True)
    inverse = lax.rsqrt(spread + EPSILON)
    return center * inverse, inverse


def norm_back(grad, unit, inverse, gain):
    e = grad * gain
    mean_e = jnp.mean(e, axis=-1, keepdims=True)
    mean_x = jnp.mean(e * unit, axis=-1, keepdims=True)
    return inverse * (e - mean_e - unit * mean_x)


def column_sum(values):
    return jnp.sum(values, axis=0, keepdims=True)


def valid_column(info, m, start, rows):
    place = start + iota((rows, 1), 0)
    first = (place >= 1) & (place < info[m, 0])
    second = (place >= info[m, 1]) & (place < info[m, 2])
    return jnp.where(first | second, 1.0, 0.0).astype(F32)


def segment_start(info, m, place):
    start = jnp.where(place >= 1, 1, 0)
    start = jnp.where(place >= info[m, 1], info[m, 1], start)
    return jnp.where(place >= info[m, 3], info[m, 3], start)


VECTORS = 5
BIAS_AT = VECTORS * UNIT


def vector_maps(width):
    lanes = width // 2
    fine = (iota((lanes, width), 0) & 15) == (iota((lanes, width), 1) & 15)
    wide = ((iota((lanes, width), 0) + 48) & 63) == (iota((lanes, width), 1) & 63)
    own_fine = iota((GROUPS, width), 1) >> 4 == iota((GROUPS, width), 0)
    own_wide = iota((GROUPS, width), 1) >> 6 == (iota((GROUPS, width), 0) & 7)
    as_bf16 = [jnp.where(m, 1.0, 0.0).astype(BF16) for m in (fine, wide)]
    as_f32 = [jnp.where(m, 1.0, 0.0).astype(F32) for m in (own_fine, own_wide)]
    return as_bf16 + as_f32


def lane_window(lanes, k):
    place = iota((GROUPS, lanes), 1)
    if k == VECTORS:
        return (place >= BIAS_AT) & (place < BIAS_AT + 64)
    return (place >= UNIT * k) & (place < UNIT * (k + 1))


def line_cuts(line):
    micro, cuts = line.shape[:2]
    found = [(m, c) for m in range(micro) for c in range(cuts)]
    return [(m, c, slice(128 * c, 128 * (c + 1))) for m, c in found]


def keep_and_compress(info, low, weights, kept, window, memory, line):
    micro = info.shape[0]
    each = low.shape[0] // micro - RIM
    slots = each // 3
    count = micro * each
    valid = [valid_column(info, m, info[m, 4], each) for m in range(micro)]
    valid += [valid_column(info, m, info[m, 4] - RIM, RIM) for m in range(micro)]
    rows = (dot(low, tile(weights, 0)) * jnp.concatenate(valid, axis=0)).astype(BF16)
    kept[...] = rows[:count]
    rows = rows.astype(F32)
    for m, cut, cols in line_cuts(line):
        line[m, cut, :RIM] = rows[count + RIM * m : count + RIM * (m + 1), cols]
        line[m, cut, RIM:] = rows[each * m : each * (m + 1), cols]
    total = None
    for tap in range(3):
        start = RIM - 2 + tap
        for m, cut, cols in line_cuts(line):
            taken = line[m, cut, pl.ds(start, slots, stride=3), :]
            window[tap, slots * m : slots * (m + 1), cols] = taken.astype(BF16)
        part = dot(window[tap], tile(weights, 1 + tap))
        total = part if total is None else total + part
    memory[...] = total.astype(BF16)


def key_kernel(info, tok, halo, weights, normed, kept, window, memory, vec, line):
    width = tok.shape[-1]
    lanes = width // 2
    fine, wide, own_fine, own_wide = vector_maps(width)
    rows = jnp.sum(weights[:, 4 * UNIT : 5 * UNIT, :lanes].astype(F32), axis=1)
    picked = [jnp.where(lane_window(lanes, k), rows, 0.0) for k in range(VECTORS + 1)]
    spread = dot(jnp.concatenate(picked[:VECTORS], axis=0).astype(BF16), fine)
    vectors = [
        column_sum(spread[GROUPS * k : GROUPS * (k + 1)] * own_fine) for k in range(VECTORS)
    ]
    bias = dot(picked[VECTORS].astype(BF16), wide) * own_wide
    bias = jnp.sum(bias.reshape(4, 8, width), axis=1)
    vec[...] = jnp.concatenate(vectors + [bias, jnp.zeros((7, width), F32)], axis=0)
    values = jnp.concatenate([tok[...], halo[...]], axis=0).astype(F32)
    unit, _ = unit_norm(values)
    low = (unit * vectors[0] + vectors[1]).astype(BF16)
    normed[...] = low
    keep_and_compress(info, low, weights, kept, window, memory, line)


def value_kernel(info, normed, weights, query, kept, window, memory, line):
    low = normed[...]
    keep_and_compress(info, low, weights, kept, window, memory, line)
    query[...] = dot(low[: query.shape[0]], tile(weights, 4)).astype(BF16)


def stacked(values, lower):
    zero = jnp.zeros_like(values)
    return jnp.concatenate(
        [jnp.where(lower, values, zero), jnp.where(lower, zero, values)], axis=0
    )


def merged(values, lower):
    half = values.shape[0] // 2
    return jnp.where(lower, values[:half], values[half:])


def reach(blocks, each):
    row = blocks * each
    size = (row - 2 - LEAST_ITEM) // each + 1
    size = min(size + size % 2, blocks)
    skipped = (LEAST_ITEM + 3) // 3 // (each // 3)
    return size if blocks - size <= skipped else blocks


def memory_pair(memory, first, size, m, pair, micro):
    slots = memory.shape[1] // micro
    rows, cols = slice(slots * m, slots * (m + 1)), slice(PAIR * pair, PAIR * (pair + 1))
    return memory[pl.ds(first, size), rows, cols].reshape(size * slots, PAIR)


def attend_kernel(info, query, keys, values, memory_keys, memory_values, attended, stats):
    micro = info.shape[0]
    count, width = query.shape
    each = count // micro
    blocks, share = memory_keys.shape[0], memory_keys.shape[1] // micro
    size = reach(blocks, each)
    slots = size * share
    pairs = width // PAIR
    lower = iota((each, PAIR), 1) < HEAD_DIM
    lane = iota((2 * each, 128), 1)
    found = jnp.zeros((2 * each, 128), F32)
    ones = jnp.ones((slots, PAIR), BF16)
    for m in range(micro):
        rows = slice(each * m, each * (m + 1))
        place = info[m, 4] + iota((each, 1), 0)
        start = segment_start(info, m, place)
        begin = jnp.where(info[m, 4] < info[m, 1], 0, blocks - size)
        end = 3 * (share * begin + iota((each, slots), 1))
        bias = jnp.where((end <= place) & (end >= start), 0.0, MASKED).astype(F32)
        bias = jnp.concatenate([bias, bias], axis=0)
        for pair in range(pairs):
            cols = slice(PAIR * pair, PAIR * (pair + 1))
            key = keys[rows, cols].astype(F32)
            value = values[rows, cols].astype(F32)
            queries = stacked(query[rows, cols].astype(F32) * SCALE, lower)
            own = jnp.sum(queries * jnp.concatenate([key, key], axis=0), axis=1, keepdims=True)
            memory_key = memory_pair(memory_keys, begin, size, m, pair, micro)
            memory_value = memory_pair(memory_values, begin, size, m, pair, micro)
            scores = dot(queries.astype(BF16), memory_key, NT) + bias
            top = jnp.maximum(jnp.max(scores, axis=1, keepdims=True), own)
            expos = jnp.exp(scores - top)
            own = jnp.exp(own - top)
            beside = jnp.concatenate([memory_value, ones], axis=1)
            mixed = dot(expos.astype(BF16), beside)
            total = mixed[:, PAIR:] + own
            inverse = 1.0 / total
            weight = own * inverse
            mixed = mixed[:, :PAIR] * inverse
            attended[rows, cols] = merged(mixed, lower) + merged(weight, lower) * value
            found = jnp.where(lane == m * pairs + pair, top + jnp.log(total), found)
    stats[...] = found


def gelu_parts(hidden):
    falling = jnp.exp(hidden * hidden * -0.5)
    step = 1.0 / (1.0 + (ERF_STEP * 0.7071067811865476) * jnp.abs(hidden))
    tail = 0.5 * ERF_TERMS[0]
    for term in ERF_TERMS[1:]:
        tail = tail * step + 0.5 * term
    tail = tail * step * falling
    return jnp.where(hidden >= 0.0, 1.0 - tail, tail), falling


def even_first(flag, rows, size):
    pairs = rows.reshape(-1, 2, size, rows.shape[-1])
    even, odd = pairs[:, 0], pairs[:, 1]
    halves = [jnp.where(flag == 0, even, odd), jnp.where(flag == 0, odd, even)]
    return jnp.concatenate(halves, axis=0).reshape(rows.shape)


def deal(value, rows, keep, send, blocks, start):
    halves = value.astype(BF16).reshape(2, -1, rows, value.shape[-1])
    keep[blocks, start : start + rows, :] = halves[0]
    send[blocks, start : start + rows, :] = halves[1]


def deal_tile(value, place, keep, send):
    deal(value, UNIT, keep, send, slice(None), UNIT * place)


def feed_kernel(
    info,
    tok,
    cot,
    attended,
    vec,
    rest,
    out,
    grad_mid,
    grad_att,
    keep,
    send,
    vec_grad,
):
    count, width = tok.shape
    wide = 4
    low_att = attended[...].astype(BF16)
    w_out = tile(rest, 0)
    middle = tok[...].astype(F32) + dot(low_att, w_out)
    unit, inverse = unit_norm(middle)
    gain = vec[2:3, :]
    low = (unit * gain + vec[3:4, :]).astype(BF16)
    flag = info[0, 5]
    low_t = even_first(flag, low.T, UNIT)
    cots = cot[...]
    total = middle + vec[4:5, :]
    grad_low = jnp.zeros((count, width), F32)
    bias_rows = []
    eighth = GROUPS // wide
    for c in range(wide):
        w_up = tile(rest, 1 + c)
        down = slice(eighth * c, eighth * (c + 1))
        w_down = rest[down, UNIT * (1 + wide) :, :].reshape(width, width)
        hidden = dot(low, w_up) + vec[5 + c : 6 + c, :]
        share, falling = gelu_parts(hidden)
        slope = share + (0.3989422804014327 * hidden) * falling
        active = (hidden * share).astype(BF16)
        total = total + dot(active, w_down)
        grad_hidden_f = dot(cots, w_down, NT) * slope
        grad_hidden = grad_hidden_f.astype(BF16)
        bias_rows.append(column_sum(grad_hidden.astype(F32)))
        grad_low = grad_low + dot(grad_hidden, w_up, NT)
        deal_tile(dot(low_t, grad_hidden), 1 + c, keep, send)
        where = slice(eighth // 2 * c, eighth // 2 * (c + 1))
        active_t = even_first(flag, active.T, UNIT * wide)
        deal(dot(active_t, cots), UNIT * wide, keep, send, where, UNIT * (1 + wide))
    out[...] = total.astype(BF16)
    cots_f = cots.astype(F32)
    grad_middle = cots_f + norm_back(grad_low, unit, inverse, gain)
    grad_mid[...] = grad_middle
    branch = grad_middle.astype(BF16)
    deal_tile(dot(even_first(flag, low_att.T, UNIT), branch), 0, keep, send)
    grad_att[...] = dot(branch, w_out, NT).astype(BF16)
    rows = [jnp.zeros((2, width), F32), column_sum(grad_low * unit), column_sum(grad_low)]
    rows += [column_sum(cots_f)] + bias_rows + [jnp.zeros((7, width), F32)]
    vec_grad[...] = jnp.concatenate(rows, axis=0)


def memory_turned(flag, memory, first, size, m, pair, micro):
    slots = memory.shape[2] // micro
    rows, cols = slice(slots * m, slots * (m + 1)), slice(PAIR * pair, PAIR * (pair + 1))
    halves = [memory[pl.ds(first, size), pl.ds(at, 1), rows, cols] for at in (flag, 1 - flag)]
    return jnp.concatenate([h.reshape(-1, PAIR) for h in halves], axis=0)


def attend_back_kernel(
    info,
    query,
    keys,
    values,
    memory_keys,
    memory_values,
    attended,
    stats,
    grad_att,
    grad_query,
    key_keep,
    key_send,
    value_keep,
    value_send,
    own_key,
    own_value,
):
    micro = info.shape[0]
    count, width = query.shape
    each = count // micro
    chips = memory_keys.shape[0]
    share = memory_keys.shape[2] // micro
    size = reach(2 * chips, each) // 2
    slots = 2 * size * share
    flag = info[0, 6]
    pairs = width // PAIR
    lower = iota((each, PAIR), 1) < HEAD_DIM
    lane = iota((2 * each, 128), 1)
    found = stats[...]
    deltas = jnp.zeros((2 * each, 128), F32)
    parts = {}
    for m in range(micro):
        rows = slice(each * m, each * (m + 1))
        for pair in range(pairs):
            cols = slice(PAIR * pair, PAIR * (pair + 1))
            grad = grad_att[rows, cols].astype(F32)
            product = stacked(grad * attended[rows, cols], lower)
            delta = jnp.sum(product, axis=1, keepdims=True)
            deltas = jnp.where(lane == m * pairs + pair, delta, deltas)
            parts[m, pair] = delta
    found_t, deltas_t = found.T, deltas.T
    for m in range(micro):
        rows = slice(each * m, each * (m + 1))
        lanes = iota((1, 2 * each), 1)
        place = info[m, 4] + jnp.where(lanes >= each, lanes - each, lanes)
        start = segment_start(info, m, place)
        row = iota((slots, 1), 0)
        late = row >= size * share
        row = jnp.where(late, row - size * share, row)
        front = info[m, 4] < info[m, 1]
        begin = jnp.where(front, 0, chips - size)
        block = jnp.zeros((slots, 1), jnp.int32) + 2 * begin
        for chip in range(1, size):
            block = block + jnp.where(row >= share * chip, 1, 0)
        core = jnp.where(late, 1 - flag, flag)
        end = 3 * (row + share * (block + core))
        bias = jnp.where((end <= place) & (end >= start), 0.0, MASKED).astype(F32)
        if size < chips:
            empty = pl.ds(jnp.where(front, size, 0), chips - size)
            zeros = jnp.zeros((chips - size, share, width), BF16)
            for half in (key_keep, key_send, value_keep, value_send):
                half[empty, share * m : share * (m + 1), :] = zeros
        for pair in range(pairs):
            cols = slice(PAIR * pair, PAIR * (pair + 1))
            at = m * pairs + pair
            key = keys[rows, cols].astype(F32)
            value = values[rows, cols].astype(F32)
            query_f = query[rows, cols].astype(F32) * SCALE
            grad_f = grad_att[rows, cols].astype(F32)
            queries = stacked(query_f, lower)
            grads = stacked(grad_f, lower)
            own = jnp.sum(queries * jnp.concatenate([key, key], axis=0), axis=1, keepdims=True)
            own = jnp.exp(own - found[:, at : at + 1])
            grad_own = jnp.sum(
                grads * jnp.concatenate([value, value], axis=0), axis=1, keepdims=True
            )
            grad_own = (own * (grad_own - parts[m, pair])).astype(BF16).astype(F32)
            queries, grads = queries.astype(BF16), grads.astype(BF16)
            memory_key = memory_turned(flag, memory_keys, begin, size, m, pair, micro)
            memory_value = memory_turned(flag, memory_values, begin, size, m, pair, micro)
            scores = dot(memory_key, queries, NT) + bias
            probs = jnp.exp(scores - found_t[at : at + 1, :])
            grad_probs = dot(memory_value, grads, NT)
            grad_scores = (probs * (grad_probs - deltas_t[at : at + 1, :])).astype(BF16)
            sides = (
                (dot(grad_scores, queries), key_keep, key_send),
                (dot(probs.astype(BF16), grads), value_keep, value_send),
            )
            for grad, keep, send in sides:
                halves = grad.astype(BF16).reshape(2, size, share, PAIR)
                into = (pl.ds(begin, size), slice(share * m, share * (m + 1)), cols)
                keep[into] = halves[0]
                send[into] = halves[1]
            turned = dot(memory_key.T, grad_scores).T
            own_grad = merged(jnp.broadcast_to(grad_own, (2 * each, PAIR)), lower)
            own_weight = merged(jnp.broadcast_to(own, (2 * each, PAIR)), lower)
            grad_query[rows, cols] = (
                SCALE * (merged(turned, lower) + own_grad * key)
            ).astype(BF16)
            own_key[rows, cols] = own_grad * query_f
            own_value[rows, cols] = own_weight * grad_f


def compress_back_kernel(
    info,
    key_memory,
    value_memory,
    key_window,
    value_window,
    key_weights,
    value_weights,
    normed,
    grad_query,
    key_grad,
    value_grad,
    rims,
    keep,
    send,
    line,
):
    micro = info.shape[0]
    count, width = key_grad.shape
    each = count // micro
    flag = info[0, 5]
    own_slots = each // 3
    edge = iota((RIM, width), 0) >= RIM - 2
    sides = (
        (key_memory, key_window, key_weights, key_grad),
        (value_memory, value_window, value_weights, value_grad),
    )
    for kind, (memory, window, weights, out) in enumerate(sides):
        grad = memory[...]
        for tap in range(3):
            window_t = even_first(flag, window[tap].T, UNIT)
            deal_tile(dot(window_t, grad), 4 * kind + tap, keep, send)
            part = dot(grad, tile(weights, 1 + tap), NT)
            for m, cut, cols in line_cuts(line):
                rows = slice(own_slots * m, own_slots * (m + 1))
                line[m, cut, pl.ds(tap, own_slots, stride=3), :] = part[rows, cols]
        for m, cut, cols in line_cuts(line):
            out[each * m : each * (m + 1), cols] = line[m, cut]
        for m in range(micro):
            first = pltpu.roll(out[each * m : each * m + RIM, :], RIM - 2, 0)
            into = (slice(RIM * m, RIM * (m + 1)), slice(width * kind, width * (kind + 1)))
            rims[into] = jnp.where(edge, first, 0.0)
    low_t = even_first(flag, normed[:count, :].T, UNIT)
    deal_tile(dot(low_t, grad_query[...]), 3, keep, send)


def input_kernel(
    info,
    tok,
    normed,
    grad_query,
    key_grad,
    value_grad,
    rims,
    own_key,
    own_value,
    key_weights,
    value_weights,
    vec,
    grad_mid,
    vec_grad,
    grad_in,
    keep,
    send,
    total,
):
    count, width = tok.shape
    micro = info.shape[0]
    each = count // micro
    valid = [valid_column(info, m, info[m, 4], each) for m in range(micro)]
    valid = jnp.concatenate(valid, axis=0)
    flag = info[0, 5]
    low_t = even_first(flag, normed[:count, :].T, UNIT)
    grad_low = dot(grad_query[...], tile(value_weights, 4), NT)
    inner = iota((each, width), 0) < each - 2
    sides = ((key_grad, own_key, key_weights), (value_grad, own_value, value_weights))
    for kind, (grad, own, weights) in enumerate(sides):
        for m in range(micro):
            rows = slice(each * m, each * (m + 1))
            moved = pltpu.roll(grad[rows, :], each - 2, 0)
            total[rows, :] = jnp.where(inner, moved, 0.0) + own[rows, :]
            rows = slice(each * (m + 1) - RIM, each * (m + 1))
            rim = rims[RIM * m : RIM * (m + 1), width * kind : width * (kind + 1)]
            total[rows, :] = total[rows, :] + rim
        low_grad = (total[...] * valid).astype(BF16)
        grad_low = grad_low + dot(low_grad, tile(weights, 0), NT)
        deal_tile(dot(low_t, low_grad), kind, keep, send)
    unit, inverse = unit_norm(tok[...].astype(F32))
    back = norm_back(grad_low, unit, inverse, vec[0:1, :])
    grad_in[...] = (grad_mid[...] + back).astype(BF16)

    lanes = width // 2
    fine, wide, own_fine, own_wide = vector_maps(width)
    vectors = [column_sum(grad_low * unit), column_sum(grad_low)]
    vectors += [vec_grad[k : k + 1, :] for k in range(2, VECTORS)]
    dealt = jnp.concatenate([own_fine * v for v in vectors], axis=0).astype(BF16)
    dealt = dot(dealt, fine, NT)
    bias = [
        jnp.broadcast_to(vec_grad[VECTORS + c : VECTORS + c + 1, :], (8, width)) for c in range(4)
    ]
    bias = (jnp.concatenate(bias, axis=0) * own_wide).astype(BF16)
    packed = jnp.where(lane_window(lanes, VECTORS), dot(bias, wide, NT), 0.0)
    for k in range(VECTORS):
        packed = jnp.where(lane_window(lanes, k), dealt[GROUPS * k : GROUPS * (k + 1)], packed)
    packed = jnp.concatenate([packed, jnp.zeros((GROUPS, width - lanes), F32)], axis=1)
    spot = iota((GROUPS, UNIT, width), 1) == 0
    spread = jnp.broadcast_to(packed[:, None, :], (GROUPS, UNIT, width))
    packed = jnp.where(spot, spread, 0.0).reshape(GROUPS * UNIT, width)
    deal_tile(even_first(flag, packed, UNIT), 2, keep, send)


def per_device(
    tokens,
    lengths,
    ln1_gain,
    ln1_bias,
    w_query,
    w_key,
    w_value,
    conv_key,
    conv_value,
    w_out,
    ln2_gain,
    ln2_bias,
    w_up,
    b_up,
    w_down,
    b_down,
    cotangent,
):
    count = device_count()
    micro, _, each, width = tokens.shape
    ff = w_up.shape[1]
    wide = ff // width
    share = width // count
    seq = lax.axis_size("seq")
    all_tokens = micro * each
    slots = micro * each // 3
    memory_bytes = 4 * seq * slots * width

    whole = count == GROUPS
    vector_lengths = [share] * VECTORS + [ff // count]
    vectors, start = 0.0, 0
    for part in (ln1_gain, ln1_bias, ln2_gain, ln2_bias, b_down, b_up):
        end = start + part.shape[0]
        pad = ((0, (UNIT if whole else 2) - 1), (start, width - end))
        vectors, start = vectors + jnp.pad(part[None], pad), end
    vectors = vectors.astype(BF16)
    across = powers(seq, count)
    along = powers(2, seq)[::-1]
    back = along[::-1]
    order = Order()
    if whole:
        moves = [(kind, None, kind, 0, UNIT) for kind in range(2)]
        moves += [(2 + k, tap, k, UNIT * (1 + tap), UNIT) for k in range(2) for tap in range(3)]
        moves += [(4 + kind, None, kind, 4 * UNIT, UNIT) for kind in range(2)]
        moves += [(6, None, 2, 0, UNIT)]
        for c in range(wide):
            cols = (slice(None), pl.ds(width * c, width))
            moves.append((7, cols, 2, UNIT * (1 + c), UNIT))
        moves.append((8, None, 2, UNIT * (1 + wide), UNIT * wide))
        rows = (5 * UNIT, 5 * UNIT, (1 + 2 * wide) * UNIT)
        args = (w_key, w_value, conv_key, conv_value, vectors, w_query, w_out, w_up, w_down)
        first, second, rest = packed(args, moves, [(r, width) for r in rows])
    else:
        first = jnp.concatenate([w_key, *conv_key, vectors], axis=0)
        second = jnp.concatenate([w_value, *conv_value, w_query], axis=0)
        ups = [w_up[:, width * c : width * (c + 1)] for c in range(wide)]
        rest = jnp.concatenate([w_out] + ups + [w_down], axis=0)
    one, two, both = Gather(order, first), Gather(order, second), Gather(order, rest, True)
    one.go(along[0])
    two.go(back[0])
    for at in range(1, len(along)):
        one.place()
        if at == 1:
            last_rows = order.turn(tokens[:, 0, each - RIM :])
            halo = lax.ppermute(last_rows, "seq", [(i, i + 1) for i in range(seq - 1)])
            halo = halo.reshape(micro * RIM, width)
        one.go(along[at])
        two.place()
        two.go(back[at])
    order.done((halo, rest))
    one.place()
    one.go(across[0])
    two.place()
    two.go(across[-1])
    both.go(along[0], wait=True)
    for at in range(1, max(len(across), len(along))):
        jobs = []
        if at < len(across):
            one.place()
            one.go(across[at])
            jobs.append((two, ()))
        if at < len(along):
            jobs.append((both, ()))
        place(order, *jobs)
        if at < len(across):
            two.go(across[-1 - at])
        if at < len(along):
            both.go(along[at])
    lengths = order.turn(lengths[:, 0])
    first_pad = 3 * ((lengths[:, 0] + 2) // 3)
    second_pad = 3 * ((lengths[:, 1] + 2) // 3)
    start = 1 + first_pad
    seats = [lax.axis_index("seq") * each, upper_half(1) if whole else 0, upper_half(1)]
    seats = [jnp.full_like(start, seat) for seat in seats]
    info = [1 + lengths[:, 0], start, start + lengths[:, 1], start + second_pad]
    info = jnp.stack(info + seats, axis=1).astype(jnp.int32)
    order.done((order.last, info))
    one.place()
    one.go(1)
    place(order, (two, ()), (both, (width // 2, width // 2)))
    two.go(1)
    both.go(across[0], across[-1])
    first = one.place().whole()
    first_sizes, rest_sizes = [1] * 5, [1] * (1 + wide) + [wide]
    if not whole:
        dealt = vector_regroup(first[:, 4 * share], GROUPS, vector_lengths)
        dealt = vector_pack(dealt, UNIT, width)
        first = jnp.concatenate([grouped(first, [1] * 4), dealt], axis=1)

    tok = tokens.reshape(all_tokens, width)
    cot = cotangent.reshape(all_tokens, width)
    rows = (all_tokens, width)
    grown = 4 * max(memory_bytes // (1 << 20) - 2, 0)
    limits = [16, 16, 16 + grown, 28, 28 + grown, 28, 28]
    matmul = 2 * all_tokens * width * width

    padded = (all_tokens + micro * RIM, width)
    windows = (3, slots, width)
    line = (pltpu.VMEM((micro, width // 128, RIM + each, 128), F32),)

    normed, keys, key_window, memory_key, vec = kernel(
        key_kernel,
        (info, order.turn(tok), halo, first),
        ((padded, BF16), (rows, BF16), (windows, BF16), ((slots, width), BF16), ((16, width), F32)),
        2 * matmul,
        limits[0],
        line,
    )
    order.done(memory_key)
    keys_side = Gather(order, memory_key)
    keys_side.go(along[0])
    second = grouped(two.place().whole(), first_sizes)
    query, values, value_window, memory_value = kernel(
        value_kernel,
        (info, normed, second),
        ((rows, BF16), (rows, BF16), (windows, BF16), ((slots, width), BF16)),
        3 * matmul,
        limits[1],
        line,
    )
    order.done(memory_value)
    values_side = Gather(order, memory_value)
    values_side.go(back[0])
    for at in range(1, max(len(across), len(along))):
        jobs = []
        if at < len(along):
            jobs += [(keys_side, ()), (values_side, ())]
        if at < len(across):
            jobs.append((both, ()))
        place(order, *jobs)
        if at < len(along):
            keys_side.go(along[at])
            values_side.go(back[at])
        if at < len(across):
            both.go(across[at], across[-1 - at])
    place(order, (keys_side, ()), (values_side, ()), (both, (width,)))
    keys_side.go(1)
    values_side.go(1)
    both.go(1)
    memories = [keys_side.place().whole(), values_side.place().whole()]
    attended, stats = kernel(
        attend_kernel,
        (info, order.turn(query), keys, values, *memories),
        ((rows, F32), ((2 * each, 128), F32)),
        4 * matmul,
        limits[2],
    )
    order.done(attended)
    rest = grouped(both.place().whole(), rest_sizes)
    half = GROUPS // 2

    def pieces(size):
        return (((half, UNIT * size, width), BF16),) * 2

    output, grad_mid, grad_att, *halves, vec_grad = kernel(
        feed_kernel,
        (info, order.turn(tok), cot, attended, vec, rest),
        ((rows, BF16), (rows, F32), (rows, BF16)) + pieces(1 + 2 * wide) + (((16, width), F32),),
        27 * matmul,
        limits[3],
    )
    order.done(halves[0])
    all_bits = powers(2, count)[::-1]

    def begin(keep, send, size, by_lanes=False):
        if not whole:
            keep, send = split_cores(scattered(joined(keep, send), size))
        return Reduce(order, keep, send, all_bits, by_lanes)

    feeds = begin(*halves, rest_sizes, True)
    feeds.go(1)
    memory_half = ((seq // 2, slots, width), BF16)
    chips = (seq // 2, 2, slots, width)
    grad_query, *halves, own_key, own_value = kernel(
        attend_back_kernel,
        (
            info,
            order.turn(query),
            keys,
            values,
            memories[0].reshape(chips),
            memories[1].reshape(chips),
            attended,
            stats,
            grad_att,
        ),
        ((rows, BF16),) + (memory_half,) * 4 + ((rows, F32), (rows, F32)),
        10 * matmul,
        limits[4],
    )
    order.done(grad_query)
    keys_side = Reduce(order, *halves[:2], along)
    values_side = Reduce(order, *halves[2:], along)
    keys_side.go(1)
    values_side.go(1)
    cross = [(across[-1 - at], across[at]) for at in range(len(across))]
    keys_side.add((back[0],))
    keys_side.go(back[0])
    cuts = (width // 2, width // 2)
    add(order, (values_side, (along[0],), ()), (feeds, cross[0], cuts))
    values_side.go(along[0])
    feeds.go(*cross[0])
    for at in range(1, max(len(along), len(cross))):
        jobs = []
        if at < len(along):
            keys_side.add((back[at],))
            keys_side.go(back[at])
            jobs.append((values_side, (along[at],), ()))
        if at < len(cross):
            jobs.append((feeds, cross[at], ()))
        add(order, *jobs)
        if at < len(along):
            values_side.go(along[at])
        if at < len(cross):
            feeds.go(*cross[at])
    feeds.add((back[0],), width)
    key_grad, value_grad = (held.total().astype(BF16) for held in (keys_side, values_side))
    key_kept, value_kept, rims, *halves = kernel(
        compress_back_kernel,
        (
            info,
            order.turn(key_grad),
            value_grad,
            key_window,
            value_window,
            first,
            second,
            normed,
            grad_query,
        ),
        ((rows, F32), (rows, F32), ((micro * RIM, 2 * width), F32)) + pieces(7),
        5 * matmul,
        limits[5],
        (pltpu.VMEM((micro, width // 128, each, 128), F32),),
    )
    order.done(rims)
    rims = lax.ppermute(rims, "seq", [(i + 1, i) for i in range(seq - 1)])
    convs = begin(*halves, [1] * 7)
    convs.go(1)
    grad_in, *halves = kernel(
        input_kernel,
        (
            info,
            order.turn(tok),
            normed,
            grad_query,
            key_kept,
            value_kept,
            rims,
            own_key,
            own_value,
            first,
            second,
            vec,
            grad_mid,
            vec_grad,
        ),
        ((rows, BF16),) + pieces(3),
        6 * matmul,
        limits[6],
        (pltpu.VMEM(rows, F32),),
    )
    order.done(grad_in)
    if whole:
        inputs = begin(*halves, [1] * 3)
    else:
        dealt = joined(*halves)
        vectors = dealt[:, 2 * UNIT, : VECTORS * UNIT + ff // GROUPS]
        vectors = vector_regroup(vectors, count, [UNIT] * VECTORS + [ff // GROUPS])
        dealt = [scattered(dealt, [1] * 2), vector_pack(vectors, 2, width)]
        dealt = split_cores(jnp.concatenate(dealt, axis=1))
        inputs = Reduce(order, *dealt, all_bits)
    inputs.go(1)
    line = [masks[1] for masks in cross]
    cuts = (5 * share, 2 * share)
    convs.add(cross[0], *cuts)
    convs.go(*cross[0])
    feeds.go(back[0])
    inputs.add((line[0],))
    inputs.go(line[0])
    for at in range(1, max(len(along), len(cross))):
        jobs = []
        if at < len(cross):
            jobs.append((convs, cross[at], ()))
        if at < len(along):
            jobs.append((feeds, (back[at],), ()))
        add(order, *jobs)
        if at < len(cross):
            convs.go(*cross[at])
        if at < len(along):
            feeds.go(back[at])
        if at < len(cross):
            inputs.add((line[at],))
            inputs.go(line[at])
    rest_total = feeds.total()
    for at in range(len(along)):
        if at == len(along) - 1:
            ups = [rest_total[share * c : share * (c + 1)] for c in range(1, 1 + wide)]
            rest_outs = (rest_total[:share], jnp.concatenate(ups, axis=1))
            rest_outs = rest_outs + (rest_total[share * (1 + wide) :],)
            rest_outs = lax.optimization_barrier(rest_outs)
            order.done(rest_outs)
        convs.add((back[at],), 7 * share)
        convs.go(back[at])
        inputs.add((along[at],))
        inputs.go(along[at])
    convs, late_inputs = convs.total(), inputs.total()
    conv_keys = convs[: 3 * share].reshape(3, share, width)
    conv_values = convs[4 * share :].reshape(3, share, width)

    def own(buffer, number):
        return buffer[share * number : share * (number + 1)]

    vector_row = late_inputs[2 * share]

    def own_vector(number, length=share):
        return vector_row[share * number : share * number + length]

    return (
        output.reshape(tokens.shape),
        grad_in.reshape(tokens.shape),
        own_vector(0),
        own_vector(1),
        own(convs, 3),
        own(late_inputs, 0),
        own(late_inputs, 1),
        conv_keys,
        conv_values,
        rest_outs[0],
        own_vector(2),
        own_vector(3),
        rest_outs[1],
        own_vector(VECTORS, ff // count),
        rest_outs[2],
        own_vector(4),
    )


def solution(mesh):
    rows = P(AXES, None)
    vector = P(AXES)
    conv = P(None, AXES, None)
    part = P(None, "batch", "seq", None)
    weights = (vector, vector, rows, rows, rows, conv, conv, rows, vector, vector)
    weights = weights + (rows, vector, rows, vector)
    return jax.shard_map(
        per_device,
        mesh=mesh,
        in_specs=(part, P(None, "batch", None)) + weights + (part,),
        out_specs=(part, part) + weights,
        check_vma=False,
    )
```

```python
import functools

import jax
import jax.numpy as jnp
from jax import lax
from jax.experimental import pallas as pl
from jax.experimental.pallas import tpu as pltpu
from jax.sharding import PartitionSpec as P

HEADS = 8
HEAD_DIM = 64
SCALE = HEAD_DIM ** (-0.5)
EPSILON = 1e-06
AXES = ("batch", "seq")
GROUPS = 32
UNIT = 16
PAIR = 2 * HEAD_DIM
RIM = 8
MASKED = -1e30
LEAST_ITEM = 501
F32 = jnp.float32
BF16 = jnp.bfloat16
TN = ((0,), (0,))
NT = ((1,), (1,))
ERF_STEP = 0.3275911
ERF_TERMS = (1.061405429, -1.453152027, 1.421413741, -0.284496736, 0.254829592)


def device_count():
    return lax.axis_size("batch") * lax.axis_size("seq")


def device_index():
    return lax.axis_index("batch") * lax.axis_size("seq") + lax.axis_index("seq")


def powers(low, high):
    masks = []
    while low < high:
        masks.append(low)
        low *= 2
    return masks


def swap(array, mask):
    return lax.ppermute(array, AXES, [(i, i ^ mask) for i in range(device_count())])


def upper_half(mask):
    return ((device_index() & mask) != 0).astype(jnp.int32)


class Order:
    def __init__(self):
        self.last = None
        bits = device_count().bit_length() - 1
        self.uppers = jnp.stack([upper_half(1 << bit) for bit in range(bits)])

    def turn(self, array):
        if self.last is not None:
            array = lax.optimization_barrier((array, self.last))[0]
        return array

    def done(self, array):
        self.last = array


def axis_of(bits, mask):
    return sum(b > mask for b in bits)


def bit_shape(bits, rows):
    return (2,) * len(bits) + tuple(rows)


def cut_of(rank, cut):
    by_lanes, part = cut
    last = (slice(None), part) if by_lanes else (part, slice(None))
    return (slice(None),) * (rank - 2) + last


def at_bit(rank, axis, index, cut):
    where = list(cut_of(rank, cut))
    where[axis] = pl.ds(index, 1)
    return tuple(where)


def cut_shape(shape, by_lanes, size):
    return (shape[0], size) if by_lanes else (size, shape[1])


def overlaps(lefts, rights):
    found, left_at = [], 0
    for i, left in enumerate(lefts):
        right_at = 0
        for j, right in enumerate(rights):
            low = max(left_at, right_at)
            high = min(left_at + left, right_at + right)
            if low < high:
                found.append(
                    (i, j, slice(low - left_at, high - left_at), slice(low - right_at, high - right_at))
                )
            right_at += right
        left_at += left
    return found


def place_kernel(axes, masks, cuts, uppers, *refs):
    count = len(axes)
    for i, j, inside, outside in cuts:
        mine, other, out = refs[2 * i], refs[2 * i + 1], refs[2 * count + j]
        rank, axis, at = len(out.shape), axes[i], uppers[masks[i].bit_length() - 1]
        source = cut_of(rank - 1, inside)
        out[at_bit(rank, axis, at, outside)] = jnp.expand_dims(mine[source], axis)
        out[at_bit(rank, axis, 1 - at, outside)] = jnp.expand_dims(other[source], axis)


def add_kernel(axes, masks, cuts, count, uppers, *refs):
    for i, j, inside, outside in cuts:
        keep, other = refs[2 * i], refs[2 * i + 1]
        next_keep, next_send = refs[2 * count + 2 * j], refs[2 * count + 2 * j + 1]
        rank, axis, at = len(keep.shape), axes[j], uppers[masks[j].bit_length() - 1]
        into = cut_of(rank - 1, outside)
        here, there = at_bit(rank, axis, at, inside), at_bit(rank, axis, 1 - at, inside)
        next_send[into] = jnp.squeeze(keep[there] + other[there], axis)
        next_keep[into] = jnp.squeeze(keep[here] + other[here], axis)


def place(order, *jobs):
    axes, masks, cuts, args, outs, plans = [], [], [], [], [], []
    for gather, sizes in jobs:
        lanes = gather.by_lanes
        whole = (gather.rows, gather.width)
        olds = [p.shape[-1 if lanes else -2] for p in gather.parts]
        sizes = sizes or olds
        bits = [sorted(b + [m], reverse=True) for b, m in zip(gather.bits, gather.masks)]
        own_axes = [axis_of(b, m) for b, m in zip(gather.bits, gather.masks)]
        bits = [bits[min(j, len(bits) - 1)] for j in range(len(sizes))]
        found = overlaps(olds, sizes)
        plans.append((gather, olds, sizes, bits, own_axes, len(outs)))
        cuts += [(len(axes) + i, len(outs) + j, (lanes, x), (lanes, y)) for i, j, x, y in found]
        axes += own_axes
        masks += gather.masks
        for mine, other in zip(gather.parts, gather.others):
            args += [order.turn(mine), other]
        outs += [(bit_shape(b, cut_shape(whole, lanes, r)), BF16) for b, r in zip(bits, sizes)]
    if device_count() == GROUPS:
        body = functools.partial(place_kernel, axes, masks, cuts)
        placed = kernel(body, (order.uppers, *args), outs, 0, 24)
        order.done(placed[0])
    for gather, olds, sizes, bits, own_axes, at in plans:
        if device_count() == GROUPS:
            parts = placed[at : at + len(sizes)]
        else:
            held = []
            sides = zip(gather.parts, gather.others, own_axes, gather.masks)
            for mine, other, axis, mask in sides:
                up = upper_half(mask)
                low, high = jnp.where(up, other, mine), jnp.where(up, mine, other)
                held.append(jnp.stack([low, high], axis=axis))
            parts = cut_parts(held, olds, sizes, gather.by_lanes)
        gather.parts, gather.bits = parts, bits


def add(order, *jobs):
    axes, all_masks, cuts, args, outs, plans, count = [], [], [], [], [], [], 0
    for chain, masks, sizes in jobs:
        lanes = chain.by_lanes
        whole = (chain.rows, chain.width)
        olds = [p.shape[-1 if lanes else -2] for p in chain.keeps]
        sizes = sizes or olds
        bits = [chain.bits[min(j, len(olds) - 1)] for j in range(len(sizes))]
        own_axes = [axis_of(b, m) for b, m in zip(bits, masks)]
        left = [[b for b in old if b != m] for old, m in zip(bits, masks)]
        plans.append((chain, masks, olds, sizes, own_axes, left, len(axes)))
        found = overlaps(olds, sizes)
        cuts += [(count + i, len(axes) + j, (lanes, x), (lanes, y)) for i, j, x, y in found]
        axes += own_axes
        all_masks += masks
        count += len(olds)
        for keep, other in zip(chain.keeps, chain.others):
            args += [order.turn(keep), other]
        for b, r in zip(left, sizes):
            outs += [(bit_shape(b, cut_shape(whole, lanes, r)), BF16)] * 2
    if device_count() == GROUPS:
        body = functools.partial(add_kernel, axes, all_masks, cuts, count)
        both = kernel(body, (order.uppers, *args), outs, 0, 24)
        order.done(both[0])
    for chain, masks, olds, sizes, own_axes, left, at in plans:
        if device_count() == GROUPS:
            found = both[2 * at : 2 * (at + len(sizes))]
            chain.keeps, chain.sends = found[0::2], found[1::2]
        else:
            sums = [
                (k.astype(F32) + o.astype(F32)).astype(BF16)
                for k, o in zip(chain.keeps, chain.others)
            ]
            sums = cut_parts(sums, olds, sizes, chain.by_lanes)
            sides = list(zip(sums, [upper_half(m) for m in masks], own_axes))
            take = lax.dynamic_index_in_dim
            chain.keeps = [take(t, u, axis, False) for t, u, axis in sides]
            chain.sends = [take(t, 1 - u, axis, False) for t, u, axis in sides]
        chain.bits = left


class Gather:
    def __init__(self, order, part, by_lanes=False):
        self.order, self.parts, self.bits = order, [part], [[]]
        self.by_lanes, (self.rows, self.width) = by_lanes, part.shape

    def go(self, *masks, wait=False):
        self.masks = masks
        parts = [self.order.turn(p) for p in self.parts] if wait else self.parts
        self.others = [swap(p, m) for p, m in zip(parts, masks)]

    def place(self, *sizes):
        place(self.order, (self, sizes))
        return self

    def whole(self):
        held = self.parts[0]
        return held.reshape((-1,) + held.shape[-2:])


def cut_parts(arrays, olds, sizes, by_lanes):
    if list(olds) == list(sizes):
        return arrays
    axis = -1 if by_lanes else -2
    joint = jnp.concatenate(arrays, axis=axis)
    ends = [sum(sizes[: j + 1]) for j in range(len(sizes) - 1)]
    return jnp.split(joint, ends, axis=axis)


class Reduce:
    def __init__(self, order, keep, send, bits, by_lanes=False):
        shape = bit_shape(bits, keep.shape[-2:])
        self.order, self.bits = order, [bits]
        self.by_lanes, (self.rows, self.width) = by_lanes, keep.shape[-2:]
        self.keeps, self.sends = [keep.reshape(shape)], [send.reshape(shape)]

    def go(self, *masks, wait=False):
        sends = [self.order.turn(p) for p in self.sends] if wait else self.sends
        self.others = [swap(p, m) for p, m in zip(sends, masks)]

    def add(self, masks, *sizes):
        add(self.order, (self, masks, sizes))
        return self

    def total(self):
        keep, other = self.keeps[0], self.others[0]
        return (keep.astype(F32) + other.astype(F32)).reshape(keep.shape[-2:])


def split_cores(blocks):
    pairs = blocks.reshape((-1, 2) + blocks.shape[1:])
    upper = upper_half(1)
    keep = lax.dynamic_index_in_dim(pairs, upper, 1, keepdims=False)
    return keep, lax.dynamic_index_in_dim(pairs, 1 - upper, 1, keepdims=False)


def joined(keep, send):
    return jnp.stack([keep, send], axis=1).reshape((-1,) + keep.shape[1:])


def grouped(buffer, sizes):
    count = buffer.shape[0]
    if count == GROUPS:
        return buffer
    width = buffer.shape[-1]
    share = width // count
    parts, start = [], 0
    for size in sizes:
        part = buffer[:, start : start + share * size]
        parts.append(part.reshape(GROUPS, UNIT * size, width))
        start += share * size
    return jnp.concatenate(parts, axis=1)


def scattered(buffer, sizes):
    count, width = device_count(), buffer.shape[-1]
    if count == GROUPS:
        return buffer
    parts, start = [], 0
    for size in sizes:
        part = buffer[:, start : start + UNIT * size]
        parts.append(part.reshape(count, width // count * size, width))
        start += UNIT * size
    return jnp.concatenate(parts, axis=1)


def vector_pack(vectors, rows, width):
    filled = jnp.pad(vectors, ((0, 0), (0, width - vectors.shape[1])))
    return jnp.pad(filled[:, None], ((0, 0), (0, rows - 1), (0, 0)))


def vector_regroup(vectors, parts, lengths):
    pieces, start = [], 0
    for length in lengths:
        pieces.append(vectors[:, start : start + length].reshape(parts, -1))
        start += length
    return jnp.concatenate(pieces, axis=1)


def dot(a, b, dims=((1,), (0,))):
    return lax.dot_general(a, b, (dims, ((), ())), preferred_element_type=F32)


def iota(shape, axis):
    return lax.broadcasted_iota(jnp.int32, shape, axis)


def tile(ref, place, size=1):
    rows = ref[:, UNIT * place : UNIT * (place + size), :]
    return rows.reshape(GROUPS * UNIT * size, rows.shape[-1])


def pack_kernel(moves, counts, *refs):
    inputs, outs, sems = refs[: counts[0]], refs[counts[0] : -1], refs[-1]
    copies = []
    for at, (source, where, out, start, rows) in enumerate(moves):
        into = outs[out].at[pl.ds(start, rows)]
        piece = inputs[source] if where is None else inputs[source].at[where]
        copies.append(pltpu.make_async_copy(piece, into, sems.at[at]))
        copies[-1].start()
    for copy in copies:
        copy.wait()


def packed(args, moves, shapes):
    return pl.pallas_call(
        functools.partial(pack_kernel, moves, (len(args),)),
        in_specs=[pl.BlockSpec(memory_space=pltpu.HBM) for _ in args],
        out_specs=[pl.BlockSpec(memory_space=pltpu.VMEM) for _ in shapes],
        out_shape=[jax.ShapeDtypeStruct(shape, BF16) for shape in shapes],
        scratch_shapes=[pltpu.SemaphoreType.DMA((len(moves),))],
        compiler_params=pltpu.CompilerParams(vmem_limit_bytes=62 << 20),
    )(*args)


def kernel(body, args, outs, flops, limit, scratch=()):
    spec = {jnp.dtype(jnp.int32): pltpu.SMEM}
    return pl.pallas_call(
        body,
        in_specs=[pl.BlockSpec(memory_space=spec.get(a.dtype, pltpu.VMEM)) for a in args],
        out_specs=[pl.BlockSpec(memory_space=pltpu.VMEM) for _ in outs],
        out_shape=[jax.ShapeDtypeStruct(shape, dtype) for shape, dtype in outs],
        scratch_shapes=list(scratch),
        compiler_params=pltpu.CompilerParams(vmem_limit_bytes=limit << 20),
        cost_estimate=pl.CostEstimate(
            flops=flops,
            bytes_accessed=sum(a.size * a.dtype.itemsize for a in args),
            transcendentals=0,
        ),
    )(*args)


def unit_norm(values):
    center = values - jnp.mean(values, axis=-1, keepdims=True)
    spread = jnp.mean(center * center, axis=-1, keepdims=True)
    inverse = lax.rsqrt(spread + EPSILON)
    return center * inverse, inverse


def norm_back(grad, unit, inverse, gain):
    e = grad * gain
    mean_e = jnp.mean(e, axis=-1, keepdims=True)
    mean_x = jnp.mean(e * unit, axis=-1, keepdims=True)
    return inverse * (e - mean_e - unit * mean_x)


def column_sum(values):
    return jnp.sum(values, axis=0, keepdims=True)


def valid_column(info, m, start, rows):
    place = start + iota((rows, 1), 0)
    first = (place >= 1) & (place < info[m, 0])
    second = (place >= info[m, 1]) & (place < info[m, 2])
    return jnp.where(first | second, 1.0, 0.0).astype(F32)


def segment_start(info, m, place):
    start = jnp.where(place >= 1, 1, 0)
    start = jnp.where(place >= info[m, 1], info[m, 1], start)
    return jnp.where(place >= info[m, 3], info[m, 3], start)


VECTORS = 5
BIAS_AT = VECTORS * UNIT


def vector_maps(width):
    lanes = width // 2
    fine = (iota((lanes, width), 0) & 15) == (iota((lanes, width), 1) & 15)
    wide = ((iota((lanes, width), 0) + 48) & 63) == (iota((lanes, width), 1) & 63)
    own_fine = iota((GROUPS, width), 1) >> 4 == iota((GROUPS, width), 0)
    own_wide = iota((GROUPS, width), 1) >> 6 == (iota((GROUPS, width), 0) & 7)
    as_bf16 = [jnp.where(m, 1.0, 0.0).astype(BF16) for m in (fine, wide)]
    as_f32 = [jnp.where(m, 1.0, 0.0).astype(F32) for m in (own_fine, own_wide)]
    return as_bf16 + as_f32


def lane_window(lanes, k):
    place = iota((GROUPS, lanes), 1)
    if k == VECTORS:
        return (place >= BIAS_AT) & (place < BIAS_AT + 64)
    return (place >= UNIT * k) & (place < UNIT * (k + 1))


def line_cuts(line):
    micro, cuts = line.shape[:2]
    found = [(m, c) for m in range(micro) for c in range(cuts)]
    return [(m, c, slice(128 * c, 128 * (c + 1))) for m, c in found]


def keep_and_compress(info, low, weights, kept, window, memory, line):
    micro = info.shape[0]
    each = low.shape[0] // micro - RIM
    slots = each // 3
    count = micro * each
    valid = [valid_column(info, m, info[m, 4], each) for m in range(micro)]
    valid += [valid_column(info, m, info[m, 4] - RIM, RIM) for m in range(micro)]
    rows = (dot(low, tile(weights, 0)) * jnp.concatenate(valid, axis=0)).astype(BF16)
    kept[...] = rows[:count]
    rows = rows.astype(F32)
    for m, cut, cols in line_cuts(line):
        line[m, cut, :RIM] = rows[count + RIM * m : count + RIM * (m + 1), cols]
        line[m, cut, RIM:] = rows[each * m : each * (m + 1), cols]
    total = None
    for tap in range(3):
        start = RIM - 2 + tap
        for m, cut, cols in line_cuts(line):
            taken = line[m, cut, pl.ds(start, slots, stride=3), :]
            window[tap, slots * m : slots * (m + 1), cols] = taken.astype(BF16)
        part = dot(window[tap], tile(weights, 1 + tap))
        total = part if total is None else total + part
    memory[...] = total.astype(BF16)


def key_kernel(info, tok, halo, weights, normed, kept, window, memory, vec, line):
    width = tok.shape[-1]
    lanes = width // 2
    fine, wide, own_fine, own_wide = vector_maps(width)
    rows = jnp.sum(weights[:, 4 * UNIT : 5 * UNIT, :lanes].astype(F32), axis=1)
    picked = [jnp.where(lane_window(lanes, k), rows, 0.0) for k in range(VECTORS + 1)]
    spread = dot(jnp.concatenate(picked[:VECTORS], axis=0).astype(BF16), fine)
    vectors = [
        column_sum(spread[GROUPS * k : GROUPS * (k + 1)] * own_fine) for k in range(VECTORS)
    ]
    bias = dot(picked[VECTORS].astype(BF16), wide) * own_wide
    bias = jnp.sum(bias.reshape(4, 8, width), axis=1)
    vec[...] = jnp.concatenate(vectors + [bias, jnp.zeros((7, width), F32)], axis=0)
    values = jnp.concatenate([tok[...], halo[...]], axis=0).astype(F32)
    unit, _ = unit_norm(values)
    low = (unit * vectors[0] + vectors[1]).astype(BF16)
    normed[...] = low
    keep_and_compress(info, low, weights, kept, window, memory, line)


def value_kernel(info, normed, weights, query, kept, window, memory, line):
    low = normed[...]
    keep_and_compress(info, low, weights, kept, window, memory, line)
    query[...] = dot(low[: query.shape[0]], tile(weights, 4)).astype(BF16)


def stacked(values, lower):
    zero = jnp.zeros_like(values)
    return jnp.concatenate(
        [jnp.where(lower, values, zero), jnp.where(lower, zero, values)], axis=0
    )


def merged(values, lower):
    half = values.shape[0] // 2
    return jnp.where(lower, values[:half], values[half:])


def reach(blocks, each):
    row = blocks * each
    size = (row - 2 - LEAST_ITEM) // each + 1
    size = min(size + size % 2, blocks)
    skipped = (LEAST_ITEM + 3) // 3 // (each // 3)
    return size if blocks - size <= skipped else blocks


def memory_pair(memory, first, size, m, pair, micro):
    slots = memory.shape[1] // micro
    rows, cols = slice(slots * m, slots * (m + 1)), slice(PAIR * pair, PAIR * (pair + 1))
    return memory[pl.ds(first, size), rows, cols].reshape(size * slots, PAIR)


def attend_kernel(info, query, keys, values, memory_keys, memory_values, attended, stats):
    micro = info.shape[0]
    count, width = query.shape
    each = count // micro
    blocks, share = memory_keys.shape[0], memory_keys.shape[1] // micro
    size = reach(blocks, each)
    slots = size * share
    pairs = width // PAIR
    lower = iota((each, PAIR), 1) < HEAD_DIM
    lane = iota((2 * each, 128), 1)
    found = jnp.zeros((2 * each, 128), F32)
    ones = jnp.ones((slots, PAIR), BF16)
    for m in range(micro):
        rows = slice(each * m, each * (m + 1))
        place = info[m, 4] + iota((each, 1), 0)
        start = segment_start(info, m, place)
        begin = jnp.where(info[m, 4] < info[m, 1], 0, blocks - size)
        end = 3 * (share * begin + iota((each, slots), 1))
        bias = jnp.where((end <= place) & (end >= start), 0.0, MASKED).astype(F32)
        bias = jnp.concatenate([bias, bias], axis=0)
        for pair in range(pairs):
            cols = slice(PAIR * pair, PAIR * (pair + 1))
            key = keys[rows, cols].astype(F32)
            value = values[rows, cols].astype(F32)
            queries = stacked(query[rows, cols].astype(F32) * SCALE, lower)
            own = jnp.sum(queries * jnp.concatenate([key, key], axis=0), axis=1, keepdims=True)
            memory_key = memory_pair(memory_keys, begin, size, m, pair, micro)
            memory_value = memory_pair(memory_values, begin, size, m, pair, micro)
            scores = dot(queries.astype(BF16), memory_key, NT) + bias
            top = jnp.maximum(jnp.max(scores, axis=1, keepdims=True), own)
            expos = jnp.exp(scores - top)
            own = jnp.exp(own - top)
            beside = jnp.concatenate([memory_value, ones], axis=1)
            mixed = dot(expos.astype(BF16), beside)
            total = mixed[:, PAIR:] + own
            inverse = 1.0 / total
            weight = own * inverse
            mixed = mixed[:, :PAIR] * inverse
            attended[rows, cols] = merged(mixed, lower) + merged(weight, lower) * value
            found = jnp.where(lane == m * pairs + pair, top + jnp.log(total), found)
    stats[...] = found


def gelu_parts(hidden):
    falling = jnp.exp(hidden * hidden * -0.5)
    step = 1.0 / (1.0 + (ERF_STEP * 0.7071067811865476) * jnp.abs(hidden))
    tail = 0.5 * ERF_TERMS[0]
    for term in ERF_TERMS[1:]:
        tail = tail * step + 0.5 * term
    tail = tail * step * falling
    return jnp.where(hidden >= 0.0, 1.0 - tail, tail), falling


def even_first(flag, rows, size):
    pairs = rows.reshape(-1, 2, size, rows.shape[-1])
    even, odd = pairs[:, 0], pairs[:, 1]
    halves = [jnp.where(flag == 0, even, odd), jnp.where(flag == 0, odd, even)]
    return jnp.concatenate(halves, axis=0).reshape(rows.shape)


def deal(value, rows, keep, send, blocks, start):
    halves = value.astype(BF16).reshape(2, -1, rows, value.shape[-1])
    keep[blocks, start : start + rows, :] = halves[0]
    send[blocks, start : start + rows, :] = halves[1]


def deal_tile(value, place, keep, send):
    deal(value, UNIT, keep, send, slice(None), UNIT * place)


def feed_kernel(
    info,
    tok,
    cot,
    attended,
    vec,
    rest,
    out,
    grad_mid,
    grad_att,
    keep,
    send,
    vec_grad,
):
    count, width = tok.shape
    wide = 4
    low_att = attended[...].astype(BF16)
    w_out = tile(rest, 0)
    middle = tok[...].astype(F32) + dot(low_att, w_out)
    unit, inverse = unit_norm(middle)
    gain = vec[2:3, :]
    low = (unit * gain + vec[3:4, :]).astype(BF16)
    flag = info[0, 5]
    low_t = even_first(flag, low.T, UNIT)
    cots = cot[...]
    total = middle + vec[4:5, :]
    grad_low = jnp.zeros((count, width), F32)
    bias_rows = []
    eighth = GROUPS // wide
    for c in range(wide):
        w_up = tile(rest, 1 + c)
        down = slice(eighth * c, eighth * (c + 1))
        w_down = rest[down, UNIT * (1 + wide) :, :].reshape(width, width)
        hidden = dot(low, w_up) + vec[5 + c : 6 + c, :]
        share, falling = gelu_parts(hidden)
        slope = share + (0.3989422804014327 * hidden) * falling
        active = (hidden * share).astype(BF16)
        total = total + dot(active, w_down)
        grad_hidden_f = dot(cots, w_down, NT) * slope
        grad_hidden = grad_hidden_f.astype(BF16)
        bias_rows.append(column_sum(grad_hidden.astype(F32)))
        grad_low = grad_low + dot(grad_hidden, w_up, NT)
        deal_tile(dot(low_t, grad_hidden), 1 + c, keep, send)
        where = slice(eighth // 2 * c, eighth // 2 * (c + 1))
        active_t = even_first(flag, active.T, UNIT * wide)
        deal(dot(active_t, cots), UNIT * wide, keep, send, where, UNIT * (1 + wide))
    out[...] = total.astype(BF16)
    cots_f = cots.astype(F32)
    grad_middle = cots_f + norm_back(grad_low, unit, inverse, gain)
    grad_mid[...] = grad_middle
    branch = grad_middle.astype(BF16)
    deal_tile(dot(even_first(flag, low_att.T, UNIT), branch), 0, keep, send)
    grad_att[...] = dot(branch, w_out, NT).astype(BF16)
    rows = [jnp.zeros((2, width), F32), column_sum(grad_low * unit), column_sum(grad_low)]
    rows += [column_sum(cots_f)] + bias_rows + [jnp.zeros((7, width), F32)]
    vec_grad[...] = jnp.concatenate(rows, axis=0)


def memory_turned(flag, memory, first, size, m, pair, micro):
    slots = memory.shape[2] // micro
    rows, cols = slice(slots * m, slots * (m + 1)), slice(PAIR * pair, PAIR * (pair + 1))
    halves = [memory[pl.ds(first, size), pl.ds(at, 1), rows, cols] for at in (flag, 1 - flag)]
    return jnp.concatenate([h.reshape(-1, PAIR) for h in halves], axis=0)


def attend_back_kernel(
    info,
    query,
    keys,
    values,
    memory_keys,
    memory_values,
    attended,
    stats,
    grad_att,
    grad_query,
    key_keep,
    key_send,
    value_keep,
    value_send,
    own_key,
    own_value,
):
    micro = info.shape[0]
    count, width = query.shape
    each = count // micro
    chips = memory_keys.shape[0]
    share = memory_keys.shape[2] // micro
    size = reach(2 * chips, each) // 2
    slots = 2 * size * share
    flag = info[0, 6]
    pairs = width // PAIR
    lower = iota((each, PAIR), 1) < HEAD_DIM
    lane = iota((2 * each, 128), 1)
    found = stats[...]
    deltas = jnp.zeros((2 * each, 128), F32)
    parts = {}
    for m in range(micro):
        rows = slice(each * m, each * (m + 1))
        for pair in range(pairs):
            cols = slice(PAIR * pair, PAIR * (pair + 1))
            grad = grad_att[rows, cols].astype(F32)
            product = stacked(grad * attended[rows, cols], lower)
            delta = jnp.sum(product, axis=1, keepdims=True)
            deltas = jnp.where(lane == m * pairs + pair, delta, deltas)
            parts[m, pair] = delta
    found_t, deltas_t = found.T, deltas.T
    for m in range(micro):
        rows = slice(each * m, each * (m + 1))
        lanes = iota((1, 2 * each), 1)
        place = info[m, 4] + jnp.where(lanes >= each, lanes - each, lanes)
        start = segment_start(info, m, place)
        row = iota((slots, 1), 0)
        late = row >= size * share
        row = jnp.where(late, row - size * share, row)
        front = info[m, 4] < info[m, 1]
        begin = jnp.where(front, 0, chips - size)
        block = jnp.zeros((slots, 1), jnp.int32) + 2 * begin
        for chip in range(1, size):
            block = block + jnp.where(row >= share * chip, 1, 0)
        core = jnp.where(late, 1 - flag, flag)
        end = 3 * (row + share * (block + core))
        bias = jnp.where((end <= place) & (end >= start), 0.0, MASKED).astype(F32)
        if size < chips:
            empty = pl.ds(jnp.where(front, size, 0), chips - size)
            zeros = jnp.zeros((chips - size, share, width), BF16)
            for half in (key_keep, key_send, value_keep, value_send):
                half[empty, share * m : share * (m + 1), :] = zeros
        for pair in range(pairs):
            cols = slice(PAIR * pair, PAIR * (pair + 1))
            at = m * pairs + pair
            key = keys[rows, cols].astype(F32)
            value = values[rows, cols].astype(F32)
            query_f = query[rows, cols].astype(F32) * SCALE
            grad_f = grad_att[rows, cols].astype(F32)
            queries = stacked(query_f, lower)
            grads = stacked(grad_f, lower)
            own = jnp.sum(queries * jnp.concatenate([key, key], axis=0), axis=1, keepdims=True)
            own = jnp.exp(own - found[:, at : at + 1])
            grad_own = jnp.sum(
                grads * jnp.concatenate([value, value], axis=0), axis=1, keepdims=True
            )
            grad_own = (own * (grad_own - parts[m, pair])).astype(BF16).astype(F32)
            queries, grads = queries.astype(BF16), grads.astype(BF16)
            memory_key = memory_turned(flag, memory_keys, begin, size, m, pair, micro)
            memory_value = memory_turned(flag, memory_values, begin, size, m, pair, micro)
            scores = dot(memory_key, queries, NT) + bias
            probs = jnp.exp(scores - found_t[at : at + 1, :])
            grad_probs = dot(memory_value, grads, NT)
            grad_scores = (probs * (grad_probs - deltas_t[at : at + 1, :])).astype(BF16)
            sides = (
                (dot(grad_scores, queries), key_keep, key_send),
                (dot(probs.astype(BF16), grads), value_keep, value_send),
            )
            for grad, keep, send in sides:
                halves = grad.astype(BF16).reshape(2, size, share, PAIR)
                into = (pl.ds(begin, size), slice(share * m, share * (m + 1)), cols)
                keep[into] = halves[0]
                send[into] = halves[1]
            turned = dot(memory_key.T, grad_scores).T
            own_grad = merged(jnp.broadcast_to(grad_own, (2 * each, PAIR)), lower)
            own_weight = merged(jnp.broadcast_to(own, (2 * each, PAIR)), lower)
            grad_query[rows, cols] = (
                SCALE * (merged(turned, lower) + own_grad * key)
            ).astype(BF16)
            own_key[rows, cols] = own_grad * query_f
            own_value[rows, cols] = own_weight * grad_f


def compress_back_kernel(
    info,
    key_memory,
    value_memory,
    key_window,
    value_window,
    key_weights,
    value_weights,
    normed,
    grad_query,
    key_grad,
    value_grad,
    rims,
    keep,
    send,
    line,
):
    micro = info.shape[0]
    count, width = key_grad.shape
    each = count // micro
    flag = info[0, 5]
    own_slots = each // 3
    edge = iota((RIM, width), 0) >= RIM - 2
    sides = (
        (key_memory, key_window, key_weights, key_grad),
        (value_memory, value_window, value_weights, value_grad),
    )
    for kind, (memory, window, weights, out) in enumerate(sides):
        grad = memory[...]
        for tap in range(3):
            window_t = even_first(flag, window[tap].T, UNIT)
            deal_tile(dot(window_t, grad), 4 * kind + tap, keep, send)
            part = dot(grad, tile(weights, 1 + tap), NT)
            for m, cut, cols in line_cuts(line):
                rows = slice(own_slots * m, own_slots * (m + 1))
                line[m, cut, pl.ds(tap, own_slots, stride=3), :] = part[rows, cols]
        for m, cut, cols in line_cuts(line):
            out[each * m : each * (m + 1), cols] = line[m, cut]
        for m in range(micro):
            first = pltpu.roll(out[each * m : each * m + RIM, :], RIM - 2, 0)
            into = (slice(RIM * m, RIM * (m + 1)), slice(width * kind, width * (kind + 1)))
            rims[into] = jnp.where(edge, first, 0.0)
    low_t = even_first(flag, normed[:count, :].T, UNIT)
    deal_tile(dot(low_t, grad_query[...]), 3, keep, send)


def input_kernel(
    info,
    tok,
    normed,
    grad_query,
    key_grad,
    value_grad,
    rims,
    own_key,
    own_value,
    key_weights,
    value_weights,
    vec,
    grad_mid,
    vec_grad,
    grad_in,
    keep,
    send,
    total,
):
    count, width = tok.shape
    micro = info.shape[0]
    each = count // micro
    valid = [valid_column(info, m, info[m, 4], each) for m in range(micro)]
    valid = jnp.concatenate(valid, axis=0)
    flag = info[0, 5]
    low_t = even_first(flag, normed[:count, :].T, UNIT)
    grad_low = dot(grad_query[...], tile(value_weights, 4), NT)
    inner = iota((each, width), 0) < each - 2
    sides = ((key_grad, own_key, key_weights), (value_grad, own_value, value_weights))
    for kind, (grad, own, weights) in enumerate(sides):
        for m in range(micro):
            rows = slice(each * m, each * (m + 1))
            moved = pltpu.roll(grad[rows, :], each - 2, 0)
            total[rows, :] = jnp.where(inner, moved, 0.0) + own[rows, :]
            rows = slice(each * (m + 1) - RIM, each * (m + 1))
            rim = rims[RIM * m : RIM * (m + 1), width * kind : width * (kind + 1)]
            total[rows, :] = total[rows, :] + rim
        low_grad = (total[...] * valid).astype(BF16)
        grad_low = grad_low + dot(low_grad, tile(weights, 0), NT)
        deal_tile(dot(low_t, low_grad), kind, keep, send)
    unit, inverse = unit_norm(tok[...].astype(F32))
    back = norm_back(grad_low, unit, inverse, vec[0:1, :])
    grad_in[...] = (grad_mid[...] + back).astype(BF16)

    lanes = width // 2
    fine, wide, own_fine, own_wide = vector_maps(width)
    vectors = [column_sum(grad_low * unit), column_sum(grad_low)]
    vectors += [vec_grad[k : k + 1, :] for k in range(2, VECTORS)]
    dealt = jnp.concatenate([own_fine * v for v in vectors], axis=0).astype(BF16)
    dealt = dot(dealt, fine, NT)
    bias = [
        jnp.broadcast_to(vec_grad[VECTORS + c : VECTORS + c + 1, :], (8, width)) for c in range(4)
    ]
    bias = (jnp.concatenate(bias, axis=0) * own_wide).astype(BF16)
    packed = jnp.where(lane_window(lanes, VECTORS), dot(bias, wide, NT), 0.0)
    for k in range(VECTORS):
        packed = jnp.where(lane_window(lanes, k), dealt[GROUPS * k : GROUPS * (k + 1)], packed)
    packed = jnp.concatenate([packed, jnp.zeros((GROUPS, width - lanes), F32)], axis=1)
    spot = iota((GROUPS, UNIT, width), 1) == 0
    spread = jnp.broadcast_to(packed[:, None, :], (GROUPS, UNIT, width))
    packed = jnp.where(spot, spread, 0.0).reshape(GROUPS * UNIT, width)
    deal_tile(even_first(flag, packed, UNIT), 2, keep, send)


def per_device(
    tokens,
    lengths,
    ln1_gain,
    ln1_bias,
    w_query,
    w_key,
    w_value,
    conv_key,
    conv_value,
    w_out,
    ln2_gain,
    ln2_bias,
    w_up,
    b_up,
    w_down,
    b_down,
    cotangent,
):
    count = device_count()
    micro, _, each, width = tokens.shape
    ff = w_up.shape[1]
    wide = ff // width
    share = width // count
    seq = lax.axis_size("seq")
    all_tokens = micro * each
    slots = micro * each // 3
    memory_bytes = 4 * seq * slots * width

    whole = count == GROUPS
    vector_lengths = [share] * VECTORS + [ff // count]
    vectors, start = 0.0, 0
    for part in (ln1_gain, ln1_bias, ln2_gain, ln2_bias, b_down, b_up):
        end = start + part.shape[0]
        pad = ((0, (UNIT if whole else 2) - 1), (start, width - end))
        vectors, start = vectors + jnp.pad(part[None], pad), end
    vectors = vectors.astype(BF16)
    across = powers(seq, count)
    along = powers(2, seq)[::-1]
    back = along[::-1]
    order = Order()
    if whole:
        moves = [(kind, None, kind, 0, UNIT) for kind in range(2)]
        moves += [(2 + k, tap, k, UNIT * (1 + tap), UNIT) for k in range(2) for tap in range(3)]
        moves += [(4 + kind, None, kind, 4 * UNIT, UNIT) for kind in range(2)]
        moves += [(6, None, 2, 0, UNIT)]
        for c in range(wide):
            cols = (slice(None), pl.ds(width * c, width))
            moves.append((7, cols, 2, UNIT * (1 + c), UNIT))
        moves.append((8, None, 2, UNIT * (1 + wide), UNIT * wide))
        rows = (5 * UNIT, 5 * UNIT, (1 + 2 * wide) * UNIT)
        args = (w_key, w_value, conv_key, conv_value, vectors, w_query, w_out, w_up, w_down)
        first, second, rest = packed(args, moves, [(r, width) for r in rows])
    else:
        first = jnp.concatenate([w_key, *conv_key, vectors], axis=0)
        second = jnp.concatenate([w_value, *conv_value, w_query], axis=0)
        ups = [w_up[:, width * c : width * (c + 1)] for c in range(wide)]
        rest = jnp.concatenate([w_out] + ups + [w_down], axis=0)
    one, two, both = Gather(order, first), Gather(order, second), Gather(order, rest, True)
    one.go(along[0])
    two.go(back[0])
    for at in range(1, len(along)):
        one.place()
        if at == 1:
            last_rows = order.turn(tokens[:, 0, each - RIM :])
            halo = lax.ppermute(last_rows, "seq", [(i, i + 1) for i in range(seq - 1)])
            halo = halo.reshape(micro * RIM, width)
        one.go(along[at])
        two.place()
        two.go(back[at])
    order.done((halo, rest))
    one.place()
    one.go(across[0])
    two.place()
    two.go(across[-1])
    both.go(along[0], wait=True)
    for at in range(1, max(len(across), len(along))):
        jobs = []
        if at < len(across):
            one.place()
            one.go(across[at])
            jobs.append((two, ()))
        if at < len(along):
            jobs.append((both, ()))
        place(order, *jobs)
        if at < len(across):
            two.go(across[-1 - at])
        if at < len(along):
            both.go(along[at])
    lengths = order.turn(lengths[:, 0])
    first_pad = 3 * ((lengths[:, 0] + 2) // 3)
    second_pad = 3 * ((lengths[:, 1] + 2) // 3)
    start = 1 + first_pad
    seats = [lax.axis_index("seq") * each, upper_half(1) if whole else 0, upper_half(1)]
    seats = [jnp.full_like(start, seat) for seat in seats]
    info = [1 + lengths[:, 0], start, start + lengths[:, 1], start + second_pad]
    info = jnp.stack(info + seats, axis=1).astype(jnp.int32)
    order.done((order.last, info))
    one.place()
    one.go(1)
    place(order, (two, ()), (both, (width // 2, width // 2)))
    two.go(1)
    both.go(across[0], across[-1])
    first = one.place().whole()
    first_sizes, rest_sizes = [1] * 5, [1] * (1 + wide) + [wide]
    if not whole:
        dealt = vector_regroup(first[:, 4 * share], GROUPS, vector_lengths)
        dealt = vector_pack(dealt, UNIT, width)
        first = jnp.concatenate([grouped(first, [1] * 4), dealt], axis=1)

    tok = tokens.reshape(all_tokens, width)
    cot = cotangent.reshape(all_tokens, width)
    rows = (all_tokens, width)
    grown = 4 * max(memory_bytes // (1 << 20) - 2, 0)
    limits = [16, 16, 16 + grown, 28, 28 + grown, 28, 28]
    matmul = 2 * all_tokens * width * width

    padded = (all_tokens + micro * RIM, width)
    windows = (3, slots, width)
    line = (pltpu.VMEM((micro, width // 128, RIM + each, 128), F32),)

    normed, keys, key_window, memory_key, vec = kernel(
        key_kernel,
        (info, order.turn(tok), halo, first),
        ((padded, BF16), (rows, BF16), (windows, BF16), ((slots, width), BF16), ((16, width), F32)),
        2 * matmul,
        limits[0],
        line,
    )
    order.done(memory_key)
    keys_side = Gather(order, memory_key)
    keys_side.go(along[0])
    second = grouped(two.place().whole(), first_sizes)
    query, values, value_window, memory_value = kernel(
        value_kernel,
        (info, normed, second),
        ((rows, BF16), (rows, BF16), (windows, BF16), ((slots, width), BF16)),
        3 * matmul,
        limits[1],
        line,
    )
    order.done(memory_value)
    values_side = Gather(order, memory_value)
    values_side.go(back[0])
    for at in range(1, max(len(across), len(along))):
        jobs = []
        if at < len(along):
            jobs += [(keys_side, ()), (values_side, ())]
        if at < len(across):
            jobs.append((both, ()))
        place(order, *jobs)
        if at < len(along):
            keys_side.go(along[at])
            values_side.go(back[at])
        if at < len(across):
            both.go(across[at], across[-1 - at])
    place(order, (keys_side, ()), (values_side, ()), (both, (width,)))
    keys_side.go(1)
    values_side.go(1)
    both.go(1)
    memories = [keys_side.place().whole(), values_side.place().whole()]
    attended, stats = kernel(
        attend_kernel,
        (info, order.turn(query), keys, values, *memories),
        ((rows, F32), ((2 * each, 128), F32)),
        4 * matmul,
        limits[2],
    )
    order.done(attended)
    rest = grouped(both.place().whole(), rest_sizes)
    half = GROUPS // 2

    def pieces(size):
        return (((half, UNIT * size, width), BF16),) * 2

    output, grad_mid, grad_att, *halves, vec_grad = kernel(
        feed_kernel,
        (info, order.turn(tok), cot, attended, vec, rest),
        ((rows, BF16), (rows, F32), (rows, BF16)) + pieces(1 + 2 * wide) + (((16, width), F32),),
        27 * matmul,
        limits[3],
    )
    order.done(halves[0])
    all_bits = powers(2, count)[::-1]

    def begin(keep, send, size, by_lanes=False):
        if not whole:
            keep, send = split_cores(scattered(joined(keep, send), size))
        return Reduce(order, keep, send, all_bits, by_lanes)

    feeds = begin(*halves, rest_sizes, True)
    feeds.go(1)
    memory_half = ((seq // 2, slots, width), BF16)
    chips = (seq // 2, 2, slots, width)
    grad_query, *halves, own_key, own_value = kernel(
        attend_back_kernel,
        (
            info,
            order.turn(query),
            keys,
            values,
            memories[0].reshape(chips),
            memories[1].reshape(chips),
            attended,
            stats,
            grad_att,
        ),
        ((rows, BF16),) + (memory_half,) * 4 + ((rows, F32), (rows, F32)),
        10 * matmul,
        limits[4],
    )
    order.done(grad_query)
    keys_side = Reduce(order, *halves[:2], along)
    values_side = Reduce(order, *halves[2:], along)
    keys_side.go(1)
    values_side.go(1)
    cross = [(across[-1 - at], across[at]) for at in range(len(across))]
    cuts = (width // 2, width // 2)
    for at in range(max(len(along), len(cross))):
        jobs = []
        if at < len(along):
            jobs = [(keys_side, (back[at],), ()), (values_side, (along[at],), ())]
        if at < len(cross):
            jobs.append((feeds, cross[at], () if at else cuts))
        add(order, *jobs)
        if at < len(along):
            keys_side.go(back[at])
            values_side.go(along[at])
        if at < len(cross):
            feeds.go(*cross[at])
    feeds.add((back[0],), width)
    key_grad, value_grad = (held.total().astype(BF16) for held in (keys_side, values_side))
    key_kept, value_kept, rims, *halves = kernel(
        compress_back_kernel,
        (
            info,
            order.turn(key_grad),
            value_grad,
            key_window,
            value_window,
            first,
            second,
            normed,
            grad_query,
        ),
        ((rows, F32), (rows, F32), ((micro * RIM, 2 * width), F32)) + pieces(7),
        5 * matmul,
        limits[5],
        (pltpu.VMEM((micro, width // 128, each, 128), F32),),
    )
    order.done(rims)
    rims = lax.ppermute(rims, "seq", [(i + 1, i) for i in range(seq - 1)])
    convs = begin(*halves, [1] * 7)
    convs.go(1)
    grad_in, *halves = kernel(
        input_kernel,
        (
            info,
            order.turn(tok),
            normed,
            grad_query,
            key_kept,
            value_kept,
            rims,
            own_key,
            own_value,
            first,
            second,
            vec,
            grad_mid,
            vec_grad,
        ),
        ((rows, BF16),) + pieces(3),
        6 * matmul,
        limits[6],
        (pltpu.VMEM(rows, F32),),
    )
    order.done(grad_in)
    if whole:
        inputs = begin(*halves, [1] * 3)
    else:
        dealt = joined(*halves)
        vectors = dealt[:, 2 * UNIT, : VECTORS * UNIT + ff // GROUPS]
        vectors = vector_regroup(vectors, count, [UNIT] * VECTORS + [ff // GROUPS])
        dealt = [scattered(dealt, [1] * 2), vector_pack(vectors, 2, width)]
        dealt = split_cores(jnp.concatenate(dealt, axis=1))
        inputs = Reduce(order, *dealt, all_bits)
    inputs.go(1)
    line = [masks[1] for masks in cross]
    cuts = (5 * share, 2 * share)
    convs.add(cross[0], *cuts)
    convs.go(*cross[0])
    feeds.go(back[0])
    inputs.add((line[0],))
    inputs.go(line[0])
    for at in range(1, max(len(along), len(cross))):
        jobs = []
        if at < len(cross):
            jobs.append((convs, cross[at], ()))
        if at < len(along):
            jobs.append((feeds, (back[at],), ()))
        add(order, *jobs)
        if at < len(cross):
            convs.go(*cross[at])
        if at < len(along):
            feeds.go(back[at])
        if at < len(cross):
            inputs.add((line[at],))
            inputs.go(line[at])
    rest_total = feeds.total()
    for at in range(len(along)):
        if at == len(along) - 1:
            ups = [rest_total[share * c : share * (c + 1)] for c in range(1, 1 + wide)]
            rest_outs = (rest_total[:share], jnp.concatenate(ups, axis=1))
            rest_outs = rest_outs + (rest_total[share * (1 + wide) :],)
            rest_outs = lax.optimization_barrier(rest_outs)
            order.done(rest_outs)
        convs.add((back[at],), 7 * share)
        convs.go(back[at])
        inputs.add((along[at],))
        inputs.go(along[at])
    convs, late_inputs = convs.total(), inputs.total()
    conv_keys = convs[: 3 * share].reshape(3, share, width)
    conv_values = convs[4 * share :].reshape(3, share, width)

    def own(buffer, number):
        return buffer[share * number : share * (number + 1)]

    vector_row = late_inputs[2 * share]

    def own_vector(number, length=share):
        return vector_row[share * number : share * number + length]

    return (
        output.reshape(tokens.shape),
        grad_in.reshape(tokens.shape),
        own_vector(0),
        own_vector(1),
        own(convs, 3),
        own(late_inputs, 0),
        own(late_inputs, 1),
        conv_keys,
        conv_values,
        rest_outs[0],
        own_vector(2),
        own_vector(3),
        rest_outs[1],
        own_vector(VECTORS, ff // count),
        rest_outs[2],
        own_vector(4),
    )


def solution(mesh):
    rows = P(AXES, None)
    vector = P(AXES)
    conv = P(None, AXES, None)
    part = P(None, "batch", "seq", None)
    weights = (vector, vector, rows, rows, rows, conv, conv, rows, vector, vector)
    weights = weights + (rows, vector, rows, vector)
    return jax.shard_map(
        per_device,
        mesh=mesh,
        in_specs=(part, P(None, "batch", None)) + weights + (part,),
        out_specs=(part, part) + weights,
        check_vma=False,
    )
```

```python
import functools

import jax
import jax.numpy as jnp
from jax import lax
from jax.experimental import pallas as pl
from jax.experimental.pallas import tpu as pltpu
from jax.sharding import PartitionSpec as P

HEADS = 8
HEAD_DIM = 64
SCALE = HEAD_DIM ** (-0.5)
EPSILON = 1e-06
AXES = ("batch", "seq")
GROUPS = 32
UNIT = 16
PAIR = 2 * HEAD_DIM
RIM = 8
MASKED = -1e30
LEAST_ITEM = 501
F32 = jnp.float32
BF16 = jnp.bfloat16
TN = ((0,), (0,))
NT = ((1,), (1,))
ERF_STEP = 0.3275911
ERF_TERMS = (1.061405429, -1.453152027, 1.421413741, -0.284496736, 0.254829592)


def device_count():
    return lax.axis_size("batch") * lax.axis_size("seq")


def device_index():
    return lax.axis_index("batch") * lax.axis_size("seq") + lax.axis_index("seq")


def powers(low, high):
    masks = []
    while low < high:
        masks.append(low)
        low *= 2
    return masks


def swap(array, mask):
    return lax.ppermute(array, AXES, [(i, i ^ mask) for i in range(device_count())])


def upper_half(mask):
    return ((device_index() & mask) != 0).astype(jnp.int32)


class Order:
    def __init__(self):
        self.last = None
        bits = device_count().bit_length() - 1
        self.uppers = jnp.stack([upper_half(1 << bit) for bit in range(bits)])

    def turn(self, array):
        if self.last is not None:
            array = lax.optimization_barrier((array, self.last))[0]
        return array

    def done(self, array):
        self.last = array


def axis_of(bits, mask):
    return sum(b > mask for b in bits)


def bit_shape(bits, rows):
    return (2,) * len(bits) + tuple(rows)


def cut_of(rank, cut):
    by_lanes, part = cut
    last = (slice(None), part) if by_lanes else (part, slice(None))
    return (slice(None),) * (rank - 2) + last


def at_bit(rank, axis, index, cut):
    where = list(cut_of(rank, cut))
    where[axis] = pl.ds(index, 1)
    return tuple(where)


def cut_shape(shape, by_lanes, size):
    return (shape[0], size) if by_lanes else (size, shape[1])


def overlaps(lefts, rights):
    found, left_at = [], 0
    for i, left in enumerate(lefts):
        right_at = 0
        for j, right in enumerate(rights):
            low = max(left_at, right_at)
            high = min(left_at + left, right_at + right)
            if low < high:
                found.append(
                    (i, j, slice(low - left_at, high - left_at), slice(low - right_at, high - right_at))
                )
            right_at += right
        left_at += left
    return found


def place_kernel(axes, masks, cuts, uppers, *refs):
    count = len(axes)
    for i, j, inside, outside in cuts:
        mine, other, out = refs[2 * i], refs[2 * i + 1], refs[2 * count + j]
        rank, axis, at = len(out.shape), axes[i], uppers[masks[i].bit_length() - 1]
        source = cut_of(rank - 1, inside)
        out[at_bit(rank, axis, at, outside)] = jnp.expand_dims(mine[source], axis)
        out[at_bit(rank, axis, 1 - at, outside)] = jnp.expand_dims(other[source], axis)


def add_kernel(axes, masks, cuts, count, uppers, *refs):
    for i, j, inside, outside in cuts:
        keep, other = refs[2 * i], refs[2 * i + 1]
        next_keep, next_send = refs[2 * count + 2 * j], refs[2 * count + 2 * j + 1]
        rank, axis, at = len(keep.shape), axes[j], uppers[masks[j].bit_length() - 1]
        into = cut_of(rank - 1, outside)
        here, there = at_bit(rank, axis, at, inside), at_bit(rank, axis, 1 - at, inside)
        next_send[into] = jnp.squeeze(keep[there] + other[there], axis)
        next_keep[into] = jnp.squeeze(keep[here] + other[here], axis)


def place(order, *jobs):
    axes, masks, cuts, args, outs, plans = [], [], [], [], [], []
    for gather, sizes in jobs:
        lanes = gather.by_lanes
        whole = (gather.rows, gather.width)
        olds = [p.shape[-1 if lanes else -2] for p in gather.parts]
        sizes = sizes or olds
        bits = [sorted(b + [m], reverse=True) for b, m in zip(gather.bits, gather.masks)]
        own_axes = [axis_of(b, m) for b, m in zip(gather.bits, gather.masks)]
        bits = [bits[min(j, len(bits) - 1)] for j in range(len(sizes))]
        found = overlaps(olds, sizes)
        plans.append((gather, olds, sizes, bits, own_axes, len(outs)))
        cuts += [(len(axes) + i, len(outs) + j, (lanes, x), (lanes, y)) for i, j, x, y in found]
        axes += own_axes
        masks += gather.masks
        for mine, other in zip(gather.parts, gather.others):
            args += [order.turn(mine), other]
        outs += [(bit_shape(b, cut_shape(whole, lanes, r)), BF16) for b, r in zip(bits, sizes)]
    if device_count() == GROUPS:
        body = functools.partial(place_kernel, axes, masks, cuts)
        placed = kernel(body, (order.uppers, *args), outs, 0, 24)
        order.done(placed[0])
    for gather, olds, sizes, bits, own_axes, at in plans:
        if device_count() == GROUPS:
            parts = placed[at : at + len(sizes)]
        else:
            held = []
            sides = zip(gather.parts, gather.others, own_axes, gather.masks)
            for mine, other, axis, mask in sides:
                up = upper_half(mask)
                low, high = jnp.where(up, other, mine), jnp.where(up, mine, other)
                held.append(jnp.stack([low, high], axis=axis))
            parts = cut_parts(held, olds, sizes, gather.by_lanes)
        gather.parts, gather.bits = parts, bits


def add(order, *jobs):
    axes, all_masks, cuts, args, outs, plans, count = [], [], [], [], [], [], 0
    for chain, masks, sizes in jobs:
        lanes = chain.by_lanes
        whole = (chain.rows, chain.width)
        olds = [p.shape[-1 if lanes else -2] for p in chain.keeps]
        sizes = sizes or olds
        bits = [chain.bits[min(j, len(olds) - 1)] for j in range(len(sizes))]
        own_axes = [axis_of(b, m) for b, m in zip(bits, masks)]
        left = [[b for b in old if b != m] for old, m in zip(bits, masks)]
        plans.append((chain, masks, olds, sizes, own_axes, left, len(axes)))
        found = overlaps(olds, sizes)
        cuts += [(count + i, len(axes) + j, (lanes, x), (lanes, y)) for i, j, x, y in found]
        axes += own_axes
        all_masks += masks
        count += len(olds)
        for keep, other in zip(chain.keeps, chain.others):
            args += [order.turn(keep), other]
        for b, r in zip(left, sizes):
            outs += [(bit_shape(b, cut_shape(whole, lanes, r)), BF16)] * 2
    if device_count() == GROUPS:
        body = functools.partial(add_kernel, axes, all_masks, cuts, count)
        both = kernel(body, (order.uppers, *args), outs, 0, 24)
        order.done(both[0])
    for chain, masks, olds, sizes, own_axes, left, at in plans:
        if device_count() == GROUPS:
            found = both[2 * at : 2 * (at + len(sizes))]
            chain.keeps, chain.sends = found[0::2], found[1::2]
        else:
            sums = [
                (k.astype(F32) + o.astype(F32)).astype(BF16)
                for k, o in zip(chain.keeps, chain.others)
            ]
            sums = cut_parts(sums, olds, sizes, chain.by_lanes)
            sides = list(zip(sums, [upper_half(m) for m in masks], own_axes))
            take = lax.dynamic_index_in_dim
            chain.keeps = [take(t, u, axis, False) for t, u, axis in sides]
            chain.sends = [take(t, 1 - u, axis, False) for t, u, axis in sides]
        chain.bits = left


class Gather:
    def __init__(self, order, part, by_lanes=False):
        self.order, self.parts, self.bits = order, [part], [[]]
        self.by_lanes, (self.rows, self.width) = by_lanes, part.shape

    def go(self, *masks, wait=False):
        self.masks = masks
        parts = [self.order.turn(p) for p in self.parts] if wait else self.parts
        self.others = [swap(p, m) for p, m in zip(parts, masks)]

    def place(self, *sizes):
        place(self.order, (self, sizes))
        return self

    def whole(self):
        held = self.parts[0]
        return held.reshape((-1,) + held.shape[-2:])


def cut_parts(arrays, olds, sizes, by_lanes):
    if list(olds) == list(sizes):
        return arrays
    axis = -1 if by_lanes else -2
    joint = jnp.concatenate(arrays, axis=axis)
    ends = [sum(sizes[: j + 1]) for j in range(len(sizes) - 1)]
    return jnp.split(joint, ends, axis=axis)


class Reduce:
    def __init__(self, order, keep, send, bits, by_lanes=False):
        shape = bit_shape(bits, keep.shape[-2:])
        self.order, self.bits = order, [bits]
        self.by_lanes, (self.rows, self.width) = by_lanes, keep.shape[-2:]
        self.keeps, self.sends = [keep.reshape(shape)], [send.reshape(shape)]

    def go(self, *masks, wait=False):
        sends = [self.order.turn(p) for p in self.sends] if wait else self.sends
        self.others = [swap(p, m) for p, m in zip(sends, masks)]

    def add(self, masks, *sizes):
        add(self.order, (self, masks, sizes))
        return self

    def total(self):
        keep, other = self.keeps[0], self.others[0]
        return (keep.astype(F32) + other.astype(F32)).reshape(keep.shape[-2:])


def split_cores(blocks):
    pairs = blocks.reshape((-1, 2) + blocks.shape[1:])
    upper = upper_half(1)
    keep = lax.dynamic_index_in_dim(pairs, upper, 1, keepdims=False)
    return keep, lax.dynamic_index_in_dim(pairs, 1 - upper, 1, keepdims=False)


def joined(keep, send):
    return jnp.stack([keep, send], axis=1).reshape((-1,) + keep.shape[1:])


def grouped(buffer, sizes):
    count = buffer.shape[0]
    if count == GROUPS:
        return buffer
    width = buffer.shape[-1]
    share = width // count
    parts, start = [], 0
    for size in sizes:
        part = buffer[:, start : start + share * size]
        parts.append(part.reshape(GROUPS, UNIT * size, width))
        start += share * size
    return jnp.concatenate(parts, axis=1)


def scattered(buffer, sizes):
    count, width = device_count(), buffer.shape[-1]
    if count == GROUPS:
        return buffer
    parts, start = [], 0
    for size in sizes:
        part = buffer[:, start : start + UNIT * size]
        parts.append(part.reshape(count, width // count * size, width))
        start += UNIT * size
    return jnp.concatenate(parts, axis=1)


def vector_pack(vectors, rows, width):
    filled = jnp.pad(vectors, ((0, 0), (0, width - vectors.shape[1])))
    return jnp.pad(filled[:, None], ((0, 0), (0, rows - 1), (0, 0)))


def vector_regroup(vectors, parts, lengths):
    pieces, start = [], 0
    for length in lengths:
        pieces.append(vectors[:, start : start + length].reshape(parts, -1))
        start += length
    return jnp.concatenate(pieces, axis=1)


def dot(a, b, dims=((1,), (0,))):
    return lax.dot_general(a, b, (dims, ((), ())), preferred_element_type=F32)


def iota(shape, axis):
    return lax.broadcasted_iota(jnp.int32, shape, axis)


def tile(ref, place, size=1):
    rows = ref[:, UNIT * place : UNIT * (place + size), :]
    return rows.reshape(GROUPS * UNIT * size, rows.shape[-1])


def pack_kernel(moves, counts, *refs):
    inputs, outs, sems = refs[: counts[0]], refs[counts[0] : -1], refs[-1]
    copies = []
    for at, (source, where, out, start, rows) in enumerate(moves):
        into = outs[out].at[pl.ds(start, rows)]
        piece = inputs[source] if where is None else inputs[source].at[where]
        copies.append(pltpu.make_async_copy(piece, into, sems.at[at]))
        copies[-1].start()
    for copy in copies:
        copy.wait()


def packed(args, moves, shapes):
    return pl.pallas_call(
        functools.partial(pack_kernel, moves, (len(args),)),
        in_specs=[pl.BlockSpec(memory_space=pltpu.HBM) for _ in args],
        out_specs=[pl.BlockSpec(memory_space=pltpu.VMEM) for _ in shapes],
        out_shape=[jax.ShapeDtypeStruct(shape, BF16) for shape in shapes],
        scratch_shapes=[pltpu.SemaphoreType.DMA((len(moves),))],
        compiler_params=pltpu.CompilerParams(vmem_limit_bytes=62 << 20),
    )(*args)


def kernel(body, args, outs, flops, limit, scratch=()):
    spec = {jnp.dtype(jnp.int32): pltpu.SMEM}
    return pl.pallas_call(
        body,
        in_specs=[pl.BlockSpec(memory_space=spec.get(a.dtype, pltpu.VMEM)) for a in args],
        out_specs=[pl.BlockSpec(memory_space=pltpu.VMEM) for _ in outs],
        out_shape=[jax.ShapeDtypeStruct(shape, dtype) for shape, dtype in outs],
        scratch_shapes=list(scratch),
        compiler_params=pltpu.CompilerParams(vmem_limit_bytes=limit << 20),
        cost_estimate=pl.CostEstimate(
            flops=flops,
            bytes_accessed=sum(a.size * a.dtype.itemsize for a in args),
            transcendentals=0,
        ),
    )(*args)


def unit_norm(values):
    center = values - jnp.mean(values, axis=-1, keepdims=True)
    spread = jnp.mean(center * center, axis=-1, keepdims=True)
    inverse = lax.rsqrt(spread + EPSILON)
    return center * inverse, inverse


def norm_back(grad, unit, inverse, gain):
    e = grad * gain
    mean_e = jnp.mean(e, axis=-1, keepdims=True)
    mean_x = jnp.mean(e * unit, axis=-1, keepdims=True)
    return inverse * (e - mean_e - unit * mean_x)


def column_sum(values):
    return jnp.sum(values, axis=0, keepdims=True)


def valid_column(info, m, start, rows):
    place = start + iota((rows, 1), 0)
    first = (place >= 1) & (place < info[m, 0])
    second = (place >= info[m, 1]) & (place < info[m, 2])
    return jnp.where(first | second, 1.0, 0.0).astype(F32)


def segment_start(info, m, place):
    start = jnp.where(place >= 1, 1, 0)
    start = jnp.where(place >= info[m, 1], info[m, 1], start)
    return jnp.where(place >= info[m, 3], info[m, 3], start)


VECTORS = 5
BIAS_AT = VECTORS * UNIT


def vector_maps(width):
    lanes = width // 2
    fine = (iota((lanes, width), 0) & 15) == (iota((lanes, width), 1) & 15)
    wide = ((iota((lanes, width), 0) + 48) & 63) == (iota((lanes, width), 1) & 63)
    own_fine = iota((GROUPS, width), 1) >> 4 == iota((GROUPS, width), 0)
    own_wide = iota((GROUPS, width), 1) >> 6 == (iota((GROUPS, width), 0) & 7)
    as_bf16 = [jnp.where(m, 1.0, 0.0).astype(BF16) for m in (fine, wide)]
    as_f32 = [jnp.where(m, 1.0, 0.0).astype(F32) for m in (own_fine, own_wide)]
    return as_bf16 + as_f32


def lane_window(lanes, k):
    place = iota((GROUPS, lanes), 1)
    if k == VECTORS:
        return (place >= BIAS_AT) & (place < BIAS_AT + 64)
    return (place >= UNIT * k) & (place < UNIT * (k + 1))


def line_cuts(line):
    micro, cuts = line.shape[:2]
    found = [(m, c) for m in range(micro) for c in range(cuts)]
    return [(m, c, slice(128 * c, 128 * (c + 1))) for m, c in found]


def keep_and_compress(info, low, weights, kept, window, memory, line):
    micro = info.shape[0]
    each = low.shape[0] // micro - RIM
    slots = each // 3
    count = micro * each
    valid = [valid_column(info, m, info[m, 4], each) for m in range(micro)]
    valid += [valid_column(info, m, info[m, 4] - RIM, RIM) for m in range(micro)]
    rows = (dot(low, tile(weights, 0)) * jnp.concatenate(valid, axis=0)).astype(BF16)
    kept[...] = rows[:count]
    rows = rows.astype(F32)
    for m, cut, cols in line_cuts(line):
        line[m, cut, :RIM] = rows[count + RIM * m : count + RIM * (m + 1), cols]
        line[m, cut, RIM:] = rows[each * m : each * (m + 1), cols]
    total = None
    for tap in range(3):
        start = RIM - 2 + tap
        for m, cut, cols in line_cuts(line):
            taken = line[m, cut, pl.ds(start, slots, stride=3), :]
            window[tap, slots * m : slots * (m + 1), cols] = taken.astype(BF16)
        part = dot(window[tap], tile(weights, 1 + tap))
        total = part if total is None else total + part
    memory[...] = total.astype(BF16)


def key_kernel(info, tok, halo, weights, normed, kept, window, memory, vec, line):
    width = tok.shape[-1]
    lanes = width // 2
    fine, wide, own_fine, own_wide = vector_maps(width)
    rows = jnp.sum(weights[:, 4 * UNIT : 5 * UNIT, :lanes].astype(F32), axis=1)
    picked = [jnp.where(lane_window(lanes, k), rows, 0.0) for k in range(VECTORS + 1)]
    spread = dot(jnp.concatenate(picked[:VECTORS], axis=0).astype(BF16), fine)
    vectors = [
        column_sum(spread[GROUPS * k : GROUPS * (k + 1)] * own_fine) for k in range(VECTORS)
    ]
    bias = dot(picked[VECTORS].astype(BF16), wide) * own_wide
    bias = jnp.sum(bias.reshape(4, 8, width), axis=1)
    vec[...] = jnp.concatenate(vectors + [bias, jnp.zeros((7, width), F32)], axis=0)
    values = jnp.concatenate([tok[...], halo[...]], axis=0).astype(F32)
    unit, _ = unit_norm(values)
    low = (unit * vectors[0] + vectors[1]).astype(BF16)
    normed[...] = low
    keep_and_compress(info, low, weights, kept, window, memory, line)


def query_kernel(normed, weights, query):
    query[...] = dot(normed[: query.shape[0], :], tile(weights, 4)).astype(BF16)


def value_kernel(info, normed, weights, kept, window, memory, line):
    low = normed[...]
    keep_and_compress(info, low, weights, kept, window, memory, line)


def stacked(values, lower):
    zero = jnp.zeros_like(values)
    return jnp.concatenate(
        [jnp.where(lower, values, zero), jnp.where(lower, zero, values)], axis=0
    )


def merged(values, lower):
    half = values.shape[0] // 2
    return jnp.where(lower, values[:half], values[half:])


def reach(blocks, each):
    row = blocks * each
    size = (row - 2 - LEAST_ITEM) // each + 1
    size = min(size + size % 2, blocks)
    skipped = (LEAST_ITEM + 3) // 3 // (each // 3)
    return size if blocks - size <= skipped else blocks


def memory_pair(memory, first, size, m, pair, micro):
    slots = memory.shape[1] // micro
    rows, cols = slice(slots * m, slots * (m + 1)), slice(PAIR * pair, PAIR * (pair + 1))
    return memory[pl.ds(first, size), rows, cols].reshape(size * slots, PAIR)


def attend_kernel(info, query, keys, values, memory_keys, memory_values, attended, stats):
    micro = info.shape[0]
    count, width = query.shape
    each = count // micro
    blocks, share = memory_keys.shape[0], memory_keys.shape[1] // micro
    size = reach(blocks, each)
    slots = size * share
    pairs = width // PAIR
    lower = iota((each, PAIR), 1) < HEAD_DIM
    lane = iota((2 * each, 128), 1)
    found = jnp.zeros((2 * each, 128), F32)
    ones = jnp.ones((slots, PAIR), BF16)
    for m in range(micro):
        rows = slice(each * m, each * (m + 1))
        place = info[m, 4] + iota((each, 1), 0)
        start = segment_start(info, m, place)
        begin = jnp.where(info[m, 4] < info[m, 1], 0, blocks - size)
        end = 3 * (share * begin + iota((each, slots), 1))
        bias = jnp.where((end <= place) & (end >= start), 0.0, MASKED).astype(F32)
        bias = jnp.concatenate([bias, bias], axis=0)
        for pair in range(pairs):
            cols = slice(PAIR * pair, PAIR * (pair + 1))
            key = keys[rows, cols].astype(F32)
            value = values[rows, cols].astype(F32)
            queries = stacked(query[rows, cols].astype(F32) * SCALE, lower)
            own = jnp.sum(queries * jnp.concatenate([key, key], axis=0), axis=1, keepdims=True)
            memory_key = memory_pair(memory_keys, begin, size, m, pair, micro)
            memory_value = memory_pair(memory_values, begin, size, m, pair, micro)
            scores = dot(queries.astype(BF16), memory_key, NT) + bias
            top = jnp.maximum(jnp.max(scores, axis=1, keepdims=True), own)
            expos = jnp.exp(scores - top)
            own = jnp.exp(own - top)
            beside = jnp.concatenate([memory_value, ones], axis=1)
            mixed = dot(expos.astype(BF16), beside)
            total = mixed[:, PAIR:] + own
            inverse = 1.0 / total
            weight = own * inverse
            mixed = mixed[:, :PAIR] * inverse
            attended[rows, cols] = merged(mixed, lower) + merged(weight, lower) * value
            found = jnp.where(lane == m * pairs + pair, top + jnp.log(total), found)
    stats[...] = found


def gelu_parts(hidden):
    falling = jnp.exp(hidden * hidden * -0.5)
    step = 1.0 / (1.0 + (ERF_STEP * 0.7071067811865476) * jnp.abs(hidden))
    tail = 0.5 * ERF_TERMS[0]
    for term in ERF_TERMS[1:]:
        tail = tail * step + 0.5 * term
    tail = tail * step * falling
    return jnp.where(hidden >= 0.0, 1.0 - tail, tail), falling


def even_first(flag, rows, size):
    pairs = rows.reshape(-1, 2, size, rows.shape[-1])
    even, odd = pairs[:, 0], pairs[:, 1]
    halves = [jnp.where(flag == 0, even, odd), jnp.where(flag == 0, odd, even)]
    return jnp.concatenate(halves, axis=0).reshape(rows.shape)


def deal(value, rows, keep, send, blocks, start):
    halves = value.astype(BF16).reshape(2, -1, rows, value.shape[-1])
    keep[blocks, start : start + rows, :] = halves[0]
    send[blocks, start : start + rows, :] = halves[1]


def deal_tile(value, place, keep, send):
    deal(value, UNIT, keep, send, slice(None), UNIT * place)


def feed_kernel(
    info,
    tok,
    cot,
    attended,
    vec,
    rest,
    out,
    grad_mid,
    grad_att,
    keep,
    send,
    vec_grad,
):
    count, width = tok.shape
    wide = 4
    low_att = attended[...].astype(BF16)
    w_out = tile(rest, 0)
    middle = tok[...].astype(F32) + dot(low_att, w_out)
    unit, inverse = unit_norm(middle)
    gain = vec[2:3, :]
    low = (unit * gain + vec[3:4, :]).astype(BF16)
    flag = info[0, 5]
    low_t = even_first(flag, low.T, UNIT)
    cots = cot[...]
    total = middle + vec[4:5, :]
    grad_low = jnp.zeros((count, width), F32)
    bias_rows = []
    eighth = GROUPS // wide
    for c in range(wide):
        w_up = tile(rest, 1 + c)
        down = slice(eighth * c, eighth * (c + 1))
        w_down = rest[down, UNIT * (1 + wide) :, :].reshape(width, width)
        hidden = dot(low, w_up) + vec[5 + c : 6 + c, :]
        share, falling = gelu_parts(hidden)
        slope = share + (0.3989422804014327 * hidden) * falling
        active = (hidden * share).astype(BF16)
        total = total + dot(active, w_down)
        grad_hidden_f = dot(cots, w_down, NT) * slope
        grad_hidden = grad_hidden_f.astype(BF16)
        bias_rows.append(column_sum(grad_hidden.astype(F32)))
        grad_low = grad_low + dot(grad_hidden, w_up, NT)
        deal_tile(dot(low_t, grad_hidden), 1 + c, keep, send)
        where = slice(eighth // 2 * c, eighth // 2 * (c + 1))
        active_t = even_first(flag, active.T, UNIT * wide)
        deal(dot(active_t, cots), UNIT * wide, keep, send, where, UNIT * (1 + wide))
    out[...] = total.astype(BF16)
    cots_f = cots.astype(F32)
    grad_middle = cots_f + norm_back(grad_low, unit, inverse, gain)
    grad_mid[...] = grad_middle
    branch = grad_middle.astype(BF16)
    deal_tile(dot(even_first(flag, low_att.T, UNIT), branch), 0, keep, send)
    grad_att[...] = dot(branch, w_out, NT).astype(BF16)
    rows = [jnp.zeros((2, width), F32), column_sum(grad_low * unit), column_sum(grad_low)]
    rows += [column_sum(cots_f)] + bias_rows + [jnp.zeros((7, width), F32)]
    vec_grad[...] = jnp.concatenate(rows, axis=0)


def memory_turned(flag, memory, first, size, m, pair, micro):
    slots = memory.shape[2] // micro
    rows, cols = slice(slots * m, slots * (m + 1)), slice(PAIR * pair, PAIR * (pair + 1))
    halves = [memory[pl.ds(first, size), pl.ds(at, 1), rows, cols] for at in (flag, 1 - flag)]
    return jnp.concatenate([h.reshape(-1, PAIR) for h in halves], axis=0)


def attend_back_kernel(
    info,
    query,
    keys,
    values,
    memory_keys,
    memory_values,
    attended,
    stats,
    grad_att,
    grad_query,
    key_keep,
    key_send,
    value_keep,
    value_send,
    own_key,
    own_value,
):
    micro = info.shape[0]
    count, width = query.shape
    each = count // micro
    chips = memory_keys.shape[0]
    share = memory_keys.shape[2] // micro
    size = reach(2 * chips, each) // 2
    slots = 2 * size * share
    flag = info[0, 6]
    pairs = width // PAIR
    lower = iota((each, PAIR), 1) < HEAD_DIM
    lane = iota((2 * each, 128), 1)
    found = stats[...]
    deltas = jnp.zeros((2 * each, 128), F32)
    parts = {}
    for m in range(micro):
        rows = slice(each * m, each * (m + 1))
        for pair in range(pairs):
            cols = slice(PAIR * pair, PAIR * (pair + 1))
            grad = grad_att[rows, cols].astype(F32)
            product = stacked(grad * attended[rows, cols], lower)
            delta = jnp.sum(product, axis=1, keepdims=True)
            deltas = jnp.where(lane == m * pairs + pair, delta, deltas)
            parts[m, pair] = delta
    found_t, deltas_t = found.T, deltas.T
    for m in range(micro):
        rows = slice(each * m, each * (m + 1))
        lanes = iota((1, 2 * each), 1)
        place = info[m, 4] + jnp.where(lanes >= each, lanes - each, lanes)
        start = segment_start(info, m, place)
        row = iota((slots, 1), 0)
        late = row >= size * share
        row = jnp.where(late, row - size * share, row)
        front = info[m, 4] < info[m, 1]
        begin = jnp.where(front, 0, chips - size)
        block = jnp.zeros((slots, 1), jnp.int32) + 2 * begin
        for chip in range(1, size):
            block = block + jnp.where(row >= share * chip, 1, 0)
        core = jnp.where(late, 1 - flag, flag)
        end = 3 * (row + share * (block + core))
        bias = jnp.where((end <= place) & (end >= start), 0.0, MASKED).astype(F32)
        if size < chips:
            empty = pl.ds(jnp.where(front, size, 0), chips - size)
            zeros = jnp.zeros((chips - size, share, width), BF16)
            for half in (key_keep, key_send, value_keep, value_send):
                half[empty, share * m : share * (m + 1), :] = zeros
        for pair in range(pairs):
            cols = slice(PAIR * pair, PAIR * (pair + 1))
            at = m * pairs + pair
            key = keys[rows, cols].astype(F32)
            value = values[rows, cols].astype(F32)
            query_f = query[rows, cols].astype(F32) * SCALE
            grad_f = grad_att[rows, cols].astype(F32)
            queries = stacked(query_f, lower)
            grads = stacked(grad_f, lower)
            own = jnp.sum(queries * jnp.concatenate([key, key], axis=0), axis=1, keepdims=True)
            own = jnp.exp(own - found[:, at : at + 1])
            grad_own = jnp.sum(
                grads * jnp.concatenate([value, value], axis=0), axis=1, keepdims=True
            )
            grad_own = (own * (grad_own - parts[m, pair])).astype(BF16).astype(F32)
            queries, grads = queries.astype(BF16), grads.astype(BF16)
            memory_key = memory_turned(flag, memory_keys, begin, size, m, pair, micro)
            memory_value = memory_turned(flag, memory_values, begin, size, m, pair, micro)
            scores = dot(memory_key, queries, NT) + bias
            probs = jnp.exp(scores - found_t[at : at + 1, :])
            grad_probs = dot(memory_value, grads, NT)
            grad_scores = (probs * (grad_probs - deltas_t[at : at + 1, :])).astype(BF16)
            sides = (
                (dot(grad_scores, queries), key_keep, key_send),
                (dot(probs.astype(BF16), grads), value_keep, value_send),
            )
            for grad, keep, send in sides:
                halves = grad.astype(BF16).reshape(2, size, share, PAIR)
                into = (pl.ds(begin, size), slice(share * m, share * (m + 1)), cols)
                keep[into] = halves[0]
                send[into] = halves[1]
            turned = dot(memory_key.T, grad_scores).T
            own_grad = merged(jnp.broadcast_to(grad_own, (2 * each, PAIR)), lower)
            own_weight = merged(jnp.broadcast_to(own, (2 * each, PAIR)), lower)
            grad_query[rows, cols] = (
                SCALE * (merged(turned, lower) + own_grad * key)
            ).astype(BF16)
            own_key[rows, cols] = own_grad * query_f
            own_value[rows, cols] = own_weight * grad_f


def compress_back_kernel(
    info,
    key_memory,
    value_memory,
    key_window,
    value_window,
    key_weights,
    value_weights,
    normed,
    grad_query,
    key_grad,
    value_grad,
    rims,
    keep,
    send,
    line,
):
    micro = info.shape[0]
    count, width = key_grad.shape
    each = count // micro
    flag = info[0, 5]
    own_slots = each // 3
    edge = iota((RIM, width), 0) >= RIM - 2
    sides = (
        (key_memory, key_window, key_weights, key_grad),
        (value_memory, value_window, value_weights, value_grad),
    )
    for kind, (memory, window, weights, out) in enumerate(sides):
        grad = memory[...]
        for tap in range(3):
            window_t = even_first(flag, window[tap].T, UNIT)
            deal_tile(dot(window_t, grad), 4 * kind + tap, keep, send)
            part = dot(grad, tile(weights, 1 + tap), NT)
            for m, cut, cols in line_cuts(line):
                rows = slice(own_slots * m, own_slots * (m + 1))
                line[m, cut, pl.ds(tap, own_slots, stride=3), :] = part[rows, cols]
        for m, cut, cols in line_cuts(line):
            out[each * m : each * (m + 1), cols] = line[m, cut]
        for m in range(micro):
            first = pltpu.roll(out[each * m : each * m + RIM, :], RIM - 2, 0)
            into = (slice(RIM * m, RIM * (m + 1)), slice(width * kind, width * (kind + 1)))
            rims[into] = jnp.where(edge, first, 0.0)
    low_t = even_first(flag, normed[:count, :].T, UNIT)
    deal_tile(dot(low_t, grad_query[...]), 3, keep, send)


def input_kernel(
    info,
    tok,
    normed,
    grad_query,
    key_grad,
    value_grad,
    rims,
    own_key,
    own_value,
    key_weights,
    value_weights,
    vec,
    grad_mid,
    vec_grad,
    grad_in,
    keep,
    send,
    total,
):
    count, width = tok.shape
    micro = info.shape[0]
    each = count // micro
    valid = [valid_column(info, m, info[m, 4], each) for m in range(micro)]
    valid = jnp.concatenate(valid, axis=0)
    flag = info[0, 5]
    low_t = even_first(flag, normed[:count, :].T, UNIT)
    grad_low = dot(grad_query[...], tile(value_weights, 4), NT)
    inner = iota((each, width), 0) < each - 2
    sides = ((key_grad, own_key, key_weights), (value_grad, own_value, value_weights))
    for kind, (grad, own, weights) in enumerate(sides):
        for m in range(micro):
            rows = slice(each * m, each * (m + 1))
            moved = pltpu.roll(grad[rows, :], each - 2, 0)
            total[rows, :] = jnp.where(inner, moved, 0.0) + own[rows, :]
            rows = slice(each * (m + 1) - RIM, each * (m + 1))
            rim = rims[RIM * m : RIM * (m + 1), width * kind : width * (kind + 1)]
            total[rows, :] = total[rows, :] + rim
        low_grad = (total[...] * valid).astype(BF16)
        grad_low = grad_low + dot(low_grad, tile(weights, 0), NT)
        deal_tile(dot(low_t, low_grad), kind, keep, send)
    unit, inverse = unit_norm(tok[...].astype(F32))
    back = norm_back(grad_low, unit, inverse, vec[0:1, :])
    grad_in[...] = (grad_mid[...] + back).astype(BF16)

    lanes = width // 2
    fine, wide, own_fine, own_wide = vector_maps(width)
    vectors = [column_sum(grad_low * unit), column_sum(grad_low)]
    vectors += [vec_grad[k : k + 1, :] for k in range(2, VECTORS)]
    dealt = jnp.concatenate([own_fine * v for v in vectors], axis=0).astype(BF16)
    dealt = dot(dealt, fine, NT)
    bias = [
        jnp.broadcast_to(vec_grad[VECTORS + c : VECTORS + c + 1, :], (8, width)) for c in range(4)
    ]
    bias = (jnp.concatenate(bias, axis=0) * own_wide).astype(BF16)
    packed = jnp.where(lane_window(lanes, VECTORS), dot(bias, wide, NT), 0.0)
    for k in range(VECTORS):
        packed = jnp.where(lane_window(lanes, k), dealt[GROUPS * k : GROUPS * (k + 1)], packed)
    packed = jnp.concatenate([packed, jnp.zeros((GROUPS, width - lanes), F32)], axis=1)
    spot = iota((GROUPS, UNIT, width), 1) == 0
    spread = jnp.broadcast_to(packed[:, None, :], (GROUPS, UNIT, width))
    packed = jnp.where(spot, spread, 0.0).reshape(GROUPS * UNIT, width)
    deal_tile(even_first(flag, packed, UNIT), 2, keep, send)


def per_device(
    tokens,
    lengths,
    ln1_gain,
    ln1_bias,
    w_query,
    w_key,
    w_value,
    conv_key,
    conv_value,
    w_out,
    ln2_gain,
    ln2_bias,
    w_up,
    b_up,
    w_down,
    b_down,
    cotangent,
):
    count = device_count()
    micro, _, each, width = tokens.shape
    ff = w_up.shape[1]
    wide = ff // width
    share = width // count
    seq = lax.axis_size("seq")
    all_tokens = micro * each
    slots = micro * each // 3
    memory_bytes = 4 * seq * slots * width

    whole = count == GROUPS
    vector_lengths = [share] * VECTORS + [ff // count]
    vectors, start = 0.0, 0
    for part in (ln1_gain, ln1_bias, ln2_gain, ln2_bias, b_down, b_up):
        end = start + part.shape[0]
        pad = ((0, (UNIT if whole else 2) - 1), (start, width - end))
        vectors, start = vectors + jnp.pad(part[None], pad), end
    vectors = vectors.astype(BF16)
    across = powers(seq, count)
    along = powers(2, seq)[::-1]
    back = along[::-1]
    order = Order()
    if whole:
        moves = [(kind, None, kind, 0, UNIT) for kind in range(2)]
        moves += [(2 + k, tap, k, UNIT * (1 + tap), UNIT) for k in range(2) for tap in range(3)]
        moves += [(4 + kind, None, kind, 4 * UNIT, UNIT) for kind in range(2)]
        moves += [(6, None, 2, 0, UNIT)]
        for c in range(wide):
            cols = (slice(None), pl.ds(width * c, width))
            moves.append((7, cols, 2, UNIT * (1 + c), UNIT))
        moves.append((8, None, 2, UNIT * (1 + wide), UNIT * wide))
        rows = (5 * UNIT, 5 * UNIT, (1 + 2 * wide) * UNIT)
        args = (w_key, w_value, conv_key, conv_value, vectors, w_query, w_out, w_up, w_down)
        first, second, rest = packed(args, moves, [(r, width) for r in rows])
    else:
        first = jnp.concatenate([w_key, *conv_key, vectors], axis=0)
        second = jnp.concatenate([w_value, *conv_value, w_query], axis=0)
        ups = [w_up[:, width * c : width * (c + 1)] for c in range(wide)]
        rest = jnp.concatenate([w_out] + ups + [w_down], axis=0)
    one, two, both = Gather(order, first), Gather(order, second), Gather(order, rest, True)
    one.go(along[0])
    two.go(back[0])
    for at in range(1, len(along)):
        one.place()
        if at == 1:
            last_rows = order.turn(tokens[:, 0, each - RIM :])
            halo = lax.ppermute(last_rows, "seq", [(i, i + 1) for i in range(seq - 1)])
            halo = halo.reshape(micro * RIM, width)
        one.go(along[at])
        two.place()
        two.go(back[at])
    order.done((halo, rest))
    one.place()
    one.go(across[0])
    two.place()
    two.go(across[-1])
    both.go(along[0], wait=True)
    for at in range(1, max(len(across), len(along))):
        jobs = []
        if at < len(across):
            one.place()
            one.go(across[at])
            jobs.append((two, ()))
        if at < len(along):
            jobs.append((both, ()))
        place(order, *jobs)
        if at < len(across):
            two.go(across[-1 - at])
        if at < len(along):
            both.go(along[at])
    lengths = order.turn(lengths[:, 0])
    first_pad = 3 * ((lengths[:, 0] + 2) // 3)
    second_pad = 3 * ((lengths[:, 1] + 2) // 3)
    start = 1 + first_pad
    seats = [lax.axis_index("seq") * each, upper_half(1) if whole else 0, upper_half(1)]
    seats = [jnp.full_like(start, seat) for seat in seats]
    info = [1 + lengths[:, 0], start, start + lengths[:, 1], start + second_pad]
    info = jnp.stack(info + seats, axis=1).astype(jnp.int32)
    order.done((order.last, info))
    one.place()
    one.go(1)
    place(order, (two, ()), (both, (width // 2, width // 2)))
    two.go(1)
    both.go(across[0], across[-1])
    first = one.place().whole()
    first_sizes, rest_sizes = [1] * 5, [1] * (1 + wide) + [wide]
    if not whole:
        dealt = vector_regroup(first[:, 4 * share], GROUPS, vector_lengths)
        dealt = vector_pack(dealt, UNIT, width)
        first = jnp.concatenate([grouped(first, [1] * 4), dealt], axis=1)

    tok = tokens.reshape(all_tokens, width)
    cot = cotangent.reshape(all_tokens, width)
    rows = (all_tokens, width)
    grown = 4 * max(memory_bytes // (1 << 20) - 2, 0)
    limits = [16, 16, 16 + grown, 28, 28 + grown, 28, 28]
    matmul = 2 * all_tokens * width * width

    padded = (all_tokens + micro * RIM, width)
    windows = (3, slots, width)
    line = (pltpu.VMEM((micro, width // 128, RIM + each, 128), F32),)

    normed, keys, key_window, memory_key, vec = kernel(
        key_kernel,
        (info, order.turn(tok), halo, first),
        ((padded, BF16), (rows, BF16), (windows, BF16), ((slots, width), BF16), ((16, width), F32)),
        2 * matmul,
        limits[0],
        line,
    )
    order.done(memory_key)
    keys_side = Gather(order, memory_key)
    keys_side.go(along[0])
    second = grouped(two.place().whole(), first_sizes)
    values, value_window, memory_value = kernel(
        value_kernel,
        (info, normed, second),
        ((rows, BF16), (windows, BF16), ((slots, width), BF16)),
        3 * matmul,
        limits[1],
        line,
    )
    order.done(memory_value)
    values_side = Gather(order, memory_value)
    values_side.go(back[0])
    (query,) = kernel(
        query_kernel, (order.turn(normed), second), ((rows, BF16),), matmul, limits[1]
    )
    order.done(query)
    for at in range(1, max(len(across), len(along))):
        jobs = []
        if at < len(along):
            jobs += [(keys_side, ()), (values_side, ())]
        if at < len(across):
            jobs.append((both, ()))
        place(order, *jobs)
        if at < len(along):
            keys_side.go(along[at])
            values_side.go(back[at])
        if at < len(across):
            both.go(across[at], across[-1 - at])
    place(order, (keys_side, ()), (values_side, ()), (both, (width,)))
    keys_side.go(1)
    values_side.go(1)
    both.go(1)
    memories = [keys_side.place().whole(), values_side.place().whole()]
    attended, stats = kernel(
        attend_kernel,
        (info, order.turn(query), keys, values, *memories),
        ((rows, F32), ((2 * each, 128), F32)),
        4 * matmul,
        limits[2],
    )
    order.done(attended)
    rest = grouped(both.place().whole(), rest_sizes)
    half = GROUPS // 2

    def pieces(size):
        return (((half, UNIT * size, width), BF16),) * 2

    output, grad_mid, grad_att, *halves, vec_grad = kernel(
        feed_kernel,
        (info, order.turn(tok), cot, attended, vec, rest),
        ((rows, BF16), (rows, F32), (rows, BF16)) + pieces(1 + 2 * wide) + (((16, width), F32),),
        27 * matmul,
        limits[3],
    )
    order.done(halves[0])
    all_bits = powers(2, count)[::-1]

    def begin(keep, send, size, by_lanes=False):
        if not whole:
            keep, send = split_cores(scattered(joined(keep, send), size))
        return Reduce(order, keep, send, all_bits, by_lanes)

    feeds = begin(*halves, rest_sizes, True)
    feeds.go(1)
    memory_half = ((seq // 2, slots, width), BF16)
    chips = (seq // 2, 2, slots, width)
    grad_query, *halves, own_key, own_value = kernel(
        attend_back_kernel,
        (
            info,
            order.turn(query),
            keys,
            values,
            memories[0].reshape(chips),
            memories[1].reshape(chips),
            attended,
            stats,
            grad_att,
        ),
        ((rows, BF16),) + (memory_half,) * 4 + ((rows, F32), (rows, F32)),
        10 * matmul,
        limits[4],
    )
    order.done(grad_query)
    keys_side = Reduce(order, *halves[:2], along)
    values_side = Reduce(order, *halves[2:], along)
    keys_side.go(1)
    values_side.go(1)
    cross = [(across[-1 - at], across[at]) for at in range(len(across))]
    keys_side.add((back[0],))
    keys_side.go(back[0])
    cuts = (width // 2, width // 2)
    add(order, (values_side, (along[0],), ()), (feeds, cross[0], cuts))
    values_side.go(along[0])
    feeds.go(*cross[0])
    for at in range(1, max(len(along), len(cross))):
        jobs = []
        if at < len(along):
            keys_side.add((back[at],))
            keys_side.go(back[at])
            jobs.append((values_side, (along[at],), ()))
        if at < len(cross):
            jobs.append((feeds, cross[at], ()))
        add(order, *jobs)
        if at < len(along):
            values_side.go(along[at])
        if at < len(cross):
            feeds.go(*cross[at])
    feeds.add((back[0],), width)
    key_grad, value_grad = (held.total().astype(BF16) for held in (keys_side, values_side))
    key_kept, value_kept, rims, *halves = kernel(
        compress_back_kernel,
        (
            info,
            order.turn(key_grad),
            value_grad,
            key_window,
            value_window,
            first,
            second,
            normed,
            grad_query,
        ),
        ((rows, F32), (rows, F32), ((micro * RIM, 2 * width), F32)) + pieces(7),
        5 * matmul,
        limits[5],
        (pltpu.VMEM((micro, width // 128, each, 128), F32),),
    )
    order.done(rims)
    rims = lax.ppermute(rims, "seq", [(i + 1, i) for i in range(seq - 1)])
    convs = begin(*halves, [1] * 7)
    convs.go(1)
    grad_in, *halves = kernel(
        input_kernel,
        (
            info,
            order.turn(tok),
            normed,
            grad_query,
            key_kept,
            value_kept,
            rims,
            own_key,
            own_value,
            first,
            second,
            vec,
            grad_mid,
            vec_grad,
        ),
        ((rows, BF16),) + pieces(3),
        6 * matmul,
        limits[6],
        (pltpu.VMEM(rows, F32),),
    )
    order.done(grad_in)
    if whole:
        inputs = begin(*halves, [1] * 3)
    else:
        dealt = joined(*halves)
        vectors = dealt[:, 2 * UNIT, : VECTORS * UNIT + ff // GROUPS]
        vectors = vector_regroup(vectors, count, [UNIT] * VECTORS + [ff // GROUPS])
        dealt = [scattered(dealt, [1] * 2), vector_pack(vectors, 2, width)]
        dealt = split_cores(jnp.concatenate(dealt, axis=1))
        inputs = Reduce(order, *dealt, all_bits)
    inputs.go(1)
    line = [masks[1] for masks in cross]
    cuts = (5 * share, 2 * share)
    convs.add(cross[0], *cuts)
    convs.go(*cross[0])
    feeds.go(back[0])
    inputs.add((line[0],))
    inputs.go(line[0])
    for at in range(1, max(len(along), len(cross))):
        jobs = []
        if at < len(cross):
            jobs.append((convs, cross[at], ()))
        if at < len(along):
            jobs.append((feeds, (back[at],), ()))
        add(order, *jobs)
        if at < len(cross):
            convs.go(*cross[at])
        if at < len(along):
            feeds.go(back[at])
        if at < len(cross):
            inputs.add((line[at],))
            inputs.go(line[at])
    rest_total = feeds.total()
    for at in range(len(along)):
        if at == len(along) - 1:
            ups = [rest_total[share * c : share * (c + 1)] for c in range(1, 1 + wide)]
            rest_outs = (rest_total[:share], jnp.concatenate(ups, axis=1))
            rest_outs = rest_outs + (rest_total[share * (1 + wide) :],)
            rest_outs = lax.optimization_barrier(rest_outs)
            order.done(rest_outs)
        convs.add((back[at],), 7 * share)
        convs.go(back[at])
        inputs.add((along[at],))
        inputs.go(along[at])
    convs, late_inputs = convs.total(), inputs.total()
    conv_keys = convs[: 3 * share].reshape(3, share, width)
    conv_values = convs[4 * share :].reshape(3, share, width)

    def own(buffer, number):
        return buffer[share * number : share * (number + 1)]

    vector_row = late_inputs[2 * share]

    def own_vector(number, length=share):
        return vector_row[share * number : share * number + length]

    return (
        output.reshape(tokens.shape),
        grad_in.reshape(tokens.shape),
        own_vector(0),
        own_vector(1),
        own(convs, 3),
        own(late_inputs, 0),
        own(late_inputs, 1),
        conv_keys,
        conv_values,
        rest_outs[0],
        own_vector(2),
        own_vector(3),
        rest_outs[1],
        own_vector(VECTORS, ff // count),
        rest_outs[2],
        own_vector(4),
    )


def solution(mesh):
    rows = P(AXES, None)
    vector = P(AXES)
    conv = P(None, AXES, None)
    part = P(None, "batch", "seq", None)
    weights = (vector, vector, rows, rows, rows, conv, conv, rows, vector, vector)
    weights = weights + (rows, vector, rows, vector)
    return jax.shard_map(
        per_device,
        mesh=mesh,
        in_specs=(part, P(None, "batch", None)) + weights + (part,),
        out_specs=(part, part) + weights,
        check_vma=False,
    )
```
